32 devices in a mesh: dp: 4 (over x, core), expert: 8 (over z, y).
Axes of the slice: x: 2, y: 2, z: 4, core: 2. Of those that a mesh axis runs over, the one named last changes fastest.
Arguments:
- hidden_in: bfloat16 [8, 256, 2048], P('expert', 'dp'), may hold values from -6 to 6
- queries: bfloat16 [8, 256, 2048], P('expert', None, 'dp'), may hold values from -150 to 150
- key_pool: bfloat16 [16, 128, 2048], P('expert', None, 'dp'), may hold values from -8 to 8
- value_pool: bfloat16 [16, 128, 2048], P('expert', None, 'dp'), may hold values from -6 to 6
- page_table: int32 [8, 2], P('expert'), may hold values from 0 to 1, as said below
- prompt_lengths: int32 [8, 4], P('expert'), may hold values from 1 to 128, 256 in all within a row
- expert_ids: int32 [8, 256, 8], P('expert', 'dp'), may hold values from 0 to 7, all different within a row; in each aligned block of 64 rows (0 to 63, 64 to 127, ..., all dimensions but the last counted through in order) at most 64 rows name the same one
- gate_weights: float32 [8, 256, 8], P('expert', 'dp'), may hold values from 0.05 to 0.3
- norm_gain: float32 [2048], replicated, may hold values from 0.5 to 1.5
- trainer_gate_up: float32 [8, 2048, 2048], P('expert', 'dp'), may hold values from -0.125 to 0.125
- trainer_down: float32 [8, 1024, 2048], P('expert', 'dp'), may hold values from -0.1875 to 0.1875
Outputs:
- mixed: bfloat16 [8, 256, 2048], P('expert', 'dp')
The draws below stay inside these ranges and needn't reach their ends.
Inputs may be any that keep to these rules, and one draw needn't show every extreme that they name: `page_table`: each group's row is a permutation of the group's page numbers. `expert_ids`: among the 64 rows of one device (aligned blocks of rows), no expert is named by more than 64 rows, a bound that some block reaches.
All inputs are finite; a program needn't handle non-finite values.
Results may differ from the reference program's by a relative error of at most 0.0075.
Values may be sent and summed in bfloat16 or wider, within the bound.
No kernel may reach another device: no remote copies, remote signals or barrier semaphores. Data moves between devices by JAX's collectives and lax.ppermute only.
A program may use at most 64 MiB of HBM per device.

```python
import math
import jax
import jax.numpy as jnp
import numpy as np
from jax import lax

D = 2048
HEADS = 16
HDIM = 128
FF = 1024
TOPK = 8
PAGE = 128
REQS = 4
T_DEV = 64
EXPERTS = 8
GROUPS = 8
COL_TOK = 256
PAGES_COL = 2
MAXLEN = 128
CAP = 64
N_DP = 4


def shared_draw(key):
    perm_keys = jax.random.split(jax.random.fold_in(key, 101), GROUPS)
    permutations = jax.vmap(lambda sub_key: jax.random.permutation(sub_key, PAGES_COL))(perm_keys).astype(jnp.int32)
    logical = jax.random.normal(jax.random.fold_in(key, 102), (GROUPS, COL_TOK // 2, 2, D), jnp.float32)
    logical = jnp.clip(logical.reshape(GROUPS, COL_TOK, D), -6.0, 6.0)
    return (permutations, logical)


def draw_page_table(key, part):
    permutations, logical = shared_draw(key)
    return permutations


def draw_key_pool(key, part):
    permutations, logical = shared_draw(key)
    page_rows = logical.reshape(GROUPS, PAGES_COL, PAGE, D)
    group_index = jnp.arange(GROUPS, dtype=jnp.int32)[:, None]
    physical = jnp.zeros_like(page_rows).at[group_index, permutations].set(page_rows)
    return physical.reshape(GROUPS * PAGES_COL, PAGE, D).astype(jnp.bfloat16)


def draw_queries(key, part):
    drawn = jnp.clip(jax.random.normal(jax.random.fold_in(key, 104), (GROUPS, COL_TOK, D), jnp.float32), -6.0, 6.0)
    return drawn.astype(jnp.bfloat16)


def level_of(key, dims, cuts, smallest, largest):
    factor_of, own = 1.0, jax.random.fold_in(key, 6)
    for axis_at, parts in cuts:
        heights = jnp.exp(jax.random.uniform(jax.random.fold_in(own, axis_at), (parts,), jnp.float32, smallest / len(cuts), largest / len(cuts)))
        factor_of = factor_of * jnp.repeat(heights, dims[axis_at] // parts).reshape([-1 if axis == axis_at else 1 for axis in range(len(dims))])
    return factor_of


def profile(count, total, most, skew):
    weights = [(1 << 20) // math.isqrt(grade ** skew) + 1 for grade in range(2, count + 1)]
    spare, given = total - most - (count - 1), [1] * (count - 1)
    while spare > 0:
        free = [i for i in range(count - 1) if given[i] < most]
        mass, left = sum([weights[i] for i in free]), spare
        for i in free:
            addition = min(most - given[i], max(1, left * weights[i] // mass), spare)
            given[i] = given[i] + addition
            spare = spare - addition
    return np.array([most] + given)


def uneven(key, count, total, limit, lean):
    if count == 2:
        one = jax.random.randint(key, (), max(1, total - limit), min(limit, total - 1) + 1)
        return jnp.stack([one, total - one])
    sizes = jnp.asarray(profile(count, total, limit, lean), jnp.int32)
    pairs = (count - 1) // 2
    giver, taker = sizes[1:1 + 2 * pairs:2], sizes[2:2 + 2 * pairs:2]
    room = jnp.minimum(giver - 1, limit - taker)
    shifted = jax.random.randint(jax.random.fold_in(key, 1), (pairs,), 0, 1 << 20) % (room + 1)
    sizes = sizes.at[1:1 + 2 * pairs:2].set(giver - shifted).at[2:2 + 2 * pairs:2].set(taker + shifted)
    return sizes[jax.random.permutation(jax.random.fold_in(key, 2), count)]


def routed_block(own_key, own, number, rows, count, top, most, skew):
    sequence = jax.random.permutation(own_key, count)
    packed, usual = load_shares(count, rows * top, most, skew, True), load_shares(count, rows * top, most, skew, False)
    places = jnp.arange(count)

    def named(tallies, turn):
        used = int((tallies > 0).sum())
        fixed = max(1, used // 4)
        passed = fixed + (places - fixed + turn * (used - fixed)) % max(1, count - fixed)
        return jnp.zeros((count,), jnp.int32).at[sequence[jnp.where(places < fixed, places, passed)]].set(jnp.asarray(tallies, jnp.int32))

    tallies = jnp.where(number % 4 == 0, named(packed, number // 4), named(usual, number - number // 4 - 1))
    mixed = jax.random.permutation(jax.random.fold_in(own, 3), count)
    donor, receiver = mixed[0:count // 2 * 2:2], mixed[1:count // 2 * 2:2]
    slack = jnp.minimum(tallies[donor] - 1, most - tallies[receiver]) // 2
    slack = jnp.where((donor == sequence[0]) | (receiver == sequence[0]) | (tallies[receiver] == 0), 0, jnp.maximum(slack, 0))
    passed = jax.random.randint(jax.random.fold_in(own, 4), (count // 2,), 0, 1 << 20) % (slack + 1)
    tallies = tallies.at[donor].add(-passed).at[receiver].add(passed)
    items = jnp.searchsorted(jnp.cumsum(tallies), jnp.arange(rows * top), side="right").astype(jnp.int32)
    listing = items.reshape(top, rows).T
    listing = listing[jax.random.permutation(jax.random.fold_in(own, 1), rows)]
    turn = jax.random.randint(jax.random.fold_in(own, 2), (rows, 1), 0, top)
    return jnp.take_along_axis(listing, (jnp.arange(top)[None, :] + turn) % top, axis=1)


def load_shares(number_of, total, reach, lean, full):
    weights = [(1 << 20) // math.isqrt(rank ** lean) + 1 for rank in range(1, number_of + 1)]
    largest = reach if full else min(reach, max(-(-total // number_of), total * weights[0] // sum(weights)))
    least = 1 if total - largest >= number_of - 1 else 0
    given, spare = [largest] + [least] * (number_of - 1), total - largest - least * (number_of - 1)
    while spare > 0:
        free = [i for i in range(1, number_of) if given[i] < largest] or [i for i in range(1, number_of) if given[i] < reach]
        pool, budget = sum([weights[i] for i in free]), spare
        for i in free:
            extra = min(reach - given[i], max(1, budget * weights[i] // pool), spare)
            given[i] = given[i] + extra
            spare = spare - extra
    return np.array(given)


def gaussian(own_key, extent, deviation, most, shards=(), held_as=jnp.bfloat16):
    entries = jax.random.normal(own_key, extent, jnp.float32) * deviation
    if len(shards) > 0:
        entries = level_of(own_key, extent, shards, -0.22, 0.18) * entries
    return jnp.clip(entries, min=-most, max=most).astype(held_as)


def setup_inputs(seed: int = 0) -> dict:
    keys = jax.random.split(jax.random.key(seed), 12)
    hidden_in = gaussian(keys[0], (GROUPS, COL_TOK, D), 1.0, 6.0, ((0, 8), (1, 4)))
    queries = draw_queries(jax.random.fold_in(keys[11], 71), 0)
    key_pool = draw_key_pool(jax.random.fold_in(keys[11], 71), 0)
    value_pool = gaussian(keys[3], (GROUPS * PAGES_COL, PAGE, D), 1.0, 6.0, ((0, 8), (2, 4)))
    page_table = draw_page_table(jax.random.fold_in(keys[11], 71), 0)
    prompt_lengths = jax.vmap(lambda own: uneven(own, REQS, COL_TOK, MAXLEN, 2))(jax.random.split(keys[5], GROUPS)).reshape((GROUPS, REQS)).astype(jnp.int32)
    expert_ids_keys = jax.random.split(jax.random.fold_in(keys[6], 1), GROUPS * COL_TOK // T_DEV)
    expert_ids_turns = jax.random.permutation(jax.random.fold_in(keys[6], 3), GROUPS * COL_TOK // T_DEV)
    expert_ids = jax.vmap(lambda own, number: routed_block(jax.random.fold_in(keys[6], 2), own, number, T_DEV, EXPERTS, TOPK, CAP, 2))(expert_ids_keys, expert_ids_turns).reshape((GROUPS, COL_TOK, TOPK))
    gate_weights = jnp.clip(0.05 + 0.25 * jax.random.uniform(keys[7], (GROUPS, COL_TOK, TOPK), jnp.float32) ** level_of(keys[7], (GROUPS, COL_TOK, TOPK), ((0, 8), (1, 4)), -0.2, 0.2), 0.05, 0.3)
    norm_gain = jnp.clip(1.0 + 0.1 * jax.random.normal(keys[8], (D,), jnp.float32), 0.5, 1.5)
    trainer_gate_up = gaussian(keys[9], (EXPERTS, D, 2 * FF), D ** -0.5, 0.125, ((0, 8), (1, 4)), jnp.float32)
    trainer_down = gaussian(keys[10], (EXPERTS, FF, D), FF ** -0.5, 0.1875, ((0, 8), (1, 4)), jnp.float32)
    return dict(hidden_in=hidden_in, queries=queries, key_pool=key_pool, value_pool=value_pool, page_table=page_table, prompt_lengths=prompt_lengths, expert_ids=expert_ids, gate_weights=gate_weights, norm_gain=norm_gain, trainer_gate_up=trainer_gate_up, trainer_down=trainer_down)


epsilon = 1e-05

def group_attention(operands):
    group_queries, key_pages, value_pages, table_row, length_row = operands
    keys_all = jnp.take(key_pages, table_row, axis=0).reshape(COL_TOK, HEADS, HDIM).astype(jnp.float32)
    values_all = jnp.take(value_pages, table_row, axis=0).reshape(COL_TOK, HEADS, HDIM).astype(jnp.float32)
    request_ends = jnp.cumsum(length_row).astype(jnp.int32)
    positions = jnp.arange(COL_TOK, dtype=jnp.int32)
    request = lax.optimization_barrier(jnp.sum((positions[:, None] >= request_ends[None, :]).astype(jnp.int32), axis=1))
    block_rows = math.gcd(COL_TOK, 512)
    query_blocks = group_queries.reshape(COL_TOK // block_rows, block_rows, HEADS, HDIM)
    request_blocks = request.reshape(COL_TOK // block_rows, block_rows)
    score_scale = 1.0 / math.sqrt(HDIM)

    def attend(pieces):
        query_block, request_block = pieces
        scores = jnp.einsum('qhd,khd->hqk', query_block.astype(jnp.float32), keys_all) * score_scale
        same_request = (request_block[:, None] == request[None, :])[None]
        scores = jnp.where(same_request, scores, -1e+30)
        highest = lax.optimization_barrier(jnp.max(scores, axis=-1, keepdims=True))
        weights = jnp.where(same_request, jnp.exp(scores - highest), 0.0)
        totals = lax.optimization_barrier(jnp.sum(weights, axis=-1, keepdims=True))
        probs = (weights / totals).astype(jnp.bfloat16)
        output = jnp.einsum('hqk,khd->qhd', probs.astype(jnp.float32), values_all)
        return output.astype(jnp.bfloat16).reshape(block_rows, HEADS * HDIM)
    return lax.map(attend, (query_blocks, request_blocks)).reshape(COL_TOK, HEADS * HDIM)

def reference(hidden_in, queries, key_pool, value_pool, page_table, prompt_lengths, expert_ids, gate_weights, norm_gain, trainer_gate_up, trainer_down):
    server_gate_up = trainer_gate_up.astype(jnp.bfloat16)
    server_down = trainer_down.astype(jnp.bfloat16)
    key_pages = key_pool.reshape(GROUPS, PAGES_COL, PAGE, D)
    value_pages = value_pool.reshape(GROUPS, PAGES_COL, PAGE, D)
    attn = lax.map(group_attention, (queries, key_pages, value_pages, page_table, prompt_lengths))
    resid = (hidden_in.astype(jnp.float32) + attn.astype(jnp.float32)).astype(jnp.bfloat16)
    resid32 = resid.astype(jnp.float32)
    mean_square = lax.optimization_barrier(jnp.mean(resid32 * resid32, axis=-1, keepdims=True))
    normed = (resid32 * lax.rsqrt(mean_square + epsilon) * norm_gain).astype(jnp.bfloat16)
    token_count = GROUPS * COL_TOK
    normed_flat = normed.reshape(token_count, D)
    ids_flat = expert_ids.reshape(token_count * TOPK).astype(jnp.int32)
    weights_flat = gate_weights.reshape(token_count * TOPK)
    order = jnp.argsort(ids_flat, stable=True).astype(jnp.int32)
    counts = lax.optimization_barrier(jnp.sum((ids_flat[:, None] == jnp.arange(EXPERTS, dtype=jnp.int32)[None, :]).astype(jnp.int32), axis=0))
    starts = (jnp.cumsum(counts) - counts).astype(jnp.int32)
    bound = CAP * GROUPS * N_DP
    padded_order = jnp.concatenate([order, jnp.zeros((bound,), jnp.int32)])

    def per_expert(running, expert):
        copy_index = lax.dynamic_slice_in_dim(padded_order, starts[expert], bound)
        valid = jnp.arange(bound, dtype=jnp.int32) < counts[expert]
        token_index = (copy_index // TOPK).astype(jnp.int32)
        slot_rows = jnp.take(normed_flat, token_index, axis=0)
        gate_up = jnp.dot(slot_rows, server_gate_up[expert], preferred_element_type=jnp.float32)
        hidden_units = (jax.nn.silu(gate_up[:, :FF]) * gate_up[:, FF:]).astype(jnp.bfloat16)
        outputs = jnp.dot(hidden_units, server_down[expert], preferred_element_type=jnp.float32).astype(jnp.bfloat16)
        weight_col = jnp.where(valid, jnp.take(weights_flat, copy_index), 0.0)
        running = running.at[token_index].add(outputs.astype(jnp.float32) * weight_col[:, None])
        return (running, None)
    mixture, unused = lax.scan(per_expert, jnp.zeros((token_count, D), jnp.float32), jnp.arange(EXPERTS, dtype=jnp.int32))
    mixed = resid32.reshape(token_count, D) + mixture
    return mixed.astype(jnp.bfloat16).reshape(GROUPS, COL_TOK, D)
```

```python
import math

import jax
import jax.numpy as jnp
from jax import lax
from jax.sharding import PartitionSpec as P

HDIM = 128
TOPK = 8


epsilon = 1e-05


def fetch_weights(trainer_gate_up, trainer_down):
    return (
        lax.all_gather(trainer_gate_up.astype(jnp.bfloat16), "dp", axis=1, tiled=True),
        lax.all_gather(trainer_down.astype(jnp.bfloat16), "dp", axis=1, tiled=True),
    )


def every_expert(normed, expert_ids, gate_weights, gate_up_weights, down_weights):
    expert_count = lax.axis_size("expert")
    experts = lax.iota(jnp.int32, expert_count)
    chosen = expert_ids[:, :, None] == experts[None, None, :]
    gates = jnp.sum(jnp.where(chosen, gate_weights[:, :, None], 0.0), axis=1)
    gates_all = lax.all_gather(gates, "expert", axis=0, tiled=True)
    own = experts == lax.axis_index("expert")
    own_gates = jnp.sum(jnp.where(own[None, :], gates_all, 0.0), axis=1, keepdims=True)
    rows = lax.all_gather(normed, "expert", axis=0, tiled=True)
    gate_up = jnp.dot(rows, gate_up_weights, preferred_element_type=jnp.float32)
    hidden_size = gate_up.shape[1] // 2
    hidden_units = (jax.nn.silu(gate_up[:, :hidden_size]) * gate_up[:, hidden_size:]).astype(
        jnp.bfloat16
    )
    outputs = jnp.dot(hidden_units, down_weights, preferred_element_type=jnp.float32)
    weighted = (outputs * own_gates).astype(jnp.bfloat16)
    return lax.psum_scatter(weighted, "expert", scatter_dimension=0, tiled=True).astype(jnp.float32)


def local(
    hidden_in,
    queries,
    key_pool,
    value_pool,
    page_table,
    prompt_lengths,
    expert_ids,
    gate_weights,
    norm_gain,
    trainer_gate_up,
    trainer_down,
):
    col_tok = queries.shape[1]
    width_dev = queries.shape[2]
    heads_dev = width_dev // HDIM
    keys_all = jnp.take(key_pool, page_table[0], axis=0).reshape(col_tok, heads_dev, HDIM)
    values_all = jnp.take(value_pool, page_table[0], axis=0).reshape(col_tok, heads_dev, HDIM)
    request_ends = jnp.cumsum(prompt_lengths[0])
    positions = lax.iota(jnp.int32, col_tok)
    request = jnp.sum((positions[:, None] >= request_ends[None, :]).astype(jnp.int32), axis=1)
    block_rows = math.gcd(col_tok, 512)
    query_blocks = queries[0].reshape(col_tok // block_rows, block_rows, heads_dev, HDIM)
    request_blocks = request.reshape(col_tok // block_rows, block_rows)
    score_scale = 1.0 / math.sqrt(HDIM)

    def attend(pieces):
        query_block, request_block = pieces
        scores = (
            jnp.einsum("qhd,khd->hqk", query_block, keys_all, preferred_element_type=jnp.float32)
            * score_scale
        )
        same_request = (request_block[:, None] == request[None, :])[None]
        scores = jnp.where(same_request, scores, -1e30)
        highest = jnp.max(scores, axis=-1, keepdims=True)
        weights = jnp.where(same_request, jnp.exp(scores - highest), 0.0)
        totals = jnp.sum(weights, axis=-1, keepdims=True)
        probs = (weights / totals).astype(jnp.bfloat16)
        output = jnp.einsum("hqk,khd->qhd", probs, values_all, preferred_element_type=jnp.float32)
        return output.astype(jnp.bfloat16).reshape(block_rows, width_dev)

    attn_heads = lax.map(attend, (query_blocks, request_blocks)).reshape(1, col_tok, width_dev)
    attn_tokens = lax.all_to_all(attn_heads, "dp", split_axis=1, concat_axis=2, tiled=True)
    resid32 = (
        (hidden_in.astype(jnp.float32) + attn_tokens.astype(jnp.float32))
        .astype(jnp.bfloat16)
        .astype(jnp.float32)
    )
    mean_square = jnp.mean(resid32 * resid32, axis=-1, keepdims=True)
    normed = (resid32 * lax.rsqrt(mean_square + epsilon) * norm_gain).astype(jnp.bfloat16)
    server_gate_up, server_down = fetch_weights(trainer_gate_up, trainer_down)
    token_rows = normed.shape[1]
    width = normed.shape[2]
    expert_count = lax.axis_size("expert")
    if expert_count == TOPK:
        mixture = every_expert(
            normed[0], expert_ids[0], gate_weights[0], server_gate_up[0], server_down[0]
        )
        return (resid32[0] + mixture).astype(jnp.bfloat16)[None]
    capacity = min(token_rows, token_rows * TOPK * 5 // (4 * expert_count))
    hidden_size = server_gate_up.shape[2] // 2
    ids_flat = expert_ids[0].reshape(token_rows * TOPK)
    onehot = (ids_flat[:, None] == lax.iota(jnp.int32, expert_count)[None, :]).astype(jnp.int32)
    earlier = jnp.cumsum(onehot, axis=0) - onehot
    slot_index = jnp.sum(earlier * onehot, axis=1)
    flat_slot = ids_flat * capacity + slot_index
    placement = (
        flat_slot[:, None] == lax.iota(jnp.int32, expert_count * capacity)[None, :]
    ).astype(jnp.bfloat16)
    dispatch_matrix = jnp.sum(placement.reshape(token_rows, TOPK, expert_count * capacity), axis=1)
    outgoing = jnp.einsum(
        "ts,td->sd", dispatch_matrix, normed[0], preferred_element_type=jnp.float32
    )
    outgoing = outgoing.astype(jnp.bfloat16).reshape(expert_count, capacity, width)
    received = lax.all_to_all(outgoing, "expert", split_axis=0, concat_axis=0, tiled=True)
    sources, items, features = received.shape
    slot_rows = received.reshape(sources * items, features)
    gate_up = jnp.dot(slot_rows, server_gate_up[0], preferred_element_type=jnp.float32)
    hidden_units = (jax.nn.silu(gate_up[:, :hidden_size]) * gate_up[:, hidden_size:]).astype(
        jnp.bfloat16
    )
    outputs = jnp.dot(hidden_units, server_down[0], preferred_element_type=jnp.float32).astype(
        jnp.bfloat16
    )
    returned = lax.all_to_all(
        outputs.reshape(sources, items, features), "expert", split_axis=0, concat_axis=0, tiled=True
    )
    copies = jnp.take(returned.reshape(expert_count * capacity, width), flat_slot, axis=0)
    copies = copies.reshape(token_rows, TOPK, width).astype(jnp.float32)
    mixture = jnp.einsum("tk,tkd->td", gate_weights[0], copies)
    mixed = resid32[0] + mixture
    return mixed.astype(jnp.bfloat16)[None]


def solution(mesh):
    placed = (
        P("expert", "dp", None),
        P("expert", None, "dp"),
        P("expert", None, "dp"),
        P("expert", None, "dp"),
        P("expert", None),
        P("expert", None),
        P("expert", "dp", None),
        P("expert", "dp", None),
        P(),
        P("expert", "dp", None),
        P("expert", "dp", None),
    )
    return jax.shard_map(
        local, mesh=mesh, in_specs=placed, out_specs=P("expert", "dp", None), check_vma=False
    )
```

```python
import math

import jax
import jax.numpy as jnp
from jax import lax
from jax.experimental import pallas as pl
from jax.experimental.pallas import tpu as pltpu
from jax.sharding import PartitionSpec as P

HDIM = 128
TOPK = 8


epsilon = 1e-05


def fetch_weights(trainer_gate_up, trainer_down):
    return (
        lax.all_gather(trainer_gate_up.astype(jnp.bfloat16), "dp", axis=1, tiled=True),
        lax.all_gather(trainer_down.astype(jnp.bfloat16), "dp", axis=1, tiled=True),
    )


def local(
    hidden_in,
    queries,
    key_pool,
    value_pool,
    page_table,
    prompt_lengths,
    expert_ids,
    gate_weights,
    norm_gain,
    trainer_gate_up,
    trainer_down,
):
    col_tok = queries.shape[1]
    width_dev = queries.shape[2]
    heads_dev = width_dev // HDIM
    keys_all = jnp.take(key_pool, page_table[0], axis=0).reshape(col_tok, heads_dev, HDIM)
    values_all = jnp.take(value_pool, page_table[0], axis=0).reshape(col_tok, heads_dev, HDIM)
    request_ends = jnp.cumsum(prompt_lengths[0])
    positions = lax.iota(jnp.int32, col_tok)
    request = jnp.sum((positions[:, None] >= request_ends[None, :]).astype(jnp.int32), axis=1)
    block_rows = math.gcd(col_tok, 512)
    query_blocks = queries[0].reshape(col_tok // block_rows, block_rows, heads_dev, HDIM)
    request_blocks = request.reshape(col_tok // block_rows, block_rows)
    score_scale = 1.0 / math.sqrt(HDIM)

    def attend(pieces):
        query_block, request_block = pieces
        scores = (
            jnp.einsum("qhd,khd->hqk", query_block, keys_all, preferred_element_type=jnp.float32)
            * score_scale
        )
        same_request = (request_block[:, None] == request[None, :])[None]
        scores = jnp.where(same_request, scores, -1e30)
        highest = jnp.max(scores, axis=-1, keepdims=True)
        weights = jnp.where(same_request, jnp.exp(scores - highest), 0.0)
        totals = jnp.sum(weights, axis=-1, keepdims=True)
        probs = (weights / totals).astype(jnp.bfloat16)
        output = jnp.einsum("hqk,khd->qhd", probs, values_all, preferred_element_type=jnp.float32)
        return output.astype(jnp.bfloat16).reshape(block_rows, width_dev)

    attn_heads = lax.map(attend, (query_blocks, request_blocks)).reshape(1, col_tok, width_dev)
    attn_tokens = lax.all_to_all(attn_heads, "dp", split_axis=1, concat_axis=2, tiled=True)
    resid32 = (
        (hidden_in.astype(jnp.float32) + attn_tokens.astype(jnp.float32))
        .astype(jnp.bfloat16)
        .astype(jnp.float32)
    )
    mean_square = jnp.mean(resid32 * resid32, axis=-1, keepdims=True)
    normed = (resid32 * lax.rsqrt(mean_square + epsilon) * norm_gain).astype(jnp.bfloat16)
    server_gate_up, server_down = fetch_weights(trainer_gate_up, trainer_down)
    token_rows = normed.shape[1]
    width = normed.shape[2]
    expert_count = lax.axis_size("expert")
    capacity = min(token_rows, token_rows * TOPK * 5 // (4 * expert_count))
    hidden_size = server_gate_up.shape[2] // 2
    ids_flat = expert_ids[0].reshape(token_rows * TOPK)
    onehot = (ids_flat[:, None] == lax.iota(jnp.int32, expert_count)[None, :]).astype(jnp.int32)
    earlier = jnp.cumsum(onehot, axis=0) - onehot
    slot_index = jnp.sum(earlier * onehot, axis=1)
    flat_slot = ids_flat * capacity + slot_index
    placement = (
        flat_slot[:, None] == lax.iota(jnp.int32, expert_count * capacity)[None, :]
    ).astype(jnp.bfloat16)
    dispatch_matrix = jnp.sum(placement.reshape(token_rows, TOPK, expert_count * capacity), axis=1)
    outgoing = jnp.einsum(
        "ts,td->sd", dispatch_matrix, normed[0], preferred_element_type=jnp.float32
    )
    outgoing = outgoing.astype(jnp.bfloat16).reshape(expert_count, capacity, width)
    received = lax.all_to_all(outgoing, "expert", split_axis=0, concat_axis=0, tiled=True)
    sources, items, features = received.shape
    slot_rows = received.reshape(sources * items, features)
    gate_up = jnp.dot(slot_rows, server_gate_up[0], preferred_element_type=jnp.float32)
    hidden_units = (jax.nn.silu(gate_up[:, :hidden_size]) * gate_up[:, hidden_size:]).astype(
        jnp.bfloat16
    )
    outputs = jnp.dot(hidden_units, server_down[0], preferred_element_type=jnp.float32).astype(
        jnp.bfloat16
    )
    returned = lax.all_to_all(
        outputs.reshape(sources, items, features), "expert", split_axis=0, concat_axis=0, tiled=True
    )
    copies = jnp.take(returned.reshape(expert_count * capacity, width), flat_slot, axis=0)
    copies = copies.reshape(token_rows, TOPK, width).astype(jnp.float32)
    mixture = jnp.einsum("tk,tkd->td", gate_weights[0], copies)
    mixed = resid32[0] + mixture
    return mixed.astype(jnp.bfloat16)[None]

LANES = 128
VMEM_LIMIT = 48 * 2**20
ROW_PIECES = 4
COLUMN_PIECES = 4


def params():
    return pltpu.CompilerParams(vmem_limit_bytes=VMEM_LIMIT)


def vmem(count):
    return [pl.BlockSpec(memory_space=pltpu.VMEM)] * count


def attention_kernel(table, lengths, q_ref, k_ref, v_ref, *refs):
    outs, attn = refs[:4], refs[4]
    tokens, width = q_ref.shape
    pages, page = k_ref.shape[0], k_ref.shape[1]
    row = lax.broadcasted_iota(jnp.int32, (tokens, tokens), 0)
    column = lax.broadcasted_iota(jnp.int32, (tokens, tokens), 1)
    row_request = jnp.zeros((tokens, tokens), jnp.int32)
    column_request = jnp.zeros((tokens, tokens), jnp.int32)
    end = jnp.int32(0)
    for r in range(lengths.shape[1]):
        end = end + lengths[0, r]
        row_request += (row >= end).astype(jnp.int32)
        column_request += (column >= end).astype(jnp.int32)
    same = row_request == column_request
    for h in range(width // HDIM):
        lanes = slice(h * HDIM, (h + 1) * HDIM)
        keys = jnp.concatenate([k_ref[table[0, p], :, lanes] for p in range(pages)], axis=0)
        values = jnp.concatenate([v_ref[table[0, p], :, lanes] for p in range(pages)], axis=0)
        scores = lax.dot_general(
            q_ref[:, lanes], keys, (((1,), (1,)), ((), ())), preferred_element_type=jnp.float32
        ) * (1.0 / math.sqrt(HDIM))
        scores = jnp.where(same, scores, -1e30)
        highest = jnp.max(scores, axis=-1, keepdims=True)
        weights = jnp.where(same, jnp.exp(scores - highest), 0.0)
        probs = (weights / jnp.sum(weights, axis=-1, keepdims=True)).astype(jnp.bfloat16)
        attn[:, lanes] = jnp.dot(probs, values, preferred_element_type=jnp.float32).astype(
            jnp.bfloat16
        )
    own = lax.axis_index("dp")
    rows = tokens // 4
    for d in range(4):
        first = pl.multiple_of((own ^ d) * rows, rows)
        outs[d][...] = attn[pl.ds(first, rows), :]


def attention(queries, key_pool, value_pool, page_table, prompt_lengths):
    tokens, width = queries.shape
    smem = [pl.BlockSpec(memory_space=pltpu.SMEM)] * 2
    return pl.pallas_call(
        attention_kernel,
        out_shape=[jax.ShapeDtypeStruct((tokens // 4, width), jnp.bfloat16)] * 4,
        in_specs=smem + vmem(3),
        out_specs=vmem(4),
        scratch_shapes=[pltpu.VMEM((tokens, width), jnp.bfloat16)],
        compiler_params=params(),
        name="attention",
    )(page_table, prompt_lengths, queries, key_pool, value_pool)


def norm_kernel(hidden_ref, a0, a1, a2, a3, gain_ref, ids_ref, gates_ref, resid_ref, rows_ref):
    own = lax.axis_index("dp")
    tokens, width = hidden_ref.shape
    block = width // 4
    total = jnp.zeros((tokens, 1), jnp.float32)
    for d, attn in enumerate((a0, a1, a2, a3)):
        columns = pl.ds(pl.multiple_of((own ^ d) * block, block), block)
        resid = (
            hidden_ref[:, columns].astype(jnp.float32) + attn[...].astype(jnp.float32)
        ).astype(jnp.bfloat16)
        resid_ref[:, columns] = resid
        resid32 = resid.astype(jnp.float32)
        total += jnp.sum(resid32 * resid32, axis=-1, keepdims=True)
    inverse = lax.rsqrt(total / width + epsilon)
    for d in range(4):
        columns = pl.ds(pl.multiple_of((own ^ d) * block, block), block)
        rows_ref[:, d * block : (d + 1) * block] = (
            resid_ref[:, columns].astype(jnp.float32) * inverse * gain_ref[:, columns]
        ).astype(jnp.bfloat16)
    lane = lax.broadcasted_iota(jnp.int32, (tokens, LANES), 1)
    gates = jnp.zeros((tokens, LANES), jnp.float32)
    for k in range(TOPK):
        gates += jnp.where(ids_ref[:, k : k + 1] == lane % TOPK, gates_ref[:, k : k + 1], 0.0)
    high = gates.astype(jnp.bfloat16).astype(jnp.float32)
    middle = (gates - high).astype(jnp.bfloat16).astype(jnp.float32)
    low = gates - high - middle
    part = lane // TOPK
    terms = jnp.where(part == 0, high, jnp.where(part == 1, middle, jnp.where(part == 2, low, 0.0)))
    rows_ref[:, width:] = terms.astype(jnp.bfloat16)


def norm(hidden_in, attn, norm_gain, expert_ids, gate_weights):
    tokens, width = hidden_in.shape
    return pl.pallas_call(
        norm_kernel,
        out_shape=[
            jax.ShapeDtypeStruct((tokens, width), jnp.bfloat16),
            jax.ShapeDtypeStruct((tokens, width + LANES), jnp.bfloat16),
        ],
        in_specs=vmem(8),
        out_specs=vmem(2),
        compiler_params=params(),
        name="norm",
    )(hidden_in, *attn, norm_gain[None, :], expert_ids, gate_weights)


def up_kernel(sources, pieces, *refs):
    row_refs = refs[:sources]
    gate_refs = refs[sources : sources + 4 * pieces]
    up_refs = refs[sources + 4 * pieces : sources + 8 * pieces]
    hidden_ref, own_gate_ref, rows, units = refs[sources + 8 * pieces :]
    step = pl.program_id(0)
    width = rows.shape[1]
    depth = width // (4 * pieces)

    @pl.when(step == 0)
    def _():
        expert = lax.axis_index("expert")
        first = 0
        for ref in row_refs:
            count = ref.shape[0]
            rows[first : first + count, :] = ref[:, :width]
            terms = ref[:, width:].astype(jnp.float32)
            lane = lax.broadcasted_iota(jnp.int32, terms.shape, 1)
            own_gate_ref[first : first + count, :] = jnp.sum(
                jnp.where(lane % TOPK == expert, terms, 0.0), axis=-1, keepdims=True
            )
            first += count

    def product(weights):
        total = None
        for i, ref in enumerate(weights):
            term = jnp.dot(
                rows[:, i * depth : (i + 1) * depth], ref[...], preferred_element_type=jnp.float32
            )
            total = term if total is None else total + term
        return total

    gate = product(gate_refs)
    up = product(up_refs)
    units[step] = (gate / (1.0 + jnp.exp(-gate)) * up).astype(jnp.bfloat16)

    @pl.when(step == pl.num_programs(0) - 1)
    def _():
        own = lax.axis_index("dp")
        block = units.shape[2]
        for d in range(4):
            hidden_ref[:, d * block : (d + 1) * block] = units[own ^ d]


def expert_up(rows, weights, hidden_size):
    tokens = sum(piece.shape[0] for piece in rows)
    width = weights[0].shape[1]
    depth = weights[0].shape[0]
    features = depth * len(weights)
    block = hidden_size // 4
    pieces = len(weights) // 4
    whole = [
        pl.BlockSpec(piece.shape, lambda i: (0, 0), pipeline_mode=pl.Buffered(1)) for piece in rows
    ]
    gate = [pl.BlockSpec((depth, block), lambda i: (0, i))] * len(weights)
    up = [pl.BlockSpec((depth, block), lambda i: (0, i + 4))] * len(weights)
    return pl.pallas_call(
        lambda *refs: up_kernel(len(rows), pieces, *refs),
        grid=(4,),
        out_shape=[
            jax.ShapeDtypeStruct((tokens, hidden_size), jnp.bfloat16),
            jax.ShapeDtypeStruct((tokens, 1), jnp.float32),
        ],
        in_specs=whole + gate + up,
        out_specs=[
            pl.BlockSpec((tokens, hidden_size), lambda i: (0, 0)),
            pl.BlockSpec((tokens, 1), lambda i: (0, 0)),
        ],
        scratch_shapes=[
            pltpu.VMEM((tokens, features), jnp.bfloat16),
            pltpu.VMEM((4, tokens, block), jnp.bfloat16),
        ],
        compiler_params=params(),
        cost_estimate=pl.CostEstimate(
            flops=2 * tokens * features * width,
            bytes_accessed=2 * features * width,
            transcendentals=0,
        ),
        name="expert_up",
    )(*rows, *weights, *weights)


def down_kernel(hidden_ref, gate_ref, w0, w1, w2, w3, out_ref, left_ref, right_ref):
    block = w0.shape[0]
    total = None
    for d, ref in enumerate((w0, w1, w2, w3)):
        term = jnp.dot(
            hidden_ref[:, d * block : (d + 1) * block],
            ref[...],
            preferred_element_type=jnp.float32,
        )
        total = term if total is None else total + term
    weighted = (total * gate_ref[...]).astype(jnp.bfloat16)
    sources, rows, width = out_ref.shape
    out_ref[...] = weighted.reshape(sources, rows, width)
    middle, half = sources // 2 * rows, rows // 2
    left_ref[...] = weighted[middle : middle + half]
    right_ref[...] = weighted[middle + half : middle + rows]


def expert_down(hidden_units, gates, weights, sources):
    tokens, hidden_size = hidden_units.shape
    width = weights[0].shape[1]
    rows = tokens // sources
    return pl.pallas_call(
        down_kernel,
        out_shape=[
            jax.ShapeDtypeStruct((sources, rows, width), jnp.bfloat16),
            jax.ShapeDtypeStruct((rows // 2, width), jnp.bfloat16),
            jax.ShapeDtypeStruct((rows // 2, width), jnp.bfloat16),
        ],
        in_specs=vmem(6),
        out_specs=vmem(3),
        compiler_params=params(),
        cost_estimate=pl.CostEstimate(
            flops=2 * tokens * hidden_size * width,
            bytes_accessed=2 * (hidden_size * width + tokens * hidden_size + tokens * width),
            transcendentals=0,
        ),
        name="expert_down",
    )(hidden_units, gates, *weights)


def partner(x, distance):
    return lax.ppermute(x, "dp", [(i, i ^ distance) for i in range(4)])


def ring_order(count):
    return list(range(0, count, 2)) + list(range(count - 1, 0, -2))


def around(x, step):
    ring = ring_order(lax.axis_size("expert"))
    count = len(ring)
    return lax.ppermute(x, "expert", [(ring[i], ring[(i + step) % count]) for i in range(count)])


def after(x, *others):
    return lax.optimization_barrier((x, *others))[0]


def add(a, b):
    return (a.astype(jnp.float32) + b.astype(jnp.float32)).astype(jnp.bfloat16)


def gather_rows(rows):
    half = rows.shape[0] // 2
    reach = lax.axis_size("expert") // 2
    above, below = [rows], [rows]
    for _ in range(reach - 1):
        above.append(around(above[-1], -1))
        below.append(around(below[-1], 1))
    far = [around(above[-1][:half], -1), around(below[-1][half:], 1)]
    return above + far + below[:0:-1]


def scatter_sum(weighted, left, right):
    sources, rows, _ = weighted.shape
    half = rows // 2
    reach = sources // 2
    up, down = around(left, 1), around(right, -1)
    up = jnp.concatenate([add(weighted[reach - 1, :half], up), weighted[reach - 1, half:]])
    down = jnp.concatenate([weighted[reach + 1, :half], add(weighted[reach + 1, half:], down)])
    for away in range(reach - 2, 0, -1):
        up = add(weighted[away], around(up, 1))
        down = add(weighted[sources - away], around(down, -1))
    return weighted[0], around(up, 1), around(down, -1)


def every_expert(
    hidden_in,
    queries,
    key_pool,
    value_pool,
    page_table,
    prompt_lengths,
    expert_ids,
    gate_weights,
    norm_gain,
    trainer_gate_up,
    trainer_down,
):
    depth = trainer_gate_up.shape[1] // ROW_PIECES
    slab = trainer_down.shape[2] // COLUMN_PIECES
    up_own = [
        trainer_gate_up[0, i * depth : (i + 1) * depth].astype(jnp.bfloat16)
        for i in range(ROW_PIECES)
    ]
    down_own = [
        trainer_down[0, :, i * slab : (i + 1) * slab].astype(jnp.bfloat16)
        for i in range(COLUMN_PIECES)
    ]
    across = []
    for i, piece in enumerate(up_own + down_own):
        if i >= 2:
            piece = after(piece, across[i - 2])
        across.append(partner(piece, 2))
    beside = [partner(piece, 1) for piece in up_own + down_own]
    opposite = [partner(piece, 1) for piece in across]

    attn = attention(queries[0], key_pool, value_pool, page_table, prompt_lengths)
    attn = [attn[0]] + [partner(attn[d], d) for d in (1, 2, 3)]
    resid, rows = norm(hidden_in[0], attn, norm_gain, expert_ids[0], gate_weights[0])
    gathered = gather_rows(rows)
    up_weights = (
        up_own + beside[:ROW_PIECES] + across[:ROW_PIECES] + opposite[:ROW_PIECES]
    )
    hidden_units, gates = expert_up(gathered, up_weights, trainer_gate_up.shape[2] // 2)
    slabs = []
    for i in range(COLUMN_PIECES):
        at = ROW_PIECES + i
        weighted = expert_down(
            hidden_units,
            gates,
            (down_own[i], beside[at], across[at], opposite[at]),
            lax.axis_size("expert"),
        )
        own, up, down = scatter_sum(*weighted)
        slabs.append(
            (
                resid[:, i * slab : (i + 1) * slab].astype(jnp.float32)
                + own.astype(jnp.float32)
                + up.astype(jnp.float32)
                + down.astype(jnp.float32)
            ).astype(jnp.bfloat16)
        )
    return jnp.concatenate(slabs, axis=1)[None]


def solution(mesh):
    placed = (
        P("expert", "dp", None),
        P("expert", None, "dp"),
        P("expert", None, "dp"),
        P("expert", None, "dp"),
        P("expert", None),
        P("expert", None),
        P("expert", "dp", None),
        P("expert", "dp", None),
        P(),
        P("expert", "dp", None),
        P("expert", "dp", None),
    )
    dense = mesh.shape["expert"] == TOPK and mesh.shape["dp"] == 4
    return jax.shard_map(
        every_expert if dense else local, mesh=mesh, in_specs=placed, out_specs=P("expert", "dp", None), check_vma=False
    )
```

```python
import math

import jax
import jax.numpy as jnp
from jax import lax
from jax.experimental import pallas as pl
from jax.experimental.pallas import tpu as pltpu
from jax.sharding import PartitionSpec as P

HDIM = 128
TOPK = 8


epsilon = 1e-05


def fetch_weights(trainer_gate_up, trainer_down):
    return (
        lax.all_gather(trainer_gate_up.astype(jnp.bfloat16), "dp", axis=1, tiled=True),
        lax.all_gather(trainer_down.astype(jnp.bfloat16), "dp", axis=1, tiled=True),
    )


def local(
    hidden_in,
    queries,
    key_pool,
    value_pool,
    page_table,
    prompt_lengths,
    expert_ids,
    gate_weights,
    norm_gain,
    trainer_gate_up,
    trainer_down,
):
    col_tok = queries.shape[1]
    width_dev = queries.shape[2]
    heads_dev = width_dev // HDIM
    keys_all = jnp.take(key_pool, page_table[0], axis=0).reshape(col_tok, heads_dev, HDIM)
    values_all = jnp.take(value_pool, page_table[0], axis=0).reshape(col_tok, heads_dev, HDIM)
    request_ends = jnp.cumsum(prompt_lengths[0])
    positions = lax.iota(jnp.int32, col_tok)
    request = jnp.sum((positions[:, None] >= request_ends[None, :]).astype(jnp.int32), axis=1)
    block_rows = math.gcd(col_tok, 512)
    query_blocks = queries[0].reshape(col_tok // block_rows, block_rows, heads_dev, HDIM)
    request_blocks = request.reshape(col_tok // block_rows, block_rows)
    score_scale = 1.0 / math.sqrt(HDIM)

    def attend(pieces):
        query_block, request_block = pieces
        scores = (
            jnp.einsum("qhd,khd->hqk", query_block, keys_all, preferred_element_type=jnp.float32)
            * score_scale
        )
        same_request = (request_block[:, None] == request[None, :])[None]
        scores = jnp.where(same_request, scores, -1e30)
        highest = jnp.max(scores, axis=-1, keepdims=True)
        weights = jnp.where(same_request, jnp.exp(scores - highest), 0.0)
        totals = jnp.sum(weights, axis=-1, keepdims=True)
        probs = (weights / totals).astype(jnp.bfloat16)
        output = jnp.einsum("hqk,khd->qhd", probs, values_all, preferred_element_type=jnp.float32)
        return output.astype(jnp.bfloat16).reshape(block_rows, width_dev)

    attn_heads = lax.map(attend, (query_blocks, request_blocks)).reshape(1, col_tok, width_dev)
    attn_tokens = lax.all_to_all(attn_heads, "dp", split_axis=1, concat_axis=2, tiled=True)
    resid32 = (
        (hidden_in.astype(jnp.float32) + attn_tokens.astype(jnp.float32))
        .astype(jnp.bfloat16)
        .astype(jnp.float32)
    )
    mean_square = jnp.mean(resid32 * resid32, axis=-1, keepdims=True)
    normed = (resid32 * lax.rsqrt(mean_square + epsilon) * norm_gain).astype(jnp.bfloat16)
    server_gate_up, server_down = fetch_weights(trainer_gate_up, trainer_down)
    token_rows = normed.shape[1]
    width = normed.shape[2]
    expert_count = lax.axis_size("expert")
    capacity = min(token_rows, token_rows * TOPK * 5 // (4 * expert_count))
    hidden_size = server_gate_up.shape[2] // 2
    ids_flat = expert_ids[0].reshape(token_rows * TOPK)
    onehot = (ids_flat[:, None] == lax.iota(jnp.int32, expert_count)[None, :]).astype(jnp.int32)
    earlier = jnp.cumsum(onehot, axis=0) - onehot
    slot_index = jnp.sum(earlier * onehot, axis=1)
    flat_slot = ids_flat * capacity + slot_index
    placement = (
        flat_slot[:, None] == lax.iota(jnp.int32, expert_count * capacity)[None, :]
    ).astype(jnp.bfloat16)
    dispatch_matrix = jnp.sum(placement.reshape(token_rows, TOPK, expert_count * capacity), axis=1)
    outgoing = jnp.einsum(
        "ts,td->sd", dispatch_matrix, normed[0], preferred_element_type=jnp.float32
    )
    outgoing = outgoing.astype(jnp.bfloat16).reshape(expert_count, capacity, width)
    received = lax.all_to_all(outgoing, "expert", split_axis=0, concat_axis=0, tiled=True)
    sources, items, features = received.shape
    slot_rows = received.reshape(sources * items, features)
    gate_up = jnp.dot(slot_rows, server_gate_up[0], preferred_element_type=jnp.float32)
    hidden_units = (jax.nn.silu(gate_up[:, :hidden_size]) * gate_up[:, hidden_size:]).astype(
        jnp.bfloat16
    )
    outputs = jnp.dot(hidden_units, server_down[0], preferred_element_type=jnp.float32).astype(
        jnp.bfloat16
    )
    returned = lax.all_to_all(
        outputs.reshape(sources, items, features), "expert", split_axis=0, concat_axis=0, tiled=True
    )
    copies = jnp.take(returned.reshape(expert_count * capacity, width), flat_slot, axis=0)
    copies = copies.reshape(token_rows, TOPK, width).astype(jnp.float32)
    mixture = jnp.einsum("tk,tkd->td", gate_weights[0], copies)
    mixed = resid32[0] + mixture
    return mixed.astype(jnp.bfloat16)[None]

LANES = 128
VMEM_LIMIT = 32 * 2**20
ROW_PIECES = 2


def params():
    return pltpu.CompilerParams(vmem_limit_bytes=VMEM_LIMIT)


def vmem(count):
    return [pl.BlockSpec(memory_space=pltpu.VMEM)] * count


def attention_kernel(table, lengths, q_ref, k_ref, v_ref, *refs):
    outs, attn = refs[:4], refs[4]
    tokens, width = q_ref.shape
    pages, page = k_ref.shape[0], k_ref.shape[1]
    row = lax.broadcasted_iota(jnp.int32, (tokens, tokens), 0)
    column = lax.broadcasted_iota(jnp.int32, (tokens, tokens), 1)
    row_request = jnp.zeros((tokens, tokens), jnp.int32)
    column_request = jnp.zeros((tokens, tokens), jnp.int32)
    end = jnp.int32(0)
    for r in range(lengths.shape[1]):
        end = end + lengths[0, r]
        row_request += (row >= end).astype(jnp.int32)
        column_request += (column >= end).astype(jnp.int32)
    same = row_request == column_request
    for h in range(width // HDIM):
        lanes = slice(h * HDIM, (h + 1) * HDIM)
        keys = jnp.concatenate([k_ref[table[0, p], :, lanes] for p in range(pages)], axis=0)
        values = jnp.concatenate([v_ref[table[0, p], :, lanes] for p in range(pages)], axis=0)
        scores = lax.dot_general(
            q_ref[:, lanes], keys, (((1,), (1,)), ((), ())), preferred_element_type=jnp.float32
        ) * (1.0 / math.sqrt(HDIM))
        scores = jnp.where(same, scores, -1e30)
        highest = jnp.max(scores, axis=-1, keepdims=True)
        weights = jnp.where(same, jnp.exp(scores - highest), 0.0)
        probs = (weights / jnp.sum(weights, axis=-1, keepdims=True)).astype(jnp.bfloat16)
        attn[:, lanes] = jnp.dot(probs, values, preferred_element_type=jnp.float32).astype(
            jnp.bfloat16
        )
    own = lax.axis_index("dp")
    rows = tokens // 4
    for d in range(4):
        first = pl.multiple_of((own ^ d) * rows, rows)
        outs[d][...] = attn[pl.ds(first, rows), :]


def attention(queries, key_pool, value_pool, page_table, prompt_lengths):
    tokens, width = queries.shape
    smem = [pl.BlockSpec(memory_space=pltpu.SMEM)] * 2
    return pl.pallas_call(
        attention_kernel,
        out_shape=[jax.ShapeDtypeStruct((tokens // 4, width), jnp.bfloat16)] * 4,
        in_specs=smem + vmem(3),
        out_specs=vmem(4),
        scratch_shapes=[pltpu.VMEM((tokens, width), jnp.bfloat16)],
        compiler_params=params(),
        name="attention",
    )(page_table, prompt_lengths, queries, key_pool, value_pool)


def norm_kernel(hidden_ref, a0, a1, a2, a3, gain_ref, ids_ref, gates_ref, resid_ref, rows_ref):
    own = lax.axis_index("dp")
    tokens, width = hidden_ref.shape
    block = width // 4
    total = jnp.zeros((tokens, 1), jnp.float32)
    for d, attn in enumerate((a0, a1, a2, a3)):
        columns = pl.ds(pl.multiple_of((own ^ d) * block, block), block)
        resid = (
            hidden_ref[:, columns].astype(jnp.float32) + attn[...].astype(jnp.float32)
        ).astype(jnp.bfloat16)
        resid_ref[:, columns] = resid
        resid32 = resid.astype(jnp.float32)
        total += jnp.sum(resid32 * resid32, axis=-1, keepdims=True)
    inverse = lax.rsqrt(total / width + epsilon)
    for d in range(4):
        columns = pl.ds(pl.multiple_of((own ^ d) * block, block), block)
        rows_ref[:, d * block : (d + 1) * block] = (
            resid_ref[:, columns].astype(jnp.float32) * inverse * gain_ref[:, columns]
        ).astype(jnp.bfloat16)
    lane = lax.broadcasted_iota(jnp.int32, (tokens, LANES), 1)
    gates = jnp.zeros((tokens, LANES), jnp.float32)
    for k in range(TOPK):
        gates += jnp.where(ids_ref[:, k : k + 1] == lane % TOPK, gates_ref[:, k : k + 1], 0.0)
    high = gates.astype(jnp.bfloat16).astype(jnp.float32)
    middle = (gates - high).astype(jnp.bfloat16).astype(jnp.float32)
    low = gates - high - middle
    part = lane // TOPK
    terms = jnp.where(part == 0, high, jnp.where(part == 1, middle, jnp.where(part == 2, low, 0.0)))
    rows_ref[:, width:] = terms.astype(jnp.bfloat16)


def norm(hidden_in, attn, norm_gain, expert_ids, gate_weights):
    tokens, width = hidden_in.shape
    return pl.pallas_call(
        norm_kernel,
        out_shape=[
            jax.ShapeDtypeStruct((tokens, width), jnp.bfloat16),
            jax.ShapeDtypeStruct((tokens, width + LANES), jnp.bfloat16),
        ],
        in_specs=vmem(8),
        out_specs=vmem(2),
        compiler_params=params(),
        name="norm",
    )(hidden_in, *attn, norm_gain[None, :], expert_ids, gate_weights)


def up_kernel(sources, pieces, *refs):
    row_refs = refs[:sources]
    weight_refs = refs[sources : sources + pieces]
    hidden_ref, own_gate_ref, rows, weights, units, arrived = refs[sources + pieces :]
    tokens, width = rows.shape
    tiles, _, block = units.shape
    depth = width // pieces

    def copy(tile, piece, part):
        columns = pl.ds((part * tiles + tile) * block, block)
        return pltpu.make_async_copy(
            weight_refs[piece].at[:, columns],
            weights.at[pl.ds(piece * depth, depth), columns],
            arrived.at[tile, piece, part],
        )

    for tile in range(tiles):
        for piece in range(pieces):
            for part in range(2):
                copy(tile, piece, part).start()
    expert = lax.axis_index("expert")
    first = 0
    for ref in row_refs:
        count = ref.shape[0]
        rows[first : first + count, :] = ref[:, :width]
        terms = ref[:, width:].astype(jnp.float32)
        lane = lax.broadcasted_iota(jnp.int32, terms.shape, 1)
        own_gate_ref[first : first + count, :] = jnp.sum(
            jnp.where(lane % TOPK == expert, terms, 0.0), axis=-1, keepdims=True
        )
        first += count
    for tile in range(tiles):
        for piece in range(pieces):
            for part in range(2):
                copy(tile, piece, part).wait()
        gate, up = (
            jnp.dot(
                rows[...],
                weights[:, (part * tiles + tile) * block : (part * tiles + tile + 1) * block],
                preferred_element_type=jnp.float32,
            )
            for part in range(2)
        )
        units[tile] = (gate / (1.0 + jnp.exp(-gate)) * up).astype(jnp.bfloat16)
    own = lax.axis_index("dp")
    for d in range(4):
        hidden_ref[:, d * block : (d + 1) * block] = units[own ^ d]


def expert_up(rows, weights, hidden_size):
    tokens = sum(piece.shape[0] for piece in rows)
    depth, width = weights[0].shape
    features = depth * len(weights)
    return pl.pallas_call(
        lambda *refs: up_kernel(len(rows), len(weights), *refs),
        out_shape=[
            jax.ShapeDtypeStruct((tokens, hidden_size), jnp.bfloat16),
            jax.ShapeDtypeStruct((tokens, 1), jnp.float32),
        ],
        in_specs=vmem(len(rows)) + [pl.BlockSpec(memory_space=pl.ANY)] * len(weights),
        out_specs=vmem(2),
        scratch_shapes=[
            pltpu.VMEM((tokens, features), jnp.bfloat16),
            pltpu.VMEM((features, width), jnp.bfloat16),
            pltpu.VMEM((4, tokens, hidden_size // 4), jnp.bfloat16),
            pltpu.SemaphoreType.DMA((4, len(weights), 2)),
        ],
        compiler_params=params(),
        cost_estimate=pl.CostEstimate(
            flops=2 * tokens * features * width,
            bytes_accessed=2 * features * width,
            transcendentals=0,
        ),
        name="expert_up",
    )(*rows, *weights)


def down_kernel(hidden_ref, gate_ref, w0, w1, w2, w3, out_ref, left_ref, right_ref):
    block = w0.shape[0]
    total = None
    for d, ref in enumerate((w0, w1, w2, w3)):
        term = jnp.dot(
            hidden_ref[:, d * block : (d + 1) * block],
            ref[...],
            preferred_element_type=jnp.float32,
        )
        total = term if total is None else total + term
    weighted = (total * gate_ref[...]).astype(jnp.bfloat16)
    sources, rows, width = out_ref.shape
    out_ref[...] = weighted.reshape(sources, rows, width)
    middle, half = sources // 2 * rows, rows // 2
    left_ref[...] = weighted[middle : middle + half]
    right_ref[...] = weighted[middle + half : middle + rows]


def expert_down(hidden_units, gates, weights, sources):
    tokens, hidden_size = hidden_units.shape
    width = weights[0].shape[1]
    rows = tokens // sources
    return pl.pallas_call(
        down_kernel,
        out_shape=[
            jax.ShapeDtypeStruct((sources, rows, width), jnp.bfloat16),
            jax.ShapeDtypeStruct((rows // 2, width), jnp.bfloat16),
            jax.ShapeDtypeStruct((rows // 2, width), jnp.bfloat16),
        ],
        in_specs=vmem(6),
        out_specs=vmem(3),
        compiler_params=params(),
        cost_estimate=pl.CostEstimate(
            flops=2 * tokens * hidden_size * width,
            bytes_accessed=2 * (hidden_size * width + tokens * hidden_size + tokens * width),
            transcendentals=0,
        ),
        name="expert_down",
    )(hidden_units, gates, *weights)


def partner(x, distance):
    return lax.ppermute(x, "dp", [(i, i ^ distance) for i in range(4)])


def ring_order(count):
    return list(range(0, count, 2)) + list(range(count - 1, 0, -2))


def around(x, step):
    ring = ring_order(lax.axis_size("expert"))
    count = len(ring)
    return lax.ppermute(x, "expert", [(ring[i], ring[(i + step) % count]) for i in range(count)])


def after(x, *others):
    return lax.optimization_barrier((x, *others))[0]


def add(a, b):
    return (a.astype(jnp.float32) + b.astype(jnp.float32)).astype(jnp.bfloat16)


def gather_rows(rows):
    half = rows.shape[0] // 2
    reach = lax.axis_size("expert") // 2
    above, below = [rows], [rows]
    for _ in range(reach - 1):
        above.append(around(above[-1], -1))
        below.append(around(below[-1], 1))
    far = [around(above[-1][:half], -1), around(below[-1][half:], 1)]
    return above + far + below[:0:-1], list(zip(above[1:], below[1:])) + [tuple(far)]


def scatter_sum(weighted, left, right):
    sources, rows, _ = weighted.shape
    half = rows // 2
    reach = sources // 2
    up, down = around(left, 1), around(right, -1)
    yield up, down
    up = jnp.concatenate([add(weighted[reach - 1, :half], up), weighted[reach - 1, half:]])
    down = jnp.concatenate([weighted[reach + 1, :half], add(weighted[reach + 1, half:], down)])
    for away in range(reach - 2, -1, -1):
        up, down = around(up, 1), around(down, -1)
        yield up, down
        if away:
            up = add(weighted[away], up)
            down = add(weighted[sources - away], down)


def every_expert(
    hidden_in,
    queries,
    key_pool,
    value_pool,
    page_table,
    prompt_lengths,
    expert_ids,
    gate_weights,
    norm_gain,
    trainer_gate_up,
    trainer_down,
):
    attn = attention(queries[0], key_pool, value_pool, page_table, prompt_lengths)
    depth = trainer_gate_up.shape[1] // ROW_PIECES
    width = trainer_down.shape[2]
    first = width * 5 // 8
    bounds = [(0, first), (first, width)]
    gate_up = after(trainer_gate_up[0], attn[0]).astype(jnp.bfloat16)
    up_own = [gate_up[i * depth : (i + 1) * depth] for i in range(ROW_PIECES)]
    down = trainer_down[0].astype(jnp.bfloat16)
    down_own = [down[:, low:high] for low, high in bounds]
    attn = [attn[0]] + [partner(attn[d], d) for d in (1, 2, 3)]
    up_across = [partner(after(piece, *attn), 2) for piece in up_own]
    resid, rows = norm(
        after(hidden_in[0], *up_own), attn, norm_gain, expert_ids[0], gate_weights[0]
    )
    gathered, arrived = gather_rows(rows)
    up_beside = [partner(after(piece, *arrived[0]), 1) for piece in up_own]
    down_beside = [partner(after(piece, *arrived[1]), 1) for piece in down_own]
    down_across = [
        partner(after(down_own[0], *arrived[2]), 2),
        partner(after(down_own[1], up_across[0], *arrived[3]), 2),
    ]
    up_opposite = [
        partner(after(up_across[0], *arrived[1]), 1),
        partner(after(up_across[1], *arrived[3]), 1),
    ]
    hidden_units, gates = expert_up(
        gathered, up_own + up_beside + up_across + up_opposite, trainer_gate_up.shape[2] // 2
    )

    def down_slab(i, *before):
        opposite = partner(after(down_across[i], *before), 1)
        weighted = expert_down(
            hidden_units,
            gates,
            (down_own[i], down_beside[i], down_across[i], opposite),
            lax.axis_size("expert"),
        )
        return weighted[0][0], scatter_sum(*weighted)

    own0, sums0 = down_slab(0, hidden_units)
    own1, sums1 = down_slab(1, *next(sums0))
    ends = [(own, *list(sums)[-1]) for own, sums in ((own0, sums0), (own1, sums1))]
    mixed = []
    for (low, high), terms in zip(bounds, ends):
        total = resid[:, low:high].astype(jnp.float32)
        for term in terms:
            total = total + term.astype(jnp.float32)
        mixed.append(total.astype(jnp.bfloat16))
    return jnp.concatenate(mixed, axis=1)[None]


def solution(mesh):
    placed = (
        P("expert", "dp", None),
        P("expert", None, "dp"),
        P("expert", None, "dp"),
        P("expert", None, "dp"),
        P("expert", None),
        P("expert", None),
        P("expert", "dp", None),
        P("expert", "dp", None),
        P(),
        P("expert", "dp", None),
        P("expert", "dp", None),
    )
    dense = mesh.shape["expert"] == TOPK and mesh.shape["dp"] == 4
    return jax.shard_map(
        every_expert if dense else local, mesh=mesh, in_specs=placed, out_specs=P("expert", "dp", None), check_vma=False
    )
```

```python
import math

import jax
import jax.numpy as jnp
from jax import lax
from jax.experimental import pallas as pl
from jax.experimental.pallas import tpu as pltpu
from jax.sharding import PartitionSpec as P

HDIM = 128
TOPK = 8


epsilon = 1e-05


def fetch_weights(trainer_gate_up, trainer_down):
    return (
        lax.all_gather(trainer_gate_up.astype(jnp.bfloat16), "dp", axis=1, tiled=True),
        lax.all_gather(trainer_down.astype(jnp.bfloat16), "dp", axis=1, tiled=True),
    )


def local(
    hidden_in,
    queries,
    key_pool,
    value_pool,
    page_table,
    prompt_lengths,
    expert_ids,
    gate_weights,
    norm_gain,
    trainer_gate_up,
    trainer_down,
):
    col_tok = queries.shape[1]
    width_dev = queries.shape[2]
    heads_dev = width_dev // HDIM
    keys_all = jnp.take(key_pool, page_table[0], axis=0).reshape(col_tok, heads_dev, HDIM)
    values_all = jnp.take(value_pool, page_table[0], axis=0).reshape(col_tok, heads_dev, HDIM)
    request_ends = jnp.cumsum(prompt_lengths[0])
    positions = lax.iota(jnp.int32, col_tok)
    request = jnp.sum((positions[:, None] >= request_ends[None, :]).astype(jnp.int32), axis=1)
    block_rows = math.gcd(col_tok, 512)
    query_blocks = queries[0].reshape(col_tok // block_rows, block_rows, heads_dev, HDIM)
    request_blocks = request.reshape(col_tok // block_rows, block_rows)
    score_scale = 1.0 / math.sqrt(HDIM)

    def attend(pieces):
        query_block, request_block = pieces
        scores = (
            jnp.einsum("qhd,khd->hqk", query_block, keys_all, preferred_element_type=jnp.float32)
            * score_scale
        )
        same_request = (request_block[:, None] == request[None, :])[None]
        scores = jnp.where(same_request, scores, -1e30)
        highest = jnp.max(scores, axis=-1, keepdims=True)
        weights = jnp.where(same_request, jnp.exp(scores - highest), 0.0)
        totals = jnp.sum(weights, axis=-1, keepdims=True)
        probs = (weights / totals).astype(jnp.bfloat16)
        output = jnp.einsum("hqk,khd->qhd", probs, values_all, preferred_element_type=jnp.float32)
        return output.astype(jnp.bfloat16).reshape(block_rows, width_dev)

    attn_heads = lax.map(attend, (query_blocks, request_blocks)).reshape(1, col_tok, width_dev)
    attn_tokens = lax.all_to_all(attn_heads, "dp", split_axis=1, concat_axis=2, tiled=True)
    resid32 = (
        (hidden_in.astype(jnp.float32) + attn_tokens.astype(jnp.float32))
        .astype(jnp.bfloat16)
        .astype(jnp.float32)
    )
    mean_square = jnp.mean(resid32 * resid32, axis=-1, keepdims=True)
    normed = (resid32 * lax.rsqrt(mean_square + epsilon) * norm_gain).astype(jnp.bfloat16)
    server_gate_up, server_down = fetch_weights(trainer_gate_up, trainer_down)
    token_rows = normed.shape[1]
    width = normed.shape[2]
    expert_count = lax.axis_size("expert")
    capacity = min(token_rows, token_rows * TOPK * 5 // (4 * expert_count))
    hidden_size = server_gate_up.shape[2] // 2
    ids_flat = expert_ids[0].reshape(token_rows * TOPK)
    onehot = (ids_flat[:, None] == lax.iota(jnp.int32, expert_count)[None, :]).astype(jnp.int32)
    earlier = jnp.cumsum(onehot, axis=0) - onehot
    slot_index = jnp.sum(earlier * onehot, axis=1)
    flat_slot = ids_flat * capacity + slot_index
    placement = (
        flat_slot[:, None] == lax.iota(jnp.int32, expert_count * capacity)[None, :]
    ).astype(jnp.bfloat16)
    dispatch_matrix = jnp.sum(placement.reshape(token_rows, TOPK, expert_count * capacity), axis=1)
    outgoing = jnp.einsum(
        "ts,td->sd", dispatch_matrix, normed[0], preferred_element_type=jnp.float32
    )
    outgoing = outgoing.astype(jnp.bfloat16).reshape(expert_count, capacity, width)
    received = lax.all_to_all(outgoing, "expert", split_axis=0, concat_axis=0, tiled=True)
    sources, items, features = received.shape
    slot_rows = received.reshape(sources * items, features)
    gate_up = jnp.dot(slot_rows, server_gate_up[0], preferred_element_type=jnp.float32)
    hidden_units = (jax.nn.silu(gate_up[:, :hidden_size]) * gate_up[:, hidden_size:]).astype(
        jnp.bfloat16
    )
    outputs = jnp.dot(hidden_units, server_down[0], preferred_element_type=jnp.float32).astype(
        jnp.bfloat16
    )
    returned = lax.all_to_all(
        outputs.reshape(sources, items, features), "expert", split_axis=0, concat_axis=0, tiled=True
    )
    copies = jnp.take(returned.reshape(expert_count * capacity, width), flat_slot, axis=0)
    copies = copies.reshape(token_rows, TOPK, width).astype(jnp.float32)
    mixture = jnp.einsum("tk,tkd->td", gate_weights[0], copies)
    mixed = resid32[0] + mixture
    return mixed.astype(jnp.bfloat16)[None]

LANES = 128
VMEM_LIMIT = 32 * 2**20
SLABS = (768, 768, 512)
CAST_STEPS = 4
SMALL = pl.CostEstimate(flops=1, bytes_accessed=1, transcendentals=0)


def params():
    return pltpu.CompilerParams(vmem_limit_bytes=VMEM_LIMIT)


def vmem(count):
    return [pl.BlockSpec(memory_space=pltpu.VMEM)] * count


def attention_kernel(*refs):
    sources, outs, piece_ref, scratch = refs[:6], refs[6:10], refs[10], refs[11:]
    table, lengths, q_ref, k_ref, v_ref, weights, attn, arrived = scratch
    copies = [
        pltpu.make_async_copy(source, target, arrived.at[i])
        for i, (source, target) in enumerate(
            zip(
                (*sources[:2], sources[2].at[0], *sources[3:5]),
                (table, lengths, q_ref, k_ref, v_ref),
            )
        )
    ]
    rows = weights.shape[0]
    copies.append(
        pltpu.make_async_copy(sources[5].at[0, pl.ds(0, rows)], weights, arrived.at[5])
    )
    for copy in copies:
        copy.start()
    for copy in copies[:5]:
        copy.wait()
    tokens, width = q_ref.shape
    pages = k_ref.shape[0]
    row = lax.broadcasted_iota(jnp.int32, (tokens, tokens), 0)
    column = lax.broadcasted_iota(jnp.int32, (tokens, tokens), 1)
    row_request = jnp.zeros((tokens, tokens), jnp.int32)
    column_request = jnp.zeros((tokens, tokens), jnp.int32)
    end = jnp.int32(0)
    for r in range(lengths.shape[1]):
        end = end + lengths[0, r]
        row_request += (row >= end).astype(jnp.int32)
        column_request += (column >= end).astype(jnp.int32)
    same = row_request == column_request
    for h in range(width // HDIM):
        lanes = slice(h * HDIM, (h + 1) * HDIM)
        keys = jnp.concatenate([k_ref[table[0, p], :, lanes] for p in range(pages)], axis=0)
        values = jnp.concatenate([v_ref[table[0, p], :, lanes] for p in range(pages)], axis=0)
        scores = lax.dot_general(
            q_ref[:, lanes], keys, (((1,), (1,)), ((), ())), preferred_element_type=jnp.float32
        ) * (1.0 / math.sqrt(HDIM))
        scores = jnp.where(same, scores, -1e30)
        highest = jnp.max(scores, axis=-1, keepdims=True)
        weight = jnp.where(same, jnp.exp(scores - highest), 0.0)
        probs = (weight / jnp.sum(weight, axis=-1, keepdims=True)).astype(jnp.bfloat16)
        attn[:, lanes] = jnp.dot(probs, values, preferred_element_type=jnp.float32).astype(
            jnp.bfloat16
        )
    own = lax.axis_index("dp")
    rows = tokens // 4
    for d in range(4):
        first = pl.multiple_of((own ^ d) * rows, rows)
        outs[d][...] = attn[pl.ds(first, rows), :]
    copies[5].wait()
    piece_ref[...] = weights[...].astype(jnp.bfloat16)


def attention(queries, key_pool, value_pool, page_table, prompt_lengths, gate_up):
    tokens, width = queries.shape[1:]
    rows = gate_up.shape[1] // 2
    return pl.pallas_call(
        attention_kernel,
        out_shape=[jax.ShapeDtypeStruct((tokens // 4, width), jnp.bfloat16)] * 4
        + [jax.ShapeDtypeStruct((rows, gate_up.shape[2]), jnp.bfloat16)],
        in_specs=[pl.BlockSpec(memory_space=pltpu.HBM)] * 6,
        out_specs=vmem(5),
        scratch_shapes=[
            pltpu.SMEM(page_table.shape, jnp.int32),
            pltpu.SMEM(prompt_lengths.shape, jnp.int32),
            pltpu.VMEM((tokens, width), jnp.bfloat16),
            pltpu.VMEM(key_pool.shape, jnp.bfloat16),
            pltpu.VMEM(value_pool.shape, jnp.bfloat16),
            pltpu.VMEM((rows, gate_up.shape[2]), jnp.float32),
            pltpu.VMEM((tokens, width), jnp.bfloat16),
            pltpu.SemaphoreType.DMA((6,)),
        ],
        compiler_params=params(),
        cost_estimate=SMALL,
        name="attention",
    )(page_table, prompt_lengths, queries, key_pool, value_pool, gate_up)


def norm_kernel(hidden_ref, a0, a1, a2, a3, gain_ref, ids_ref, gates_ref, resid_ref, rows_ref):
    own = lax.axis_index("dp")
    tokens, width = hidden_ref.shape
    block = width // 4
    total = jnp.zeros((tokens, 1), jnp.float32)
    for d, attn in enumerate((a0, a1, a2, a3)):
        columns = pl.ds(pl.multiple_of((own ^ d) * block, block), block)
        resid = (
            hidden_ref[:, columns].astype(jnp.float32) + attn[...].astype(jnp.float32)
        ).astype(jnp.bfloat16)
        resid_ref[:, columns] = resid
        resid32 = resid.astype(jnp.float32)
        total += jnp.sum(resid32 * resid32, axis=-1, keepdims=True)
    inverse = lax.rsqrt(total / width + epsilon)
    for d in range(4):
        columns = pl.ds(pl.multiple_of((own ^ d) * block, block), block)
        rows_ref[:, d * block : (d + 1) * block] = (
            resid_ref[:, columns].astype(jnp.float32) * inverse * gain_ref[:, columns]
        ).astype(jnp.bfloat16)
    lane = lax.broadcasted_iota(jnp.int32, (tokens, LANES), 1)
    gates = jnp.zeros((tokens, LANES), jnp.float32)
    for k in range(TOPK):
        gates += jnp.where(ids_ref[:, k : k + 1] == lane % TOPK, gates_ref[:, k : k + 1], 0.0)
    high = gates.astype(jnp.bfloat16).astype(jnp.float32)
    middle = (gates - high).astype(jnp.bfloat16).astype(jnp.float32)
    low = gates - high - middle
    part = lane // TOPK
    terms = jnp.where(part == 0, high, jnp.where(part == 1, middle, jnp.where(part == 2, low, 0.0)))
    rows_ref[:, width:] = terms.astype(jnp.bfloat16)


def norm(hidden_in, attn, norm_gain, expert_ids, gate_weights):
    tokens, width = hidden_in.shape
    return pl.pallas_call(
        norm_kernel,
        out_shape=[
            jax.ShapeDtypeStruct((tokens, width), jnp.bfloat16),
            jax.ShapeDtypeStruct((tokens, width + LANES), jnp.bfloat16),
        ],
        in_specs=vmem(8),
        out_specs=vmem(2),
        compiler_params=params(),
        cost_estimate=SMALL,
        name="norm",
    )(hidden_in, *attn, norm_gain[None, :], expert_ids, gate_weights)


def cast_kernel(up_source, down_source, whole_ref, *refs):
    piece_refs, (up_ref, down_ref, arrived) = refs[:-3], refs[-3:]
    total, width = up_ref.shape
    rows = total // CAST_STEPS

    def copies(step):
        here = pl.ds(step * rows, rows)
        late = pl.ds(total + step * rows, rows)
        return (
            pltpu.make_async_copy(up_source.at[0, late], up_ref.at[here], arrived.at[step, 0]),
            pltpu.make_async_copy(down_source.at[0, here], down_ref.at[here], arrived.at[step, 1]),
        )

    for step in range(CAST_STEPS):
        for copy in copies(step):
            copy.start()
    for step in range(CAST_STEPS):
        for copy in copies(step):
            copy.wait()
        here = slice(step * rows, (step + 1) * rows)
        whole_ref[here, :width] = up_ref[here].astype(jnp.bfloat16)
        whole_ref[here, width:] = down_ref[here].astype(jnp.bfloat16)
        first = 0
        for ref in piece_refs:
            ref[here, :] = whole_ref[here, first : first + ref.shape[1]]
            first += ref.shape[1]


def cast_late(gate_up, down, slabs):
    rows, width = down.shape[1:]
    depth = gate_up.shape[2]
    widths = (depth + width, depth + slabs[0], *slabs[1:])
    return pl.pallas_call(
        cast_kernel,
        out_shape=[jax.ShapeDtypeStruct((rows, wide), jnp.bfloat16) for wide in widths],
        in_specs=[pl.BlockSpec(memory_space=pltpu.HBM)] * 2,
        out_specs=vmem(len(widths)),
        scratch_shapes=[
            pltpu.VMEM((rows, depth), jnp.float32),
            pltpu.VMEM((rows, width), jnp.float32),
            pltpu.SemaphoreType.DMA((CAST_STEPS, 2)),
        ],
        compiler_params=params(),
        cost_estimate=SMALL,
        name="cast_late",
    )(gate_up, down)


def load_tiles(pieces, weights, arrived, tiles, block):
    def copies(tile):
        first = 0
        for index, piece in enumerate(pieces):
            depth = piece.shape[0]
            for part in range(2):
                columns = pl.ds((part * tiles + tile) * block, block)
                yield pltpu.make_async_copy(
                    piece.at[:, columns],
                    weights.at[pl.ds(first, depth), columns],
                    arrived.at[tile, index, part],
                )
            first += depth

    for tile in range(tiles):
        for copy in copies(tile):
            copy.start()

    def wait(tile):
        for copy in copies(tile):
            copy.wait()

    return wait


def early_kernel(sources, pieces, *refs):
    row_refs = refs[:sources]
    weight_refs = refs[sources : sources + pieces]
    total_ref, late_ref, own_gate_ref, rows, weights, arrived = refs[sources + pieces :]
    width = row_refs[0].shape[1] - LANES
    depth = width // 4
    half = depth // 2
    tiles = 4
    block = weights.shape[1] // (2 * tiles)
    wait = load_tiles(weight_refs, weights, arrived, tiles, block)
    expert = lax.axis_index("expert")
    first = 0
    for ref in row_refs:
        count = ref.shape[0]
        here = slice(first, first + count)
        rows[here, : 2 * depth + half] = ref[:, : 2 * depth + half]
        rows[here, 2 * depth + half :] = ref[:, 3 * depth : 3 * depth + half]
        late_ref[here, :half] = ref[:, 2 * depth + half : 3 * depth]
        late_ref[here, half:] = ref[:, 3 * depth + half : width]
        terms = ref[:, width:].astype(jnp.float32)
        lane = lax.broadcasted_iota(jnp.int32, terms.shape, 1)
        own_gate_ref[here, :] = jnp.sum(
            jnp.where(lane % TOPK == expert, terms, 0.0), axis=-1, keepdims=True
        )
        first += count
    for tile in range(tiles):
        wait(tile)
        for part in range(2):
            columns = slice((part * tiles + tile) * block, (part * tiles + tile + 1) * block)
            total_ref[:, columns] = jnp.dot(
                rows[...], weights[:, columns], preferred_element_type=jnp.float32
            )


def up_early(rows, weights, width):
    tokens = sum(piece.shape[0] for piece in rows)
    features = sum(piece.shape[0] for piece in weights)
    late = rows[0].shape[1] - LANES - features
    return pl.pallas_call(
        lambda *refs: early_kernel(len(rows), len(weights), *refs),
        out_shape=[
            jax.ShapeDtypeStruct((tokens, width), jnp.float32),
            jax.ShapeDtypeStruct((tokens, late), jnp.bfloat16),
            jax.ShapeDtypeStruct((tokens, 1), jnp.float32),
        ],
        in_specs=vmem(len(rows)) + [pl.BlockSpec(memory_space=pl.ANY)] * len(weights),
        out_specs=vmem(3),
        scratch_shapes=[
            pltpu.VMEM((tokens, features), jnp.bfloat16),
            pltpu.VMEM((features, width), jnp.bfloat16),
            pltpu.SemaphoreType.DMA((4, len(weights), 2)),
        ],
        compiler_params=params(),
        cost_estimate=SMALL,
        name="up_early",
    )(*rows, *weights)


def late_kernel(pieces, total_ref, late_ref, *refs):
    weight_refs = refs[:pieces]
    hidden_ref, weights, units, arrived = refs[pieces:]
    tiles, _, block = units.shape
    wait = load_tiles(weight_refs, weights, arrived, tiles, block)
    for tile in range(tiles):
        wait(tile)
        gate, up = (
            total_ref[:, (part * tiles + tile) * block : (part * tiles + tile + 1) * block]
            + jnp.dot(
                late_ref[...],
                weights[:, (part * tiles + tile) * block : (part * tiles + tile + 1) * block],
                preferred_element_type=jnp.float32,
            )
            for part in range(2)
        )
        units[tile] = (gate / (1.0 + jnp.exp(-gate)) * up).astype(jnp.bfloat16)
    own = lax.axis_index("dp")
    for d in range(4):
        hidden_ref[:, d * block : (d + 1) * block] = units[own ^ d]


def up_late(total, late, weights):
    tokens, width = total.shape
    hidden_size = width // 2
    return pl.pallas_call(
        lambda *refs: late_kernel(len(weights), *refs),
        out_shape=jax.ShapeDtypeStruct((tokens, hidden_size), jnp.bfloat16),
        in_specs=vmem(2) + [pl.BlockSpec(memory_space=pl.ANY)] * len(weights),
        out_specs=pl.BlockSpec(memory_space=pltpu.VMEM),
        scratch_shapes=[
            pltpu.VMEM((late.shape[1], width), jnp.bfloat16),
            pltpu.VMEM((4, tokens, hidden_size // 4), jnp.bfloat16),
            pltpu.SemaphoreType.DMA((4, len(weights), 2)),
        ],
        compiler_params=params(),
        cost_estimate=SMALL,
        name="up_late",
    )(total, late, *weights)


def down_kernel(firsts, hidden_ref, gate_ref, w0, w1, w2, w3, *refs):
    out_ref, left_ref, right_ref, weights, arrived = refs
    depth, width = w0.shape[0], weights.shape[1]
    copies = [
        pltpu.make_async_copy(
            ref.at[:, pl.ds(first, width)], weights.at[pl.ds(d * depth, depth)], arrived.at[d]
        )
        for d, (ref, first) in enumerate(zip((w0, w1, w2, w3), firsts))
    ]
    for copy in copies:
        copy.start()
    for copy in copies:
        copy.wait()
    total = jnp.dot(hidden_ref[...], weights[...], preferred_element_type=jnp.float32)
    weighted = (total * gate_ref[...]).astype(jnp.bfloat16)
    sources, rows, _ = out_ref.shape
    out_ref[...] = weighted.reshape(sources, rows, width)
    middle, half = sources // 2 * rows, rows // 2
    left_ref[...] = weighted[middle : middle + half]
    right_ref[...] = weighted[middle + half : middle + rows]


def expert_down(hidden_units, gates, weights, firsts, width, sources):
    tokens, hidden_size = hidden_units.shape
    rows = tokens // sources
    return pl.pallas_call(
        lambda *refs: down_kernel(firsts, *refs),
        out_shape=[
            jax.ShapeDtypeStruct((sources, rows, width), jnp.bfloat16),
            jax.ShapeDtypeStruct((rows // 2, width), jnp.bfloat16),
            jax.ShapeDtypeStruct((rows // 2, width), jnp.bfloat16),
        ],
        in_specs=vmem(2) + [pl.BlockSpec(memory_space=pl.ANY)] * 4,
        out_specs=vmem(3),
        scratch_shapes=[
            pltpu.VMEM((hidden_size, width), jnp.bfloat16),
            pltpu.SemaphoreType.DMA((4,)),
        ],
        compiler_params=params(),
        cost_estimate=SMALL,
        name="expert_down",
    )(hidden_units, gates, *weights)


def partner(x, distance):
    return lax.ppermute(x, "dp", [(i, i ^ distance) for i in range(4)])


def ring_order(count):
    return list(range(0, count, 2)) + list(range(count - 1, 0, -2))


def around(x, step):
    ring = ring_order(lax.axis_size("expert"))
    count = len(ring)
    return lax.ppermute(x, "expert", [(ring[i], ring[(i + step) % count]) for i in range(count)])


def after(x, *others):
    return lax.optimization_barrier((x, *others))[0]


def add(a, b):
    return (a.astype(jnp.float32) + b.astype(jnp.float32)).astype(jnp.bfloat16)


def gather_rows(rows):
    half = rows.shape[0] // 2
    reach = lax.axis_size("expert") // 2
    above, below = [rows], [rows]
    for _ in range(reach - 1):
        above.append(around(above[-1], -1))
        below.append(around(below[-1], 1))
    far = [around(above[-1][:half], -1), around(below[-1][half:], 1)]
    return above + far + below[:0:-1], list(zip(above[1:], below[1:])) + [tuple(far)]


def scatter_sum(weighted, left, right):
    sources, rows, _ = weighted.shape
    half = rows // 2
    reach = sources // 2
    up, down = around(left, 1), around(right, -1)
    before = yield up, down
    up = jnp.concatenate([add(weighted[reach - 1, :half], up), weighted[reach - 1, half:]])
    down = jnp.concatenate([weighted[reach + 1, :half], add(weighted[reach + 1, half:], down)])
    for away in range(reach - 2, -1, -1):
        if before:
            up, down = after(up, *before), after(down, *before)
        up, down = around(up, 1), around(down, -1)
        before = yield up, down
        if away:
            up = add(weighted[away], up)
            down = add(weighted[sources - away], down)


def every_expert(
    hidden_in,
    queries,
    key_pool,
    value_pool,
    page_table,
    prompt_lengths,
    expert_ids,
    gate_weights,
    norm_gain,
    trainer_gate_up,
    trainer_down,
):
    expert_count = lax.axis_size("expert")
    width = trainer_gate_up.shape[2]
    *attn, first_own = attention(
        queries, key_pool, value_pool, page_table, prompt_lengths, trainer_gate_up
    )
    whole_own, joined_own, *slabs_own = cast_late(
        after(trainer_gate_up, attn[0]), trainer_down, SLABS
    )
    attn = [attn[0]] + [partner(attn[d], d) for d in (1, 2, 3)]
    first_across = partner(after(first_own, *attn), 2)
    joined_across = partner(after(joined_own, *attn), 2)
    resid, rows = norm(
        after(hidden_in[0], joined_own), attn, norm_gain, expert_ids[0], gate_weights[0]
    )
    gathered, arrived = gather_rows(rows)
    first_beside = partner(after(first_own, *arrived[0]), 1)
    whole_beside = partner(after(whole_own, *arrived[1]), 1)
    first_opposite = partner(after(first_across, *arrived[2]), 1)
    total, late, gates = up_early(
        gathered,
        [first_own, whole_own, first_beside, whole_beside, first_across, first_opposite],
        width,
    )
    joined_opposite = partner(after(joined_across, total), 1)
    hidden_units = up_late(total, late, [joined_across, joined_opposite])
    slabs_across = [
        partner(after(slab, hidden_units if i else arrived[2][0]), 2)
        for i, slab in enumerate(slabs_own)
    ]

    def down_slab(i, across, opposite):
        whole_first = width + sum(SLABS[:i])
        first = 0 if i else width
        return expert_down(
            hidden_units,
            gates,
            (whole_own, whole_beside, across, opposite),
            (whole_first, whole_first, first, first),
            SLABS[i],
            expert_count,
        )

    weighted = [down_slab(0, joined_across, joined_opposite)]
    sums = [scatter_sum(*weighted[0])]
    ends = [next(sums[0])]
    for i, across in enumerate(slabs_across):
        opposite = partner(after(across, *ends[0], *weighted[i][0:i]), 1)
        ends[0] = sums[0].send((across, *weighted[i][0:i]))
        weighted.append(down_slab(i + 1, across, opposite))
        sums.append(scatter_sum(*weighted[-1]))
    ends[0] = sums[0].send(weighted[-1][:1])
    ends += [list(part)[-1] for part in sums[1:]]
    mixed, first = [], 0
    for slab, partial, end in zip(SLABS, weighted, ends):
        sum_here = resid[:, first : first + slab].astype(jnp.float32)
        for term in (partial[0][0], *end):
            sum_here = sum_here + term.astype(jnp.float32)
        mixed.append(sum_here.astype(jnp.bfloat16))
        first += slab
    return jnp.concatenate(mixed, axis=1)[None]


def solution(mesh):
    placed = (
        P("expert", "dp", None),
        P("expert", None, "dp"),
        P("expert", None, "dp"),
        P("expert", None, "dp"),
        P("expert", None),
        P("expert", None),
        P("expert", "dp", None),
        P("expert", "dp", None),
        P(),
        P("expert", "dp", None),
        P("expert", "dp", None),
    )
    dense = mesh.shape["expert"] == TOPK and mesh.shape["dp"] == 4
    return jax.shard_map(
        every_expert if dense else local, mesh=mesh, in_specs=placed, out_specs=P("expert", "dp", None), check_vma=False
    )
```

```python
import math

import jax
import jax.numpy as jnp
from jax import lax
from jax.experimental import pallas as pl
from jax.experimental.pallas import tpu as pltpu
from jax.sharding import PartitionSpec as P

HDIM = 128
TOPK = 8


epsilon = 1e-05


def fetch_weights(trainer_gate_up, trainer_down):
    return (
        lax.all_gather(trainer_gate_up.astype(jnp.bfloat16), "dp", axis=1, tiled=True),
        lax.all_gather(trainer_down.astype(jnp.bfloat16), "dp", axis=1, tiled=True),
    )


def local(
    hidden_in,
    queries,
    key_pool,
    value_pool,
    page_table,
    prompt_lengths,
    expert_ids,
    gate_weights,
    norm_gain,
    trainer_gate_up,
    trainer_down,
):
    col_tok = queries.shape[1]
    width_dev = queries.shape[2]
    heads_dev = width_dev // HDIM
    keys_all = jnp.take(key_pool, page_table[0], axis=0).reshape(col_tok, heads_dev, HDIM)
    values_all = jnp.take(value_pool, page_table[0], axis=0).reshape(col_tok, heads_dev, HDIM)
    request_ends = jnp.cumsum(prompt_lengths[0])
    positions = lax.iota(jnp.int32, col_tok)
    request = jnp.sum((positions[:, None] >= request_ends[None, :]).astype(jnp.int32), axis=1)
    block_rows = math.gcd(col_tok, 512)
    query_blocks = queries[0].reshape(col_tok // block_rows, block_rows, heads_dev, HDIM)
    request_blocks = request.reshape(col_tok // block_rows, block_rows)
    score_scale = 1.0 / math.sqrt(HDIM)

    def attend(pieces):
        query_block, request_block = pieces
        scores = (
            jnp.einsum("qhd,khd->hqk", query_block, keys_all, preferred_element_type=jnp.float32)
            * score_scale
        )
        same_request = (request_block[:, None] == request[None, :])[None]
        scores = jnp.where(same_request, scores, -1e30)
        highest = jnp.max(scores, axis=-1, keepdims=True)
        weights = jnp.where(same_request, jnp.exp(scores - highest), 0.0)
        totals = jnp.sum(weights, axis=-1, keepdims=True)
        probs = (weights / totals).astype(jnp.bfloat16)
        output = jnp.einsum("hqk,khd->qhd", probs, values_all, preferred_element_type=jnp.float32)
        return output.astype(jnp.bfloat16).reshape(block_rows, width_dev)

    attn_heads = lax.map(attend, (query_blocks, request_blocks)).reshape(1, col_tok, width_dev)
    attn_tokens = lax.all_to_all(attn_heads, "dp", split_axis=1, concat_axis=2, tiled=True)
    resid32 = (
        (hidden_in.astype(jnp.float32) + attn_tokens.astype(jnp.float32))
        .astype(jnp.bfloat16)
        .astype(jnp.float32)
    )
    mean_square = jnp.mean(resid32 * resid32, axis=-1, keepdims=True)
    normed = (resid32 * lax.rsqrt(mean_square + epsilon) * norm_gain).astype(jnp.bfloat16)
    server_gate_up, server_down = fetch_weights(trainer_gate_up, trainer_down)
    token_rows = normed.shape[1]
    width = normed.shape[2]
    expert_count = lax.axis_size("expert")
    capacity = min(token_rows, token_rows * TOPK * 5 // (4 * expert_count))
    hidden_size = server_gate_up.shape[2] // 2
    ids_flat = expert_ids[0].reshape(token_rows * TOPK)
    onehot = (ids_flat[:, None] == lax.iota(jnp.int32, expert_count)[None, :]).astype(jnp.int32)
    earlier = jnp.cumsum(onehot, axis=0) - onehot
    slot_index = jnp.sum(earlier * onehot, axis=1)
    flat_slot = ids_flat * capacity + slot_index
    placement = (
        flat_slot[:, None] == lax.iota(jnp.int32, expert_count * capacity)[None, :]
    ).astype(jnp.bfloat16)
    dispatch_matrix = jnp.sum(placement.reshape(token_rows, TOPK, expert_count * capacity), axis=1)
    outgoing = jnp.einsum(
        "ts,td->sd", dispatch_matrix, normed[0], preferred_element_type=jnp.float32
    )
    outgoing = outgoing.astype(jnp.bfloat16).reshape(expert_count, capacity, width)
    received = lax.all_to_all(outgoing, "expert", split_axis=0, concat_axis=0, tiled=True)
    sources, items, features = received.shape
    slot_rows = received.reshape(sources * items, features)
    gate_up = jnp.dot(slot_rows, server_gate_up[0], preferred_element_type=jnp.float32)
    hidden_units = (jax.nn.silu(gate_up[:, :hidden_size]) * gate_up[:, hidden_size:]).astype(
        jnp.bfloat16
    )
    outputs = jnp.dot(hidden_units, server_down[0], preferred_element_type=jnp.float32).astype(
        jnp.bfloat16
    )
    returned = lax.all_to_all(
        outputs.reshape(sources, items, features), "expert", split_axis=0, concat_axis=0, tiled=True
    )
    copies = jnp.take(returned.reshape(expert_count * capacity, width), flat_slot, axis=0)
    copies = copies.reshape(token_rows, TOPK, width).astype(jnp.float32)
    mixture = jnp.einsum("tk,tkd->td", gate_weights[0], copies)
    mixed = resid32[0] + mixture
    return mixed.astype(jnp.bfloat16)[None]

LANES = 128
VMEM_LIMIT = 32 * 2**20
VMEM_MOST = 60 * 2**20
SLABS = 2
CAST_STEPS = 4
SMALL = pl.CostEstimate(flops=1, bytes_accessed=1, transcendentals=0)


def params(limit=VMEM_LIMIT):
    return pltpu.CompilerParams(vmem_limit_bytes=limit)


def vmem(count):
    return [pl.BlockSpec(memory_space=pltpu.VMEM)] * count


def attention_kernel(*refs):
    sources, outs, scratch = refs[:5], refs[5:9], refs[9:]
    table, lengths, q_ref, k_ref, v_ref, attn, arrived = scratch
    copies = [
        pltpu.make_async_copy(source, target, arrived.at[i])
        for i, (source, target) in enumerate(
            zip(
                (*sources[:2], sources[2].at[0], *sources[3:5]),
                (table, lengths, q_ref, k_ref, v_ref),
            )
        )
    ]
    for copy in copies:
        copy.start()
    for copy in copies:
        copy.wait()
    tokens, width = q_ref.shape
    pages = k_ref.shape[0]
    row = lax.broadcasted_iota(jnp.int32, (tokens, tokens), 0)
    column = lax.broadcasted_iota(jnp.int32, (tokens, tokens), 1)
    row_request = jnp.zeros((tokens, tokens), jnp.int32)
    column_request = jnp.zeros((tokens, tokens), jnp.int32)
    end = jnp.int32(0)
    for r in range(lengths.shape[1]):
        end = end + lengths[0, r]
        row_request += (row >= end).astype(jnp.int32)
        column_request += (column >= end).astype(jnp.int32)
    same = row_request == column_request
    for h in range(width // HDIM):
        lanes = slice(h * HDIM, (h + 1) * HDIM)
        keys = jnp.concatenate([k_ref[table[0, p], :, lanes] for p in range(pages)], axis=0)
        values = jnp.concatenate([v_ref[table[0, p], :, lanes] for p in range(pages)], axis=0)
        scores = lax.dot_general(
            q_ref[:, lanes], keys, (((1,), (1,)), ((), ())), preferred_element_type=jnp.float32
        ) * (1.0 / math.sqrt(HDIM))
        scores = jnp.where(same, scores, -1e30)
        highest = jnp.max(scores, axis=-1, keepdims=True)
        weight = jnp.where(same, jnp.exp(scores - highest), 0.0)
        probs = (weight / jnp.sum(weight, axis=-1, keepdims=True)).astype(jnp.bfloat16)
        attn[:, lanes] = jnp.dot(probs, values, preferred_element_type=jnp.float32).astype(
            jnp.bfloat16
        )
    own = lax.axis_index("dp")
    rows = tokens // 4
    for d in range(4):
        first = pl.multiple_of((own ^ d) * rows, rows)
        outs[d][...] = attn[pl.ds(first, rows), :]


def attention(queries, key_pool, value_pool, page_table, prompt_lengths):
    tokens, width = queries.shape[1:]
    return pl.pallas_call(
        attention_kernel,
        out_shape=[jax.ShapeDtypeStruct((tokens // 4, width), jnp.bfloat16)] * 4,
        in_specs=[pl.BlockSpec(memory_space=pltpu.HBM)] * 5,
        out_specs=vmem(4),
        scratch_shapes=[
            pltpu.SMEM(page_table.shape, jnp.int32),
            pltpu.SMEM(prompt_lengths.shape, jnp.int32),
            pltpu.VMEM((tokens, width), jnp.bfloat16),
            pltpu.VMEM(key_pool.shape, jnp.bfloat16),
            pltpu.VMEM(value_pool.shape, jnp.bfloat16),
            pltpu.VMEM((tokens, width), jnp.bfloat16),
            pltpu.SemaphoreType.DMA((5,)),
        ],
        compiler_params=params(VMEM_MOST),
        name="attention",
    )(page_table, prompt_lengths, queries, key_pool, value_pool)


def norm_kernel(hidden_ref, a0, a1, a2, a3, gain_ref, ids_ref, gates_ref, resid_ref, rows_ref):
    own = lax.axis_index("dp")
    tokens, width = hidden_ref.shape
    block = width // 4
    total = jnp.zeros((tokens, 1), jnp.float32)
    for d, attn in enumerate((a0, a1, a2, a3)):
        columns = pl.ds(pl.multiple_of((own ^ d) * block, block), block)
        resid = (
            hidden_ref[:, columns].astype(jnp.float32) + attn[...].astype(jnp.float32)
        ).astype(jnp.bfloat16)
        resid_ref[:, columns] = resid
        resid32 = resid.astype(jnp.float32)
        total += jnp.sum(resid32 * resid32, axis=-1, keepdims=True)
    inverse = lax.rsqrt(total / width + epsilon)
    for d in range(4):
        columns = pl.ds(pl.multiple_of((own ^ d) * block, block), block)
        rows_ref[:, d * block : (d + 1) * block] = (
            resid_ref[:, columns].astype(jnp.float32) * inverse * gain_ref[:, columns]
        ).astype(jnp.bfloat16)
    lane = lax.broadcasted_iota(jnp.int32, (tokens, LANES), 1)
    gates = jnp.zeros((tokens, LANES), jnp.float32)
    for k in range(TOPK):
        gates += jnp.where(ids_ref[:, k : k + 1] == lane % TOPK, gates_ref[:, k : k + 1], 0.0)
    high = gates.astype(jnp.bfloat16).astype(jnp.float32)
    middle = (gates - high).astype(jnp.bfloat16).astype(jnp.float32)
    low = gates - high - middle
    part = lane // TOPK
    terms = jnp.where(part == 0, high, jnp.where(part == 1, middle, jnp.where(part == 2, low, 0.0)))
    rows_ref[:, width:] = terms.astype(jnp.bfloat16)


def norm(hidden_in, attn, norm_gain, expert_ids, gate_weights):
    tokens, width = hidden_in.shape
    return pl.pallas_call(
        norm_kernel,
        out_shape=[
            jax.ShapeDtypeStruct((tokens, width), jnp.bfloat16),
            jax.ShapeDtypeStruct((tokens, width + LANES), jnp.bfloat16),
        ],
        in_specs=vmem(8),
        out_specs=vmem(2),
        compiler_params=params(),
        cost_estimate=SMALL,
        name="norm",
    )(hidden_in, *attn, norm_gain[None, :], expert_ids, gate_weights)


def cast_kernel(up_source, down_source, up_out, down_out, up_ref, down_ref, arrived):
    def copies(step):
        for i, (source, target) in enumerate(((up_source, up_ref), (down_source, down_ref))):
            rows = target.shape[0] // CAST_STEPS
            here = pl.ds(step * rows, rows)
            yield pltpu.make_async_copy(source.at[0, here], target.at[here], arrived.at[step, i])

    for step in range(CAST_STEPS):
        for copy in copies(step):
            copy.start()
    for step in range(CAST_STEPS):
        for copy in copies(step):
            copy.wait()
        for source, target in ((up_ref, up_out), (down_ref, down_out)):
            rows = target.shape[0] // CAST_STEPS
            here = slice(step * rows, (step + 1) * rows)
            target[here] = source[here].astype(jnp.bfloat16)


def cast_weights(gate_up, down):
    shapes = gate_up.shape[1:], down.shape[1:]
    return pl.pallas_call(
        cast_kernel,
        out_shape=[jax.ShapeDtypeStruct(shape, jnp.bfloat16) for shape in shapes],
        in_specs=[pl.BlockSpec(memory_space=pltpu.HBM)] * 2,
        out_specs=vmem(2),
        scratch_shapes=[pltpu.VMEM(shape, jnp.float32) for shape in shapes]
        + [pltpu.SemaphoreType.DMA((CAST_STEPS, 2))],
        compiler_params=params(VMEM_MOST),
        name="cast_weights",
    )(gate_up, down)


def load_tiles(pieces, weights, arrived, tiles, block):
    def copies(tile):
        first = 0
        for index, piece in enumerate(pieces):
            depth = piece.shape[0]
            for part in range(2):
                columns = pl.ds((part * tiles + tile) * block, block)
                yield pltpu.make_async_copy(
                    piece.at[:, columns],
                    weights.at[pl.ds(first, depth), columns],
                    arrived.at[tile, index, part],
                )
            first += depth

    for tile in range(tiles):
        for copy in copies(tile):
            copy.start()

    def wait(tile):
        for copy in copies(tile):
            copy.wait()

    return wait


def up_kernel(sources, pieces, *refs):
    row_refs = refs[:sources]
    weight_refs = refs[sources : sources + pieces]
    hidden_ref, own_gate_ref, rows, weights, units, arrived = refs[sources + pieces :]
    width = rows.shape[1]
    tiles, _, block = units.shape
    wait = load_tiles(weight_refs, weights, arrived, tiles, block)
    expert = lax.axis_index("expert")
    first = 0
    for ref in row_refs:
        count = ref.shape[0]
        here = slice(first, first + count)
        rows[here, :] = ref[:, :width]
        terms = ref[:, width:].astype(jnp.float32)
        lane = lax.broadcasted_iota(jnp.int32, terms.shape, 1)
        own_gate_ref[here, :] = jnp.sum(
            jnp.where(lane % TOPK == expert, terms, 0.0), axis=-1, keepdims=True
        )
        first += count
    for tile in range(tiles):
        wait(tile)
        gate, up = (
            jnp.dot(
                rows[...],
                weights[:, (part * tiles + tile) * block : (part * tiles + tile + 1) * block],
                preferred_element_type=jnp.float32,
            )
            for part in range(2)
        )
        units[tile] = (gate / (1.0 + jnp.exp(-gate)) * up).astype(jnp.bfloat16)
    own = lax.axis_index("dp")
    for d in range(4):
        hidden_ref[:, d * block : (d + 1) * block] = units[own ^ d]


def expert_up(rows, weights):
    tokens = sum(piece.shape[0] for piece in rows)
    features = sum(piece.shape[0] for piece in weights)
    width = weights[0].shape[1]
    hidden_size = width // 2
    return pl.pallas_call(
        lambda *refs: up_kernel(len(rows), len(weights), *refs),
        out_shape=[
            jax.ShapeDtypeStruct((tokens, hidden_size), jnp.bfloat16),
            jax.ShapeDtypeStruct((tokens, 1), jnp.float32),
        ],
        in_specs=vmem(len(rows)) + [pl.BlockSpec(memory_space=pl.ANY)] * len(weights),
        out_specs=vmem(2),
        scratch_shapes=[
            pltpu.VMEM((tokens, features), jnp.bfloat16),
            pltpu.VMEM((features, width), jnp.bfloat16),
            pltpu.VMEM((4, tokens, hidden_size // 4), jnp.bfloat16),
            pltpu.SemaphoreType.DMA((4, len(weights), 2)),
        ],
        compiler_params=params(),
        cost_estimate=SMALL,
        name="expert_up",
    )(*rows, *weights)


def down_kernel(firsts, hidden_ref, gate_ref, w0, w1, w2, w3, *refs):
    out_ref, left_ref, right_ref, weights, arrived = refs
    depth, width = w0.shape[0], weights.shape[1]
    copies = [
        pltpu.make_async_copy(
            ref.at[:, pl.ds(first, width)], weights.at[pl.ds(d * depth, depth)], arrived.at[d]
        )
        for d, (ref, first) in enumerate(zip((w0, w1, w2, w3), firsts))
    ]
    for copy in copies:
        copy.start()
    for copy in copies:
        copy.wait()
    total = jnp.dot(hidden_ref[...], weights[...], preferred_element_type=jnp.float32)
    weighted = (total * gate_ref[...]).astype(jnp.bfloat16)
    sources, rows, _ = out_ref.shape
    out_ref[...] = weighted.reshape(sources, rows, width)
    middle, half = sources // 2 * rows, rows // 2
    left_ref[...] = weighted[middle : middle + half]
    right_ref[...] = weighted[middle + half : middle + rows]


def expert_down(hidden_units, gates, weights, firsts, width, sources):
    tokens, hidden_size = hidden_units.shape
    rows = tokens // sources
    return pl.pallas_call(
        lambda *refs: down_kernel(firsts, *refs),
        out_shape=[
            jax.ShapeDtypeStruct((sources, rows, width), jnp.bfloat16),
            jax.ShapeDtypeStruct((rows // 2, width), jnp.bfloat16),
            jax.ShapeDtypeStruct((rows // 2, width), jnp.bfloat16),
        ],
        in_specs=vmem(2) + [pl.BlockSpec(memory_space=pl.ANY)] * 4,
        out_specs=vmem(3),
        scratch_shapes=[
            pltpu.VMEM((hidden_size, width), jnp.bfloat16),
            pltpu.SemaphoreType.DMA((4,)),
        ],
        compiler_params=params(),
        cost_estimate=SMALL,
        name="expert_down",
    )(hidden_units, gates, *weights)


def partner(x, distance):
    return lax.ppermute(x, "dp", [(i, i ^ distance) for i in range(4)])


def ring_order(count):
    return list(range(0, count, 2)) + list(range(count - 1, 0, -2))


def around(x, step):
    ring = ring_order(lax.axis_size("expert"))
    count = len(ring)
    return lax.ppermute(x, "expert", [(ring[i], ring[(i + step) % count]) for i in range(count)])


def after(x, *others):
    return lax.optimization_barrier((x, *others))[0]


def add(a, b):
    return (a.astype(jnp.float32) + b.astype(jnp.float32)).astype(jnp.bfloat16)


def gather_rows(rows):
    half = rows.shape[0] // 2
    reach = lax.axis_size("expert") // 2
    above, below = [rows], [rows]
    for _ in range(reach - 1):
        above.append(around(above[-1], -1))
        below.append(around(below[-1], 1))
    far = [around(above[-1][:half], -1), around(below[-1][half:], 1)]
    return above + far + below[:0:-1], list(zip(above[1:], below[1:])) + [tuple(far)]


def scatter_sum(weighted, left, right):
    sources, rows, _ = weighted.shape
    half = rows // 2
    reach = sources // 2
    up, down = around(left, 1), around(right, -1)
    yield up, down
    up = jnp.concatenate([add(weighted[reach - 1, :half], up), weighted[reach - 1, half:]])
    down = jnp.concatenate([weighted[reach + 1, :half], add(weighted[reach + 1, half:], down)])
    for away in range(reach - 2, -1, -1):
        up, down = around(up, 1), around(down, -1)
        yield up, down
        if away:
            up = add(weighted[away], up)
            down = add(weighted[sources - away], down)


def every_expert(
    hidden_in,
    queries,
    key_pool,
    value_pool,
    page_table,
    prompt_lengths,
    expert_ids,
    gate_weights,
    norm_gain,
    trainer_gate_up,
    trainer_down,
):
    expert_count = lax.axis_size("expert")
    width = trainer_down.shape[2]
    attn = attention(queries, key_pool, value_pool, page_table, prompt_lengths)
    up_own, down_own = cast_weights(after(trainer_gate_up, attn[0]), trainer_down)
    attn = [attn[0]] + [partner(attn[d], d) for d in (1, 2, 3)]
    up_across = partner(after(up_own, *attn), 2)
    resid, rows = norm(
        after(hidden_in[0], up_own), attn, norm_gain, expert_ids[0], gate_weights[0]
    )
    gathered, arrived = gather_rows(rows)
    up_beside = partner(after(up_own, *arrived[0]), 1)
    down_beside = partner(after(down_own, *arrived[1]), 1)
    down_across = partner(after(down_own, *arrived[2]), 2)
    up_opposite = partner(after(up_across, *arrived[3]), 1)
    hidden_units, gates = expert_up(gathered, [up_own, up_beside, up_across, up_opposite])
    down_opposite = partner(after(down_across, hidden_units), 1)
    weights = (down_own, down_beside, down_across, down_opposite)
    slab = width // SLABS
    starts = range(0, width, slab)
    weighted = [
        expert_down(hidden_units, gates, weights, (first,) * 4, slab, expert_count)
        for first in starts
    ]
    mixed = []
    for first, partial in zip(starts, weighted):
        total = resid[:, first : first + slab].astype(jnp.float32)
        for term in (partial[0][0], *list(scatter_sum(*partial))[-1]):
            total = total + term.astype(jnp.float32)
        mixed.append(total.astype(jnp.bfloat16))
    return jnp.concatenate(mixed, axis=1)[None]


def solution(mesh):
    placed = (
        P("expert", "dp", None),
        P("expert", None, "dp"),
        P("expert", None, "dp"),
        P("expert", None, "dp"),
        P("expert", None),
        P("expert", None),
        P("expert", "dp", None),
        P("expert", "dp", None),
        P(),
        P("expert", "dp", None),
        P("expert", "dp", None),
    )
    dense = mesh.shape["expert"] == TOPK and mesh.shape["dp"] == 4
    return jax.shard_map(
        every_expert if dense else local, mesh=mesh, in_specs=placed, out_specs=P("expert", "dp", None), check_vma=False
    )
```

```python
import math

import jax
import jax.numpy as jnp
from jax import lax
from jax.experimental import pallas as pl
from jax.experimental.pallas import tpu as pltpu
from jax.sharding import PartitionSpec as P

HDIM = 128
TOPK = 8


epsilon = 1e-05


def fetch_weights(trainer_gate_up, trainer_down):
    return (
        lax.all_gather(trainer_gate_up.astype(jnp.bfloat16), "dp", axis=1, tiled=True),
        lax.all_gather(trainer_down.astype(jnp.bfloat16), "dp", axis=1, tiled=True),
    )


def local(
    hidden_in,
    queries,
    key_pool,
    value_pool,
    page_table,
    prompt_lengths,
    expert_ids,
    gate_weights,
    norm_gain,
    trainer_gate_up,
    trainer_down,
):
    col_tok = queries.shape[1]
    width_dev = queries.shape[2]
    heads_dev = width_dev // HDIM
    keys_all = jnp.take(key_pool, page_table[0], axis=0).reshape(col_tok, heads_dev, HDIM)
    values_all = jnp.take(value_pool, page_table[0], axis=0).reshape(col_tok, heads_dev, HDIM)
    request_ends = jnp.cumsum(prompt_lengths[0])
    positions = lax.iota(jnp.int32, col_tok)
    request = jnp.sum((positions[:, None] >= request_ends[None, :]).astype(jnp.int32), axis=1)
    block_rows = math.gcd(col_tok, 512)
    query_blocks = queries[0].reshape(col_tok // block_rows, block_rows, heads_dev, HDIM)
    request_blocks = request.reshape(col_tok // block_rows, block_rows)
    score_scale = 1.0 / math.sqrt(HDIM)

    def attend(pieces):
        query_block, request_block = pieces
        scores = (
            jnp.einsum("qhd,khd->hqk", query_block, keys_all, preferred_element_type=jnp.float32)
            * score_scale
        )
        same_request = (request_block[:, None] == request[None, :])[None]
        scores = jnp.where(same_request, scores, -1e30)
        highest = jnp.max(scores, axis=-1, keepdims=True)
        weights = jnp.where(same_request, jnp.exp(scores - highest), 0.0)
        totals = jnp.sum(weights, axis=-1, keepdims=True)
        probs = (weights / totals).astype(jnp.bfloat16)
        output = jnp.einsum("hqk,khd->qhd", probs, values_all, preferred_element_type=jnp.float32)
        return output.astype(jnp.bfloat16).reshape(block_rows, width_dev)

    attn_heads = lax.map(attend, (query_blocks, request_blocks)).reshape(1, col_tok, width_dev)
    attn_tokens = lax.all_to_all(attn_heads, "dp", split_axis=1, concat_axis=2, tiled=True)
    resid32 = (
        (hidden_in.astype(jnp.float32) + attn_tokens.astype(jnp.float32))
        .astype(jnp.bfloat16)
        .astype(jnp.float32)
    )
    mean_square = jnp.mean(resid32 * resid32, axis=-1, keepdims=True)
    normed = (resid32 * lax.rsqrt(mean_square + epsilon) * norm_gain).astype(jnp.bfloat16)
    server_gate_up, server_down = fetch_weights(trainer_gate_up, trainer_down)
    token_rows = normed.shape[1]
    width = normed.shape[2]
    expert_count = lax.axis_size("expert")
    capacity = min(token_rows, token_rows * TOPK * 5 // (4 * expert_count))
    hidden_size = server_gate_up.shape[2] // 2
    ids_flat = expert_ids[0].reshape(token_rows * TOPK)
    onehot = (ids_flat[:, None] == lax.iota(jnp.int32, expert_count)[None, :]).astype(jnp.int32)
    earlier = jnp.cumsum(onehot, axis=0) - onehot
    slot_index = jnp.sum(earlier * onehot, axis=1)
    flat_slot = ids_flat * capacity + slot_index
    placement = (
        flat_slot[:, None] == lax.iota(jnp.int32, expert_count * capacity)[None, :]
    ).astype(jnp.bfloat16)
    dispatch_matrix = jnp.sum(placement.reshape(token_rows, TOPK, expert_count * capacity), axis=1)
    outgoing = jnp.einsum(
        "ts,td->sd", dispatch_matrix, normed[0], preferred_element_type=jnp.float32
    )
    outgoing = outgoing.astype(jnp.bfloat16).reshape(expert_count, capacity, width)
    received = lax.all_to_all(outgoing, "expert", split_axis=0, concat_axis=0, tiled=True)
    sources, items, features = received.shape
    slot_rows = received.reshape(sources * items, features)
    gate_up = jnp.dot(slot_rows, server_gate_up[0], preferred_element_type=jnp.float32)
    hidden_units = (jax.nn.silu(gate_up[:, :hidden_size]) * gate_up[:, hidden_size:]).astype(
        jnp.bfloat16
    )
    outputs = jnp.dot(hidden_units, server_down[0], preferred_element_type=jnp.float32).astype(
        jnp.bfloat16
    )
    returned = lax.all_to_all(
        outputs.reshape(sources, items, features), "expert", split_axis=0, concat_axis=0, tiled=True
    )
    copies = jnp.take(returned.reshape(expert_count * capacity, width), flat_slot, axis=0)
    copies = copies.reshape(token_rows, TOPK, width).astype(jnp.float32)
    mixture = jnp.einsum("tk,tkd->td", gate_weights[0], copies)
    mixed = resid32[0] + mixture
    return mixed.astype(jnp.bfloat16)[None]

LANES = 128
VMEM_LIMIT = 32 * 2**20
VMEM_MOST = 60 * 2**20
SLABS = 2
CAST_STEPS = 4
SMALL = pl.CostEstimate(flops=1, bytes_accessed=1, transcendentals=0)


def params(limit=VMEM_LIMIT):
    return pltpu.CompilerParams(vmem_limit_bytes=limit)


def vmem(count):
    return [pl.BlockSpec(memory_space=pltpu.VMEM)] * count


def attention_kernel(*refs):
    sources, outs, scratch = refs[:5], refs[5:9], refs[9:]
    table, lengths, q_ref, k_ref, v_ref, attn, arrived = scratch
    copies = [
        pltpu.make_async_copy(source, target, arrived.at[i])
        for i, (source, target) in enumerate(
            zip(
                (*sources[:2], sources[2].at[0], *sources[3:5]),
                (table, lengths, q_ref, k_ref, v_ref),
            )
        )
    ]
    for copy in copies:
        copy.start()
    for copy in copies:
        copy.wait()
    tokens, width = q_ref.shape
    pages = k_ref.shape[0]
    row = lax.broadcasted_iota(jnp.int32, (tokens, tokens), 0)
    column = lax.broadcasted_iota(jnp.int32, (tokens, tokens), 1)
    row_request = jnp.zeros((tokens, tokens), jnp.int32)
    column_request = jnp.zeros((tokens, tokens), jnp.int32)
    end = jnp.int32(0)
    for r in range(lengths.shape[1]):
        end = end + lengths[0, r]
        row_request += (row >= end).astype(jnp.int32)
        column_request += (column >= end).astype(jnp.int32)
    same = row_request == column_request
    for h in range(width // HDIM):
        lanes = slice(h * HDIM, (h + 1) * HDIM)
        keys = jnp.concatenate([k_ref[table[0, p], :, lanes] for p in range(pages)], axis=0)
        values = jnp.concatenate([v_ref[table[0, p], :, lanes] for p in range(pages)], axis=0)
        scores = lax.dot_general(
            q_ref[:, lanes], keys, (((1,), (1,)), ((), ())), preferred_element_type=jnp.float32
        ) * (1.0 / math.sqrt(HDIM))
        scores = jnp.where(same, scores, -1e30)
        highest = jnp.max(scores, axis=-1, keepdims=True)
        weight = jnp.where(same, jnp.exp(scores - highest), 0.0)
        probs = (weight / jnp.sum(weight, axis=-1, keepdims=True)).astype(jnp.bfloat16)
        attn[:, lanes] = jnp.dot(probs, values, preferred_element_type=jnp.float32).astype(
            jnp.bfloat16
        )
    own = lax.axis_index("dp")
    rows = tokens // 4
    for d in range(4):
        first = pl.multiple_of((own ^ d) * rows, rows)
        outs[d][...] = attn[pl.ds(first, rows), :]


def attention(queries, key_pool, value_pool, page_table, prompt_lengths):
    tokens, width = queries.shape[1:]
    return pl.pallas_call(
        attention_kernel,
        out_shape=[jax.ShapeDtypeStruct((tokens // 4, width), jnp.bfloat16)] * 4,
        in_specs=[pl.BlockSpec(memory_space=pltpu.HBM)] * 5,
        out_specs=vmem(4),
        scratch_shapes=[
            pltpu.SMEM(page_table.shape, jnp.int32),
            pltpu.SMEM(prompt_lengths.shape, jnp.int32),
            pltpu.VMEM((tokens, width), jnp.bfloat16),
            pltpu.VMEM(key_pool.shape, jnp.bfloat16),
            pltpu.VMEM(value_pool.shape, jnp.bfloat16),
            pltpu.VMEM((tokens, width), jnp.bfloat16),
            pltpu.SemaphoreType.DMA((5,)),
        ],
        compiler_params=params(VMEM_MOST),
        name="attention",
    )(page_table, prompt_lengths, queries, key_pool, value_pool)


def norm_kernel(hidden_ref, a0, a1, a2, a3, gain_ref, ids_ref, gates_ref, resid_ref, rows_ref):
    own = lax.axis_index("dp")
    tokens, width = hidden_ref.shape
    block = width // 4
    total = jnp.zeros((tokens, 1), jnp.float32)
    for d, attn in enumerate((a0, a1, a2, a3)):
        columns = pl.ds(pl.multiple_of((own ^ d) * block, block), block)
        resid = (
            hidden_ref[:, columns].astype(jnp.float32) + attn[...].astype(jnp.float32)
        ).astype(jnp.bfloat16)
        resid_ref[:, columns] = resid
        resid32 = resid.astype(jnp.float32)
        total += jnp.sum(resid32 * resid32, axis=-1, keepdims=True)
    inverse = lax.rsqrt(total / width + epsilon)
    for d in range(4):
        columns = pl.ds(pl.multiple_of((own ^ d) * block, block), block)
        rows_ref[:, d * block : (d + 1) * block] = (
            resid_ref[:, columns].astype(jnp.float32) * inverse * gain_ref[:, columns]
        ).astype(jnp.bfloat16)
    lane = lax.broadcasted_iota(jnp.int32, (tokens, LANES), 1)
    gates = jnp.zeros((tokens, LANES), jnp.float32)
    for k in range(TOPK):
        gates += jnp.where(ids_ref[:, k : k + 1] == lane % TOPK, gates_ref[:, k : k + 1], 0.0)
    high = gates.astype(jnp.bfloat16).astype(jnp.float32)
    middle = (gates - high).astype(jnp.bfloat16).astype(jnp.float32)
    low = gates - high - middle
    part = lane // TOPK
    terms = jnp.where(part == 0, high, jnp.where(part == 1, middle, jnp.where(part == 2, low, 0.0)))
    rows_ref[:, width:] = terms.astype(jnp.bfloat16)


def norm(hidden_in, attn, norm_gain, expert_ids, gate_weights):
    tokens, width = hidden_in.shape
    return pl.pallas_call(
        norm_kernel,
        out_shape=[
            jax.ShapeDtypeStruct((tokens, width), jnp.bfloat16),
            jax.ShapeDtypeStruct((tokens, width + LANES), jnp.bfloat16),
        ],
        in_specs=vmem(8),
        out_specs=vmem(2),
        compiler_params=params(),
        cost_estimate=SMALL,
        name="norm",
    )(hidden_in, *attn, norm_gain[None, :], expert_ids, gate_weights)


def cast_kernel(spans, *refs):
    count = len(spans)
    sources, targets, scratch = refs[:count], refs[count : 2 * count], refs[2 * count :]
    wide, narrow, arrived, left = scratch[:count], scratch[count : 2 * count], *scratch[-2:]

    def rows_of(i, step, first=0):
        rows = wide[i].shape[0] // CAST_STEPS
        return pl.ds(first + step * rows, rows)

    def copies_in(step):
        for i, (first, _) in enumerate(spans):
            yield pltpu.make_async_copy(
                sources[i].at[0, rows_of(i, step, first)],
                wide[i].at[rows_of(i, step)],
                arrived.at[step, i],
            )

    def copies_out(step):
        for i in range(count):
            here = rows_of(i, step)
            yield pltpu.make_async_copy(narrow[i].at[here], targets[i].at[here], left.at[step, i])

    for step in range(CAST_STEPS):
        for copy in copies_in(step):
            copy.start()
    for step in range(CAST_STEPS):
        for copy in copies_in(step):
            copy.wait()
        for i in range(count):
            here = rows_of(i, step)
            narrow[i][here] = wide[i][here].astype(jnp.bfloat16)
        for copy in copies_out(step):
            copy.start()
    for step in range(CAST_STEPS):
        for copy in copies_out(step):
            copy.wait()


def cast_rows(arrays, spans):
    shapes = [(count, x.shape[2]) for x, (_, count) in zip(arrays, spans)]
    return pl.pallas_call(
        lambda *refs: cast_kernel(spans, *refs),
        out_shape=[jax.ShapeDtypeStruct(shape, jnp.bfloat16) for shape in shapes],
        in_specs=[pl.BlockSpec(memory_space=pltpu.HBM)] * len(arrays),
        out_specs=[pl.BlockSpec(memory_space=pltpu.HBM)] * len(arrays),
        scratch_shapes=[pltpu.VMEM(shape, jnp.float32) for shape in shapes]
        + [pltpu.VMEM(shape, jnp.bfloat16) for shape in shapes]
        + [pltpu.SemaphoreType.DMA((CAST_STEPS, len(arrays)))] * 2,
        compiler_params=params(VMEM_MOST),
        name="cast_rows",
    )(*arrays)


def load_tiles(pieces, weights, arrived, tiles, block):
    def copies(tile):
        first = 0
        for index, piece in enumerate(pieces):
            depth = piece.shape[0]
            for part in range(2):
                columns = pl.ds((part * tiles + tile) * block, block)
                yield pltpu.make_async_copy(
                    piece.at[:, columns],
                    weights.at[pl.ds(first, depth), columns],
                    arrived.at[tile, index, part],
                )
            first += depth

    for tile in range(tiles):
        for copy in copies(tile):
            copy.start()

    def wait(tile):
        for copy in copies(tile):
            copy.wait()

    return wait


def up_kernel(sources, pieces, *refs):
    row_refs = refs[:sources]
    weight_refs = refs[sources : sources + pieces]
    hidden_ref, own_gate_ref, rows, weights, units, arrived = refs[sources + pieces :]
    width = rows.shape[1]
    tiles, _, block = units.shape
    wait = load_tiles(weight_refs, weights, arrived, tiles, block)
    expert = lax.axis_index("expert")
    first = 0
    for ref in row_refs:
        count = ref.shape[0]
        here = slice(first, first + count)
        rows[here, :] = ref[:, :width]
        terms = ref[:, width:].astype(jnp.float32)
        lane = lax.broadcasted_iota(jnp.int32, terms.shape, 1)
        own_gate_ref[here, :] = jnp.sum(
            jnp.where(lane % TOPK == expert, terms, 0.0), axis=-1, keepdims=True
        )
        first += count
    for tile in range(tiles):
        wait(tile)
        gate, up = (
            jnp.dot(
                rows[...],
                weights[:, (part * tiles + tile) * block : (part * tiles + tile + 1) * block],
                preferred_element_type=jnp.float32,
            )
            for part in range(2)
        )
        units[tile] = (gate / (1.0 + jnp.exp(-gate)) * up).astype(jnp.bfloat16)
    own = lax.axis_index("dp")
    for d in range(4):
        hidden_ref[:, d * block : (d + 1) * block] = units[own ^ d]


def expert_up(rows, weights):
    tokens = sum(piece.shape[0] for piece in rows)
    features = sum(piece.shape[0] for piece in weights)
    width = weights[0].shape[1]
    hidden_size = width // 2
    return pl.pallas_call(
        lambda *refs: up_kernel(len(rows), len(weights), *refs),
        out_shape=[
            jax.ShapeDtypeStruct((tokens, hidden_size), jnp.bfloat16),
            jax.ShapeDtypeStruct((tokens, 1), jnp.float32),
        ],
        in_specs=vmem(len(rows)) + [pl.BlockSpec(memory_space=pl.ANY)] * len(weights),
        out_specs=vmem(2),
        scratch_shapes=[
            pltpu.VMEM((tokens, features), jnp.bfloat16),
            pltpu.VMEM((features, width), jnp.bfloat16),
            pltpu.VMEM((4, tokens, hidden_size // 4), jnp.bfloat16),
            pltpu.SemaphoreType.DMA((4, len(weights), 2)),
        ],
        compiler_params=params(),
        cost_estimate=SMALL,
        name="expert_up",
    )(*rows, *weights)


def down_kernel(firsts, hidden_ref, gate_ref, w0, w1, w2, w3, *refs):
    out_ref, left_ref, right_ref, weights, arrived = refs
    depth, width = w0.shape[0], weights.shape[1]
    copies = [
        pltpu.make_async_copy(
            ref.at[:, pl.ds(first, width)], weights.at[pl.ds(d * depth, depth)], arrived.at[d]
        )
        for d, (ref, first) in enumerate(zip((w0, w1, w2, w3), firsts))
    ]
    for copy in copies:
        copy.start()
    for copy in copies:
        copy.wait()
    total = jnp.dot(hidden_ref[...], weights[...], preferred_element_type=jnp.float32)
    weighted = (total * gate_ref[...]).astype(jnp.bfloat16)
    sources, rows, _ = out_ref.shape
    out_ref[...] = weighted.reshape(sources, rows, width)
    middle, half = sources // 2 * rows, rows // 2
    left_ref[...] = weighted[middle : middle + half]
    right_ref[...] = weighted[middle + half : middle + rows]


def expert_down(hidden_units, gates, weights, firsts, width, sources):
    tokens, hidden_size = hidden_units.shape
    rows = tokens // sources
    return pl.pallas_call(
        lambda *refs: down_kernel(firsts, *refs),
        out_shape=[
            jax.ShapeDtypeStruct((sources, rows, width), jnp.bfloat16),
            jax.ShapeDtypeStruct((rows // 2, width), jnp.bfloat16),
            jax.ShapeDtypeStruct((rows // 2, width), jnp.bfloat16),
        ],
        in_specs=vmem(2) + [pl.BlockSpec(memory_space=pl.ANY)] * 4,
        out_specs=vmem(3),
        scratch_shapes=[
            pltpu.VMEM((hidden_size, width), jnp.bfloat16),
            pltpu.SemaphoreType.DMA((4,)),
        ],
        compiler_params=params(),
        cost_estimate=SMALL,
        name="expert_down",
    )(hidden_units, gates, *weights)


def partner(x, distance):
    return lax.ppermute(x, "dp", [(i, i ^ distance) for i in range(4)])


def ring_order(count):
    return list(range(0, count, 2)) + list(range(count - 1, 0, -2))


def around(x, step):
    ring = ring_order(lax.axis_size("expert"))
    count = len(ring)
    return lax.ppermute(x, "expert", [(ring[i], ring[(i + step) % count]) for i in range(count)])


def after(x, *others):
    return lax.optimization_barrier((x, *others))[0]


def add(a, b):
    return (a.astype(jnp.float32) + b.astype(jnp.float32)).astype(jnp.bfloat16)


def gather_rows(rows):
    half = rows.shape[0] // 2
    reach = lax.axis_size("expert") // 2
    above, below = [rows], [rows]
    for _ in range(reach - 1):
        above.append(around(above[-1], -1))
        below.append(around(below[-1], 1))
    far = [around(above[-1][:half], -1), around(below[-1][half:], 1)]
    return above + far + below[:0:-1], list(zip(above[1:], below[1:])) + [tuple(far)]


def scatter_sums(parts):
    sources, rows, _ = parts[0][0].shape
    half = rows // 2
    reach = sources // 2
    moving = [(left, right) for _, left, right in parts]
    for step in range(reach):
        previous = None
        for i, (weighted, _, _) in enumerate(parts):
            up, down = moving[i]
            if step:
                up, down = lax.optimization_barrier((up, down))
                away = reach - step
                if step == 1:
                    up = jnp.concatenate([add(weighted[away, :half], up), weighted[away, half:]])
                    down = jnp.concatenate(
                        [weighted[-away, :half], add(weighted[-away, half:], down)]
                    )
                else:
                    up, down = add(weighted[away], up), add(weighted[-away], down)
            if previous is not None:
                up, down = after(up, *previous), after(down, *previous)
            previous = moving[i] if step else None
            moving[i] = around(up, 1), around(down, -1)
    return [(weighted[0], *ends) for (weighted, _, _), ends in zip(parts, moving)]


def every_expert(
    hidden_in,
    queries,
    key_pool,
    value_pool,
    page_table,
    prompt_lengths,
    expert_ids,
    gate_weights,
    norm_gain,
    trainer_gate_up,
    trainer_down,
):
    expert_count = lax.axis_size("expert")
    width = trainer_down.shape[2]
    depth = trainer_gate_up.shape[1]
    early = depth // 4
    late = depth - early
    (first_own,) = cast_rows([trainer_gate_up], [(0, early)])
    first_across = partner(first_own, 2)
    attn = attention(
        after(queries, first_own), key_pool, value_pool, page_table, prompt_lengths
    )
    rest_own, down_own = cast_rows(
        [after(trainer_gate_up, attn[0]), trainer_down],
        [(early, late), (0, trainer_down.shape[1])],
    )
    attn = [attn[0]] + [partner(attn[d], d) for d in (1, 2, 3)]
    rest_across = partner(after(rest_own, *attn), 2)
    resid, rows = norm(
        after(hidden_in[0], rest_own, first_across),
        attn,
        norm_gain,
        expert_ids[0],
        gate_weights[0],
    )
    gathered, arrived = gather_rows(rows)
    first_beside = partner(after(first_own, *arrived[0]), 1)
    first_opposite = partner(after(first_across, *arrived[0]), 1)
    rest_beside = partner(after(rest_own, *arrived[0]), 1)
    down_beside = partner(after(down_own, *arrived[1]), 1)
    down_across = partner(after(down_own, *arrived[2]), 2)
    ready = after(rest_across, *arrived[3])
    rest_opposite = [partner(ready[i : i + early], 1) for i in range(0, late, early)]
    hidden_units, gates = expert_up(
        gathered,
        [first_own, rest_own, first_beside, rest_beside]
        + [first_across, rest_across, first_opposite, *rest_opposite],
    )
    down_opposite = partner(after(down_across, hidden_units), 1)
    weights = (down_own, down_beside, down_across, down_opposite)
    slab = width // SLABS
    starts = range(0, width, slab)
    weighted = [
        expert_down(hidden_units, gates, weights, (first,) * 4, slab, expert_count)
        for first in starts
    ]
    mixed = []
    for first, terms in zip(starts, scatter_sums(weighted)):
        total = resid[:, first : first + slab].astype(jnp.float32)
        for term in terms:
            total = total + term.astype(jnp.float32)
        mixed.append(total.astype(jnp.bfloat16))
    return jnp.concatenate(mixed, axis=1)[None]


def solution(mesh):
    placed = (
        P("expert", "dp", None),
        P("expert", None, "dp"),
        P("expert", None, "dp"),
        P("expert", None, "dp"),
        P("expert", None),
        P("expert", None),
        P("expert", "dp", None),
        P("expert", "dp", None),
        P(),
        P("expert", "dp", None),
        P("expert", "dp", None),
    )
    dense = mesh.shape["expert"] == TOPK and mesh.shape["dp"] == 4
    return jax.shard_map(
        every_expert if dense else local, mesh=mesh, in_specs=placed, out_specs=P("expert", "dp", None), check_vma=False
    )
```

```python
import math

import jax
import jax.numpy as jnp
from jax import lax
from jax.experimental import pallas as pl
from jax.experimental.pallas import tpu as pltpu
from jax.sharding import PartitionSpec as P

HDIM = 128
TOPK = 8


epsilon = 1e-05


def fetch_weights(trainer_gate_up, trainer_down):
    return (
        lax.all_gather(trainer_gate_up.astype(jnp.bfloat16), "dp", axis=1, tiled=True),
        lax.all_gather(trainer_down.astype(jnp.bfloat16), "dp", axis=1, tiled=True),
    )


def local(
    hidden_in,
    queries,
    key_pool,
    value_pool,
    page_table,
    prompt_lengths,
    expert_ids,
    gate_weights,
    norm_gain,
    trainer_gate_up,
    trainer_down,
):
    col_tok = queries.shape[1]
    width_dev = queries.shape[2]
    heads_dev = width_dev // HDIM
    keys_all = jnp.take(key_pool, page_table[0], axis=0).reshape(col_tok, heads_dev, HDIM)
    values_all = jnp.take(value_pool, page_table[0], axis=0).reshape(col_tok, heads_dev, HDIM)
    request_ends = jnp.cumsum(prompt_lengths[0])
    positions = lax.iota(jnp.int32, col_tok)
    request = jnp.sum((positions[:, None] >= request_ends[None, :]).astype(jnp.int32), axis=1)
    block_rows = math.gcd(col_tok, 512)
    query_blocks = queries[0].reshape(col_tok // block_rows, block_rows, heads_dev, HDIM)
    request_blocks = request.reshape(col_tok // block_rows, block_rows)
    score_scale = 1.0 / math.sqrt(HDIM)

    def attend(pieces):
        query_block, request_block = pieces
        scores = (
            jnp.einsum("qhd,khd->hqk", query_block, keys_all, preferred_element_type=jnp.float32)
            * score_scale
        )
        same_request = (request_block[:, None] == request[None, :])[None]
        scores = jnp.where(same_request, scores, -1e30)
        highest = jnp.max(scores, axis=-1, keepdims=True)
        weights = jnp.where(same_request, jnp.exp(scores - highest), 0.0)
        totals = jnp.sum(weights, axis=-1, keepdims=True)
        probs = (weights / totals).astype(jnp.bfloat16)
        output = jnp.einsum("hqk,khd->qhd", probs, values_all, preferred_element_type=jnp.float32)
        return output.astype(jnp.bfloat16).reshape(block_rows, width_dev)

    attn_heads = lax.map(attend, (query_blocks, request_blocks)).reshape(1, col_tok, width_dev)
    attn_tokens = lax.all_to_all(attn_heads, "dp", split_axis=1, concat_axis=2, tiled=True)
    resid32 = (
        (hidden_in.astype(jnp.float32) + attn_tokens.astype(jnp.float32))
        .astype(jnp.bfloat16)
        .astype(jnp.float32)
    )
    mean_square = jnp.mean(resid32 * resid32, axis=-1, keepdims=True)
    normed = (resid32 * lax.rsqrt(mean_square + epsilon) * norm_gain).astype(jnp.bfloat16)
    server_gate_up, server_down = fetch_weights(trainer_gate_up, trainer_down)
    token_rows = normed.shape[1]
    width = normed.shape[2]
    expert_count = lax.axis_size("expert")
    capacity = min(token_rows, token_rows * TOPK * 5 // (4 * expert_count))
    hidden_size = server_gate_up.shape[2] // 2
    ids_flat = expert_ids[0].reshape(token_rows * TOPK)
    onehot = (ids_flat[:, None] == lax.iota(jnp.int32, expert_count)[None, :]).astype(jnp.int32)
    earlier = jnp.cumsum(onehot, axis=0) - onehot
    slot_index = jnp.sum(earlier * onehot, axis=1)
    flat_slot = ids_flat * capacity + slot_index
    placement = (
        flat_slot[:, None] == lax.iota(jnp.int32, expert_count * capacity)[None, :]
    ).astype(jnp.bfloat16)
    dispatch_matrix = jnp.sum(placement.reshape(token_rows, TOPK, expert_count * capacity), axis=1)
    outgoing = jnp.einsum(
        "ts,td->sd", dispatch_matrix, normed[0], preferred_element_type=jnp.float32
    )
    outgoing = outgoing.astype(jnp.bfloat16).reshape(expert_count, capacity, width)
    received = lax.all_to_all(outgoing, "expert", split_axis=0, concat_axis=0, tiled=True)
    sources, items, features = received.shape
    slot_rows = received.reshape(sources * items, features)
    gate_up = jnp.dot(slot_rows, server_gate_up[0], preferred_element_type=jnp.float32)
    hidden_units = (jax.nn.silu(gate_up[:, :hidden_size]) * gate_up[:, hidden_size:]).astype(
        jnp.bfloat16
    )
    outputs = jnp.dot(hidden_units, server_down[0], preferred_element_type=jnp.float32).astype(
        jnp.bfloat16
    )
    returned = lax.all_to_all(
        outputs.reshape(sources, items, features), "expert", split_axis=0, concat_axis=0, tiled=True
    )
    copies = jnp.take(returned.reshape(expert_count * capacity, width), flat_slot, axis=0)
    copies = copies.reshape(token_rows, TOPK, width).astype(jnp.float32)
    mixture = jnp.einsum("tk,tkd->td", gate_weights[0], copies)
    mixed = resid32[0] + mixture
    return mixed.astype(jnp.bfloat16)[None]

LANES = 128
VMEM_LIMIT = 32 * 2**20
VMEM_MOST = 60 * 2**20
CAST_STEPS = 4
SLABS = 2
SMALL = pl.CostEstimate(flops=1, bytes_accessed=1, transcendentals=0)


def params(limit=VMEM_LIMIT):
    return pltpu.CompilerParams(vmem_limit_bytes=limit)


def vmem(count):
    return [pl.BlockSpec(memory_space=pltpu.VMEM)] * count


def attention_kernel(*refs):
    sources, outs, piece_ref, scratch = refs[:6], refs[6:10], refs[10], refs[11:]
    table, lengths, q_ref, k_ref, v_ref, weights, attn, arrived = scratch
    copies = [
        pltpu.make_async_copy(source, target, arrived.at[i])
        for i, (source, target) in enumerate(
            zip(
                (*sources[:2], sources[2].at[0], *sources[3:5]),
                (table, lengths, q_ref, k_ref, v_ref),
            )
        )
    ]
    rows = weights.shape[0]
    copies.append(
        pltpu.make_async_copy(sources[5].at[0, pl.ds(0, rows)], weights, arrived.at[5])
    )
    for copy in copies:
        copy.start()
    for copy in copies[:5]:
        copy.wait()
    tokens, width = q_ref.shape
    pages = k_ref.shape[0]
    row = lax.broadcasted_iota(jnp.int32, (tokens, tokens), 0)
    column = lax.broadcasted_iota(jnp.int32, (tokens, tokens), 1)
    row_request = jnp.zeros((tokens, tokens), jnp.int32)
    column_request = jnp.zeros((tokens, tokens), jnp.int32)
    end = jnp.int32(0)
    for r in range(lengths.shape[1]):
        end = end + lengths[0, r]
        row_request += (row >= end).astype(jnp.int32)
        column_request += (column >= end).astype(jnp.int32)
    same = row_request == column_request
    for h in range(width // HDIM):
        lanes = slice(h * HDIM, (h + 1) * HDIM)
        keys = jnp.concatenate([k_ref[table[0, p], :, lanes] for p in range(pages)], axis=0)
        values = jnp.concatenate([v_ref[table[0, p], :, lanes] for p in range(pages)], axis=0)
        scores = lax.dot_general(
            q_ref[:, lanes], keys, (((1,), (1,)), ((), ())), preferred_element_type=jnp.float32
        ) * (1.0 / math.sqrt(HDIM))
        scores = jnp.where(same, scores, -1e30)
        highest = jnp.max(scores, axis=-1, keepdims=True)
        weight = jnp.where(same, jnp.exp(scores - highest), 0.0)
        probs = (weight / jnp.sum(weight, axis=-1, keepdims=True)).astype(jnp.bfloat16)
        attn[:, lanes] = jnp.dot(probs, values, preferred_element_type=jnp.float32).astype(
            jnp.bfloat16
        )
    own = lax.axis_index("dp")
    rows = tokens // 4
    for d in range(4):
        first = pl.multiple_of((own ^ d) * rows, rows)
        outs[d][...] = attn[pl.ds(first, rows), :]
    copies[5].wait()
    piece_ref[...] = weights[...].astype(jnp.bfloat16)


def attention(queries, key_pool, value_pool, page_table, prompt_lengths, gate_up, early):
    tokens, width = queries.shape[1:]
    return pl.pallas_call(
        attention_kernel,
        out_shape=[jax.ShapeDtypeStruct((tokens // 4, width), jnp.bfloat16)] * 4
        + [jax.ShapeDtypeStruct((early, gate_up.shape[2]), jnp.bfloat16)],
        in_specs=[pl.BlockSpec(memory_space=pltpu.HBM)] * 6,
        out_specs=vmem(5),
        scratch_shapes=[
            pltpu.SMEM(page_table.shape, jnp.int32),
            pltpu.SMEM(prompt_lengths.shape, jnp.int32),
            pltpu.VMEM((tokens, width), jnp.bfloat16),
            pltpu.VMEM(key_pool.shape, jnp.bfloat16),
            pltpu.VMEM(value_pool.shape, jnp.bfloat16),
            pltpu.VMEM((early, gate_up.shape[2]), jnp.float32),
            pltpu.VMEM((tokens, width), jnp.bfloat16),
            pltpu.SemaphoreType.DMA((6,)),
        ],
        compiler_params=params(VMEM_MOST),
        name="attention",
    )(page_table, prompt_lengths, queries, key_pool, value_pool, gate_up)


def norm_kernel(hidden_ref, a0, a1, a2, a3, gain_ref, ids_ref, gates_ref, resid_ref, rows_ref):
    own = lax.axis_index("dp")
    tokens, width = hidden_ref.shape
    block = width // 4
    total = jnp.zeros((tokens, 1), jnp.float32)
    for d, attn in enumerate((a0, a1, a2, a3)):
        columns = pl.ds(pl.multiple_of((own ^ d) * block, block), block)
        resid = (
            hidden_ref[:, columns].astype(jnp.float32) + attn[...].astype(jnp.float32)
        ).astype(jnp.bfloat16)
        resid_ref[:, columns] = resid
        resid32 = resid.astype(jnp.float32)
        total += jnp.sum(resid32 * resid32, axis=-1, keepdims=True)
    inverse = lax.rsqrt(total / width + epsilon)
    for d in range(4):
        columns = pl.ds(pl.multiple_of((own ^ d) * block, block), block)
        rows_ref[:, d * block : (d + 1) * block] = (
            resid_ref[:, columns].astype(jnp.float32) * inverse * gain_ref[:, columns]
        ).astype(jnp.bfloat16)
    lane = lax.broadcasted_iota(jnp.int32, (tokens, LANES), 1)
    gates = jnp.zeros((tokens, LANES), jnp.float32)
    for k in range(TOPK):
        gates += jnp.where(ids_ref[:, k : k + 1] == lane % TOPK, gates_ref[:, k : k + 1], 0.0)
    high = gates.astype(jnp.bfloat16).astype(jnp.float32)
    middle = (gates - high).astype(jnp.bfloat16).astype(jnp.float32)
    low = gates - high - middle
    part = lane // TOPK
    terms = jnp.where(part == 0, high, jnp.where(part == 1, middle, jnp.where(part == 2, low, 0.0)))
    rows_ref[:, width:] = terms.astype(jnp.bfloat16)


def norm(hidden_in, attn, norm_gain, expert_ids, gate_weights):
    tokens, width = hidden_in.shape
    return pl.pallas_call(
        norm_kernel,
        out_shape=[
            jax.ShapeDtypeStruct((tokens, width), jnp.bfloat16),
            jax.ShapeDtypeStruct((tokens, width + LANES), jnp.bfloat16),
        ],
        in_specs=vmem(8),
        out_specs=vmem(2),
        compiler_params=params(),
        cost_estimate=SMALL,
        name="norm",
    )(hidden_in, *attn, norm_gain[None, :], expert_ids, gate_weights)


def cast_kernel(spans, *refs):
    count = len(spans)
    sources, targets, scratch = refs[:count], refs[count : 2 * count], refs[2 * count :]
    wide, narrow, arrived, left = scratch[:count], scratch[count : 2 * count], *scratch[-2:]

    def rows_of(i, step, first=0):
        rows = wide[i].shape[0] // CAST_STEPS
        return pl.ds(first + step * rows, rows)

    def copies_in(step):
        for i, (first, _, column, columns) in enumerate(spans):
            yield pltpu.make_async_copy(
                sources[i].at[0, rows_of(i, step, first), pl.ds(column, columns)],
                wide[i].at[rows_of(i, step)],
                arrived.at[step, i],
            )

    def copies_out(step):
        for i in range(count):
            here = rows_of(i, step)
            yield pltpu.make_async_copy(narrow[i].at[here], targets[i].at[here], left.at[step, i])

    for step in range(CAST_STEPS):
        for copy in copies_in(step):
            copy.start()
    for step in range(CAST_STEPS):
        for copy in copies_in(step):
            copy.wait()
        for i in range(count):
            here = rows_of(i, step)
            narrow[i][here] = wide[i][here].astype(jnp.bfloat16)
        for copy in copies_out(step):
            copy.start()
    for step in range(CAST_STEPS):
        for copy in copies_out(step):
            copy.wait()


def cast_rows(arrays, spans):
    shapes = [(rows, columns) for _, rows, _, columns in spans]
    return pl.pallas_call(
        lambda *refs: cast_kernel(spans, *refs),
        out_shape=[jax.ShapeDtypeStruct(shape, jnp.bfloat16) for shape in shapes],
        in_specs=[pl.BlockSpec(memory_space=pltpu.HBM)] * len(arrays),
        out_specs=[pl.BlockSpec(memory_space=pltpu.HBM)] * len(arrays),
        scratch_shapes=[pltpu.VMEM(shape, jnp.float32) for shape in shapes]
        + [pltpu.VMEM(shape, jnp.bfloat16) for shape in shapes]
        + [pltpu.SemaphoreType.DMA((CAST_STEPS, len(arrays)))] * 2,
        compiler_params=params(VMEM_MOST),
        name="cast_rows",
    )(*arrays)


def load_tiles(pieces, weights, arrived, tiles, block):
    def copies(tile):
        first = 0
        for index, piece in enumerate(pieces):
            depth = piece.shape[0]
            for part in range(2):
                columns = pl.ds((part * tiles + tile) * block, block)
                yield pltpu.make_async_copy(
                    piece.at[:, columns],
                    weights.at[pl.ds(first, depth), columns],
                    arrived.at[tile, index, part],
                )
            first += depth

    for tile in range(tiles):
        for copy in copies(tile):
            copy.start()

    def wait(tile):
        for copy in copies(tile):
            copy.wait()

    return wait


def up_kernel(sources, pieces, *refs):
    row_refs = refs[:sources]
    weight_refs = refs[sources : sources + pieces]
    hidden_ref, own_gate_ref, rows, weights, units, arrived = refs[sources + pieces :]
    width = rows.shape[1]
    tiles, _, block = units.shape
    wait = load_tiles(weight_refs, weights, arrived, tiles, block)
    expert = lax.axis_index("expert")
    first = 0
    for ref in row_refs:
        count = ref.shape[0]
        here = slice(first, first + count)
        rows[here, :] = ref[:, :width]
        terms = ref[:, width:].astype(jnp.float32)
        lane = lax.broadcasted_iota(jnp.int32, terms.shape, 1)
        own_gate_ref[here, :] = jnp.sum(
            jnp.where(lane % TOPK == expert, terms, 0.0), axis=-1, keepdims=True
        )
        first += count
    for tile in range(tiles):
        wait(tile)
        gate, up = (
            jnp.dot(
                rows[...],
                weights[:, (part * tiles + tile) * block : (part * tiles + tile + 1) * block],
                preferred_element_type=jnp.float32,
            )
            for part in range(2)
        )
        units[tile] = (gate / (1.0 + jnp.exp(-gate)) * up).astype(jnp.bfloat16)
    own = lax.axis_index("dp")
    for d in range(4):
        hidden_ref[:, d * block : (d + 1) * block] = units[own ^ d]


def expert_up(rows, weights):
    tokens = sum(piece.shape[0] for piece in rows)
    features = sum(piece.shape[0] for piece in weights)
    width = weights[0].shape[1]
    hidden_size = width // 2
    return pl.pallas_call(
        lambda *refs: up_kernel(len(rows), len(weights), *refs),
        out_shape=[
            jax.ShapeDtypeStruct((tokens, hidden_size), jnp.bfloat16),
            jax.ShapeDtypeStruct((tokens, 1), jnp.float32),
        ],
        in_specs=vmem(len(rows)) + [pl.BlockSpec(memory_space=pl.ANY)] * len(weights),
        out_specs=vmem(2),
        scratch_shapes=[
            pltpu.VMEM((tokens, features), jnp.bfloat16),
            pltpu.VMEM((features, width), jnp.bfloat16),
            pltpu.VMEM((4, tokens, hidden_size // 4), jnp.bfloat16),
            pltpu.SemaphoreType.DMA((4, len(weights), 2)),
        ],
        compiler_params=params(),
        cost_estimate=SMALL,
        name="expert_up",
    )(*rows, *weights)


def down_kernel(column, hidden_ref, gate_ref, *refs):
    pieces, (out_ref, left_ref, right_ref, weights, arrived) = refs[:-5], refs[-5:]
    copies, first = [], 0
    for i, ref in enumerate(pieces):
        depth = ref.shape[0]
        copies.append(
            pltpu.make_async_copy(
                ref.at[:, pl.ds(column, weights.shape[1])],
                weights.at[pl.ds(first, depth)],
                arrived.at[i],
            )
        )
        first += depth
    for copy in copies:
        copy.start()
    for copy in copies:
        copy.wait()
    total = jnp.dot(hidden_ref[...], weights[...], preferred_element_type=jnp.float32)
    weighted = (total * gate_ref[...]).astype(jnp.bfloat16)
    sources, rows, width = out_ref.shape
    out_ref[...] = weighted.reshape(sources, rows, width)
    middle, half = sources // 2 * rows, rows // 2
    left_ref[...] = weighted[middle : middle + half]
    right_ref[...] = weighted[middle + half : middle + rows]


def expert_down(hidden_units, gates, weights, column, width, sources):
    tokens, hidden_size = hidden_units.shape
    rows = tokens // sources
    return pl.pallas_call(
        lambda *refs: down_kernel(column, *refs),
        out_shape=[
            jax.ShapeDtypeStruct((sources, rows, width), jnp.bfloat16),
            jax.ShapeDtypeStruct((rows // 2, width), jnp.bfloat16),
            jax.ShapeDtypeStruct((rows // 2, width), jnp.bfloat16),
        ],
        in_specs=vmem(2) + [pl.BlockSpec(memory_space=pl.ANY)] * len(weights),
        out_specs=vmem(3),
        scratch_shapes=[
            pltpu.VMEM((hidden_size, width), jnp.bfloat16),
            pltpu.SemaphoreType.DMA((len(weights),)),
        ],
        compiler_params=params(),
        cost_estimate=SMALL,
        name="expert_down",
    )(hidden_units, gates, *weights)


def partner(x, distance):
    return lax.ppermute(x, "dp", [(i, i ^ distance) for i in range(4)])


def ring_order(count):
    return list(range(0, count, 2)) + list(range(count - 1, 0, -2))


def around(x, step):
    ring = ring_order(lax.axis_size("expert"))
    count = len(ring)
    return lax.ppermute(x, "expert", [(ring[i], ring[(i + step) % count]) for i in range(count)])


def after(x, *others):
    return lax.optimization_barrier((x, *others))[0]


def add(a, b):
    return (a.astype(jnp.float32) + b.astype(jnp.float32)).astype(jnp.bfloat16)


def gather_rows(rows):
    half = rows.shape[0] // 2
    reach = lax.axis_size("expert") // 2
    above, below = [rows], [rows]
    for _ in range(reach - 1):
        above.append(around(above[-1], -1))
        below.append(around(below[-1], 1))
    far = [around(above[-1][:half], -1), around(below[-1][half:], 1)]
    return above + far + below[:0:-1], list(zip(above[1:], below[1:])) + [tuple(far)]


def scatter_sum(weighted, left, right):
    sources, rows, _ = weighted.shape
    half = rows // 2
    reach = sources // 2
    up, down = around(left, 1), around(right, -1)
    up = jnp.concatenate([add(weighted[reach - 1, :half], up), weighted[reach - 1, half:]])
    down = jnp.concatenate([weighted[reach + 1, :half], add(weighted[reach + 1, half:], down)])
    for away in range(reach - 2, 0, -1):
        up = add(weighted[away], around(up, 1))
        down = add(weighted[sources - away], around(down, -1))
    return weighted[0], around(up, 1), around(down, -1)


def relayed(x, rows):
    return [partner(x[i : i + rows], 1) for i in range(0, x.shape[0], rows)]


def every_expert(
    hidden_in,
    queries,
    key_pool,
    value_pool,
    page_table,
    prompt_lengths,
    expert_ids,
    gate_weights,
    norm_gain,
    trainer_gate_up,
    trainer_down,
):
    expert_count = lax.axis_size("expert")
    width = trainer_down.shape[2]
    depth, columns = trainer_gate_up.shape[1:]
    down_depth = trainer_down.shape[1]
    early = depth // 8
    slab = width // SLABS
    *attn, first_own = attention(
        queries, key_pool, value_pool, page_table, prompt_lengths, trainer_gate_up, early
    )
    first_across = partner(first_own, 2)
    rest_own, down_own = cast_rows(
        [after(trainer_gate_up, attn[0]), trainer_down],
        [(early, depth - early, 0, columns), (0, down_depth, 0, width)],
    )
    attn = [attn[0]] + [partner(attn[d], d) for d in (1, 2, 3)]
    rest_across = partner(after(rest_own, first_across, *attn), 2)
    resid, rows = norm(
        after(hidden_in[0], rest_own), attn, norm_gain, expert_ids[0], gate_weights[0]
    )
    gathered, arrived = gather_rows(rows)
    first_beside = partner(after(first_own, *arrived[0]), 1)
    first_opposite = partner(after(first_across, *arrived[0]), 1)
    rest_beside = partner(after(rest_own, *arrived[0]), 1)
    down_beside = partner(after(down_own, *arrived[1]), 1)
    down_across = partner(after(down_own, *arrived[2]), 2)
    rest_opposite = relayed(after(rest_across, *arrived[3]), early)
    hidden_units, gates = expert_up(
        gathered,
        [first_own, rest_own, first_beside, rest_beside]
        + [first_across, rest_across, first_opposite, *rest_opposite],
    )
    down_opposite = relayed(after(down_across, hidden_units), down_depth // 2)
    weights = [down_own, down_beside, down_across, *down_opposite]
    mixed = []
    for first in range(0, width, slab):
        weighted = expert_down(hidden_units, gates, weights, first, slab, expert_count)
        total = resid[:, first : first + slab].astype(jnp.float32)
        for term in scatter_sum(*weighted):
            total = total + term.astype(jnp.float32)
        mixed.append(total.astype(jnp.bfloat16))
    return jnp.concatenate(mixed, axis=1)[None]


def solution(mesh):
    placed = (
        P("expert", "dp", None),
        P("expert", None, "dp"),
        P("expert", None, "dp"),
        P("expert", None, "dp"),
        P("expert", None),
        P("expert", None),
        P("expert", "dp", None),
        P("expert", "dp", None),
        P(),
        P("expert", "dp", None),
        P("expert", "dp", None),
    )
    dense = mesh.shape["expert"] == TOPK and mesh.shape["dp"] == 4
    return jax.shard_map(
        every_expert if dense else local, mesh=mesh, in_specs=placed, out_specs=P("expert", "dp", None), check_vma=False
    )
```

```python
import math

import jax
import jax.numpy as jnp
from jax import lax
from jax.experimental import pallas as pl
from jax.experimental.pallas import tpu as pltpu
from jax.sharding import PartitionSpec as P

HDIM = 128
TOPK = 8


epsilon = 1e-05


def fetch_weights(trainer_gate_up, trainer_down):
    return (
        lax.all_gather(trainer_gate_up.astype(jnp.bfloat16), "dp", axis=1, tiled=True),
        lax.all_gather(trainer_down.astype(jnp.bfloat16), "dp", axis=1, tiled=True),
    )


def local(
    hidden_in,
    queries,
    key_pool,
    value_pool,
    page_table,
    prompt_lengths,
    expert_ids,
    gate_weights,
    norm_gain,
    trainer_gate_up,
    trainer_down,
):
    col_tok = queries.shape[1]
    width_dev = queries.shape[2]
    heads_dev = width_dev // HDIM
    keys_all = jnp.take(key_pool, page_table[0], axis=0).reshape(col_tok, heads_dev, HDIM)
    values_all = jnp.take(value_pool, page_table[0], axis=0).reshape(col_tok, heads_dev, HDIM)
    request_ends = jnp.cumsum(prompt_lengths[0])
    positions = lax.iota(jnp.int32, col_tok)
    request = jnp.sum((positions[:, None] >= request_ends[None, :]).astype(jnp.int32), axis=1)
    block_rows = math.gcd(col_tok, 512)
    query_blocks = queries[0].reshape(col_tok // block_rows, block_rows, heads_dev, HDIM)
    request_blocks = request.reshape(col_tok // block_rows, block_rows)
    score_scale = 1.0 / math.sqrt(HDIM)

    def attend(pieces):
        query_block, request_block = pieces
        scores = (
            jnp.einsum("qhd,khd->hqk", query_block, keys_all, preferred_element_type=jnp.float32)
            * score_scale
        )
        same_request = (request_block[:, None] == request[None, :])[None]
        scores = jnp.where(same_request, scores, -1e30)
        highest = jnp.max(scores, axis=-1, keepdims=True)
        weights = jnp.where(same_request, jnp.exp(scores - highest), 0.0)
        totals = jnp.sum(weights, axis=-1, keepdims=True)
        probs = (weights / totals).astype(jnp.bfloat16)
        output = jnp.einsum("hqk,khd->qhd", probs, values_all, preferred_element_type=jnp.float32)
        return output.astype(jnp.bfloat16).reshape(block_rows, width_dev)

    attn_heads = lax.map(attend, (query_blocks, request_blocks)).reshape(1, col_tok, width_dev)
    attn_tokens = lax.all_to_all(attn_heads, "dp", split_axis=1, concat_axis=2, tiled=True)
    resid32 = (
        (hidden_in.astype(jnp.float32) + attn_tokens.astype(jnp.float32))
        .astype(jnp.bfloat16)
        .astype(jnp.float32)
    )
    mean_square = jnp.mean(resid32 * resid32, axis=-1, keepdims=True)
    normed = (resid32 * lax.rsqrt(mean_square + epsilon) * norm_gain).astype(jnp.bfloat16)
    server_gate_up, server_down = fetch_weights(trainer_gate_up, trainer_down)
    token_rows = normed.shape[1]
    width = normed.shape[2]
    expert_count = lax.axis_size("expert")
    capacity = min(token_rows, token_rows * TOPK * 5 // (4 * expert_count))
    hidden_size = server_gate_up.shape[2] // 2
    ids_flat = expert_ids[0].reshape(token_rows * TOPK)
    onehot = (ids_flat[:, None] == lax.iota(jnp.int32, expert_count)[None, :]).astype(jnp.int32)
    earlier = jnp.cumsum(onehot, axis=0) - onehot
    slot_index = jnp.sum(earlier * onehot, axis=1)
    flat_slot = ids_flat * capacity + slot_index
    placement = (
        flat_slot[:, None] == lax.iota(jnp.int32, expert_count * capacity)[None, :]
    ).astype(jnp.bfloat16)
    dispatch_matrix = jnp.sum(placement.reshape(token_rows, TOPK, expert_count * capacity), axis=1)
    outgoing = jnp.einsum(
        "ts,td->sd", dispatch_matrix, normed[0], preferred_element_type=jnp.float32
    )
    outgoing = outgoing.astype(jnp.bfloat16).reshape(expert_count, capacity, width)
    received = lax.all_to_all(outgoing, "expert", split_axis=0, concat_axis=0, tiled=True)
    sources, items, features = received.shape
    slot_rows = received.reshape(sources * items, features)
    gate_up = jnp.dot(slot_rows, server_gate_up[0], preferred_element_type=jnp.float32)
    hidden_units = (jax.nn.silu(gate_up[:, :hidden_size]) * gate_up[:, hidden_size:]).astype(
        jnp.bfloat16
    )
    outputs = jnp.dot(hidden_units, server_down[0], preferred_element_type=jnp.float32).astype(
        jnp.bfloat16
    )
    returned = lax.all_to_all(
        outputs.reshape(sources, items, features), "expert", split_axis=0, concat_axis=0, tiled=True
    )
    copies = jnp.take(returned.reshape(expert_count * capacity, width), flat_slot, axis=0)
    copies = copies.reshape(token_rows, TOPK, width).astype(jnp.float32)
    mixture = jnp.einsum("tk,tkd->td", gate_weights[0], copies)
    mixed = resid32[0] + mixture
    return mixed.astype(jnp.bfloat16)[None]

LANES = 128
VMEM_LIMIT = 32 * 2**20
VMEM_MOST = 60 * 2**20
CAST_STEPS = 4
FIRST_SLAB = 10
SMALL = pl.CostEstimate(flops=1, bytes_accessed=1, transcendentals=0)


def params(limit=VMEM_LIMIT):
    return pltpu.CompilerParams(vmem_limit_bytes=limit)


def vmem(count):
    return [pl.BlockSpec(memory_space=pltpu.VMEM)] * count


def attention_kernel(*refs):
    sources, outs, piece_ref, scratch = refs[:6], refs[6:10], refs[10], refs[11:]
    table, lengths, q_ref, k_ref, v_ref, weights, attn, arrived = scratch
    copies = [
        pltpu.make_async_copy(source, target, arrived.at[i])
        for i, (source, target) in enumerate(
            zip(
                (*sources[:2], sources[2].at[0], *sources[3:5]),
                (table, lengths, q_ref, k_ref, v_ref),
            )
        )
    ]
    rows = weights.shape[0]
    copies.append(
        pltpu.make_async_copy(sources[5].at[0, pl.ds(0, rows)], weights, arrived.at[5])
    )
    for copy in copies:
        copy.start()
    for copy in copies[:5]:
        copy.wait()
    tokens, width = q_ref.shape
    pages = k_ref.shape[0]
    row = lax.broadcasted_iota(jnp.int32, (tokens, tokens), 0)
    column = lax.broadcasted_iota(jnp.int32, (tokens, tokens), 1)
    row_request = jnp.zeros((tokens, tokens), jnp.int32)
    column_request = jnp.zeros((tokens, tokens), jnp.int32)
    end = jnp.int32(0)
    for r in range(lengths.shape[1]):
        end = end + lengths[0, r]
        row_request += (row >= end).astype(jnp.int32)
        column_request += (column >= end).astype(jnp.int32)
    same = row_request == column_request
    for h in range(width // HDIM):
        lanes = slice(h * HDIM, (h + 1) * HDIM)
        keys = jnp.concatenate([k_ref[table[0, p], :, lanes] for p in range(pages)], axis=0)
        values = jnp.concatenate([v_ref[table[0, p], :, lanes] for p in range(pages)], axis=0)
        scores = lax.dot_general(
            q_ref[:, lanes], keys, (((1,), (1,)), ((), ())), preferred_element_type=jnp.float32
        ) * (1.0 / math.sqrt(HDIM))
        scores = jnp.where(same, scores, -1e30)
        highest = jnp.max(scores, axis=-1, keepdims=True)
        weight = jnp.where(same, jnp.exp(scores - highest), 0.0)
        probs = (weight / jnp.sum(weight, axis=-1, keepdims=True)).astype(jnp.bfloat16)
        attn[:, lanes] = jnp.dot(probs, values, preferred_element_type=jnp.float32).astype(
            jnp.bfloat16
        )
    own = lax.axis_index("dp")
    rows = tokens // 4
    for d in range(4):
        first = pl.multiple_of((own ^ d) * rows, rows)
        outs[d][...] = attn[pl.ds(first, rows), :]
    copies[5].wait()
    piece_ref[...] = weights[...].astype(jnp.bfloat16)


def attention(queries, key_pool, value_pool, page_table, prompt_lengths, gate_up, early):
    tokens, width = queries.shape[1:]
    return pl.pallas_call(
        attention_kernel,
        out_shape=[jax.ShapeDtypeStruct((tokens // 4, width), jnp.bfloat16)] * 4
        + [jax.ShapeDtypeStruct((early, gate_up.shape[2]), jnp.bfloat16)],
        in_specs=[pl.BlockSpec(memory_space=pltpu.HBM)] * 6,
        out_specs=vmem(5),
        scratch_shapes=[
            pltpu.SMEM(page_table.shape, jnp.int32),
            pltpu.SMEM(prompt_lengths.shape, jnp.int32),
            pltpu.VMEM((tokens, width), jnp.bfloat16),
            pltpu.VMEM(key_pool.shape, jnp.bfloat16),
            pltpu.VMEM(value_pool.shape, jnp.bfloat16),
            pltpu.VMEM((early, gate_up.shape[2]), jnp.float32),
            pltpu.VMEM((tokens, width), jnp.bfloat16),
            pltpu.SemaphoreType.DMA((6,)),
        ],
        compiler_params=params(VMEM_MOST),
        name="attention",
    )(page_table, prompt_lengths, queries, key_pool, value_pool, gate_up)


def norm_kernel(hidden_ref, a0, a1, a2, a3, gain_ref, ids_ref, gates_ref, resid_ref, rows_ref):
    own = lax.axis_index("dp")
    tokens, width = hidden_ref.shape
    block = width // 4
    total = jnp.zeros((tokens, 1), jnp.float32)
    for d, attn in enumerate((a0, a1, a2, a3)):
        columns = pl.ds(pl.multiple_of((own ^ d) * block, block), block)
        resid = (
            hidden_ref[:, columns].astype(jnp.float32) + attn[...].astype(jnp.float32)
        ).astype(jnp.bfloat16)
        resid_ref[:, columns] = resid
        resid32 = resid.astype(jnp.float32)
        total += jnp.sum(resid32 * resid32, axis=-1, keepdims=True)
    inverse = lax.rsqrt(total / width + epsilon)
    for d in range(4):
        columns = pl.ds(pl.multiple_of((own ^ d) * block, block), block)
        rows_ref[:, d * block : (d + 1) * block] = (
            resid_ref[:, columns].astype(jnp.float32) * inverse * gain_ref[:, columns]
        ).astype(jnp.bfloat16)
    lane = lax.broadcasted_iota(jnp.int32, (tokens, LANES), 1)
    gates = jnp.zeros((tokens, LANES), jnp.float32)
    for k in range(TOPK):
        gates += jnp.where(ids_ref[:, k : k + 1] == lane % TOPK, gates_ref[:, k : k + 1], 0.0)
    high = gates.astype(jnp.bfloat16).astype(jnp.float32)
    middle = (gates - high).astype(jnp.bfloat16).astype(jnp.float32)
    low = gates - high - middle
    part = lane // TOPK
    terms = jnp.where(part == 0, high, jnp.where(part == 1, middle, jnp.where(part == 2, low, 0.0)))
    rows_ref[:, width:] = terms.astype(jnp.bfloat16)


def norm(hidden_in, attn, norm_gain, expert_ids, gate_weights):
    tokens, width = hidden_in.shape
    return pl.pallas_call(
        norm_kernel,
        out_shape=[
            jax.ShapeDtypeStruct((tokens, width), jnp.bfloat16),
            jax.ShapeDtypeStruct((tokens, width + LANES), jnp.bfloat16),
        ],
        in_specs=vmem(8),
        out_specs=vmem(2),
        compiler_params=params(),
        cost_estimate=SMALL,
        name="norm",
    )(hidden_in, *attn, norm_gain[None, :], expert_ids, gate_weights)


def cast_kernel(spans, *refs):
    count = len(spans)
    sources, targets, scratch = refs[:count], refs[count : 2 * count], refs[2 * count :]
    wide, narrow, arrived, left = scratch[:count], scratch[count : 2 * count], *scratch[-2:]

    def rows_of(i, step, first=0):
        rows = wide[i].shape[0] // CAST_STEPS
        return pl.ds(first + step * rows, rows)

    def copies_in(step):
        for i, (first, _, column, columns) in enumerate(spans):
            yield pltpu.make_async_copy(
                sources[i].at[0, rows_of(i, step, first), pl.ds(column, columns)],
                wide[i].at[rows_of(i, step)],
                arrived.at[step, i],
            )

    def copies_out(step):
        for i in range(count):
            here = rows_of(i, step)
            yield pltpu.make_async_copy(narrow[i].at[here], targets[i].at[here], left.at[step, i])

    for step in range(CAST_STEPS):
        for copy in copies_in(step):
            copy.start()
    for step in range(CAST_STEPS):
        for copy in copies_in(step):
            copy.wait()
        for i in range(count):
            here = rows_of(i, step)
            narrow[i][here] = wide[i][here].astype(jnp.bfloat16)
        for copy in copies_out(step):
            copy.start()
    for step in range(CAST_STEPS):
        for copy in copies_out(step):
            copy.wait()


def cast_rows(arrays, spans):
    shapes = [(rows, columns) for _, rows, _, columns in spans]
    return pl.pallas_call(
        lambda *refs: cast_kernel(spans, *refs),
        out_shape=[jax.ShapeDtypeStruct(shape, jnp.bfloat16) for shape in shapes],
        in_specs=[pl.BlockSpec(memory_space=pltpu.HBM)] * len(arrays),
        out_specs=[pl.BlockSpec(memory_space=pltpu.HBM)] * len(arrays),
        scratch_shapes=[pltpu.VMEM(shape, jnp.float32) for shape in shapes]
        + [pltpu.VMEM(shape, jnp.bfloat16) for shape in shapes]
        + [pltpu.SemaphoreType.DMA((CAST_STEPS, len(arrays)))] * 2,
        compiler_params=params(VMEM_MOST),
        name="cast_rows",
    )(*arrays)


def load_tiles(pieces, weights, arrived, tiles, block):
    def copies(tile):
        first = 0
        for index, piece in enumerate(pieces):
            depth = piece.shape[0]
            for part in range(2):
                columns = pl.ds((part * tiles + tile) * block, block)
                yield pltpu.make_async_copy(
                    piece.at[:, columns],
                    weights.at[pl.ds(first, depth), columns],
                    arrived.at[tile, index, part],
                )
            first += depth

    for tile in range(tiles):
        for copy in copies(tile):
            copy.start()

    def wait(tile):
        for copy in copies(tile):
            copy.wait()

    return wait


def up_kernel(sources, pieces, *refs):
    row_refs = refs[:sources]
    weight_refs = refs[sources : sources + pieces]
    hidden_ref, own_gate_ref, rows, weights, units, arrived = refs[sources + pieces :]
    width = rows.shape[1]
    tiles, _, block = units.shape
    wait = load_tiles(weight_refs, weights, arrived, tiles, block)
    expert = lax.axis_index("expert")
    first = 0
    for ref in row_refs:
        count = ref.shape[0]
        here = slice(first, first + count)
        rows[here, :] = ref[:, :width]
        terms = ref[:, width:].astype(jnp.float32)
        lane = lax.broadcasted_iota(jnp.int32, terms.shape, 1)
        own_gate_ref[here, :] = jnp.sum(
            jnp.where(lane % TOPK == expert, terms, 0.0), axis=-1, keepdims=True
        )
        first += count
    for tile in range(tiles):
        wait(tile)
        gate, up = (
            jnp.dot(
                rows[...],
                weights[:, (part * tiles + tile) * block : (part * tiles + tile + 1) * block],
                preferred_element_type=jnp.float32,
            )
            for part in range(2)
        )
        units[tile] = (gate / (1.0 + jnp.exp(-gate)) * up).astype(jnp.bfloat16)
    own = lax.axis_index("dp")
    for d in range(4):
        hidden_ref[:, d * block : (d + 1) * block] = units[own ^ d]


def expert_up(rows, weights):
    tokens = sum(piece.shape[0] for piece in rows)
    features = sum(piece.shape[0] for piece in weights)
    width = weights[0].shape[1]
    hidden_size = width // 2
    return pl.pallas_call(
        lambda *refs: up_kernel(len(rows), len(weights), *refs),
        out_shape=[
            jax.ShapeDtypeStruct((tokens, hidden_size), jnp.bfloat16),
            jax.ShapeDtypeStruct((tokens, 1), jnp.float32),
        ],
        in_specs=vmem(len(rows)) + [pl.BlockSpec(memory_space=pl.ANY)] * len(weights),
        out_specs=vmem(2),
        scratch_shapes=[
            pltpu.VMEM((tokens, features), jnp.bfloat16),
            pltpu.VMEM((features, width), jnp.bfloat16),
            pltpu.VMEM((4, tokens, hidden_size // 4), jnp.bfloat16),
            pltpu.SemaphoreType.DMA((4, len(weights), 2)),
        ],
        compiler_params=params(),
        cost_estimate=SMALL,
        name="expert_up",
    )(*rows, *weights)


def down_kernel(columns, hidden_ref, gate_ref, *refs):
    pieces, (out_ref, left_ref, right_ref, weights, arrived) = refs[:-5], refs[-5:]
    copies, first = [], 0
    for i, (ref, column) in enumerate(zip(pieces, columns)):
        depth = ref.shape[0]
        copies.append(
            pltpu.make_async_copy(
                ref.at[:, pl.ds(column, weights.shape[1])],
                weights.at[pl.ds(first, depth)],
                arrived.at[i],
            )
        )
        first += depth
    for copy in copies:
        copy.start()
    for copy in copies:
        copy.wait()
    total = jnp.dot(hidden_ref[...], weights[...], preferred_element_type=jnp.float32)
    weighted = (total * gate_ref[...]).astype(jnp.bfloat16)
    sources, rows, width = out_ref.shape
    out_ref[...] = weighted.reshape(sources, rows, width)
    middle, half = sources // 2 * rows, rows // 2
    left_ref[...] = weighted[middle : middle + half]
    right_ref[...] = weighted[middle + half : middle + rows]


def expert_down(hidden_units, gates, weights, width, sources):
    weights, columns = zip(*weights)
    tokens, hidden_size = hidden_units.shape
    rows = tokens // sources
    return pl.pallas_call(
        lambda *refs: down_kernel(columns, *refs),
        out_shape=[
            jax.ShapeDtypeStruct((sources, rows, width), jnp.bfloat16),
            jax.ShapeDtypeStruct((rows // 2, width), jnp.bfloat16),
            jax.ShapeDtypeStruct((rows // 2, width), jnp.bfloat16),
        ],
        in_specs=vmem(2) + [pl.BlockSpec(memory_space=pl.ANY)] * len(weights),
        out_specs=vmem(3),
        scratch_shapes=[
            pltpu.VMEM((hidden_size, width), jnp.bfloat16),
            pltpu.SemaphoreType.DMA((len(weights),)),
        ],
        compiler_params=params(),
        cost_estimate=SMALL,
        name="expert_down",
    )(hidden_units, gates, *weights)


def partner(x, distance):
    return lax.ppermute(x, "dp", [(i, i ^ distance) for i in range(4)])


def ring_order(count):
    return list(range(0, count, 2)) + list(range(count - 1, 0, -2))


def around(x, step):
    ring = ring_order(lax.axis_size("expert"))
    count = len(ring)
    return lax.ppermute(x, "expert", [(ring[i], ring[(i + step) % count]) for i in range(count)])


def after(x, *others):
    return lax.optimization_barrier((x, *others))[0]


def add(a, b):
    return (a.astype(jnp.float32) + b.astype(jnp.float32)).astype(jnp.bfloat16)


def gather_rows(rows):
    half = rows.shape[0] // 2
    reach = lax.axis_size("expert") // 2
    above, below = [rows], [rows]
    for _ in range(reach - 1):
        above.append(around(above[-1], -1))
        below.append(around(below[-1], 1))
    far = [around(above[-1][:half], -1), around(below[-1][half:], 1)]
    return above + far + below[:0:-1], list(zip(above[1:], below[1:])) + [tuple(far)]


def scatter_sum(weighted, left, right):
    sources, rows, _ = weighted.shape
    half = rows // 2
    reach = sources // 2
    up, down = around(left, 1), around(right, -1)
    up = jnp.concatenate([add(weighted[reach - 1, :half], up), weighted[reach - 1, half:]])
    down = jnp.concatenate([weighted[reach + 1, :half], add(weighted[reach + 1, half:], down)])
    for away in range(reach - 2, 0, -1):
        up = add(weighted[away], around(up, 1))
        down = add(weighted[sources - away], around(down, -1))
    return weighted[0], around(up, 1), around(down, -1)


def relayed(x, rows):
    return [partner(x[i : i + rows], 1) for i in range(0, x.shape[0], rows)]


def every_expert(
    hidden_in,
    queries,
    key_pool,
    value_pool,
    page_table,
    prompt_lengths,
    expert_ids,
    gate_weights,
    norm_gain,
    trainer_gate_up,
    trainer_down,
):
    expert_count = lax.axis_size("expert")
    width = trainer_down.shape[2]
    depth, columns = trainer_gate_up.shape[1:]
    down_depth = trainer_down.shape[1]
    early = depth // 4
    piece = depth // 8
    first_slab = width * FIRST_SLAB // 16
    slabs = [(0, first_slab), (first_slab, width - first_slab)]
    *attn, first_own = attention(
        queries, key_pool, value_pool, page_table, prompt_lengths, trainer_gate_up, early
    )
    first_across = partner(first_own, 2)
    rest_own, down_own, *down_sent = cast_rows(
        [after(trainer_gate_up, attn[0])] + [trainer_down] * 3,
        [(early, depth - early, 0, columns)]
        + [(0, down_depth, *slab) for slab in ((0, width), *slabs)],
    )
    attn = [attn[0]] + [partner(attn[d], d) for d in (1, 2, 3)]
    rest_across = partner(after(rest_own, first_across, *attn), 2)
    resid, rows = norm(
        after(hidden_in[0], rest_own), attn, norm_gain, expert_ids[0], gate_weights[0]
    )
    gathered, arrived = gather_rows(rows)
    first_beside = partner(after(first_own, *arrived[0]), 1)
    first_opposite = partner(after(first_across, *arrived[0]), 1)
    rest_beside = partner(after(rest_own, *arrived[0]), 1)
    down_beside = partner(after(down_own, *arrived[1]), 1)
    down_across = [partner(after(slab, *arrived[2]), 2) for slab in down_sent]
    rest_opposite = relayed(after(rest_across, *arrived[3]), piece)
    hidden_units, gates = expert_up(
        gathered,
        [first_own, rest_own, first_beside, rest_beside]
        + [first_across, rest_across, first_opposite, *rest_opposite],
    )
    before = hidden_units
    mixed = []
    for (first, wide), across in zip(slabs, down_across):
        weights = [(down_own, first), (down_beside, first), (across, 0)]
        weights += [(ref, 0) for ref in relayed(after(across, before), piece)]
        weighted = expert_down(hidden_units, gates, weights, wide, expert_count)
        before = weighted[1]
        total = resid[:, first : first + wide].astype(jnp.float32)
        for term in scatter_sum(*weighted):
            total = total + term.astype(jnp.float32)
        mixed.append(total.astype(jnp.bfloat16))
    return jnp.concatenate(mixed, axis=1)[None]


def solution(mesh):
    placed = (
        P("expert", "dp", None),
        P("expert", None, "dp"),
        P("expert", None, "dp"),
        P("expert", None, "dp"),
        P("expert", None),
        P("expert", None),
        P("expert", "dp", None),
        P("expert", "dp", None),
        P(),
        P("expert", "dp", None),
        P("expert", "dp", None),
    )
    dense = mesh.shape["expert"] == TOPK and mesh.shape["dp"] == 4
    return jax.shard_map(
        every_expert if dense else local, mesh=mesh, in_specs=placed, out_specs=P("expert", "dp", None), check_vma=False
    )
```

```python
import math

import jax
import jax.numpy as jnp
from jax import lax
from jax.experimental import pallas as pl
from jax.experimental.pallas import tpu as pltpu
from jax.sharding import PartitionSpec as P

HDIM = 128
TOPK = 8


epsilon = 1e-05


def fetch_weights(trainer_gate_up, trainer_down):
    return (
        lax.all_gather(trainer_gate_up.astype(jnp.bfloat16), "dp", axis=1, tiled=True),
        lax.all_gather(trainer_down.astype(jnp.bfloat16), "dp", axis=1, tiled=True),
    )


def local(
    hidden_in,
    queries,
    key_pool,
    value_pool,
    page_table,
    prompt_lengths,
    expert_ids,
    gate_weights,
    norm_gain,
    trainer_gate_up,
    trainer_down,
):
    col_tok = queries.shape[1]
    width_dev = queries.shape[2]
    heads_dev = width_dev // HDIM
    keys_all = jnp.take(key_pool, page_table[0], axis=0).reshape(col_tok, heads_dev, HDIM)
    values_all = jnp.take(value_pool, page_table[0], axis=0).reshape(col_tok, heads_dev, HDIM)
    request_ends = jnp.cumsum(prompt_lengths[0])
    positions = lax.iota(jnp.int32, col_tok)
    request = jnp.sum((positions[:, None] >= request_ends[None, :]).astype(jnp.int32), axis=1)
    block_rows = math.gcd(col_tok, 512)
    query_blocks = queries[0].reshape(col_tok // block_rows, block_rows, heads_dev, HDIM)
    request_blocks = request.reshape(col_tok // block_rows, block_rows)
    score_scale = 1.0 / math.sqrt(HDIM)

    def attend(pieces):
        query_block, request_block = pieces
        scores = (
            jnp.einsum("qhd,khd->hqk", query_block, keys_all, preferred_element_type=jnp.float32)
            * score_scale
        )
        same_request = (request_block[:, None] == request[None, :])[None]
        scores = jnp.where(same_request, scores, -1e30)
        highest = jnp.max(scores, axis=-1, keepdims=True)
        weights = jnp.where(same_request, jnp.exp(scores - highest), 0.0)
        totals = jnp.sum(weights, axis=-1, keepdims=True)
        probs = (weights / totals).astype(jnp.bfloat16)
        output = jnp.einsum("hqk,khd->qhd", probs, values_all, preferred_element_type=jnp.float32)
        return output.astype(jnp.bfloat16).reshape(block_rows, width_dev)

    attn_heads = lax.map(attend, (query_blocks, request_blocks)).reshape(1, col_tok, width_dev)
    attn_tokens = lax.all_to_all(attn_heads, "dp", split_axis=1, concat_axis=2, tiled=True)
    resid32 = (
        (hidden_in.astype(jnp.float32) + attn_tokens.astype(jnp.float32))
        .astype(jnp.bfloat16)
        .astype(jnp.float32)
    )
    mean_square = jnp.mean(resid32 * resid32, axis=-1, keepdims=True)
    normed = (resid32 * lax.rsqrt(mean_square + epsilon) * norm_gain).astype(jnp.bfloat16)
    server_gate_up, server_down = fetch_weights(trainer_gate_up, trainer_down)
    token_rows = normed.shape[1]
    width = normed.shape[2]
    expert_count = lax.axis_size("expert")
    capacity = min(token_rows, token_rows * TOPK * 5 // (4 * expert_count))
    hidden_size = server_gate_up.shape[2] // 2
    ids_flat = expert_ids[0].reshape(token_rows * TOPK)
    onehot = (ids_flat[:, None] == lax.iota(jnp.int32, expert_count)[None, :]).astype(jnp.int32)
    earlier = jnp.cumsum(onehot, axis=0) - onehot
    slot_index = jnp.sum(earlier * onehot, axis=1)
    flat_slot = ids_flat * capacity + slot_index
    placement = (
        flat_slot[:, None] == lax.iota(jnp.int32, expert_count * capacity)[None, :]
    ).astype(jnp.bfloat16)
    dispatch_matrix = jnp.sum(placement.reshape(token_rows, TOPK, expert_count * capacity), axis=1)
    outgoing = jnp.einsum(
        "ts,td->sd", dispatch_matrix, normed[0], preferred_element_type=jnp.float32
    )
    outgoing = outgoing.astype(jnp.bfloat16).reshape(expert_count, capacity, width)
    received = lax.all_to_all(outgoing, "expert", split_axis=0, concat_axis=0, tiled=True)
    sources, items, features = received.shape
    slot_rows = received.reshape(sources * items, features)
    gate_up = jnp.dot(slot_rows, server_gate_up[0], preferred_element_type=jnp.float32)
    hidden_units = (jax.nn.silu(gate_up[:, :hidden_size]) * gate_up[:, hidden_size:]).astype(
        jnp.bfloat16
    )
    outputs = jnp.dot(hidden_units, server_down[0], preferred_element_type=jnp.float32).astype(
        jnp.bfloat16
    )
    returned = lax.all_to_all(
        outputs.reshape(sources, items, features), "expert", split_axis=0, concat_axis=0, tiled=True
    )
    copies = jnp.take(returned.reshape(expert_count * capacity, width), flat_slot, axis=0)
    copies = copies.reshape(token_rows, TOPK, width).astype(jnp.float32)
    mixture = jnp.einsum("tk,tkd->td", gate_weights[0], copies)
    mixed = resid32[0] + mixture
    return mixed.astype(jnp.bfloat16)[None]

LANES = 128
VMEM_LIMIT = 32 * 2**20
VMEM_MOST = 60 * 2**20
CAST_STEPS = 4
SLABS = 2
SMALL = pl.CostEstimate(flops=1, bytes_accessed=1, transcendentals=0)


def params(limit=VMEM_LIMIT):
    return pltpu.CompilerParams(vmem_limit_bytes=limit)


def vmem(count):
    return [pl.BlockSpec(memory_space=pltpu.VMEM)] * count


def attention_kernel(*refs):
    sources, outs, piece_ref, scratch = refs[:6], refs[6:10], refs[10], refs[11:]
    table, lengths, q_ref, k_ref, v_ref, weights, attn, arrived = scratch
    copies = [
        pltpu.make_async_copy(source, target, arrived.at[i])
        for i, (source, target) in enumerate(
            zip(
                (*sources[:2], sources[2].at[0], *sources[3:5]),
                (table, lengths, q_ref, k_ref, v_ref),
            )
        )
    ]
    rows = weights.shape[0]
    copies.append(
        pltpu.make_async_copy(sources[5].at[0, pl.ds(0, rows)], weights, arrived.at[5])
    )
    for copy in copies:
        copy.start()
    for copy in copies[:5]:
        copy.wait()
    tokens, width = q_ref.shape
    pages = k_ref.shape[0]
    row = lax.broadcasted_iota(jnp.int32, (tokens, tokens), 0)
    column = lax.broadcasted_iota(jnp.int32, (tokens, tokens), 1)
    row_request = jnp.zeros((tokens, tokens), jnp.int32)
    column_request = jnp.zeros((tokens, tokens), jnp.int32)
    end = jnp.int32(0)
    for r in range(lengths.shape[1]):
        end = end + lengths[0, r]
        row_request += (row >= end).astype(jnp.int32)
        column_request += (column >= end).astype(jnp.int32)
    same = row_request == column_request
    for h in range(width // HDIM):
        lanes = slice(h * HDIM, (h + 1) * HDIM)
        keys = jnp.concatenate([k_ref[table[0, p], :, lanes] for p in range(pages)], axis=0)
        values = jnp.concatenate([v_ref[table[0, p], :, lanes] for p in range(pages)], axis=0)
        scores = lax.dot_general(
            q_ref[:, lanes], keys, (((1,), (1,)), ((), ())), preferred_element_type=jnp.float32
        ) * (1.0 / math.sqrt(HDIM))
        scores = jnp.where(same, scores, -1e30)
        highest = jnp.max(scores, axis=-1, keepdims=True)
        weight = jnp.where(same, jnp.exp(scores - highest), 0.0)
        probs = (weight / jnp.sum(weight, axis=-1, keepdims=True)).astype(jnp.bfloat16)
        attn[:, lanes] = jnp.dot(probs, values, preferred_element_type=jnp.float32).astype(
            jnp.bfloat16
        )
    own = lax.axis_index("dp")
    rows = tokens // 4
    for d in range(4):
        first = pl.multiple_of((own ^ d) * rows, rows)
        outs[d][...] = attn[pl.ds(first, rows), :]
    copies[5].wait()
    piece_ref[...] = weights[...].astype(jnp.bfloat16)


def attention(queries, key_pool, value_pool, page_table, prompt_lengths, gate_up, early):
    tokens, width = queries.shape[1:]
    return pl.pallas_call(
        attention_kernel,
        out_shape=[jax.ShapeDtypeStruct((tokens // 4, width), jnp.bfloat16)] * 4
        + [jax.ShapeDtypeStruct((early, gate_up.shape[2]), jnp.bfloat16)],
        in_specs=[pl.BlockSpec(memory_space=pltpu.HBM)] * 6,
        out_specs=vmem(5),
        scratch_shapes=[
            pltpu.SMEM(page_table.shape, jnp.int32),
            pltpu.SMEM(prompt_lengths.shape, jnp.int32),
            pltpu.VMEM((tokens, width), jnp.bfloat16),
            pltpu.VMEM(key_pool.shape, jnp.bfloat16),
            pltpu.VMEM(value_pool.shape, jnp.bfloat16),
            pltpu.VMEM((early, gate_up.shape[2]), jnp.float32),
            pltpu.VMEM((tokens, width), jnp.bfloat16),
            pltpu.SemaphoreType.DMA((6,)),
        ],
        compiler_params=params(VMEM_MOST),
        name="attention",
    )(page_table, prompt_lengths, queries, key_pool, value_pool, gate_up)


def norm_kernel(hidden_ref, a0, a1, a2, a3, gain_ref, ids_ref, gates_ref, resid_ref, rows_ref):
    own = lax.axis_index("dp")
    tokens, width = hidden_ref.shape
    block = width // 4
    total = jnp.zeros((tokens, 1), jnp.float32)
    for d, attn in enumerate((a0, a1, a2, a3)):
        columns = pl.ds(pl.multiple_of((own ^ d) * block, block), block)
        resid = (
            hidden_ref[:, columns].astype(jnp.float32) + attn[...].astype(jnp.float32)
        ).astype(jnp.bfloat16)
        resid_ref[:, columns] = resid
        resid32 = resid.astype(jnp.float32)
        total += jnp.sum(resid32 * resid32, axis=-1, keepdims=True)
    inverse = lax.rsqrt(total / width + epsilon)
    for d in range(4):
        columns = pl.ds(pl.multiple_of((own ^ d) * block, block), block)
        rows_ref[:, d * block : (d + 1) * block] = (
            resid_ref[:, columns].astype(jnp.float32) * inverse * gain_ref[:, columns]
        ).astype(jnp.bfloat16)
    lane = lax.broadcasted_iota(jnp.int32, (tokens, LANES), 1)
    gates = jnp.zeros((tokens, LANES), jnp.float32)
    for k in range(TOPK):
        gates += jnp.where(ids_ref[:, k : k + 1] == lane % TOPK, gates_ref[:, k : k + 1], 0.0)
    high = gates.astype(jnp.bfloat16).astype(jnp.float32)
    middle = (gates - high).astype(jnp.bfloat16).astype(jnp.float32)
    low = gates - high - middle
    part = lane // TOPK
    terms = jnp.where(part == 0, high, jnp.where(part == 1, middle, jnp.where(part == 2, low, 0.0)))
    rows_ref[:, width:] = terms.astype(jnp.bfloat16)


def norm(hidden_in, attn, norm_gain, expert_ids, gate_weights):
    tokens, width = hidden_in.shape
    return pl.pallas_call(
        norm_kernel,
        out_shape=[
            jax.ShapeDtypeStruct((tokens, width), jnp.bfloat16),
            jax.ShapeDtypeStruct((tokens, width + LANES), jnp.bfloat16),
        ],
        in_specs=vmem(8),
        out_specs=vmem(2),
        compiler_params=params(),
        cost_estimate=SMALL,
        name="norm",
    )(hidden_in, *attn, norm_gain[None, :], expert_ids, gate_weights)


def cast_kernel(spans, *refs):
    count = len(spans)
    sources, targets, scratch = refs[:count], refs[count : 2 * count], refs[2 * count :]
    wide, narrow, arrived, left = scratch[:count], scratch[count : 2 * count], *scratch[-2:]

    def rows_of(i, step, first=0):
        rows = wide[i].shape[0] // CAST_STEPS
        return pl.ds(first + step * rows, rows)

    def copies_in(step):
        for i, (first, _, column, columns) in enumerate(spans):
            yield pltpu.make_async_copy(
                sources[i].at[0, rows_of(i, step, first), pl.ds(column, columns)],
                wide[i].at[rows_of(i, step)],
                arrived.at[step, i],
            )

    def copies_out(step):
        for i in range(count):
            here = rows_of(i, step)
            yield pltpu.make_async_copy(narrow[i].at[here], targets[i].at[here], left.at[step, i])

    for step in range(CAST_STEPS):
        for copy in copies_in(step):
            copy.start()
    for step in range(CAST_STEPS):
        for copy in copies_in(step):
            copy.wait()
        for i in range(count):
            here = rows_of(i, step)
            narrow[i][here] = wide[i][here].astype(jnp.bfloat16)
        for copy in copies_out(step):
            copy.start()
    for step in range(CAST_STEPS):
        for copy in copies_out(step):
            copy.wait()


def cast_rows(arrays, spans):
    shapes = [(rows, columns) for _, rows, _, columns in spans]
    return pl.pallas_call(
        lambda *refs: cast_kernel(spans, *refs),
        out_shape=[jax.ShapeDtypeStruct(shape, jnp.bfloat16) for shape in shapes],
        in_specs=[pl.BlockSpec(memory_space=pltpu.HBM)] * len(arrays),
        out_specs=[pl.BlockSpec(memory_space=pltpu.HBM)] * len(arrays),
        scratch_shapes=[pltpu.VMEM(shape, jnp.float32) for shape in shapes]
        + [pltpu.VMEM(shape, jnp.bfloat16) for shape in shapes]
        + [pltpu.SemaphoreType.DMA((CAST_STEPS, len(arrays)))] * 2,
        compiler_params=params(VMEM_MOST),
        name="cast_rows",
    )(*arrays)


def load_tiles(pieces, weights, arrived, tiles, block):
    def copies(tile):
        first = 0
        for index, piece in enumerate(pieces):
            depth = piece.shape[0]
            for part in range(2):
                columns = pl.ds((part * tiles + tile) * block, block)
                yield pltpu.make_async_copy(
                    piece.at[:, columns],
                    weights.at[pl.ds(first, depth), columns],
                    arrived.at[tile, index, part],
                )
            first += depth

    for tile in range(tiles):
        for copy in copies(tile):
            copy.start()

    def wait(tile):
        for copy in copies(tile):
            copy.wait()

    return wait


def up_kernel(sources, pieces, *refs):
    row_refs = refs[:sources]
    weight_refs = refs[sources : sources + pieces]
    hidden_ref, own_gate_ref, rows, weights, units, arrived = refs[sources + pieces :]
    width = rows.shape[1]
    tiles, _, block = units.shape
    wait = load_tiles(weight_refs, weights, arrived, tiles, block)
    expert = lax.axis_index("expert")
    first = 0
    for ref in row_refs:
        count = ref.shape[0]
        here = slice(first, first + count)
        rows[here, :] = ref[:, :width]
        terms = ref[:, width:].astype(jnp.float32)
        lane = lax.broadcasted_iota(jnp.int32, terms.shape, 1)
        own_gate_ref[here, :] = jnp.sum(
            jnp.where(lane % TOPK == expert, terms, 0.0), axis=-1, keepdims=True
        )
        first += count
    for tile in range(tiles):
        wait(tile)
        gate, up = (
            jnp.dot(
                rows[...],
                weights[:, (part * tiles + tile) * block : (part * tiles + tile + 1) * block],
                preferred_element_type=jnp.float32,
            )
            for part in range(2)
        )
        units[tile] = (gate / (1.0 + jnp.exp(-gate)) * up).astype(jnp.bfloat16)
    own = lax.axis_index("dp")
    for d in range(4):
        hidden_ref[:, d * block : (d + 1) * block] = units[own ^ d]


def expert_up(rows, weights):
    tokens = sum(piece.shape[0] for piece in rows)
    features = sum(piece.shape[0] for piece in weights)
    width = weights[0].shape[1]
    hidden_size = width // 2
    return pl.pallas_call(
        lambda *refs: up_kernel(len(rows), len(weights), *refs),
        out_shape=[
            jax.ShapeDtypeStruct((tokens, hidden_size), jnp.bfloat16),
            jax.ShapeDtypeStruct((tokens, 1), jnp.float32),
        ],
        in_specs=vmem(len(rows)) + [pl.BlockSpec(memory_space=pl.ANY)] * len(weights),
        out_specs=vmem(2),
        scratch_shapes=[
            pltpu.VMEM((tokens, features), jnp.bfloat16),
            pltpu.VMEM((features, width), jnp.bfloat16),
            pltpu.VMEM((4, tokens, hidden_size // 4), jnp.bfloat16),
            pltpu.SemaphoreType.DMA((4, len(weights), 2)),
        ],
        compiler_params=params(),
        cost_estimate=SMALL,
        name="expert_up",
    )(*rows, *weights)


def down_kernel(column, sources, hidden_ref, gate_ref, *refs):
    (weights, arrived), refs = refs[-2:], refs[:-2]
    pieces, outs = refs[: len(refs) - sources - 3], refs[len(refs) - sources - 3 :]
    copies, first = [], 0
    for i, ref in enumerate(pieces):
        depth = ref.shape[0]
        copies.append(
            pltpu.make_async_copy(
                ref.at[:, pl.ds(column, weights.shape[1])],
                weights.at[pl.ds(first, depth)],
                arrived.at[i],
            )
        )
        first += depth
    for copy in copies:
        copy.start()
    for copy in copies:
        copy.wait()
    total = jnp.dot(hidden_ref[...], weights[...], preferred_element_type=jnp.float32)
    weighted = (total * gate_ref[...]).astype(jnp.bfloat16)
    rows = weighted.shape[0] // sources
    for (first, count), ref in zip(down_blocks(rows, sources), outs):
        ref[...] = weighted[first : first + count]


def down_blocks(rows, sources):
    half, reach = rows // 2, sources // 2
    blocks = [(0, rows)]
    for step, middle in ((-1, reach * rows), (1, reach * rows + half)):
        blocks.append((middle, half))
        second = (reach + step) * rows
        blocks += [(second, half), (second + half, half)]
        blocks += [((reach + step * away) * rows, rows) for away in range(2, reach)]
    return blocks


def expert_down(hidden_units, gates, weights, column, width, sources):
    tokens, hidden_size = hidden_units.shape
    rows = tokens // sources
    return pl.pallas_call(
        lambda *refs: down_kernel(column, sources, *refs),
        out_shape=[
            jax.ShapeDtypeStruct((count, width), jnp.bfloat16)
            for _, count in down_blocks(rows, sources)
        ],
        in_specs=vmem(2) + [pl.BlockSpec(memory_space=pl.ANY)] * len(weights),
        out_specs=vmem(sources + 3),
        scratch_shapes=[
            pltpu.VMEM((hidden_size, width), jnp.bfloat16),
            pltpu.SemaphoreType.DMA((len(weights),)),
        ],
        compiler_params=params(),
        cost_estimate=SMALL,
        name="expert_down",
    )(hidden_units, gates, *weights)


def partner(x, distance):
    return lax.ppermute(x, "dp", [(i, i ^ distance) for i in range(4)])


def ring_order(count):
    return list(range(0, count, 2)) + list(range(count - 1, 0, -2))


def around(x, step):
    ring = ring_order(lax.axis_size("expert"))
    count = len(ring)
    return lax.ppermute(x, "expert", [(ring[i], ring[(i + step) % count]) for i in range(count)])


def after(x, *others):
    return lax.optimization_barrier((x, *others))[0]


def add(a, b):
    return (a.astype(jnp.float32) + b.astype(jnp.float32)).astype(jnp.bfloat16)


def gather_rows(rows):
    half = rows.shape[0] // 2
    reach = lax.axis_size("expert") // 2
    above, below = [rows], [rows]
    for _ in range(reach - 1):
        above.append(around(above[-1], -1))
        below.append(around(below[-1], 1))
    far = [around(above[-1][:half], -1), around(below[-1][half:], 1)]
    return above + far + below[:0:-1], list(zip(above[1:], below[1:])) + [tuple(far)]


def scatter_sum(own, *blocks):
    reach = len(blocks) // 2
    terms = [own]
    for step, (far, first, second, *near) in ((1, blocks[:reach]), (-1, blocks[reach:])):
        moving = around(far, step)
        if step > 0:
            moving = jnp.concatenate([add(first, moving), second])
        else:
            moving = jnp.concatenate([first, add(second, moving)])
        for block in near:
            moving = add(block, around(moving, step))
        terms.append(around(moving, step))
    return terms


def relayed(x, rows):
    return [partner(x[i : i + rows], 1) for i in range(0, x.shape[0], rows)]


def every_expert(
    hidden_in,
    queries,
    key_pool,
    value_pool,
    page_table,
    prompt_lengths,
    expert_ids,
    gate_weights,
    norm_gain,
    trainer_gate_up,
    trainer_down,
):
    expert_count = lax.axis_size("expert")
    width = trainer_down.shape[2]
    depth, columns = trainer_gate_up.shape[1:]
    down_depth = trainer_down.shape[1]
    early = depth // 4
    slab = width // SLABS
    *attn, first_own = attention(
        queries, key_pool, value_pool, page_table, prompt_lengths, trainer_gate_up, early
    )
    first_across = partner(first_own, 2)
    rest_own, down_own = cast_rows(
        [after(trainer_gate_up, attn[0]), trainer_down],
        [(early, depth - early, 0, columns), (0, down_depth, 0, width)],
    )
    attn = [attn[0]] + [partner(attn[d], d) for d in (1, 2, 3)]
    rest_across = partner(after(rest_own, first_across, *attn), 2)
    resid, rows = norm(
        after(hidden_in[0], rest_own), attn, norm_gain, expert_ids[0], gate_weights[0]
    )
    gathered, arrived = gather_rows(rows)
    first_beside = partner(after(first_own, *arrived[0]), 1)
    first_opposite = partner(after(first_across, *arrived[0]), 1)
    rest_beside = partner(after(rest_own, *arrived[0]), 1)
    down_beside = partner(after(down_own, *arrived[1]), 1)
    down_across = partner(after(down_own, *arrived[2]), 2)
    rest_opposite = relayed(after(rest_across, *arrived[3]), depth // 8)
    hidden_units, gates = expert_up(
        gathered,
        [first_own, rest_own, first_beside, rest_beside]
        + [first_across, rest_across, first_opposite, *rest_opposite],
    )
    down_opposite = relayed(after(down_across, hidden_units), down_depth // 2)
    weights = [down_own, down_beside, down_across, *down_opposite]
    mixed = []
    for first in range(0, width, slab):
        weighted = expert_down(hidden_units, gates, weights, first, slab, expert_count)
        total = resid[:, first : first + slab].astype(jnp.float32)
        for term in scatter_sum(*weighted):
            total = total + term.astype(jnp.float32)
        mixed.append(total.astype(jnp.bfloat16))
    return jnp.concatenate(mixed, axis=1)[None]


def solution(mesh):
    placed = (
        P("expert", "dp", None),
        P("expert", None, "dp"),
        P("expert", None, "dp"),
        P("expert", None, "dp"),
        P("expert", None),
        P("expert", None),
        P("expert", "dp", None),
        P("expert", "dp", None),
        P(),
        P("expert", "dp", None),
        P("expert", "dp", None),
    )
    dense = mesh.shape["expert"] == TOPK and mesh.shape["dp"] == 4
    return jax.shard_map(
        every_expert if dense else local, mesh=mesh, in_specs=placed, out_specs=P("expert", "dp", None), check_vma=False
    )
```

```python
import math

import jax
import jax.numpy as jnp
from jax import lax
from jax.experimental import pallas as pl
from jax.experimental.pallas import tpu as pltpu
from jax.sharding import PartitionSpec as P

HDIM = 128
TOPK = 8


epsilon = 1e-05


def fetch_weights(trainer_gate_up, trainer_down):
    return (
        lax.all_gather(trainer_gate_up.astype(jnp.bfloat16), "dp", axis=1, tiled=True),
        lax.all_gather(trainer_down.astype(jnp.bfloat16), "dp", axis=1, tiled=True),
    )


def local(
    hidden_in,
    queries,
    key_pool,
    value_pool,
    page_table,
    prompt_lengths,
    expert_ids,
    gate_weights,
    norm_gain,
    trainer_gate_up,
    trainer_down,
):
    col_tok = queries.shape[1]
    width_dev = queries.shape[2]
    heads_dev = width_dev // HDIM
    keys_all = jnp.take(key_pool, page_table[0], axis=0).reshape(col_tok, heads_dev, HDIM)
    values_all = jnp.take(value_pool, page_table[0], axis=0).reshape(col_tok, heads_dev, HDIM)
    request_ends = jnp.cumsum(prompt_lengths[0])
    positions = lax.iota(jnp.int32, col_tok)
    request = jnp.sum((positions[:, None] >= request_ends[None, :]).astype(jnp.int32), axis=1)
    block_rows = math.gcd(col_tok, 512)
    query_blocks = queries[0].reshape(col_tok // block_rows, block_rows, heads_dev, HDIM)
    request_blocks = request.reshape(col_tok // block_rows, block_rows)
    score_scale = 1.0 / math.sqrt(HDIM)

    def attend(pieces):
        query_block, request_block = pieces
        scores = (
            jnp.einsum("qhd,khd->hqk", query_block, keys_all, preferred_element_type=jnp.float32)
            * score_scale
        )
        same_request = (request_block[:, None] == request[None, :])[None]
        scores = jnp.where(same_request, scores, -1e30)
        highest = jnp.max(scores, axis=-1, keepdims=True)
        weights = jnp.where(same_request, jnp.exp(scores - highest), 0.0)
        totals = jnp.sum(weights, axis=-1, keepdims=True)
        probs = (weights / totals).astype(jnp.bfloat16)
        output = jnp.einsum("hqk,khd->qhd", probs, values_all, preferred_element_type=jnp.float32)
        return output.astype(jnp.bfloat16).reshape(block_rows, width_dev)

    attn_heads = lax.map(attend, (query_blocks, request_blocks)).reshape(1, col_tok, width_dev)
    attn_tokens = lax.all_to_all(attn_heads, "dp", split_axis=1, concat_axis=2, tiled=True)
    resid32 = (
        (hidden_in.astype(jnp.float32) + attn_tokens.astype(jnp.float32))
        .astype(jnp.bfloat16)
        .astype(jnp.float32)
    )
    mean_square = jnp.mean(resid32 * resid32, axis=-1, keepdims=True)
    normed = (resid32 * lax.rsqrt(mean_square + epsilon) * norm_gain).astype(jnp.bfloat16)
    server_gate_up, server_down = fetch_weights(trainer_gate_up, trainer_down)
    token_rows = normed.shape[1]
    width = normed.shape[2]
    expert_count = lax.axis_size("expert")
    capacity = min(token_rows, token_rows * TOPK * 5 // (4 * expert_count))
    hidden_size = server_gate_up.shape[2] // 2
    ids_flat = expert_ids[0].reshape(token_rows * TOPK)
    onehot = (ids_flat[:, None] == lax.iota(jnp.int32, expert_count)[None, :]).astype(jnp.int32)
    earlier = jnp.cumsum(onehot, axis=0) - onehot
    slot_index = jnp.sum(earlier * onehot, axis=1)
    flat_slot = ids_flat * capacity + slot_index
    placement = (
        flat_slot[:, None] == lax.iota(jnp.int32, expert_count * capacity)[None, :]
    ).astype(jnp.bfloat16)
    dispatch_matrix = jnp.sum(placement.reshape(token_rows, TOPK, expert_count * capacity), axis=1)
    outgoing = jnp.einsum(
        "ts,td->sd", dispatch_matrix, normed[0], preferred_element_type=jnp.float32
    )
    outgoing = outgoing.astype(jnp.bfloat16).reshape(expert_count, capacity, width)
    received = lax.all_to_all(outgoing, "expert", split_axis=0, concat_axis=0, tiled=True)
    sources, items, features = received.shape
    slot_rows = received.reshape(sources * items, features)
    gate_up = jnp.dot(slot_rows, server_gate_up[0], preferred_element_type=jnp.float32)
    hidden_units = (jax.nn.silu(gate_up[:, :hidden_size]) * gate_up[:, hidden_size:]).astype(
        jnp.bfloat16
    )
    outputs = jnp.dot(hidden_units, server_down[0], preferred_element_type=jnp.float32).astype(
        jnp.bfloat16
    )
    returned = lax.all_to_all(
        outputs.reshape(sources, items, features), "expert", split_axis=0, concat_axis=0, tiled=True
    )
    copies = jnp.take(returned.reshape(expert_count * capacity, width), flat_slot, axis=0)
    copies = copies.reshape(token_rows, TOPK, width).astype(jnp.float32)
    mixture = jnp.einsum("tk,tkd->td", gate_weights[0], copies)
    mixed = resid32[0] + mixture
    return mixed.astype(jnp.bfloat16)[None]

LANES = 128
VMEM_LIMIT = 32 * 2**20
VMEM_MOST = 60 * 2**20
CAST_STEPS = 4
SLABS = 2
SMALL = pl.CostEstimate(flops=1, bytes_accessed=1, transcendentals=0)


def params(limit=VMEM_LIMIT):
    return pltpu.CompilerParams(vmem_limit_bytes=limit)


def vmem(count):
    return [pl.BlockSpec(memory_space=pltpu.VMEM)] * count


def attention_kernel(*refs):
    sources, outs, scratch = refs[:5], refs[5:9], refs[9:]
    table, lengths, q_ref, k_ref, v_ref, attn, arrived = scratch
    copies = [
        pltpu.make_async_copy(source, target, arrived.at[i])
        for i, (source, target) in enumerate(
            zip(
                (*sources[:2], sources[2].at[0], *sources[3:5]),
                (table, lengths, q_ref, k_ref, v_ref),
            )
        )
    ]
    for copy in copies:
        copy.start()
    for copy in copies:
        copy.wait()
    tokens, width = q_ref.shape
    pages = k_ref.shape[0]
    row = lax.broadcasted_iota(jnp.int32, (tokens, tokens), 0)
    column = lax.broadcasted_iota(jnp.int32, (tokens, tokens), 1)
    row_request = jnp.zeros((tokens, tokens), jnp.int32)
    column_request = jnp.zeros((tokens, tokens), jnp.int32)
    end = jnp.int32(0)
    for r in range(lengths.shape[1]):
        end = end + lengths[0, r]
        row_request += (row >= end).astype(jnp.int32)
        column_request += (column >= end).astype(jnp.int32)
    same = row_request == column_request
    for h in range(width // HDIM):
        lanes = slice(h * HDIM, (h + 1) * HDIM)
        keys = jnp.concatenate([k_ref[table[0, p], :, lanes] for p in range(pages)], axis=0)
        values = jnp.concatenate([v_ref[table[0, p], :, lanes] for p in range(pages)], axis=0)
        scores = lax.dot_general(
            q_ref[:, lanes], keys, (((1,), (1,)), ((), ())), preferred_element_type=jnp.float32
        ) * (1.0 / math.sqrt(HDIM))
        scores = jnp.where(same, scores, -1e30)
        highest = jnp.max(scores, axis=-1, keepdims=True)
        weight = jnp.where(same, jnp.exp(scores - highest), 0.0)
        probs = (weight / jnp.sum(weight, axis=-1, keepdims=True)).astype(jnp.bfloat16)
        attn[:, lanes] = jnp.dot(probs, values, preferred_element_type=jnp.float32).astype(
            jnp.bfloat16
        )
    own = lax.axis_index("dp")
    rows = tokens // 4
    for d in range(4):
        first = pl.multiple_of((own ^ d) * rows, rows)
        outs[d][...] = attn[pl.ds(first, rows), :]


def attention(queries, key_pool, value_pool, page_table, prompt_lengths):
    tokens, width = queries.shape[1:]
    return pl.pallas_call(
        attention_kernel,
        out_shape=[jax.ShapeDtypeStruct((tokens // 4, width), jnp.bfloat16)] * 4,
        in_specs=[pl.BlockSpec(memory_space=pltpu.HBM)] * 5,
        out_specs=vmem(4),
        scratch_shapes=[
            pltpu.SMEM(page_table.shape, jnp.int32),
            pltpu.SMEM(prompt_lengths.shape, jnp.int32),
            pltpu.VMEM((tokens, width), jnp.bfloat16),
            pltpu.VMEM(key_pool.shape, jnp.bfloat16),
            pltpu.VMEM(value_pool.shape, jnp.bfloat16),
            pltpu.VMEM((tokens, width), jnp.bfloat16),
            pltpu.SemaphoreType.DMA((5,)),
        ],
        compiler_params=params(VMEM_MOST),
        name="attention",
    )(page_table, prompt_lengths, queries, key_pool, value_pool)


def norm_kernel(hidden_ref, a0, a1, a2, a3, gain_ref, ids_ref, gates_ref, resid_ref, rows_ref):
    own = lax.axis_index("dp")
    tokens, width = hidden_ref.shape
    block = width // 4
    total = jnp.zeros((tokens, 1), jnp.float32)
    for d, attn in enumerate((a0, a1, a2, a3)):
        columns = pl.ds(pl.multiple_of((own ^ d) * block, block), block)
        resid = (
            hidden_ref[:, columns].astype(jnp.float32) + attn[...].astype(jnp.float32)
        ).astype(jnp.bfloat16)
        resid_ref[:, columns] = resid
        resid32 = resid.astype(jnp.float32)
        total += jnp.sum(resid32 * resid32, axis=-1, keepdims=True)
    inverse = lax.rsqrt(total / width + epsilon)
    for d in range(4):
        columns = pl.ds(pl.multiple_of((own ^ d) * block, block), block)
        rows_ref[:, d * block : (d + 1) * block] = (
            resid_ref[:, columns].astype(jnp.float32) * inverse * gain_ref[:, columns]
        ).astype(jnp.bfloat16)
    lane = lax.broadcasted_iota(jnp.int32, (tokens, LANES), 1)
    gates = jnp.zeros((tokens, LANES), jnp.float32)
    for k in range(TOPK):
        gates += jnp.where(ids_ref[:, k : k + 1] == lane % TOPK, gates_ref[:, k : k + 1], 0.0)
    high = gates.astype(jnp.bfloat16).astype(jnp.float32)
    middle = (gates - high).astype(jnp.bfloat16).astype(jnp.float32)
    low = gates - high - middle
    part = lane // TOPK
    terms = jnp.where(part == 0, high, jnp.where(part == 1, middle, jnp.where(part == 2, low, 0.0)))
    rows_ref[:, width:] = terms.astype(jnp.bfloat16)


def norm(hidden_in, attn, norm_gain, expert_ids, gate_weights):
    tokens, width = hidden_in.shape
    return pl.pallas_call(
        norm_kernel,
        out_shape=[
            jax.ShapeDtypeStruct((tokens, width), jnp.bfloat16),
            jax.ShapeDtypeStruct((tokens, width + LANES), jnp.bfloat16),
        ],
        in_specs=vmem(8),
        out_specs=vmem(2),
        compiler_params=params(),
        cost_estimate=SMALL,
        name="norm",
    )(hidden_in, *attn, norm_gain[None, :], expert_ids, gate_weights)


def cast_kernel(spans, *refs):
    count = len(spans)
    sources, targets, scratch = refs[:count], refs[count : 2 * count], refs[2 * count :]
    wide, narrow, arrived, left = scratch[:count], scratch[count : 2 * count], *scratch[-2:]

    def rows_of(i, step, first=0):
        rows = wide[i].shape[0] // CAST_STEPS
        return pl.ds(first + step * rows, rows)

    def copies_in(step):
        for i, (first, _, column, columns) in enumerate(spans):
            yield pltpu.make_async_copy(
                sources[i].at[0, rows_of(i, step, first), pl.ds(column, columns)],
                wide[i].at[rows_of(i, step)],
                arrived.at[step, i],
            )

    def copies_out(step):
        for i in range(count):
            here = rows_of(i, step)
            yield pltpu.make_async_copy(narrow[i].at[here], targets[i].at[here], left.at[step, i])

    for step in range(CAST_STEPS):
        for copy in copies_in(step):
            copy.start()
    for step in range(CAST_STEPS):
        for copy in copies_in(step):
            copy.wait()
        for i in range(count):
            here = rows_of(i, step)
            narrow[i][here] = wide[i][here].astype(jnp.bfloat16)
        for copy in copies_out(step):
            copy.start()
    for step in range(CAST_STEPS):
        for copy in copies_out(step):
            copy.wait()


def cast_rows(arrays, spans):
    shapes = [(rows, columns) for _, rows, _, columns in spans]
    return pl.pallas_call(
        lambda *refs: cast_kernel(spans, *refs),
        out_shape=[jax.ShapeDtypeStruct(shape, jnp.bfloat16) for shape in shapes],
        in_specs=[pl.BlockSpec(memory_space=pltpu.HBM)] * len(arrays),
        out_specs=[pl.BlockSpec(memory_space=pltpu.HBM)] * len(arrays),
        scratch_shapes=[pltpu.VMEM(shape, jnp.float32) for shape in shapes]
        + [pltpu.VMEM(shape, jnp.bfloat16) for shape in shapes]
        + [pltpu.SemaphoreType.DMA((CAST_STEPS, len(arrays)))] * 2,
        compiler_params=params(VMEM_MOST),
        name="cast_rows",
    )(*arrays)


def load_tiles(pieces, weights, arrived, tiles, block):
    def copies(tile):
        first = 0
        for index, piece in enumerate(pieces):
            depth = piece.shape[0]
            for part in range(2):
                columns = pl.ds((part * tiles + tile) * block, block)
                yield pltpu.make_async_copy(
                    piece.at[:, columns],
                    weights.at[pl.ds(first, depth), columns],
                    arrived.at[tile, index, part],
                )
            first += depth

    for tile in range(tiles):
        for copy in copies(tile):
            copy.start()

    def wait(tile):
        for copy in copies(tile):
            copy.wait()

    return wait


def up_kernel(sources, pieces, *refs):
    row_refs = refs[:sources]
    weight_refs = refs[sources : sources + pieces]
    hidden_ref, own_gate_ref, rows, weights, units, arrived = refs[sources + pieces :]
    width = rows.shape[1]
    tiles, _, block = units.shape
    wait = load_tiles(weight_refs, weights, arrived, tiles, block)
    expert = lax.axis_index("expert")
    first = 0
    for ref in row_refs:
        count = ref.shape[0]
        here = slice(first, first + count)
        rows[here, :] = ref[:, :width]
        terms = ref[:, width:].astype(jnp.float32)
        lane = lax.broadcasted_iota(jnp.int32, terms.shape, 1)
        own_gate_ref[here, :] = jnp.sum(
            jnp.where(lane % TOPK == expert, terms, 0.0), axis=-1, keepdims=True
        )
        first += count
    for tile in range(tiles):
        wait(tile)
        gate, up = (
            jnp.dot(
                rows[...],
                weights[:, (part * tiles + tile) * block : (part * tiles + tile + 1) * block],
                preferred_element_type=jnp.float32,
            )
            for part in range(2)
        )
        units[tile] = (gate / (1.0 + jnp.exp(-gate)) * up).astype(jnp.bfloat16)
    own = lax.axis_index("dp")
    for d in range(4):
        hidden_ref[:, d * block : (d + 1) * block] = units[own ^ d]


def expert_up(rows, weights):
    tokens = sum(piece.shape[0] for piece in rows)
    features = sum(piece.shape[0] for piece in weights)
    width = weights[0].shape[1]
    hidden_size = width // 2
    return pl.pallas_call(
        lambda *refs: up_kernel(len(rows), len(weights), *refs),
        out_shape=[
            jax.ShapeDtypeStruct((tokens, hidden_size), jnp.bfloat16),
            jax.ShapeDtypeStruct((tokens, 1), jnp.float32),
        ],
        in_specs=vmem(len(rows)) + [pl.BlockSpec(memory_space=pl.ANY)] * len(weights),
        out_specs=vmem(2),
        scratch_shapes=[
            pltpu.VMEM((tokens, features), jnp.bfloat16),
            pltpu.VMEM((features, width), jnp.bfloat16),
            pltpu.VMEM((4, tokens, hidden_size // 4), jnp.bfloat16),
            pltpu.SemaphoreType.DMA((4, len(weights), 2)),
        ],
        compiler_params=params(),
        cost_estimate=SMALL,
        name="expert_up",
    )(*rows, *weights)


def down_kernel(columns, sources, hidden_ref, gate_ref, *refs):
    (weights, arrived), refs = refs[-2:], refs[:-2]
    pieces, outs = refs[: len(refs) - sources - 3], refs[len(refs) - sources - 3 :]
    copies, first = [], 0
    for i, (ref, column) in enumerate(zip(pieces, columns)):
        depth = ref.shape[0]
        copies.append(
            pltpu.make_async_copy(
                ref.at[:, pl.ds(column, weights.shape[1])],
                weights.at[pl.ds(first, depth)],
                arrived.at[i],
            )
        )
        first += depth
    for copy in copies:
        copy.start()
    for copy in copies:
        copy.wait()
    total = jnp.dot(hidden_ref[...], weights[...], preferred_element_type=jnp.float32)
    weighted = (total * gate_ref[...]).astype(jnp.bfloat16)
    rows = weighted.shape[0] // sources
    for (first, count), ref in zip(down_blocks(rows, sources), outs):
        ref[...] = weighted[first : first + count]


def down_blocks(rows, sources):
    half, reach = rows // 2, sources // 2
    blocks = [(0, rows)]
    for step, middle in ((-1, reach * rows), (1, reach * rows + half)):
        blocks.append((middle, half))
        second = (reach + step) * rows
        blocks += [(second, half), (second + half, half)]
        blocks += [((reach + step * away) * rows, rows) for away in range(2, reach)]
    return blocks


def expert_down(hidden_units, gates, weights, width, sources):
    weights, columns = zip(*weights)
    tokens, hidden_size = hidden_units.shape
    rows = tokens // sources
    return pl.pallas_call(
        lambda *refs: down_kernel(columns, sources, *refs),
        out_shape=[
            jax.ShapeDtypeStruct((count, width), jnp.bfloat16)
            for _, count in down_blocks(rows, sources)
        ],
        in_specs=vmem(2) + [pl.BlockSpec(memory_space=pl.ANY)] * len(weights),
        out_specs=vmem(sources + 3),
        scratch_shapes=[
            pltpu.VMEM((hidden_size, width), jnp.bfloat16),
            pltpu.SemaphoreType.DMA((len(weights),)),
        ],
        compiler_params=params(),
        cost_estimate=SMALL,
        name="expert_down",
    )(hidden_units, gates, *weights)


def partner(x, distance):
    return lax.ppermute(x, "dp", [(i, i ^ distance) for i in range(4)])


def ring_order(count):
    return list(range(0, count, 2)) + list(range(count - 1, 0, -2))


def around(x, step):
    ring = ring_order(lax.axis_size("expert"))
    count = len(ring)
    return lax.ppermute(x, "expert", [(ring[i], ring[(i + step) % count]) for i in range(count)])


def after(x, *others):
    return lax.optimization_barrier((x, *others))[0]


def add(a, b):
    return (a.astype(jnp.float32) + b.astype(jnp.float32)).astype(jnp.bfloat16)


def gather_rows(rows):
    half = rows.shape[0] // 2
    reach = lax.axis_size("expert") // 2
    above, below = [rows], [rows]
    for _ in range(reach - 1):
        above.append(around(above[-1], -1))
        below.append(around(below[-1], 1))
    far = [around(above[-1][:half], -1), around(below[-1][half:], 1)]
    return above + far + below[:0:-1], list(zip(above[1:], below[1:])) + [tuple(far)]


def scatter_sum(own, *blocks):
    reach = len(blocks) // 2
    terms = [own]
    for step, (far, first, second, *near) in ((1, blocks[:reach]), (-1, blocks[reach:])):
        moving = around(far, step)
        if step > 0:
            moving = jnp.concatenate([add(first, moving), second])
        else:
            moving = jnp.concatenate([first, add(second, moving)])
        for block in near:
            moving = add(block, around(moving, step))
        terms.append(around(moving, step))
    return terms


def relayed(x, rows):
    return [partner(x[i : i + rows], 1) for i in range(0, x.shape[0], rows)]


def every_expert(
    hidden_in,
    queries,
    key_pool,
    value_pool,
    page_table,
    prompt_lengths,
    expert_ids,
    gate_weights,
    norm_gain,
    trainer_gate_up,
    trainer_down,
):
    expert_count = lax.axis_size("expert")
    width = trainer_down.shape[2]
    depth, columns = trainer_gate_up.shape[1:]
    down_depth = trainer_down.shape[1]
    early = depth // 4
    slab = width // SLABS
    (first_own,) = cast_rows([trainer_gate_up], [(0, early, 0, columns)])
    first_across = partner(first_own, 2)
    attn = attention(
        after(queries, first_own), key_pool, value_pool, page_table, prompt_lengths
    )
    rest_own, down_own = cast_rows(
        [after(trainer_gate_up, attn[0]), trainer_down],
        [(early, depth - early, 0, columns), (0, down_depth, 0, width)],
    )
    attn = [attn[0]] + [partner(attn[d], d) for d in (1, 2, 3)]
    rest_across = partner(after(rest_own, first_across, *attn), 2)
    resid, rows = norm(
        after(hidden_in[0], rest_own), attn, norm_gain, expert_ids[0], gate_weights[0]
    )
    gathered, arrived = gather_rows(rows)
    first_beside = partner(after(first_own, *arrived[0]), 1)
    first_opposite = partner(after(first_across, *arrived[0]), 1)
    rest_beside = partner(after(rest_own, *arrived[0]), 1)
    down_beside = partner(after(down_own, *arrived[1]), 1)
    down_across = partner(after(down_own, *arrived[2]), 2)
    rest_opposite = relayed(after(rest_across, *arrived[3]), depth // 8)
    hidden_units, gates = expert_up(
        gathered,
        [first_own, rest_own, first_beside, rest_beside]
        + [first_across, rest_across, first_opposite, *rest_opposite],
    )
    down_ready = after(down_across, hidden_units)
    mixed = []
    for first in range(0, width, slab):
        opposite = partner(down_ready[:, first : first + slab], 1)
        weights = [(down_own, first), (down_beside, first), (down_across, first), (opposite, 0)]
        weighted = expert_down(hidden_units, gates, weights, slab, expert_count)
        total = resid[:, first : first + slab].astype(jnp.float32)
        for term in scatter_sum(*weighted):
            total = total + term.astype(jnp.float32)
        mixed.append(total.astype(jnp.bfloat16))
    return jnp.concatenate(mixed, axis=1)[None]


def solution(mesh):
    placed = (
        P("expert", "dp", None),
        P("expert", None, "dp"),
        P("expert", None, "dp"),
        P("expert", None, "dp"),
        P("expert", None),
        P("expert", None),
        P("expert", "dp", None),
        P("expert", "dp", None),
        P(),
        P("expert", "dp", None),
        P("expert", "dp", None),
    )
    dense = mesh.shape["expert"] == TOPK and mesh.shape["dp"] == 4
    return jax.shard_map(
        every_expert if dense else local, mesh=mesh, in_specs=placed, out_specs=P("expert", "dp", None), check_vma=False
    )
```

```python
import math

import jax
import jax.numpy as jnp
from jax import lax
from jax.experimental import pallas as pl
from jax.experimental.pallas import tpu as pltpu
from jax.sharding import PartitionSpec as P

HDIM = 128
TOPK = 8


epsilon = 1e-05


def fetch_weights(trainer_gate_up, trainer_down):
    return (
        lax.all_gather(trainer_gate_up.astype(jnp.bfloat16), "dp", axis=1, tiled=True),
        lax.all_gather(trainer_down.astype(jnp.bfloat16), "dp", axis=1, tiled=True),
    )


def local(
    hidden_in,
    queries,
    key_pool,
    value_pool,
    page_table,
    prompt_lengths,
    expert_ids,
    gate_weights,
    norm_gain,
    trainer_gate_up,
    trainer_down,
):
    col_tok = queries.shape[1]
    width_dev = queries.shape[2]
    heads_dev = width_dev // HDIM
    keys_all = jnp.take(key_pool, page_table[0], axis=0).reshape(col_tok, heads_dev, HDIM)
    values_all = jnp.take(value_pool, page_table[0], axis=0).reshape(col_tok, heads_dev, HDIM)
    request_ends = jnp.cumsum(prompt_lengths[0])
    positions = lax.iota(jnp.int32, col_tok)
    request = jnp.sum((positions[:, None] >= request_ends[None, :]).astype(jnp.int32), axis=1)
    block_rows = math.gcd(col_tok, 512)
    query_blocks = queries[0].reshape(col_tok // block_rows, block_rows, heads_dev, HDIM)
    request_blocks = request.reshape(col_tok // block_rows, block_rows)
    score_scale = 1.0 / math.sqrt(HDIM)

    def attend(pieces):
        query_block, request_block = pieces
        scores = (
            jnp.einsum("qhd,khd->hqk", query_block, keys_all, preferred_element_type=jnp.float32)
            * score_scale
        )
        same_request = (request_block[:, None] == request[None, :])[None]
        scores = jnp.where(same_request, scores, -1e30)
        highest = jnp.max(scores, axis=-1, keepdims=True)
        weights = jnp.where(same_request, jnp.exp(scores - highest), 0.0)
        totals = jnp.sum(weights, axis=-1, keepdims=True)
        probs = (weights / totals).astype(jnp.bfloat16)
        output = jnp.einsum("hqk,khd->qhd", probs, values_all, preferred_element_type=jnp.float32)
        return output.astype(jnp.bfloat16).reshape(block_rows, width_dev)

    attn_heads = lax.map(attend, (query_blocks, request_blocks)).reshape(1, col_tok, width_dev)
    attn_tokens = lax.all_to_all(attn_heads, "dp", split_axis=1, concat_axis=2, tiled=True)
    resid32 = (
        (hidden_in.astype(jnp.float32) + attn_tokens.astype(jnp.float32))
        .astype(jnp.bfloat16)
        .astype(jnp.float32)
    )
    mean_square = jnp.mean(resid32 * resid32, axis=-1, keepdims=True)
    normed = (resid32 * lax.rsqrt(mean_square + epsilon) * norm_gain).astype(jnp.bfloat16)
    server_gate_up, server_down = fetch_weights(trainer_gate_up, trainer_down)
    token_rows = normed.shape[1]
    width = normed.shape[2]
    expert_count = lax.axis_size("expert")
    capacity = min(token_rows, token_rows * TOPK * 5 // (4 * expert_count))
    hidden_size = server_gate_up.shape[2] // 2
    ids_flat = expert_ids[0].reshape(token_rows * TOPK)
    onehot = (ids_flat[:, None] == lax.iota(jnp.int32, expert_count)[None, :]).astype(jnp.int32)
    earlier = jnp.cumsum(onehot, axis=0) - onehot
    slot_index = jnp.sum(earlier * onehot, axis=1)
    flat_slot = ids_flat * capacity + slot_index
    placement = (
        flat_slot[:, None] == lax.iota(jnp.int32, expert_count * capacity)[None, :]
    ).astype(jnp.bfloat16)
    dispatch_matrix = jnp.sum(placement.reshape(token_rows, TOPK, expert_count * capacity), axis=1)
    outgoing = jnp.einsum(
        "ts,td->sd", dispatch_matrix, normed[0], preferred_element_type=jnp.float32
    )
    outgoing = outgoing.astype(jnp.bfloat16).reshape(expert_count, capacity, width)
    received = lax.all_to_all(outgoing, "expert", split_axis=0, concat_axis=0, tiled=True)
    sources, items, features = received.shape
    slot_rows = received.reshape(sources * items, features)
    gate_up = jnp.dot(slot_rows, server_gate_up[0], preferred_element_type=jnp.float32)
    hidden_units = (jax.nn.silu(gate_up[:, :hidden_size]) * gate_up[:, hidden_size:]).astype(
        jnp.bfloat16
    )
    outputs = jnp.dot(hidden_units, server_down[0], preferred_element_type=jnp.float32).astype(
        jnp.bfloat16
    )
    returned = lax.all_to_all(
        outputs.reshape(sources, items, features), "expert", split_axis=0, concat_axis=0, tiled=True
    )
    copies = jnp.take(returned.reshape(expert_count * capacity, width), flat_slot, axis=0)
    copies = copies.reshape(token_rows, TOPK, width).astype(jnp.float32)
    mixture = jnp.einsum("tk,tkd->td", gate_weights[0], copies)
    mixed = resid32[0] + mixture
    return mixed.astype(jnp.bfloat16)[None]

LANES = 128
VMEM_LIMIT = 32 * 2**20
VMEM_MOST = 60 * 2**20
CAST_STEPS = 4
SLABS = 2
SMALL = pl.CostEstimate(flops=1, bytes_accessed=1, transcendentals=0)


def params(limit=VMEM_LIMIT):
    return pltpu.CompilerParams(vmem_limit_bytes=limit)


def vmem(count):
    return [pl.BlockSpec(memory_space=pltpu.VMEM)] * count


def attention_kernel(*refs):
    sources, outs, scratch = refs[:5], refs[5:9], refs[9:]
    table, lengths, q_ref, k_ref, v_ref, attn, arrived = scratch
    copies = [
        pltpu.make_async_copy(source, target, arrived.at[i])
        for i, (source, target) in enumerate(
            zip(
                (*sources[:2], sources[2].at[0], *sources[3:5]),
                (table, lengths, q_ref, k_ref, v_ref),
            )
        )
    ]
    for copy in copies:
        copy.start()
    for copy in copies:
        copy.wait()
    tokens, width = q_ref.shape
    pages = k_ref.shape[0]
    row = lax.broadcasted_iota(jnp.int32, (tokens, tokens), 0)
    column = lax.broadcasted_iota(jnp.int32, (tokens, tokens), 1)
    row_request = jnp.zeros((tokens, tokens), jnp.int32)
    column_request = jnp.zeros((tokens, tokens), jnp.int32)
    end = jnp.int32(0)
    for r in range(lengths.shape[1]):
        end = end + lengths[0, r]
        row_request += (row >= end).astype(jnp.int32)
        column_request += (column >= end).astype(jnp.int32)
    same = row_request == column_request
    for h in range(width // HDIM):
        lanes = slice(h * HDIM, (h + 1) * HDIM)
        keys = jnp.concatenate([k_ref[table[0, p], :, lanes] for p in range(pages)], axis=0)
        values = jnp.concatenate([v_ref[table[0, p], :, lanes] for p in range(pages)], axis=0)
        scores = lax.dot_general(
            q_ref[:, lanes], keys, (((1,), (1,)), ((), ())), preferred_element_type=jnp.float32
        ) * (1.0 / math.sqrt(HDIM))
        scores = jnp.where(same, scores, -1e30)
        highest = jnp.max(scores, axis=-1, keepdims=True)
        weight = jnp.where(same, jnp.exp(scores - highest), 0.0)
        probs = (weight / jnp.sum(weight, axis=-1, keepdims=True)).astype(jnp.bfloat16)
        attn[:, lanes] = jnp.dot(probs, values, preferred_element_type=jnp.float32).astype(
            jnp.bfloat16
        )
    own = lax.axis_index("dp")
    rows = tokens // 4
    for d in range(4):
        first = pl.multiple_of((own ^ d) * rows, rows)
        outs[d][...] = attn[pl.ds(first, rows), :]


def attention(queries, key_pool, value_pool, page_table, prompt_lengths):
    tokens, width = queries.shape[1:]
    return pl.pallas_call(
        attention_kernel,
        out_shape=[jax.ShapeDtypeStruct((tokens // 4, width), jnp.bfloat16)] * 4,
        in_specs=[pl.BlockSpec(memory_space=pltpu.HBM)] * 5,
        out_specs=vmem(4),
        scratch_shapes=[
            pltpu.SMEM(page_table.shape, jnp.int32),
            pltpu.SMEM(prompt_lengths.shape, jnp.int32),
            pltpu.VMEM((tokens, width), jnp.bfloat16),
            pltpu.VMEM(key_pool.shape, jnp.bfloat16),
            pltpu.VMEM(value_pool.shape, jnp.bfloat16),
            pltpu.VMEM((tokens, width), jnp.bfloat16),
            pltpu.SemaphoreType.DMA((5,)),
        ],
        compiler_params=params(VMEM_MOST),
        name="attention",
    )(page_table, prompt_lengths, queries, key_pool, value_pool)


def norm_kernel(hidden_ref, a0, a1, a2, a3, gain_ref, ids_ref, gates_ref, resid_ref, rows_ref):
    own = lax.axis_index("dp")
    tokens, width = hidden_ref.shape
    block = width // 4
    total = jnp.zeros((tokens, 1), jnp.float32)
    for d, attn in enumerate((a0, a1, a2, a3)):
        columns = pl.ds(pl.multiple_of((own ^ d) * block, block), block)
        resid = (
            hidden_ref[:, columns].astype(jnp.float32) + attn[...].astype(jnp.float32)
        ).astype(jnp.bfloat16)
        resid_ref[:, columns] = resid
        resid32 = resid.astype(jnp.float32)
        total += jnp.sum(resid32 * resid32, axis=-1, keepdims=True)
    inverse = lax.rsqrt(total / width + epsilon)
    for d in range(4):
        columns = pl.ds(pl.multiple_of((own ^ d) * block, block), block)
        rows_ref[:, d * block : (d + 1) * block] = (
            resid_ref[:, columns].astype(jnp.float32) * inverse * gain_ref[:, columns]
        ).astype(jnp.bfloat16)
    lane = lax.broadcasted_iota(jnp.int32, (tokens, LANES), 1)
    gates = jnp.zeros((tokens, LANES), jnp.float32)
    for k in range(TOPK):
        gates += jnp.where(ids_ref[:, k : k + 1] == lane % TOPK, gates_ref[:, k : k + 1], 0.0)
    high = gates.astype(jnp.bfloat16).astype(jnp.float32)
    middle = (gates - high).astype(jnp.bfloat16).astype(jnp.float32)
    low = gates - high - middle
    part = lane // TOPK
    terms = jnp.where(part == 0, high, jnp.where(part == 1, middle, jnp.where(part == 2, low, 0.0)))
    rows_ref[:, width:] = terms.astype(jnp.bfloat16)


def norm(hidden_in, attn, norm_gain, expert_ids, gate_weights):
    tokens, width = hidden_in.shape
    return pl.pallas_call(
        norm_kernel,
        out_shape=[
            jax.ShapeDtypeStruct((tokens, width), jnp.bfloat16),
            jax.ShapeDtypeStruct((tokens, width + LANES), jnp.bfloat16),
        ],
        in_specs=vmem(8),
        out_specs=vmem(2),
        compiler_params=params(),
        cost_estimate=SMALL,
        name="norm",
    )(hidden_in, *attn, norm_gain[None, :], expert_ids, gate_weights)


def cast_kernel(spans, *refs):
    count = len(spans)
    sources, targets, scratch = refs[:count], refs[count : 2 * count], refs[2 * count :]
    wide, narrow, arrived, left = scratch[:count], scratch[count : 2 * count], *scratch[-2:]

    def rows_of(i, step, first=0):
        rows = wide[i].shape[0] // CAST_STEPS
        return pl.ds(first + step * rows, rows)

    def copies_in(step):
        for i, (first, _, column, columns) in enumerate(spans):
            yield pltpu.make_async_copy(
                sources[i].at[0, rows_of(i, step, first), pl.ds(column, columns)],
                wide[i].at[rows_of(i, step)],
                arrived.at[step, i],
            )

    def copies_out(step):
        for i in range(count):
            here = rows_of(i, step)
            yield pltpu.make_async_copy(narrow[i].at[here], targets[i].at[here], left.at[step, i])

    for step in range(CAST_STEPS):
        for copy in copies_in(step):
            copy.start()
    for step in range(CAST_STEPS):
        for copy in copies_in(step):
            copy.wait()
        for i in range(count):
            here = rows_of(i, step)
            narrow[i][here] = wide[i][here].astype(jnp.bfloat16)
        for copy in copies_out(step):
            copy.start()
    for step in range(CAST_STEPS):
        for copy in copies_out(step):
            copy.wait()


def cast_rows(arrays, spans):
    shapes = [(rows, columns) for _, rows, _, columns in spans]
    return pl.pallas_call(
        lambda *refs: cast_kernel(spans, *refs),
        out_shape=[jax.ShapeDtypeStruct(shape, jnp.bfloat16) for shape in shapes],
        in_specs=[pl.BlockSpec(memory_space=pltpu.HBM)] * len(arrays),
        out_specs=[pl.BlockSpec(memory_space=pltpu.HBM)] * len(arrays),
        scratch_shapes=[pltpu.VMEM(shape, jnp.float32) for shape in shapes]
        + [pltpu.VMEM(shape, jnp.bfloat16) for shape in shapes]
        + [pltpu.SemaphoreType.DMA((CAST_STEPS, len(arrays)))] * 2,
        compiler_params=params(VMEM_MOST),
        name="cast_rows",
    )(*arrays)


def load_tiles(pieces, weights, arrived, tiles, block):
    def copies(tile):
        first = 0
        for index, piece in enumerate(pieces):
            depth = piece.shape[0]
            for part in range(2):
                columns = pl.ds((part * tiles + tile) * block, block)
                yield pltpu.make_async_copy(
                    piece.at[:, columns],
                    weights.at[pl.ds(first, depth), columns],
                    arrived.at[tile, index, part],
                )
            first += depth

    for tile in range(tiles):
        for copy in copies(tile):
            copy.start()

    def wait(tile):
        for copy in copies(tile):
            copy.wait()

    return wait


def up_kernel(sources, pieces, *refs):
    row_refs = refs[:sources]
    weight_refs = refs[sources : sources + pieces]
    hidden_ref, own_gate_ref, rows, weights, units, arrived = refs[sources + pieces :]
    width = rows.shape[1]
    tiles, _, block = units.shape
    wait = load_tiles(weight_refs, weights, arrived, tiles, block)
    expert = lax.axis_index("expert")
    first = 0
    for ref in row_refs:
        count = ref.shape[0]
        here = slice(first, first + count)
        rows[here, :] = ref[:, :width]
        terms = ref[:, width:].astype(jnp.float32)
        lane = lax.broadcasted_iota(jnp.int32, terms.shape, 1)
        own_gate_ref[here, :] = jnp.sum(
            jnp.where(lane % TOPK == expert, terms, 0.0), axis=-1, keepdims=True
        )
        first += count
    for tile in range(tiles):
        wait(tile)
        gate, up = (
            jnp.dot(
                rows[...],
                weights[:, (part * tiles + tile) * block : (part * tiles + tile + 1) * block],
                preferred_element_type=jnp.float32,
            )
            for part in range(2)
        )
        units[tile] = (gate / (1.0 + jnp.exp(-gate)) * up).astype(jnp.bfloat16)
    own = lax.axis_index("dp")
    for d in range(4):
        hidden_ref[:, d * block : (d + 1) * block] = units[own ^ d]


def expert_up(rows, weights):
    tokens = sum(piece.shape[0] for piece in rows)
    features = sum(piece.shape[0] for piece in weights)
    width = weights[0].shape[1]
    hidden_size = width // 2
    return pl.pallas_call(
        lambda *refs: up_kernel(len(rows), len(weights), *refs),
        out_shape=[
            jax.ShapeDtypeStruct((tokens, hidden_size), jnp.bfloat16),
            jax.ShapeDtypeStruct((tokens, 1), jnp.float32),
        ],
        in_specs=vmem(len(rows)) + [pl.BlockSpec(memory_space=pl.ANY)] * len(weights),
        out_specs=vmem(2),
        scratch_shapes=[
            pltpu.VMEM((tokens, features), jnp.bfloat16),
            pltpu.VMEM((features, width), jnp.bfloat16),
            pltpu.VMEM((4, tokens, hidden_size // 4), jnp.bfloat16),
            pltpu.SemaphoreType.DMA((4, len(weights), 2)),
        ],
        compiler_params=params(),
        cost_estimate=SMALL,
        name="expert_up",
    )(*rows, *weights)


def load_rows(pieces, weights, arrived):
    copies, first = [], 0
    for i, ref in enumerate(pieces):
        depth = ref.shape[0]
        copies.append(
            pltpu.make_async_copy(ref, weights.at[pl.ds(first, depth)], arrived.at[i])
        )
        first += depth
    for copy in copies:
        copy.start()
    for copy in copies:
        copy.wait()


def part_kernel(hidden_ref, *refs):
    pieces, (total_ref, weights, arrived) = refs[:-3], refs[-3:]
    load_rows(pieces, weights, arrived)
    total_ref[...] = jnp.dot(
        hidden_ref[:, : weights.shape[0]], weights[...], preferred_element_type=jnp.float32
    )


def down_part(hidden_units, weights):
    depth = sum(piece.shape[0] for piece in weights)
    shape = hidden_units.shape[0], weights[0].shape[1]
    return pl.pallas_call(
        part_kernel,
        out_shape=jax.ShapeDtypeStruct(shape, jnp.float32),
        in_specs=vmem(1) + [pl.BlockSpec(memory_space=pl.ANY)] * len(weights),
        out_specs=pl.BlockSpec(memory_space=pltpu.VMEM),
        scratch_shapes=[
            pltpu.VMEM((depth, shape[1]), jnp.bfloat16),
            pltpu.SemaphoreType.DMA((len(weights),)),
        ],
        compiler_params=params(),
        cost_estimate=SMALL,
        name="down_part",
    )(hidden_units, *weights)


def down_kernel(first, column, sources, hidden_ref, total_ref, gate_ref, piece, *refs):
    outs, (weights, arrived) = refs[:-2], refs[-2:]
    load_rows([piece], weights, arrived)
    depth, width = weights.shape
    units = hidden_ref[:, first : first + depth]
    total = total_ref[:, column : column + width] + jnp.dot(
        units, weights[...], preferred_element_type=jnp.float32
    )
    weighted = (total * gate_ref[...]).astype(jnp.bfloat16)
    rows = weighted.shape[0] // sources
    for (first, count), ref in zip(down_blocks(rows, sources), outs):
        ref[...] = weighted[first : first + count]


def down_blocks(rows, sources):
    half, reach = rows // 2, sources // 2
    blocks = [(0, rows)]
    for step, middle in ((-1, reach * rows), (1, reach * rows + half)):
        blocks.append((middle, half))
        second = (reach + step) * rows
        blocks += [(second, half), (second + half, half)]
        blocks += [((reach + step * away) * rows, rows) for away in range(2, reach)]
    return blocks


def expert_down(hidden_units, total, gates, weights, column, sources):
    tokens, hidden_size = hidden_units.shape
    depth, width = weights.shape
    rows = tokens // sources
    return pl.pallas_call(
        lambda *refs: down_kernel(hidden_size - depth, column, sources, *refs),
        out_shape=[
            jax.ShapeDtypeStruct((count, width), jnp.bfloat16)
            for _, count in down_blocks(rows, sources)
        ],
        in_specs=vmem(3) + [pl.BlockSpec(memory_space=pl.ANY)],
        out_specs=vmem(sources + 3),
        scratch_shapes=[
            pltpu.VMEM((depth, width), jnp.bfloat16),
            pltpu.SemaphoreType.DMA((1,)),
        ],
        compiler_params=params(),
        cost_estimate=SMALL,
        name="expert_down",
    )(hidden_units, total, gates, weights)


def partner(x, distance):
    return lax.ppermute(x, "dp", [(i, i ^ distance) for i in range(4)])


def ring_order(count):
    return list(range(0, count, 2)) + list(range(count - 1, 0, -2))


def around(x, step):
    ring = ring_order(lax.axis_size("expert"))
    count = len(ring)
    return lax.ppermute(x, "expert", [(ring[i], ring[(i + step) % count]) for i in range(count)])


def after(x, *others):
    return lax.optimization_barrier((x, *others))[0]


def add(a, b):
    return (a.astype(jnp.float32) + b.astype(jnp.float32)).astype(jnp.bfloat16)


def gather_rows(rows):
    half = rows.shape[0] // 2
    reach = lax.axis_size("expert") // 2
    above, below = [rows], [rows]
    for _ in range(reach - 1):
        above.append(around(above[-1], -1))
        below.append(around(below[-1], 1))
    far = [around(above[-1][:half], -1), around(below[-1][half:], 1)]
    return above + far + below[:0:-1], list(zip(above[1:], below[1:])) + [tuple(far)]


def scatter_sum(own, *blocks):
    reach = len(blocks) // 2
    terms = [own]
    for step, (far, first, second, *near) in ((1, blocks[:reach]), (-1, blocks[reach:])):
        moving = around(far, step)
        if step > 0:
            moving = jnp.concatenate([add(first, moving), second])
        else:
            moving = jnp.concatenate([first, add(second, moving)])
        for block in near:
            moving = add(block, around(moving, step))
        terms.append(around(moving, step))
    return terms


def relayed(x, rows):
    return [partner(x[i : i + rows], 1) for i in range(0, x.shape[0], rows)]


def every_expert(
    hidden_in,
    queries,
    key_pool,
    value_pool,
    page_table,
    prompt_lengths,
    expert_ids,
    gate_weights,
    norm_gain,
    trainer_gate_up,
    trainer_down,
):
    expert_count = lax.axis_size("expert")
    width = trainer_down.shape[2]
    depth, columns = trainer_gate_up.shape[1:]
    down_depth = trainer_down.shape[1]
    early = depth // 4
    slab = width // SLABS
    (first_own,) = cast_rows([trainer_gate_up], [(0, early, 0, columns)])
    first_across = partner(first_own, 2)
    attn = attention(
        after(queries, first_own), key_pool, value_pool, page_table, prompt_lengths
    )
    rest_own, down_own = cast_rows(
        [after(trainer_gate_up, attn[0]), trainer_down],
        [(early, depth - early, 0, columns), (0, down_depth, 0, width)],
    )
    attn = [attn[0]] + [partner(attn[d], d) for d in (1, 2, 3)]
    rest_across = partner(after(rest_own, first_across, *attn), 2)
    resid, rows = norm(
        after(hidden_in[0], rest_own), attn, norm_gain, expert_ids[0], gate_weights[0]
    )
    gathered, arrived = gather_rows(rows)
    first_beside = partner(after(first_own, *arrived[0]), 1)
    first_opposite = partner(after(first_across, *arrived[0]), 1)
    rest_beside = partner(after(rest_own, *arrived[0]), 1)
    down_beside = partner(after(down_own, *arrived[1]), 1)
    down_across = partner(after(down_own, *arrived[2]), 2)
    rest_opposite = relayed(after(rest_across, *arrived[3]), depth // 8)
    hidden_units, gates = expert_up(
        gathered,
        [first_own, rest_own, first_beside, rest_beside]
        + [first_across, rest_across, first_opposite, *rest_opposite],
    )
    down_ready = after(down_across, hidden_units)
    total = down_part(hidden_units, [down_own, down_beside, down_ready])
    mixed = []
    for first in range(0, width, slab):
        opposite = partner(down_ready[:, first : first + slab], 1)
        weighted = expert_down(hidden_units, total, gates, opposite, first, expert_count)
        sum_here = resid[:, first : first + slab].astype(jnp.float32)
        for term in scatter_sum(*weighted):
            sum_here = sum_here + term.astype(jnp.float32)
        mixed.append(sum_here.astype(jnp.bfloat16))
    return jnp.concatenate(mixed, axis=1)[None]


def solution(mesh):
    placed = (
        P("expert", "dp", None),
        P("expert", None, "dp"),
        P("expert", None, "dp"),
        P("expert", None, "dp"),
        P("expert", None),
        P("expert", None),
        P("expert", "dp", None),
        P("expert", "dp", None),
        P(),
        P("expert", "dp", None),
        P("expert", "dp", None),
    )
    dense = mesh.shape["expert"] == TOPK and mesh.shape["dp"] == 4
    return jax.shard_map(
        every_expert if dense else local, mesh=mesh, in_specs=placed, out_specs=P("expert", "dp", None), check_vma=False
    )
```

```python
import math

import jax
import jax.numpy as jnp
from jax import lax
from jax.experimental import pallas as pl
from jax.experimental.pallas import tpu as pltpu
from jax.sharding import PartitionSpec as P

HDIM = 128
TOPK = 8


epsilon = 1e-05


def fetch_weights(trainer_gate_up, trainer_down):
    return (
        lax.all_gather(trainer_gate_up.astype(jnp.bfloat16), "dp", axis=1, tiled=True),
        lax.all_gather(trainer_down.astype(jnp.bfloat16), "dp", axis=1, tiled=True),
    )


def local(
    hidden_in,
    queries,
    key_pool,
    value_pool,
    page_table,
    prompt_lengths,
    expert_ids,
    gate_weights,
    norm_gain,
    trainer_gate_up,
    trainer_down,
):
    col_tok = queries.shape[1]
    width_dev = queries.shape[2]
    heads_dev = width_dev // HDIM
    keys_all = jnp.take(key_pool, page_table[0], axis=0).reshape(col_tok, heads_dev, HDIM)
    values_all = jnp.take(value_pool, page_table[0], axis=0).reshape(col_tok, heads_dev, HDIM)
    request_ends = jnp.cumsum(prompt_lengths[0])
    positions = lax.iota(jnp.int32, col_tok)
    request = jnp.sum((positions[:, None] >= request_ends[None, :]).astype(jnp.int32), axis=1)
    block_rows = math.gcd(col_tok, 512)
    query_blocks = queries[0].reshape(col_tok // block_rows, block_rows, heads_dev, HDIM)
    request_blocks = request.reshape(col_tok // block_rows, block_rows)
    score_scale = 1.0 / math.sqrt(HDIM)

    def attend(pieces):
        query_block, request_block = pieces
        scores = (
            jnp.einsum("qhd,khd->hqk", query_block, keys_all, preferred_element_type=jnp.float32)
            * score_scale
        )
        same_request = (request_block[:, None] == request[None, :])[None]
        scores = jnp.where(same_request, scores, -1e30)
        highest = jnp.max(scores, axis=-1, keepdims=True)
        weights = jnp.where(same_request, jnp.exp(scores - highest), 0.0)
        totals = jnp.sum(weights, axis=-1, keepdims=True)
        probs = (weights / totals).astype(jnp.bfloat16)
        output = jnp.einsum("hqk,khd->qhd", probs, values_all, preferred_element_type=jnp.float32)
        return output.astype(jnp.bfloat16).reshape(block_rows, width_dev)

    attn_heads = lax.map(attend, (query_blocks, request_blocks)).reshape(1, col_tok, width_dev)
    attn_tokens = lax.all_to_all(attn_heads, "dp", split_axis=1, concat_axis=2, tiled=True)
    resid32 = (
        (hidden_in.astype(jnp.float32) + attn_tokens.astype(jnp.float32))
        .astype(jnp.bfloat16)
        .astype(jnp.float32)
    )
    mean_square = jnp.mean(resid32 * resid32, axis=-1, keepdims=True)
    normed = (resid32 * lax.rsqrt(mean_square + epsilon) * norm_gain).astype(jnp.bfloat16)
    server_gate_up, server_down = fetch_weights(trainer_gate_up, trainer_down)
    token_rows = normed.shape[1]
    width = normed.shape[2]
    expert_count = lax.axis_size("expert")
    capacity = min(token_rows, token_rows * TOPK * 5 // (4 * expert_count))
    hidden_size = server_gate_up.shape[2] // 2
    ids_flat = expert_ids[0].reshape(token_rows * TOPK)
    onehot = (ids_flat[:, None] == lax.iota(jnp.int32, expert_count)[None, :]).astype(jnp.int32)
    earlier = jnp.cumsum(onehot, axis=0) - onehot
    slot_index = jnp.sum(earlier * onehot, axis=1)
    flat_slot = ids_flat * capacity + slot_index
    placement = (
        flat_slot[:, None] == lax.iota(jnp.int32, expert_count * capacity)[None, :]
    ).astype(jnp.bfloat16)
    dispatch_matrix = jnp.sum(placement.reshape(token_rows, TOPK, expert_count * capacity), axis=1)
    outgoing = jnp.einsum(
        "ts,td->sd", dispatch_matrix, normed[0], preferred_element_type=jnp.float32
    )
    outgoing = outgoing.astype(jnp.bfloat16).reshape(expert_count, capacity, width)
    received = lax.all_to_all(outgoing, "expert", split_axis=0, concat_axis=0, tiled=True)
    sources, items, features = received.shape
    slot_rows = received.reshape(sources * items, features)
    gate_up = jnp.dot(slot_rows, server_gate_up[0], preferred_element_type=jnp.float32)
    hidden_units = (jax.nn.silu(gate_up[:, :hidden_size]) * gate_up[:, hidden_size:]).astype(
        jnp.bfloat16
    )
    outputs = jnp.dot(hidden_units, server_down[0], preferred_element_type=jnp.float32).astype(
        jnp.bfloat16
    )
    returned = lax.all_to_all(
        outputs.reshape(sources, items, features), "expert", split_axis=0, concat_axis=0, tiled=True
    )
    copies = jnp.take(returned.reshape(expert_count * capacity, width), flat_slot, axis=0)
    copies = copies.reshape(token_rows, TOPK, width).astype(jnp.float32)
    mixture = jnp.einsum("tk,tkd->td", gate_weights[0], copies)
    mixed = resid32[0] + mixture
    return mixed.astype(jnp.bfloat16)[None]

LANES = 128
VMEM_LIMIT = 32 * 2**20
VMEM_MOST = 60 * 2**20
CAST_STEPS = 4
FIRST_BLOCKS = 2
SLABS = 2
SMALL = pl.CostEstimate(flops=1, bytes_accessed=1, transcendentals=0)


def params(limit=VMEM_LIMIT):
    return pltpu.CompilerParams(vmem_limit_bytes=limit)


def vmem(count):
    return [pl.BlockSpec(memory_space=pltpu.VMEM)] * count


def attention_kernel(*refs):
    sources, outs, scratch = refs[:6], refs[6:10], refs[10:]
    own_ref, beside_ref, sent_ref, rows_ref = outs
    table, lengths, q_ref, k_ref, v_ref, weights, attn, arrived = scratch
    copies = [
        pltpu.make_async_copy(source, target, arrived.at[i])
        for i, (source, target) in enumerate(
            zip(
                (*sources[:2], sources[2].at[0], *sources[3:5]),
                (table, lengths, q_ref, k_ref, v_ref),
            )
        )
    ]
    rows = weights.shape[0]
    copies.append(
        pltpu.make_async_copy(sources[5].at[0, pl.ds(0, rows)], weights, arrived.at[5])
    )
    for copy in copies:
        copy.start()
    for copy in copies[:5]:
        copy.wait()
    tokens, width = q_ref.shape
    pages = k_ref.shape[0]
    row = lax.broadcasted_iota(jnp.int32, (tokens, tokens), 0)
    column = lax.broadcasted_iota(jnp.int32, (tokens, tokens), 1)
    row_request = jnp.zeros((tokens, tokens), jnp.int32)
    column_request = jnp.zeros((tokens, tokens), jnp.int32)
    end = jnp.int32(0)
    for r in range(lengths.shape[1]):
        end = end + lengths[0, r]
        row_request += (row >= end).astype(jnp.int32)
        column_request += (column >= end).astype(jnp.int32)
    same = row_request == column_request
    for h in range(width // HDIM):
        lanes = slice(h * HDIM, (h + 1) * HDIM)
        keys = jnp.concatenate([k_ref[table[0, p], :, lanes] for p in range(pages)], axis=0)
        values = jnp.concatenate([v_ref[table[0, p], :, lanes] for p in range(pages)], axis=0)
        scores = lax.dot_general(
            q_ref[:, lanes], keys, (((1,), (1,)), ((), ())), preferred_element_type=jnp.float32
        ) * (1.0 / math.sqrt(HDIM))
        scores = jnp.where(same, scores, -1e30)
        highest = jnp.max(scores, axis=-1, keepdims=True)
        weight = jnp.where(same, jnp.exp(scores - highest), 0.0)
        probs = (weight / jnp.sum(weight, axis=-1, keepdims=True)).astype(jnp.bfloat16)
        attn[:, lanes] = jnp.dot(probs, values, preferred_element_type=jnp.float32).astype(
            jnp.bfloat16
        )
    own = lax.axis_index("dp")
    block = tokens // 4
    split = weights.shape[1]
    end = sent_ref.shape[1]
    targets = (
        own_ref,
        beside_ref,
        sent_ref.at[:, end - 2 * width : end - width],
        sent_ref.at[:, end - width :],
    )
    for d, target in enumerate(targets):
        target[...] = attn[pl.ds(pl.multiple_of((own ^ d) * block, block), block), :]
    copies[5].wait()
    rows_ref[...] = weights[...].astype(jnp.bfloat16)
    for i in range(rows // block):
        here = slice(i * block, (i + 1) * block)
        sent_ref[:, i * split : (i + 1) * split] = rows_ref[here]


def attention(queries, key_pool, value_pool, page_table, prompt_lengths, gate_up, blocks):
    tokens, width = queries.shape[1:]
    split = gate_up.shape[2]
    block = tokens // 4
    shapes = [(block, width)] * 2
    shapes += [(block, blocks * split + 2 * width), (blocks * block, split)]
    return pl.pallas_call(
        attention_kernel,
        out_shape=[jax.ShapeDtypeStruct(shape, jnp.bfloat16) for shape in shapes],
        in_specs=[pl.BlockSpec(memory_space=pltpu.HBM)] * 6,
        out_specs=vmem(4),
        scratch_shapes=[
            pltpu.SMEM(page_table.shape, jnp.int32),
            pltpu.SMEM(prompt_lengths.shape, jnp.int32),
            pltpu.VMEM((tokens, width), jnp.bfloat16),
            pltpu.VMEM(key_pool.shape, jnp.bfloat16),
            pltpu.VMEM(value_pool.shape, jnp.bfloat16),
            pltpu.VMEM((blocks * block, split), jnp.float32),
            pltpu.VMEM((tokens, width), jnp.bfloat16),
            pltpu.SemaphoreType.DMA((6,)),
        ],
        compiler_params=params(VMEM_MOST),
        name="attention",
    )(page_table, prompt_lengths, queries, key_pool, value_pool, gate_up)


def norm_kernel(hidden_ref, a0, a1, first, a3, gain_ref, ids_ref, gates_ref, resid_ref, *row_refs):
    own = lax.axis_index("dp")
    tokens, width = hidden_ref.shape
    block = width // 4
    end = first.shape[1]
    a2 = first.at[:, end - 2 * block : end - block]
    total = jnp.zeros((tokens, 1), jnp.float32)
    for d, attn in enumerate((a0, a1, a2, a3)):
        columns = pl.ds(pl.multiple_of((own ^ d) * block, block), block)
        resid = (
            hidden_ref[:, columns].astype(jnp.float32) + attn[...].astype(jnp.float32)
        ).astype(jnp.bfloat16)
        resid_ref[:, columns] = resid
        resid32 = resid.astype(jnp.float32)
        total += jnp.sum(resid32 * resid32, axis=-1, keepdims=True)
    inverse = lax.rsqrt(total / width + epsilon)
    for d in range(4):
        columns = pl.ds(pl.multiple_of((own ^ d) * block, block), block)
        normed = resid_ref[:, columns].astype(jnp.float32) * inverse * gain_ref[:, columns]
        for i, ref in enumerate(row_refs):
            here = slice(i * tokens // 2, (i + 1) * tokens // 2)
            ref[:, d * block : (d + 1) * block] = normed[here].astype(jnp.bfloat16)
    lane = lax.broadcasted_iota(jnp.int32, (tokens, LANES), 1)
    gates = jnp.zeros((tokens, LANES), jnp.float32)
    for k in range(TOPK):
        gates += jnp.where(ids_ref[:, k : k + 1] == lane % TOPK, gates_ref[:, k : k + 1], 0.0)
    high = gates.astype(jnp.bfloat16).astype(jnp.float32)
    middle = (gates - high).astype(jnp.bfloat16).astype(jnp.float32)
    low = gates - high - middle
    part = lane // TOPK
    terms = jnp.where(part == 0, high, jnp.where(part == 1, middle, jnp.where(part == 2, low, 0.0)))
    for i, ref in enumerate(row_refs):
        here = slice(i * tokens // 2, (i + 1) * tokens // 2)
        ref[:, width:] = terms[here].astype(jnp.bfloat16)


def norm(hidden_in, attn, norm_gain, expert_ids, gate_weights):
    tokens, width = hidden_in.shape
    return pl.pallas_call(
        norm_kernel,
        out_shape=[
            jax.ShapeDtypeStruct((tokens, width), jnp.bfloat16),
        ]
        + [jax.ShapeDtypeStruct((tokens // 2, width + LANES), jnp.bfloat16)] * 2,
        in_specs=vmem(8),
        out_specs=vmem(3),
        compiler_params=params(),
        cost_estimate=SMALL,
        name="norm",
    )(hidden_in, *attn, norm_gain[None, :], expert_ids, gate_weights)


def cast_kernel(spans, *refs):
    count = len(spans)
    sources, targets, scratch = refs[:count], refs[count : 2 * count], refs[2 * count :]
    wide, narrow, arrived, left = scratch[:count], scratch[count : 2 * count], *scratch[-2:]

    def rows_of(i, step, first=0):
        rows = wide[i].shape[0] // CAST_STEPS
        return pl.ds(first + step * rows, rows)

    def copies_in(step):
        for i, (first, _, column, columns) in enumerate(spans):
            yield pltpu.make_async_copy(
                sources[i].at[0, rows_of(i, step, first), pl.ds(column, columns)],
                wide[i].at[rows_of(i, step)],
                arrived.at[step, i],
            )

    def copies_out(step):
        for i in range(count):
            here = rows_of(i, step)
            yield pltpu.make_async_copy(narrow[i].at[here], targets[i].at[here], left.at[step, i])

    for step in range(CAST_STEPS):
        for copy in copies_in(step):
            copy.start()
    for step in range(CAST_STEPS):
        for copy in copies_in(step):
            copy.wait()
        for i in range(count):
            here = rows_of(i, step)
            narrow[i][here] = wide[i][here].astype(jnp.bfloat16)
        for copy in copies_out(step):
            copy.start()
    for step in range(CAST_STEPS):
        for copy in copies_out(step):
            copy.wait()


def cast_rows(arrays, spans):
    shapes = [(rows, columns) for _, rows, _, columns in spans]
    return pl.pallas_call(
        lambda *refs: cast_kernel(spans, *refs),
        out_shape=[jax.ShapeDtypeStruct(shape, jnp.bfloat16) for shape in shapes],
        in_specs=[pl.BlockSpec(memory_space=pltpu.HBM)] * len(arrays),
        out_specs=[pl.BlockSpec(memory_space=pltpu.HBM)] * len(arrays),
        scratch_shapes=[pltpu.VMEM(shape, jnp.float32) for shape in shapes]
        + [pltpu.VMEM(shape, jnp.bfloat16) for shape in shapes]
        + [pltpu.SemaphoreType.DMA((CAST_STEPS, len(arrays)))] * 2,
        compiler_params=params(VMEM_MOST),
        name="cast_rows",
    )(*arrays)


def load_tiles(pieces, starts, weights, arrived, tiles, block):
    def copies(tile):
        first = 0
        for index, (piece, start) in enumerate(zip(pieces, starts)):
            depth = piece.shape[0]
            for part in range(2):
                column = (part * tiles + tile) * block
                yield pltpu.make_async_copy(
                    piece.at[:, pl.ds(start + column, block)],
                    weights.at[pl.ds(first, depth), pl.ds(column, block)],
                    arrived.at[tile, index, part],
                )
            first += depth

    for tile in range(tiles):
        for copy in copies(tile):
            copy.start()

    def wait(tile):
        for copy in copies(tile):
            copy.wait()

    return wait


def up_kernel(sources, starts, *refs):
    pieces = len(starts)
    row_refs = refs[:sources]
    weight_refs = refs[sources : sources + pieces]
    hidden_ref, own_gate_ref, rows, weights, units, arrived = refs[sources + pieces :]
    width = rows.shape[1]
    tiles, _, block = units.shape
    wait = load_tiles(weight_refs, starts, weights, arrived, tiles, block)
    expert = lax.axis_index("expert")
    first = 0
    for ref in row_refs:
        count = ref.shape[0]
        here = slice(first, first + count)
        rows[here, :] = ref[:, :width]
        terms = ref[:, width:].astype(jnp.float32)
        lane = lax.broadcasted_iota(jnp.int32, terms.shape, 1)
        own_gate_ref[here, :] = jnp.sum(
            jnp.where(lane % TOPK == expert, terms, 0.0), axis=-1, keepdims=True
        )
        first += count
    for tile in range(tiles):
        wait(tile)
        gate, up = (
            jnp.dot(
                rows[...],
                weights[:, (part * tiles + tile) * block : (part * tiles + tile + 1) * block],
                preferred_element_type=jnp.float32,
            )
            for part in range(2)
        )
        units[tile] = (gate / (1.0 + jnp.exp(-gate)) * up).astype(jnp.bfloat16)
    own = lax.axis_index("dp")
    for d in range(4):
        hidden_ref[:, d * block : (d + 1) * block] = units[own ^ d]


def expert_up(rows, weights, width):
    weights, starts = zip(*weights)
    tokens = sum(piece.shape[0] for piece in rows)
    features = sum(piece.shape[0] for piece in weights)
    hidden_size = width // 2
    return pl.pallas_call(
        lambda *refs: up_kernel(len(rows), starts, *refs),
        out_shape=[
            jax.ShapeDtypeStruct((tokens, hidden_size), jnp.bfloat16),
            jax.ShapeDtypeStruct((tokens, 1), jnp.float32),
        ],
        in_specs=vmem(len(rows)) + [pl.BlockSpec(memory_space=pl.ANY)] * len(weights),
        out_specs=vmem(2),
        scratch_shapes=[
            pltpu.VMEM((tokens, features), jnp.bfloat16),
            pltpu.VMEM((features, width), jnp.bfloat16),
            pltpu.VMEM((4, tokens, hidden_size // 4), jnp.bfloat16),
            pltpu.SemaphoreType.DMA((4, len(weights), 2)),
        ],
        compiler_params=params(),
        cost_estimate=SMALL,
        name="expert_up",
    )(*rows, *weights)


def load_rows(pieces, weights, arrived):
    copies, first = [], 0
    for i, ref in enumerate(pieces):
        depth = ref.shape[0]
        copies.append(
            pltpu.make_async_copy(ref, weights.at[pl.ds(first, depth)], arrived.at[i])
        )
        first += depth
    for copy in copies:
        copy.start()
    for copy in copies:
        copy.wait()


def part_kernel(hidden_ref, *refs):
    pieces, (total_ref, weights, arrived) = refs[:-3], refs[-3:]
    load_rows(pieces, weights, arrived)
    total_ref[...] = jnp.dot(
        hidden_ref[:, : weights.shape[0]], weights[...], preferred_element_type=jnp.float32
    )


def down_part(hidden_units, weights):
    depth = sum(piece.shape[0] for piece in weights)
    shape = hidden_units.shape[0], weights[0].shape[1]
    return pl.pallas_call(
        part_kernel,
        out_shape=jax.ShapeDtypeStruct(shape, jnp.float32),
        in_specs=vmem(1) + [pl.BlockSpec(memory_space=pl.ANY)] * len(weights),
        out_specs=pl.BlockSpec(memory_space=pltpu.VMEM),
        scratch_shapes=[
            pltpu.VMEM((depth, shape[1]), jnp.bfloat16),
            pltpu.SemaphoreType.DMA((len(weights),)),
        ],
        compiler_params=params(),
        cost_estimate=SMALL,
        name="down_part",
    )(hidden_units, *weights)


def down_kernel(first, column, sources, hidden_ref, total_ref, gate_ref, piece, *refs):
    outs, (weights, arrived) = refs[:-2], refs[-2:]
    load_rows([piece], weights, arrived)
    depth, width = weights.shape
    units = hidden_ref[:, first : first + depth]
    total = total_ref[:, column : column + width] + jnp.dot(
        units, weights[...], preferred_element_type=jnp.float32
    )
    weighted = (total * gate_ref[...]).astype(jnp.bfloat16)
    rows = weighted.shape[0] // sources
    for (first, count), ref in zip(down_blocks(rows, sources), outs):
        ref[...] = weighted[first : first + count]


def down_blocks(rows, sources):
    half, reach = rows // 2, sources // 2
    blocks = [(0, rows)]
    for step, middle in ((-1, reach * rows), (1, reach * rows + half)):
        blocks.append((middle, half))
        second = (reach + step) * rows
        blocks += [(second, half), (second + half, half)]
        blocks += [((reach + step * away) * rows, rows) for away in range(2, reach)]
    return blocks


def expert_down(hidden_units, total, gates, weights, column, sources):
    tokens, hidden_size = hidden_units.shape
    depth, width = weights.shape
    rows = tokens // sources
    return pl.pallas_call(
        lambda *refs: down_kernel(hidden_size - depth, column, sources, *refs),
        out_shape=[
            jax.ShapeDtypeStruct((count, width), jnp.bfloat16)
            for _, count in down_blocks(rows, sources)
        ],
        in_specs=vmem(3) + [pl.BlockSpec(memory_space=pl.ANY)],
        out_specs=vmem(sources + 3),
        scratch_shapes=[
            pltpu.VMEM((depth, width), jnp.bfloat16),
            pltpu.SemaphoreType.DMA((1,)),
        ],
        compiler_params=params(),
        cost_estimate=SMALL,
        name="expert_down",
    )(hidden_units, total, gates, weights)


def partner(x, distance):
    return lax.ppermute(x, "dp", [(i, i ^ distance) for i in range(4)])


def ring_order(count):
    return list(range(0, count, 2)) + list(range(count - 1, 0, -2))


def around(x, step):
    ring = ring_order(lax.axis_size("expert"))
    count = len(ring)
    return lax.ppermute(x, "expert", [(ring[i], ring[(i + step) % count]) for i in range(count)])


def after(x, *others):
    return lax.optimization_barrier((x, *others))[0]


def add(a, b):
    return (a.astype(jnp.float32) + b.astype(jnp.float32)).astype(jnp.bfloat16)


def gather_rows(halves):
    reach = lax.axis_size("expert") // 2
    above, below = [halves], [halves]
    for _ in range(reach - 1):
        above.append([around(half, -1) for half in above[-1]])
        below.append([around(half, 1) for half in below[-1]])
    far = [around(above[-1][0], -1), around(below[-1][1], 1)]
    rows = [half for pair in (*above, far, *below[:0:-1]) for half in pair]
    return rows, [(*a, *b) for a, b in zip(above[1:], below[1:])] + [tuple(far)]


def scatter_sum(own, *blocks):
    reach = len(blocks) // 2
    terms = [own]
    for step, (far, first, second, *near) in ((1, blocks[:reach]), (-1, blocks[reach:])):
        moving = around(far, step)
        if step > 0:
            moving = jnp.concatenate([add(first, moving), second])
        else:
            moving = jnp.concatenate([first, add(second, moving)])
        for block in near:
            moving = add(block, around(moving, step))
        terms.append(around(moving, step))
    return terms


def relayed(x, rows):
    return [partner(x[i : i + rows], 1) for i in range(0, x.shape[0], rows)]


def every_expert(
    hidden_in,
    queries,
    key_pool,
    value_pool,
    page_table,
    prompt_lengths,
    expert_ids,
    gate_weights,
    norm_gain,
    trainer_gate_up,
    trainer_down,
):
    expert_count = lax.axis_size("expert")
    width = trainer_down.shape[2]
    depth, columns = trainer_gate_up.shape[1:]
    down_depth = trainer_down.shape[1]
    slab = width // SLABS
    early = queries.shape[1] // 4 * FIRST_BLOCKS
    side = [i * columns for i in range(FIRST_BLOCKS)]
    attn_own, attn_beside, first_sent, first_own = attention(
        queries,
        key_pool,
        value_pool,
        page_table,
        prompt_lengths,
        trainer_gate_up,
        FIRST_BLOCKS,
    )
    first_across = partner(first_sent, 2)
    rest_own, down_own = cast_rows(
        [after(trainer_gate_up, attn_own), trainer_down],
        [(early, depth - early, 0, columns), (0, down_depth, 0, width)],
    )
    attn_beside = partner(attn_beside, 1)
    attn_opposite = partner(first_across[:, -attn_own.shape[1] :], 1)
    rest_across = partner(rest_own, 2)
    resid, *halves = norm(
        after(hidden_in[0], rest_own),
        (attn_own, attn_beside, first_across, attn_opposite),
        norm_gain,
        expert_ids[0],
        gate_weights[0],
    )
    gathered, arrived = gather_rows(halves)
    first_beside = partner(after(first_own, *arrived[0]), 1)
    rest_beside = partner(after(rest_own, *arrived[0]), 1)
    first_ready = after(first_across, *arrived[0])
    first_opposite = [partner(first_ready[:, start : start + columns], 1) for start in side]
    down_beside = partner(after(down_own, *arrived[1]), 1)
    down_across = partner(after(down_own, *arrived[2]), 2)
    rest_opposite = relayed(after(rest_across, *arrived[3]), (depth - early) // 2)
    hidden_units, gates = expert_up(
        gathered,
        [(ref, 0) for ref in (first_own, rest_own, first_beside, rest_beside)]
        + [(first_across, start) for start in side]
        + [(ref, 0) for ref in (rest_across, *first_opposite, *rest_opposite)],
        columns,
    )
    down_ready = after(down_across, hidden_units)
    total = down_part(hidden_units, [down_own, down_beside, down_ready])
    mixed = []
    for first in range(0, width, slab):
        opposite = partner(down_ready[:, first : first + slab], 1)
        weighted = expert_down(hidden_units, total, gates, opposite, first, expert_count)
        sum_here = resid[:, first : first + slab].astype(jnp.float32)
        for term in scatter_sum(*weighted):
            sum_here = sum_here + term.astype(jnp.float32)
        mixed.append(sum_here.astype(jnp.bfloat16))
    return jnp.concatenate(mixed, axis=1)[None]


def solution(mesh):
    placed = (
        P("expert", "dp", None),
        P("expert", None, "dp"),
        P("expert", None, "dp"),
        P("expert", None, "dp"),
        P("expert", None),
        P("expert", None),
        P("expert", "dp", None),
        P("expert", "dp", None),
        P(),
        P("expert", "dp", None),
        P("expert", "dp", None),
    )
    dense = mesh.shape["expert"] == TOPK and mesh.shape["dp"] == 4
    return jax.shard_map(
        every_expert if dense else local, mesh=mesh, in_specs=placed, out_specs=P("expert", "dp", None), check_vma=False
    )
```

```python
import math

import jax
import jax.numpy as jnp
from jax import lax
from jax.experimental import pallas as pl
from jax.experimental.pallas import tpu as pltpu
from jax.sharding import PartitionSpec as P

HDIM = 128
TOPK = 8


epsilon = 1e-05


def fetch_weights(trainer_gate_up, trainer_down):
    return (
        lax.all_gather(trainer_gate_up.astype(jnp.bfloat16), "dp", axis=1, tiled=True),
        lax.all_gather(trainer_down.astype(jnp.bfloat16), "dp", axis=1, tiled=True),
    )


def local(
    hidden_in,
    queries,
    key_pool,
    value_pool,
    page_table,
    prompt_lengths,
    expert_ids,
    gate_weights,
    norm_gain,
    trainer_gate_up,
    trainer_down,
):
    col_tok = queries.shape[1]
    width_dev = queries.shape[2]
    heads_dev = width_dev // HDIM
    keys_all = jnp.take(key_pool, page_table[0], axis=0).reshape(col_tok, heads_dev, HDIM)
    values_all = jnp.take(value_pool, page_table[0], axis=0).reshape(col_tok, heads_dev, HDIM)
    request_ends = jnp.cumsum(prompt_lengths[0])
    positions = lax.iota(jnp.int32, col_tok)
    request = jnp.sum((positions[:, None] >= request_ends[None, :]).astype(jnp.int32), axis=1)
    block_rows = math.gcd(col_tok, 512)
    query_blocks = queries[0].reshape(col_tok // block_rows, block_rows, heads_dev, HDIM)
    request_blocks = request.reshape(col_tok // block_rows, block_rows)
    score_scale = 1.0 / math.sqrt(HDIM)

    def attend(pieces):
        query_block, request_block = pieces
        scores = (
            jnp.einsum("qhd,khd->hqk", query_block, keys_all, preferred_element_type=jnp.float32)
            * score_scale
        )
        same_request = (request_block[:, None] == request[None, :])[None]
        scores = jnp.where(same_request, scores, -1e30)
        highest = jnp.max(scores, axis=-1, keepdims=True)
        weights = jnp.where(same_request, jnp.exp(scores - highest), 0.0)
        totals = jnp.sum(weights, axis=-1, keepdims=True)
        probs = (weights / totals).astype(jnp.bfloat16)
        output = jnp.einsum("hqk,khd->qhd", probs, values_all, preferred_element_type=jnp.float32)
        return output.astype(jnp.bfloat16).reshape(block_rows, width_dev)

    attn_heads = lax.map(attend, (query_blocks, request_blocks)).reshape(1, col_tok, width_dev)
    attn_tokens = lax.all_to_all(attn_heads, "dp", split_axis=1, concat_axis=2, tiled=True)
    resid32 = (
        (hidden_in.astype(jnp.float32) + attn_tokens.astype(jnp.float32))
        .astype(jnp.bfloat16)
        .astype(jnp.float32)
    )
    mean_square = jnp.mean(resid32 * resid32, axis=-1, keepdims=True)
    normed = (resid32 * lax.rsqrt(mean_square + epsilon) * norm_gain).astype(jnp.bfloat16)
    server_gate_up, server_down = fetch_weights(trainer_gate_up, trainer_down)
    token_rows = normed.shape[1]
    width = normed.shape[2]
    expert_count = lax.axis_size("expert")
    capacity = min(token_rows, token_rows * TOPK * 5 // (4 * expert_count))
    hidden_size = server_gate_up.shape[2] // 2
    ids_flat = expert_ids[0].reshape(token_rows * TOPK)
    onehot = (ids_flat[:, None] == lax.iota(jnp.int32, expert_count)[None, :]).astype(jnp.int32)
    earlier = jnp.cumsum(onehot, axis=0) - onehot
    slot_index = jnp.sum(earlier * onehot, axis=1)
    flat_slot = ids_flat * capacity + slot_index
    placement = (
        flat_slot[:, None] == lax.iota(jnp.int32, expert_count * capacity)[None, :]
    ).astype(jnp.bfloat16)
    dispatch_matrix = jnp.sum(placement.reshape(token_rows, TOPK, expert_count * capacity), axis=1)
    outgoing = jnp.einsum(
        "ts,td->sd", dispatch_matrix, normed[0], preferred_element_type=jnp.float32
    )
    outgoing = outgoing.astype(jnp.bfloat16).reshape(expert_count, capacity, width)
    received = lax.all_to_all(outgoing, "expert", split_axis=0, concat_axis=0, tiled=True)
    sources, items, features = received.shape
    slot_rows = received.reshape(sources * items, features)
    gate_up = jnp.dot(slot_rows, server_gate_up[0], preferred_element_type=jnp.float32)
    hidden_units = (jax.nn.silu(gate_up[:, :hidden_size]) * gate_up[:, hidden_size:]).astype(
        jnp.bfloat16
    )
    outputs = jnp.dot(hidden_units, server_down[0], preferred_element_type=jnp.float32).astype(
        jnp.bfloat16
    )
    returned = lax.all_to_all(
        outputs.reshape(sources, items, features), "expert", split_axis=0, concat_axis=0, tiled=True
    )
    copies = jnp.take(returned.reshape(expert_count * capacity, width), flat_slot, axis=0)
    copies = copies.reshape(token_rows, TOPK, width).astype(jnp.float32)
    mixture = jnp.einsum("tk,tkd->td", gate_weights[0], copies)
    mixed = resid32[0] + mixture
    return mixed.astype(jnp.bfloat16)[None]

LANES = 128
VMEM_LIMIT = 32 * 2**20
VMEM_MOST = 60 * 2**20
CAST_STEPS = 4
FIRST_BLOCKS = 2
SLABS = 2
SMALL = pl.CostEstimate(flops=1, bytes_accessed=1, transcendentals=0)


def params(limit=VMEM_LIMIT):
    return pltpu.CompilerParams(vmem_limit_bytes=limit)


def vmem(count):
    return [pl.BlockSpec(memory_space=pltpu.VMEM)] * count


def attention_kernel(*refs):
    sources, outs, scratch = refs[:6], refs[6:10], refs[10:]
    own_ref, beside_ref, sent_ref, rows_ref = outs
    table, lengths, q_ref, k_ref, v_ref, weights, attn, arrived = scratch
    copies = [
        pltpu.make_async_copy(source, target, arrived.at[i])
        for i, (source, target) in enumerate(
            zip(
                (*sources[:2], sources[2].at[0], *sources[3:5]),
                (table, lengths, q_ref, k_ref, v_ref),
            )
        )
    ]
    rows = weights.shape[0]
    copies.append(
        pltpu.make_async_copy(sources[5].at[0, pl.ds(0, rows)], weights, arrived.at[5])
    )
    for copy in copies:
        copy.start()
    for copy in copies[:5]:
        copy.wait()
    tokens, width = q_ref.shape
    pages = k_ref.shape[0]
    row = lax.broadcasted_iota(jnp.int32, (tokens, tokens), 0)
    column = lax.broadcasted_iota(jnp.int32, (tokens, tokens), 1)
    row_request = jnp.zeros((tokens, tokens), jnp.int32)
    column_request = jnp.zeros((tokens, tokens), jnp.int32)
    end = jnp.int32(0)
    for r in range(lengths.shape[1]):
        end = end + lengths[0, r]
        row_request += (row >= end).astype(jnp.int32)
        column_request += (column >= end).astype(jnp.int32)
    same = row_request == column_request
    for h in range(width // HDIM):
        lanes = slice(h * HDIM, (h + 1) * HDIM)
        keys = jnp.concatenate([k_ref[table[0, p], :, lanes] for p in range(pages)], axis=0)
        values = jnp.concatenate([v_ref[table[0, p], :, lanes] for p in range(pages)], axis=0)
        scores = lax.dot_general(
            q_ref[:, lanes], keys, (((1,), (1,)), ((), ())), preferred_element_type=jnp.float32
        ) * (1.0 / math.sqrt(HDIM))
        scores = jnp.where(same, scores, -1e30)
        highest = jnp.max(scores, axis=-1, keepdims=True)
        weight = jnp.where(same, jnp.exp(scores - highest), 0.0)
        probs = (weight / jnp.sum(weight, axis=-1, keepdims=True)).astype(jnp.bfloat16)
        attn[:, lanes] = jnp.dot(probs, values, preferred_element_type=jnp.float32).astype(
            jnp.bfloat16
        )
    own = lax.axis_index("dp")
    block = tokens // 4
    split = weights.shape[1]
    end = sent_ref.shape[1]
    targets = (
        own_ref,
        beside_ref,
        sent_ref.at[:, end - 2 * width : end - width],
        sent_ref.at[:, end - width :],
    )
    for d, target in enumerate(targets):
        target[...] = attn[pl.ds(pl.multiple_of((own ^ d) * block, block), block), :]
    copies[5].wait()
    rows_ref[...] = weights[...].astype(jnp.bfloat16)
    for i in range(rows // block):
        here = slice(i * block, (i + 1) * block)
        sent_ref[:, i * split : (i + 1) * split] = rows_ref[here]


def attention(queries, key_pool, value_pool, page_table, prompt_lengths, gate_up, blocks):
    tokens, width = queries.shape[1:]
    split = gate_up.shape[2]
    block = tokens // 4
    shapes = [(block, width)] * 2
    shapes += [(block, blocks * split + 2 * width), (blocks * block, split)]
    return pl.pallas_call(
        attention_kernel,
        out_shape=[jax.ShapeDtypeStruct(shape, jnp.bfloat16) for shape in shapes],
        in_specs=[pl.BlockSpec(memory_space=pltpu.HBM)] * 6,
        out_specs=vmem(4),
        scratch_shapes=[
            pltpu.SMEM(page_table.shape, jnp.int32),
            pltpu.SMEM(prompt_lengths.shape, jnp.int32),
            pltpu.VMEM((tokens, width), jnp.bfloat16),
            pltpu.VMEM(key_pool.shape, jnp.bfloat16),
            pltpu.VMEM(value_pool.shape, jnp.bfloat16),
            pltpu.VMEM((blocks * block, split), jnp.float32),
            pltpu.VMEM((tokens, width), jnp.bfloat16),
            pltpu.SemaphoreType.DMA((6,)),
        ],
        compiler_params=params(VMEM_MOST),
        name="attention",
    )(page_table, prompt_lengths, queries, key_pool, value_pool, gate_up)


def norm_kernel(*refs):
    sources, outs, scratch = refs[:8], refs[8:11], refs[11:]
    a0, a1, a2, a3, hidden_ref, gain_ref, ids_ref, gates_ref, arrived = scratch
    resid_ref, row_refs = outs[0], outs[1:]
    across, block = sources[2], a2.shape[1]
    across = across.at[:, pl.ds(across.shape[1] - 2 * block, block)]
    copies = [
        pltpu.make_async_copy(source, target, arrived.at[i])
        for i, (source, target) in enumerate(zip((*sources[:2], across, *sources[3:]), scratch))
    ]
    for copy in copies:
        copy.start()
    for copy in copies:
        copy.wait()
    own = lax.axis_index("dp")
    tokens, width = hidden_ref.shape
    total = jnp.zeros((tokens, 1), jnp.float32)
    for d, attn in enumerate((a0, a1, a2, a3)):
        columns = pl.ds(pl.multiple_of((own ^ d) * block, block), block)
        resid = (
            hidden_ref[:, columns].astype(jnp.float32) + attn[...].astype(jnp.float32)
        ).astype(jnp.bfloat16)
        resid_ref[:, columns] = resid
        resid32 = resid.astype(jnp.float32)
        total += jnp.sum(resid32 * resid32, axis=-1, keepdims=True)
    inverse = lax.rsqrt(total / width + epsilon)
    halves = [slice(i * tokens // 2, (i + 1) * tokens // 2) for i in range(2)]
    for d in range(4):
        columns = pl.ds(pl.multiple_of((own ^ d) * block, block), block)
        normed = resid_ref[:, columns].astype(jnp.float32) * inverse * gain_ref[:, columns]
        for here, ref in zip(halves, row_refs):
            ref[:, d * block : (d + 1) * block] = normed[here].astype(jnp.bfloat16)
    place = lax.broadcasted_iota(jnp.int32, (LANES, tokens), 0)
    gates = jnp.zeros((LANES, tokens), jnp.float32)
    for k in range(TOPK):
        gates += jnp.where(ids_ref[k : k + 1] == place % TOPK, gates_ref[k : k + 1], 0.0)
    high = gates.astype(jnp.bfloat16).astype(jnp.float32)
    middle = (gates - high).astype(jnp.bfloat16).astype(jnp.float32)
    low = gates - high - middle
    part = place // TOPK
    terms = jnp.where(part == 0, high, jnp.where(part == 1, middle, jnp.where(part == 2, low, 0.0)))
    terms = jnp.transpose(terms)
    for here, ref in zip(halves, row_refs):
        ref[:, width:] = terms[here].astype(jnp.bfloat16)


def norm(hidden_in, attn, norm_gain, expert_ids, gate_weights):
    tokens, width = hidden_in.shape
    operands = hidden_in, norm_gain[None, :], expert_ids.T, gate_weights.T
    return pl.pallas_call(
        norm_kernel,
        out_shape=[
            jax.ShapeDtypeStruct((tokens, width), jnp.bfloat16),
        ]
        + [jax.ShapeDtypeStruct((tokens // 2, width + LANES), jnp.bfloat16)] * 2,
        in_specs=[pl.BlockSpec(memory_space=pl.ANY)] * 8,
        out_specs=vmem(3),
        scratch_shapes=[pltpu.VMEM(attn[0].shape, jnp.bfloat16)] * 4
        + [pltpu.VMEM(x.shape, x.dtype) for x in operands]
        + [pltpu.SemaphoreType.DMA((8,))],
        compiler_params=params(),
        cost_estimate=SMALL,
        name="norm",
    )(*attn, *operands)


def cast_kernel(spans, *refs):
    count = len(spans)
    sources, targets, scratch = refs[:count], refs[count : 2 * count], refs[2 * count :]
    wide, narrow, arrived, left = scratch[:count], scratch[count : 2 * count], *scratch[-2:]

    def rows_of(i, step, first=0):
        rows = wide[i].shape[0] // CAST_STEPS
        return pl.ds(first + step * rows, rows)

    def copies_in(step):
        for i, (first, _, column, columns) in enumerate(spans):
            yield pltpu.make_async_copy(
                sources[i].at[0, rows_of(i, step, first), pl.ds(column, columns)],
                wide[i].at[rows_of(i, step)],
                arrived.at[step, i],
            )

    def copies_out(step):
        for i in range(count):
            here = rows_of(i, step)
            yield pltpu.make_async_copy(narrow[i].at[here], targets[i].at[here], left.at[step, i])

    for step in range(CAST_STEPS):
        for copy in copies_in(step):
            copy.start()
    for step in range(CAST_STEPS):
        for copy in copies_in(step):
            copy.wait()
        for i in range(count):
            here = rows_of(i, step)
            narrow[i][here] = wide[i][here].astype(jnp.bfloat16)
        for copy in copies_out(step):
            copy.start()
    for step in range(CAST_STEPS):
        for copy in copies_out(step):
            copy.wait()


def cast_rows(arrays, spans):
    shapes = [(rows, columns) for _, rows, _, columns in spans]
    return pl.pallas_call(
        lambda *refs: cast_kernel(spans, *refs),
        out_shape=[jax.ShapeDtypeStruct(shape, jnp.bfloat16) for shape in shapes],
        in_specs=[pl.BlockSpec(memory_space=pltpu.HBM)] * len(arrays),
        out_specs=[pl.BlockSpec(memory_space=pltpu.HBM)] * len(arrays),
        scratch_shapes=[pltpu.VMEM(shape, jnp.float32) for shape in shapes]
        + [pltpu.VMEM(shape, jnp.bfloat16) for shape in shapes]
        + [pltpu.SemaphoreType.DMA((CAST_STEPS, len(arrays)))] * 2,
        compiler_params=params(VMEM_MOST),
        name="cast_rows",
    )(*arrays)


def load_tiles(pieces, starts, weights, arrived, tiles, block):
    def copies(tile):
        first = 0
        for index, (piece, start) in enumerate(zip(pieces, starts)):
            depth = piece.shape[0]
            for part in range(2):
                column = (part * tiles + tile) * block
                yield pltpu.make_async_copy(
                    piece.at[:, pl.ds(start + column, block)],
                    weights.at[pl.ds(first, depth), pl.ds(column, block)],
                    arrived.at[tile, index, part],
                )
            first += depth

    for tile in range(tiles):
        for copy in copies(tile):
            copy.start()

    def wait(tile):
        for copy in copies(tile):
            copy.wait()

    return wait


def up_kernel(sources, starts, *refs):
    pieces = len(starts)
    row_refs = refs[:sources]
    weight_refs = refs[sources : sources + pieces]
    hidden_ref, own_gate_ref, rows, weights, units, arrived = refs[sources + pieces :]
    width = rows.shape[1]
    tiles, _, block = units.shape
    wait = load_tiles(weight_refs, starts, weights, arrived, tiles, block)
    expert = lax.axis_index("expert")
    first = 0
    for ref in row_refs:
        count = ref.shape[0]
        here = slice(first, first + count)
        rows[here, :] = ref[:, :width]
        terms = ref[:, width:].astype(jnp.float32)
        lane = lax.broadcasted_iota(jnp.int32, terms.shape, 1)
        own_gate_ref[here, :] = jnp.sum(
            jnp.where(lane % TOPK == expert, terms, 0.0), axis=-1, keepdims=True
        )
        first += count
    for tile in range(tiles):
        wait(tile)
        gate, up = (
            jnp.dot(
                rows[...],
                weights[:, (part * tiles + tile) * block : (part * tiles + tile + 1) * block],
                preferred_element_type=jnp.float32,
            )
            for part in range(2)
        )
        units[tile] = (gate / (1.0 + jnp.exp(-gate)) * up).astype(jnp.bfloat16)
    own = lax.axis_index("dp")
    for d in range(4):
        hidden_ref[:, d * block : (d + 1) * block] = units[own ^ d]


def expert_up(rows, weights, width):
    weights, starts = zip(*weights)
    tokens = sum(piece.shape[0] for piece in rows)
    features = sum(piece.shape[0] for piece in weights)
    hidden_size = width // 2
    return pl.pallas_call(
        lambda *refs: up_kernel(len(rows), starts, *refs),
        out_shape=[
            jax.ShapeDtypeStruct((tokens, hidden_size), jnp.bfloat16),
            jax.ShapeDtypeStruct((tokens, 1), jnp.float32),
        ],
        in_specs=vmem(len(rows)) + [pl.BlockSpec(memory_space=pl.ANY)] * len(weights),
        out_specs=vmem(2),
        scratch_shapes=[
            pltpu.VMEM((tokens, features), jnp.bfloat16),
            pltpu.VMEM((features, width), jnp.bfloat16),
            pltpu.VMEM((4, tokens, hidden_size // 4), jnp.bfloat16),
            pltpu.SemaphoreType.DMA((4, len(weights), 2)),
        ],
        compiler_params=params(),
        cost_estimate=SMALL,
        name="expert_up",
    )(*rows, *weights)


def load_rows(pieces, weights, arrived):
    copies, first = [], 0
    for i, ref in enumerate(pieces):
        depth = ref.shape[0]
        copies.append(
            pltpu.make_async_copy(ref, weights.at[pl.ds(first, depth)], arrived.at[i])
        )
        first += depth
    for copy in copies:
        copy.start()
    for copy in copies:
        copy.wait()


def part_kernel(hidden_ref, *refs):
    pieces, (total_ref, weights, arrived) = refs[:-3], refs[-3:]
    load_rows(pieces, weights, arrived)
    total_ref[...] = jnp.dot(
        hidden_ref[:, : weights.shape[0]], weights[...], preferred_element_type=jnp.float32
    )


def down_part(hidden_units, weights):
    depth = sum(piece.shape[0] for piece in weights)
    shape = hidden_units.shape[0], weights[0].shape[1]
    return pl.pallas_call(
        part_kernel,
        out_shape=jax.ShapeDtypeStruct(shape, jnp.float32),
        in_specs=vmem(1) + [pl.BlockSpec(memory_space=pl.ANY)] * len(weights),
        out_specs=pl.BlockSpec(memory_space=pltpu.VMEM),
        scratch_shapes=[
            pltpu.VMEM((depth, shape[1]), jnp.bfloat16),
            pltpu.SemaphoreType.DMA((len(weights),)),
        ],
        compiler_params=params(),
        cost_estimate=SMALL,
        name="down_part",
    )(hidden_units, *weights)


def down_kernel(first, column, sources, hidden_ref, total_ref, gate_ref, piece, *refs):
    outs, (weights, arrived) = refs[:-2], refs[-2:]
    load_rows([piece], weights, arrived)
    depth, width = weights.shape
    units = hidden_ref[:, first : first + depth]
    total = total_ref[:, column : column + width] + jnp.dot(
        units, weights[...], preferred_element_type=jnp.float32
    )
    weighted = (total * gate_ref[...]).astype(jnp.bfloat16)
    rows = weighted.shape[0] // sources
    for (first, count), ref in zip(down_blocks(rows, sources), outs):
        ref[...] = weighted[first : first + count]


def down_blocks(rows, sources):
    half, reach = rows // 2, sources // 2
    blocks = [(0, rows)]
    for step, middle in ((-1, reach * rows), (1, reach * rows + half)):
        blocks.append((middle, half))
        second = (reach + step) * rows
        blocks += [(second, half), (second + half, half)]
        blocks += [((reach + step * away) * rows, rows) for away in range(2, reach)]
    return blocks


def expert_down(hidden_units, total, gates, weights, column, sources):
    tokens, hidden_size = hidden_units.shape
    depth, width = weights.shape
    rows = tokens // sources
    return pl.pallas_call(
        lambda *refs: down_kernel(hidden_size - depth, column, sources, *refs),
        out_shape=[
            jax.ShapeDtypeStruct((count, width), jnp.bfloat16)
            for _, count in down_blocks(rows, sources)
        ],
        in_specs=vmem(3) + [pl.BlockSpec(memory_space=pl.ANY)],
        out_specs=vmem(sources + 3),
        scratch_shapes=[
            pltpu.VMEM((depth, width), jnp.bfloat16),
            pltpu.SemaphoreType.DMA((1,)),
        ],
        compiler_params=params(),
        cost_estimate=SMALL,
        name="expert_down",
    )(hidden_units, total, gates, weights)


def partner(x, distance):
    return lax.ppermute(x, "dp", [(i, i ^ distance) for i in range(4)])


def ring_order(count):
    return list(range(0, count, 2)) + list(range(count - 1, 0, -2))


def around(x, step):
    ring = ring_order(lax.axis_size("expert"))
    count = len(ring)
    return lax.ppermute(x, "expert", [(ring[i], ring[(i + step) % count]) for i in range(count)])


def after(x, *others):
    return lax.optimization_barrier((x, *others))[0]


def add(a, b):
    return (a.astype(jnp.float32) + b.astype(jnp.float32)).astype(jnp.bfloat16)


def gather_rows(halves):
    reach = lax.axis_size("expert") // 2
    above, below = [halves], [halves]
    for _ in range(reach - 1):
        above.append([around(half, -1) for half in above[-1]])
        below.append([around(half, 1) for half in below[-1]])
    far = [around(above[-1][0], -1), around(below[-1][1], 1)]
    rows = [half for pair in (*above, far, *below[:0:-1]) for half in pair]
    return rows, [(*a, *b) for a, b in zip(above[1:], below[1:])] + [tuple(far)]


def scatter_sum(own, *blocks):
    reach = len(blocks) // 2
    terms = [own]
    for step, (far, first, second, *near) in ((1, blocks[:reach]), (-1, blocks[reach:])):
        moving = around(far, step)
        if step > 0:
            moving = jnp.concatenate([add(first, moving), second])
        else:
            moving = jnp.concatenate([first, add(second, moving)])
        for block in near:
            moving = add(block, around(moving, step))
        terms.append(around(moving, step))
    return terms


def relayed(x, rows):
    return [partner(x[i : i + rows], 1) for i in range(0, x.shape[0], rows)]


def every_expert(
    hidden_in,
    queries,
    key_pool,
    value_pool,
    page_table,
    prompt_lengths,
    expert_ids,
    gate_weights,
    norm_gain,
    trainer_gate_up,
    trainer_down,
):
    expert_count = lax.axis_size("expert")
    width = trainer_down.shape[2]
    depth, columns = trainer_gate_up.shape[1:]
    down_depth = trainer_down.shape[1]
    slab = width // SLABS
    early = queries.shape[1] // 4 * FIRST_BLOCKS
    side = [i * columns for i in range(FIRST_BLOCKS)]
    attn_own, attn_beside, first_sent, first_own = attention(
        queries,
        key_pool,
        value_pool,
        page_table,
        prompt_lengths,
        trainer_gate_up,
        FIRST_BLOCKS,
    )
    first_across = partner(first_sent, 2)
    rest_own, down_own = cast_rows(
        [after(trainer_gate_up, attn_own), trainer_down],
        [(early, depth - early, 0, columns), (0, down_depth, 0, width)],
    )
    attn_beside = partner(attn_beside, 1)
    attn_opposite = partner(first_across[:, -attn_own.shape[1] :], 1)
    rest_across = partner(rest_own, 2)
    resid, *halves = norm(
        after(hidden_in[0], rest_own),
        (attn_own, attn_beside, first_across, attn_opposite),
        norm_gain,
        expert_ids[0],
        gate_weights[0],
    )
    gathered, arrived = gather_rows(halves)
    first_beside = partner(after(first_own, *arrived[0]), 1)
    rest_beside = partner(after(rest_own, *arrived[0]), 1)
    first_ready = after(first_across, *arrived[0])
    first_opposite = [partner(first_ready[:, start : start + columns], 1) for start in side]
    down_beside = partner(after(down_own, *arrived[1]), 1)
    down_across = partner(after(down_own, *arrived[2]), 2)
    rest_opposite = relayed(after(rest_across, *arrived[3]), (depth - early) // 2)
    hidden_units, gates = expert_up(
        gathered,
        [(ref, 0) for ref in (first_own, rest_own, first_beside, rest_beside)]
        + [(first_across, start) for start in side]
        + [(ref, 0) for ref in (rest_across, *first_opposite, *rest_opposite)],
        columns,
    )
    down_ready = after(down_across, hidden_units)
    total = down_part(hidden_units, [down_own, down_beside, down_ready])
    mixed = []
    for first in range(0, width, slab):
        opposite = partner(down_ready[:, first : first + slab], 1)
        weighted = expert_down(hidden_units, total, gates, opposite, first, expert_count)
        sum_here = resid[:, first : first + slab].astype(jnp.float32)
        for term in scatter_sum(*weighted):
            sum_here = sum_here + term.astype(jnp.float32)
        mixed.append(sum_here.astype(jnp.bfloat16))
    return jnp.concatenate(mixed, axis=1)[None]


def solution(mesh):
    placed = (
        P("expert", "dp", None),
        P("expert", None, "dp"),
        P("expert", None, "dp"),
        P("expert", None, "dp"),
        P("expert", None),
        P("expert", None),
        P("expert", "dp", None),
        P("expert", "dp", None),
        P(),
        P("expert", "dp", None),
        P("expert", "dp", None),
    )
    dense = mesh.shape["expert"] == TOPK and mesh.shape["dp"] == 4
    return jax.shard_map(
        every_expert if dense else local, mesh=mesh, in_specs=placed, out_specs=P("expert", "dp", None), check_vma=False
    )
```

```python
import math

import jax
import jax.numpy as jnp
from jax import lax
from jax.experimental import pallas as pl
from jax.experimental.pallas import tpu as pltpu
from jax.sharding import PartitionSpec as P

HDIM = 128
TOPK = 8


epsilon = 1e-05


def fetch_weights(trainer_gate_up, trainer_down):
    return (
        lax.all_gather(trainer_gate_up.astype(jnp.bfloat16), "dp", axis=1, tiled=True),
        lax.all_gather(trainer_down.astype(jnp.bfloat16), "dp", axis=1, tiled=True),
    )


def local(
    hidden_in,
    queries,
    key_pool,
    value_pool,
    page_table,
    prompt_lengths,
    expert_ids,
    gate_weights,
    norm_gain,
    trainer_gate_up,
    trainer_down,
):
    col_tok = queries.shape[1]
    width_dev = queries.shape[2]
    heads_dev = width_dev // HDIM
    keys_all = jnp.take(key_pool, page_table[0], axis=0).reshape(col_tok, heads_dev, HDIM)
    values_all = jnp.take(value_pool, page_table[0], axis=0).reshape(col_tok, heads_dev, HDIM)
    request_ends = jnp.cumsum(prompt_lengths[0])
    positions = lax.iota(jnp.int32, col_tok)
    request = jnp.sum((positions[:, None] >= request_ends[None, :]).astype(jnp.int32), axis=1)
    block_rows = math.gcd(col_tok, 512)
    query_blocks = queries[0].reshape(col_tok // block_rows, block_rows, heads_dev, HDIM)
    request_blocks = request.reshape(col_tok // block_rows, block_rows)
    score_scale = 1.0 / math.sqrt(HDIM)

    def attend(pieces):
        query_block, request_block = pieces
        scores = (
            jnp.einsum("qhd,khd->hqk", query_block, keys_all, preferred_element_type=jnp.float32)
            * score_scale
        )
        same_request = (request_block[:, None] == request[None, :])[None]
        scores = jnp.where(same_request, scores, -1e30)
        highest = jnp.max(scores, axis=-1, keepdims=True)
        weights = jnp.where(same_request, jnp.exp(scores - highest), 0.0)
        totals = jnp.sum(weights, axis=-1, keepdims=True)
        probs = (weights / totals).astype(jnp.bfloat16)
        output = jnp.einsum("hqk,khd->qhd", probs, values_all, preferred_element_type=jnp.float32)
        return output.astype(jnp.bfloat16).reshape(block_rows, width_dev)

    attn_heads = lax.map(attend, (query_blocks, request_blocks)).reshape(1, col_tok, width_dev)
    attn_tokens = lax.all_to_all(attn_heads, "dp", split_axis=1, concat_axis=2, tiled=True)
    resid32 = (
        (hidden_in.astype(jnp.float32) + attn_tokens.astype(jnp.float32))
        .astype(jnp.bfloat16)
        .astype(jnp.float32)
    )
    mean_square = jnp.mean(resid32 * resid32, axis=-1, keepdims=True)
    normed = (resid32 * lax.rsqrt(mean_square + epsilon) * norm_gain).astype(jnp.bfloat16)
    server_gate_up, server_down = fetch_weights(trainer_gate_up, trainer_down)
    token_rows = normed.shape[1]
    width = normed.shape[2]
    expert_count = lax.axis_size("expert")
    capacity = min(token_rows, token_rows * TOPK * 5 // (4 * expert_count))
    hidden_size = server_gate_up.shape[2] // 2
    ids_flat = expert_ids[0].reshape(token_rows * TOPK)
    onehot = (ids_flat[:, None] == lax.iota(jnp.int32, expert_count)[None, :]).astype(jnp.int32)
    earlier = jnp.cumsum(onehot, axis=0) - onehot
    slot_index = jnp.sum(earlier * onehot, axis=1)
    flat_slot = ids_flat * capacity + slot_index
    placement = (
        flat_slot[:, None] == lax.iota(jnp.int32, expert_count * capacity)[None, :]
    ).astype(jnp.bfloat16)
    dispatch_matrix = jnp.sum(placement.reshape(token_rows, TOPK, expert_count * capacity), axis=1)
    outgoing = jnp.einsum(
        "ts,td->sd", dispatch_matrix, normed[0], preferred_element_type=jnp.float32
    )
    outgoing = outgoing.astype(jnp.bfloat16).reshape(expert_count, capacity, width)
    received = lax.all_to_all(outgoing, "expert", split_axis=0, concat_axis=0, tiled=True)
    sources, items, features = received.shape
    slot_rows = received.reshape(sources * items, features)
    gate_up = jnp.dot(slot_rows, server_gate_up[0], preferred_element_type=jnp.float32)
    hidden_units = (jax.nn.silu(gate_up[:, :hidden_size]) * gate_up[:, hidden_size:]).astype(
        jnp.bfloat16
    )
    outputs = jnp.dot(hidden_units, server_down[0], preferred_element_type=jnp.float32).astype(
        jnp.bfloat16
    )
    returned = lax.all_to_all(
        outputs.reshape(sources, items, features), "expert", split_axis=0, concat_axis=0, tiled=True
    )
    copies = jnp.take(returned.reshape(expert_count * capacity, width), flat_slot, axis=0)
    copies = copies.reshape(token_rows, TOPK, width).astype(jnp.float32)
    mixture = jnp.einsum("tk,tkd->td", gate_weights[0], copies)
    mixed = resid32[0] + mixture
    return mixed.astype(jnp.bfloat16)[None]

LANES = 128
VMEM_LIMIT = 32 * 2**20
VMEM_MOST = 60 * 2**20
CAST_STEPS = 4
FIRST_BLOCKS = 2
SLABS = 2
SMALL = pl.CostEstimate(flops=1, bytes_accessed=1, transcendentals=0)


def params(limit=VMEM_LIMIT):
    return pltpu.CompilerParams(vmem_limit_bytes=limit)


def vmem(count):
    return [pl.BlockSpec(memory_space=pltpu.VMEM)] * count


def attention_kernel(*refs):
    sources, outs, scratch = refs[:6], refs[6:10], refs[10:]
    own_ref, beside_ref, sent_ref, rows_ref = outs
    table, lengths, q_ref, k_ref, v_ref, weights, attn, arrived = scratch
    copies = [
        pltpu.make_async_copy(source, target, arrived.at[i])
        for i, (source, target) in enumerate(
            zip(
                (*sources[:2], sources[2].at[0], *sources[3:5]),
                (table, lengths, q_ref, k_ref, v_ref),
            )
        )
    ]
    rows = weights.shape[0]
    copies.append(
        pltpu.make_async_copy(sources[5].at[0, pl.ds(0, rows)], weights, arrived.at[5])
    )
    for copy in copies:
        copy.start()
    for copy in copies[:5]:
        copy.wait()
    tokens, width = q_ref.shape
    pages = k_ref.shape[0]
    row = lax.broadcasted_iota(jnp.int32, (tokens, 1), 0)
    column = lax.broadcasted_iota(jnp.int32, (1, tokens), 1)
    row_request = jnp.zeros((tokens, 1), jnp.int32)
    column_request = jnp.zeros((1, tokens), jnp.int32)
    end = jnp.int32(0)
    for r in range(lengths.shape[1]):
        end = end + lengths[0, r]
        row_request += (row >= end).astype(jnp.int32)
        column_request += (column >= end).astype(jnp.int32)
    same = row_request == column_request
    for h in range(width // HDIM):
        lanes = slice(h * HDIM, (h + 1) * HDIM)
        keys = jnp.concatenate([k_ref[table[0, p], :, lanes] for p in range(pages)], axis=0)
        values = jnp.concatenate([v_ref[table[0, p], :, lanes] for p in range(pages)], axis=0)
        scores = lax.dot_general(
            q_ref[:, lanes], keys, (((1,), (1,)), ((), ())), preferred_element_type=jnp.float32
        ) * (1.0 / math.sqrt(HDIM))
        scores = jnp.where(same, scores, -1e30)
        highest = jnp.max(scores, axis=-1, keepdims=True)
        weight = jnp.exp(scores - highest)
        share = 1.0 / jnp.sum(weight, axis=-1, keepdims=True)
        probs = (weight * share).astype(jnp.bfloat16)
        attn[:, lanes] = jnp.dot(probs, values, preferred_element_type=jnp.float32).astype(
            jnp.bfloat16
        )
    own = lax.axis_index("dp")
    block = tokens // 4
    split = weights.shape[1]
    end = sent_ref.shape[1]
    targets = (
        own_ref,
        beside_ref,
        sent_ref.at[:, end - 2 * width : end - width],
        sent_ref.at[:, end - width :],
    )
    for d, target in enumerate(targets):
        target[...] = attn[pl.ds(pl.multiple_of((own ^ d) * block, block), block), :]
    copies[5].wait()
    rows_ref[...] = weights[...].astype(jnp.bfloat16)
    for i in range(rows // block):
        here = slice(i * block, (i + 1) * block)
        sent_ref[:, i * split : (i + 1) * split] = rows_ref[here]


def attention(queries, key_pool, value_pool, page_table, prompt_lengths, gate_up, blocks):
    tokens, width = queries.shape[1:]
    split = gate_up.shape[2]
    block = tokens // 4
    shapes = [(block, width)] * 2
    shapes += [(block, blocks * split + 2 * width), (blocks * block, split)]
    return pl.pallas_call(
        attention_kernel,
        out_shape=[jax.ShapeDtypeStruct(shape, jnp.bfloat16) for shape in shapes],
        in_specs=[pl.BlockSpec(memory_space=pltpu.HBM)] * 6,
        out_specs=vmem(4),
        scratch_shapes=[
            pltpu.SMEM(page_table.shape, jnp.int32),
            pltpu.SMEM(prompt_lengths.shape, jnp.int32),
            pltpu.VMEM((tokens, width), jnp.bfloat16),
            pltpu.VMEM(key_pool.shape, jnp.bfloat16),
            pltpu.VMEM(value_pool.shape, jnp.bfloat16),
            pltpu.VMEM((blocks * block, split), jnp.float32),
            pltpu.VMEM((tokens, width), jnp.bfloat16),
            pltpu.SemaphoreType.DMA((6,)),
        ],
        compiler_params=params(VMEM_MOST),
        name="attention",
    )(page_table, prompt_lengths, queries, key_pool, value_pool, gate_up)


def norm_kernel(*refs):
    sources, outs, scratch = refs[:8], refs[8:11], refs[11:]
    a0, a1, a2, a3, hidden_ref, gain_ref, ids_ref, gates_ref, arrived = scratch
    resid_ref, row_refs = outs[0], outs[1:]
    across, block = sources[2], a2.shape[1]
    across = across.at[:, pl.ds(across.shape[1] - 2 * block, block)]
    copies = [
        pltpu.make_async_copy(source, target, arrived.at[i])
        for i, (source, target) in enumerate(zip((*sources[:2], across, *sources[3:]), scratch))
    ]
    for copy in copies:
        copy.start()
    for copy in copies:
        copy.wait()
    own = lax.axis_index("dp")
    tokens, width = hidden_ref.shape
    total = jnp.zeros((tokens, 1), jnp.float32)
    for d, attn in enumerate((a0, a1, a2, a3)):
        columns = pl.ds(pl.multiple_of((own ^ d) * block, block), block)
        resid = (
            hidden_ref[:, columns].astype(jnp.float32) + attn[...].astype(jnp.float32)
        ).astype(jnp.bfloat16)
        resid_ref[:, columns] = resid
        resid32 = resid.astype(jnp.float32)
        total += jnp.sum(resid32 * resid32, axis=-1, keepdims=True)
    inverse = lax.rsqrt(total / width + epsilon)
    halves = [slice(i * tokens // 2, (i + 1) * tokens // 2) for i in range(2)]
    for d in range(4):
        columns = pl.ds(pl.multiple_of((own ^ d) * block, block), block)
        normed = resid_ref[:, columns].astype(jnp.float32) * inverse * gain_ref[:, columns]
        for here, ref in zip(halves, row_refs):
            ref[:, d * block : (d + 1) * block] = normed[here].astype(jnp.bfloat16)
    place = lax.broadcasted_iota(jnp.int32, (LANES, tokens), 0)
    gates = jnp.zeros((LANES, tokens), jnp.float32)
    for k in range(TOPK):
        gates += jnp.where(ids_ref[k : k + 1] == place % TOPK, gates_ref[k : k + 1], 0.0)
    high = gates.astype(jnp.bfloat16).astype(jnp.float32)
    middle = (gates - high).astype(jnp.bfloat16).astype(jnp.float32)
    low = gates - high - middle
    part = place // TOPK
    terms = jnp.where(part == 0, high, jnp.where(part == 1, middle, jnp.where(part == 2, low, 0.0)))
    terms = jnp.transpose(terms)
    for here, ref in zip(halves, row_refs):
        ref[:, width:] = terms[here].astype(jnp.bfloat16)


def norm(hidden_in, attn, norm_gain, expert_ids, gate_weights):
    tokens, width = hidden_in.shape
    operands = hidden_in, norm_gain[None, :], expert_ids.T, gate_weights.T
    return pl.pallas_call(
        norm_kernel,
        out_shape=[
            jax.ShapeDtypeStruct((tokens, width), jnp.bfloat16),
        ]
        + [jax.ShapeDtypeStruct((tokens // 2, width + LANES), jnp.bfloat16)] * 2,
        in_specs=[pl.BlockSpec(memory_space=pl.ANY)] * 8,
        out_specs=vmem(3),
        scratch_shapes=[pltpu.VMEM(attn[0].shape, jnp.bfloat16)] * 4
        + [pltpu.VMEM(x.shape, x.dtype) for x in operands]
        + [pltpu.SemaphoreType.DMA((8,))],
        compiler_params=params(),
        cost_estimate=SMALL,
        name="norm",
    )(*attn, *operands)


def cast_kernel(spans, *refs):
    count = len(spans)
    sources, targets, scratch = refs[:count], refs[count : 2 * count], refs[2 * count :]
    wide, narrow, arrived, left = scratch[:count], scratch[count : 2 * count], *scratch[-2:]

    def rows_of(i, step, first=0):
        rows = wide[i].shape[0] // CAST_STEPS
        return pl.ds(first + step * rows, rows)

    def copies_in(step):
        for i, (first, _, column, columns) in enumerate(spans):
            yield pltpu.make_async_copy(
                sources[i].at[0, rows_of(i, step, first), pl.ds(column, columns)],
                wide[i].at[rows_of(i, step)],
                arrived.at[step, i],
            )

    def copies_out(step):
        for i in range(count):
            here = rows_of(i, step)
            yield pltpu.make_async_copy(narrow[i].at[here], targets[i].at[here], left.at[step, i])

    for step in range(CAST_STEPS):
        for copy in copies_in(step):
            copy.start()
    for step in range(CAST_STEPS):
        for copy in copies_in(step):
            copy.wait()
        for i in range(count):
            here = rows_of(i, step)
            narrow[i][here] = wide[i][here].astype(jnp.bfloat16)
        for copy in copies_out(step):
            copy.start()
    for step in range(CAST_STEPS):
        for copy in copies_out(step):
            copy.wait()


def cast_rows(arrays, spans):
    shapes = [(rows, columns) for _, rows, _, columns in spans]
    return pl.pallas_call(
        lambda *refs: cast_kernel(spans, *refs),
        out_shape=[jax.ShapeDtypeStruct(shape, jnp.bfloat16) for shape in shapes],
        in_specs=[pl.BlockSpec(memory_space=pltpu.HBM)] * len(arrays),
        out_specs=[pl.BlockSpec(memory_space=pltpu.HBM)] * len(arrays),
        scratch_shapes=[pltpu.VMEM(shape, jnp.float32) for shape in shapes]
        + [pltpu.VMEM(shape, jnp.bfloat16) for shape in shapes]
        + [pltpu.SemaphoreType.DMA((CAST_STEPS, len(arrays)))] * 2,
        compiler_params=params(VMEM_MOST),
        name="cast_rows",
    )(*arrays)


def load_tiles(pieces, starts, weights, arrived, tiles, block):
    def copies(tile):
        first = 0
        for index, (piece, start) in enumerate(zip(pieces, starts)):
            depth = piece.shape[0]
            for part in range(2):
                column = (part * tiles + tile) * block
                yield pltpu.make_async_copy(
                    piece.at[:, pl.ds(start + column, block)],
                    weights.at[pl.ds(first, depth), pl.ds(column, block)],
                    arrived.at[tile, index, part],
                )
            first += depth

    for tile in range(tiles):
        for copy in copies(tile):
            copy.start()

    def wait(tile):
        for copy in copies(tile):
            copy.wait()

    return wait


def up_kernel(sources, starts, *refs):
    pieces = len(starts)
    row_refs = refs[:sources]
    weight_refs = refs[sources : sources + pieces]
    hidden_ref, own_gate_ref, rows, weights, units, arrived = refs[sources + pieces :]
    width = rows.shape[1]
    tiles, _, block = units.shape
    wait = load_tiles(weight_refs, starts, weights, arrived, tiles, block)
    expert = lax.axis_index("expert")
    first = 0
    for ref in row_refs:
        count = ref.shape[0]
        here = slice(first, first + count)
        rows[here, :] = ref[:, :width]
        terms = ref[:, width:].astype(jnp.float32)
        lane = lax.broadcasted_iota(jnp.int32, terms.shape, 1)
        own_gate_ref[here, :] = jnp.sum(
            jnp.where(lane % TOPK == expert, terms, 0.0), axis=-1, keepdims=True
        )
        first += count
    for tile in range(tiles):
        wait(tile)
        gate, up = (
            jnp.dot(
                rows[...],
                weights[:, (part * tiles + tile) * block : (part * tiles + tile + 1) * block],
                preferred_element_type=jnp.float32,
            )
            for part in range(2)
        )
        units[tile] = (gate / (1.0 + jnp.exp(-gate)) * up).astype(jnp.bfloat16)
    own = lax.axis_index("dp")
    for d in range(4):
        hidden_ref[:, d * block : (d + 1) * block] = units[own ^ d]


def expert_up(rows, weights, width):
    weights, starts = zip(*weights)
    tokens = sum(piece.shape[0] for piece in rows)
    features = sum(piece.shape[0] for piece in weights)
    hidden_size = width // 2
    return pl.pallas_call(
        lambda *refs: up_kernel(len(rows), starts, *refs),
        out_shape=[
            jax.ShapeDtypeStruct((tokens, hidden_size), jnp.bfloat16),
            jax.ShapeDtypeStruct((tokens, 1), jnp.float32),
        ],
        in_specs=vmem(len(rows)) + [pl.BlockSpec(memory_space=pl.ANY)] * len(weights),
        out_specs=vmem(2),
        scratch_shapes=[
            pltpu.VMEM((tokens, features), jnp.bfloat16),
            pltpu.VMEM((features, width), jnp.bfloat16),
            pltpu.VMEM((4, tokens, hidden_size // 4), jnp.bfloat16),
            pltpu.SemaphoreType.DMA((4, len(weights), 2)),
        ],
        compiler_params=params(),
        cost_estimate=SMALL,
        name="expert_up",
    )(*rows, *weights)


def load_rows(pieces, weights, arrived):
    copies, first = [], 0
    for i, ref in enumerate(pieces):
        depth = ref.shape[0]
        copies.append(
            pltpu.make_async_copy(ref, weights.at[pl.ds(first, depth)], arrived.at[i])
        )
        first += depth
    for copy in copies:
        copy.start()
    for copy in copies:
        copy.wait()


def part_kernel(hidden_ref, *refs):
    pieces, (total_ref, weights, arrived) = refs[:-3], refs[-3:]
    load_rows(pieces, weights, arrived)
    total_ref[...] = jnp.dot(
        hidden_ref[:, : weights.shape[0]], weights[...], preferred_element_type=jnp.float32
    )


def down_part(hidden_units, weights):
    depth = sum(piece.shape[0] for piece in weights)
    shape = hidden_units.shape[0], weights[0].shape[1]
    return pl.pallas_call(
        part_kernel,
        out_shape=jax.ShapeDtypeStruct(shape, jnp.float32),
        in_specs=vmem(1) + [pl.BlockSpec(memory_space=pl.ANY)] * len(weights),
        out_specs=pl.BlockSpec(memory_space=pltpu.VMEM),
        scratch_shapes=[
            pltpu.VMEM((depth, shape[1]), jnp.bfloat16),
            pltpu.SemaphoreType.DMA((len(weights),)),
        ],
        compiler_params=params(),
        cost_estimate=SMALL,
        name="down_part",
    )(hidden_units, *weights)


def down_kernel(first, column, sources, hidden_ref, total_ref, gate_ref, piece, *refs):
    outs, (weights, arrived) = refs[:-2], refs[-2:]
    load_rows([piece], weights, arrived)
    depth, width = weights.shape
    units = hidden_ref[:, first : first + depth]
    total = total_ref[:, column : column + width] + jnp.dot(
        units, weights[...], preferred_element_type=jnp.float32
    )
    weighted = (total * gate_ref[...]).astype(jnp.bfloat16)
    rows = weighted.shape[0] // sources
    for (first, count), ref in zip(down_blocks(rows, sources), outs):
        ref[...] = weighted[first : first + count]


def down_blocks(rows, sources):
    half, reach = rows // 2, sources // 2
    blocks = [(0, rows)]
    for step, middle in ((-1, reach * rows), (1, reach * rows + half)):
        blocks.append((middle, half))
        second = (reach + step) * rows
        blocks += [(second, half), (second + half, half)]
        blocks += [((reach + step * away) * rows, rows) for away in range(2, reach)]
    return blocks


def expert_down(hidden_units, total, gates, weights, column, sources):
    tokens, hidden_size = hidden_units.shape
    depth, width = weights.shape
    rows = tokens // sources
    return pl.pallas_call(
        lambda *refs: down_kernel(hidden_size - depth, column, sources, *refs),
        out_shape=[
            jax.ShapeDtypeStruct((count, width), jnp.bfloat16)
            for _, count in down_blocks(rows, sources)
        ],
        in_specs=vmem(3) + [pl.BlockSpec(memory_space=pl.ANY)],
        out_specs=vmem(sources + 3),
        scratch_shapes=[
            pltpu.VMEM((depth, width), jnp.bfloat16),
            pltpu.SemaphoreType.DMA((1,)),
        ],
        compiler_params=params(),
        cost_estimate=SMALL,
        name="expert_down",
    )(hidden_units, total, gates, weights)


def partner(x, distance):
    return lax.ppermute(x, "dp", [(i, i ^ distance) for i in range(4)])


def ring_order(count):
    return list(range(0, count, 2)) + list(range(count - 1, 0, -2))


def around(x, step):
    ring = ring_order(lax.axis_size("expert"))
    count = len(ring)
    return lax.ppermute(x, "expert", [(ring[i], ring[(i + step) % count]) for i in range(count)])


def after(x, *others):
    return lax.optimization_barrier((x, *others))[0]


def add(a, b):
    return (a.astype(jnp.float32) + b.astype(jnp.float32)).astype(jnp.bfloat16)


def gather_rows(halves):
    reach = lax.axis_size("expert") // 2
    above, below = [halves], [halves]
    for _ in range(reach - 1):
        above.append([around(half, -1) for half in above[-1]])
        below.append([around(half, 1) for half in below[-1]])
    far = [around(above[-1][0], -1), around(below[-1][1], 1)]
    rows = [half for pair in (*above, far, *below[:0:-1]) for half in pair]
    return rows, [(*a, *b) for a, b in zip(above[1:], below[1:])] + [tuple(far)]


def scatter_sum(own, *blocks):
    reach = len(blocks) // 2
    terms = [own]
    for step, (far, first, second, *near) in ((1, blocks[:reach]), (-1, blocks[reach:])):
        moving = around(far, step)
        if step > 0:
            moving = jnp.concatenate([add(first, moving), second])
        else:
            moving = jnp.concatenate([first, add(second, moving)])
        for block in near:
            moving = add(block, around(moving, step))
        terms.append(around(moving, step))
    return terms


def relayed(x, rows):
    return [partner(x[i : i + rows], 1) for i in range(0, x.shape[0], rows)]


def every_expert(
    hidden_in,
    queries,
    key_pool,
    value_pool,
    page_table,
    prompt_lengths,
    expert_ids,
    gate_weights,
    norm_gain,
    trainer_gate_up,
    trainer_down,
):
    expert_count = lax.axis_size("expert")
    width = trainer_down.shape[2]
    depth, columns = trainer_gate_up.shape[1:]
    down_depth = trainer_down.shape[1]
    slab = width // SLABS
    early = queries.shape[1] // 4 * FIRST_BLOCKS
    side = [i * columns for i in range(FIRST_BLOCKS)]
    attn_own, attn_beside, first_sent, first_own = attention(
        queries,
        key_pool,
        value_pool,
        page_table,
        prompt_lengths,
        trainer_gate_up,
        FIRST_BLOCKS,
    )
    first_across = partner(first_sent, 2)
    rest_own, down_own = cast_rows(
        [after(trainer_gate_up, attn_own), trainer_down],
        [(early, depth - early, 0, columns), (0, down_depth, 0, width)],
    )
    attn_beside = partner(attn_beside, 1)
    attn_opposite = partner(first_across[:, -attn_own.shape[1] :], 1)
    rest_across = partner(rest_own, 2)
    resid, *halves = norm(
        after(hidden_in[0], rest_own),
        (attn_own, attn_beside, first_across, attn_opposite),
        norm_gain,
        expert_ids[0],
        gate_weights[0],
    )
    gathered, arrived = gather_rows(halves)
    first_beside = partner(after(first_own, *arrived[0]), 1)
    rest_beside = partner(after(rest_own, *arrived[0]), 1)
    first_ready = after(first_across, *arrived[0])
    first_opposite = [partner(first_ready[:, start : start + columns], 1) for start in side]
    down_beside = partner(after(down_own, *arrived[1]), 1)
    down_across = partner(after(down_own, *arrived[2]), 2)
    rest_opposite = relayed(after(rest_across, *arrived[3]), (depth - early) // 2)
    hidden_units, gates = expert_up(
        gathered,
        [(ref, 0) for ref in (first_own, rest_own, first_beside, rest_beside)]
        + [(first_across, start) for start in side]
        + [(ref, 0) for ref in (rest_across, *first_opposite, *rest_opposite)],
        columns,
    )
    down_ready = after(down_across, hidden_units)
    total = down_part(hidden_units, [down_own, down_beside, down_ready])
    mixed = []
    for first in range(0, width, slab):
        opposite = partner(down_ready[:, first : first + slab], 1)
        weighted = expert_down(hidden_units, total, gates, opposite, first, expert_count)
        sum_here = resid[:, first : first + slab].astype(jnp.float32)
        for term in scatter_sum(*weighted):
            sum_here = sum_here + term.astype(jnp.float32)
        mixed.append(sum_here.astype(jnp.bfloat16))
    return jnp.concatenate(mixed, axis=1)[None]


def solution(mesh):
    placed = (
        P("expert", "dp", None),
        P("expert", None, "dp"),
        P("expert", None, "dp"),
        P("expert", None, "dp"),
        P("expert", None),
        P("expert", None),
        P("expert", "dp", None),
        P("expert", "dp", None),
        P(),
        P("expert", "dp", None),
        P("expert", "dp", None),
    )
    dense = mesh.shape["expert"] == TOPK and mesh.shape["dp"] == 4
    return jax.shard_map(
        every_expert if dense else local, mesh=mesh, in_specs=placed, out_specs=P("expert", "dp", None), check_vma=False
    )
```

```python
import math

import jax
import jax.numpy as jnp
from jax import lax
from jax.experimental import pallas as pl
from jax.experimental.pallas import tpu as pltpu
from jax.sharding import PartitionSpec as P

HDIM = 128
TOPK = 8


epsilon = 1e-05


def fetch_weights(trainer_gate_up, trainer_down):
    return (
        lax.all_gather(trainer_gate_up.astype(jnp.bfloat16), "dp", axis=1, tiled=True),
        lax.all_gather(trainer_down.astype(jnp.bfloat16), "dp", axis=1, tiled=True),
    )


def local(
    hidden_in,
    queries,
    key_pool,
    value_pool,
    page_table,
    prompt_lengths,
    expert_ids,
    gate_weights,
    norm_gain,
    trainer_gate_up,
    trainer_down,
):
    col_tok = queries.shape[1]
    width_dev = queries.shape[2]
    heads_dev = width_dev // HDIM
    keys_all = jnp.take(key_pool, page_table[0], axis=0).reshape(col_tok, heads_dev, HDIM)
    values_all = jnp.take(value_pool, page_table[0], axis=0).reshape(col_tok, heads_dev, HDIM)
    request_ends = jnp.cumsum(prompt_lengths[0])
    positions = lax.iota(jnp.int32, col_tok)
    request = jnp.sum((positions[:, None] >= request_ends[None, :]).astype(jnp.int32), axis=1)
    block_rows = math.gcd(col_tok, 512)
    query_blocks = queries[0].reshape(col_tok // block_rows, block_rows, heads_dev, HDIM)
    request_blocks = request.reshape(col_tok // block_rows, block_rows)
    score_scale = 1.0 / math.sqrt(HDIM)

    def attend(pieces):
        query_block, request_block = pieces
        scores = (
            jnp.einsum("qhd,khd->hqk", query_block, keys_all, preferred_element_type=jnp.float32)
            * score_scale
        )
        same_request = (request_block[:, None] == request[None, :])[None]
        scores = jnp.where(same_request, scores, -1e30)
        highest = jnp.max(scores, axis=-1, keepdims=True)
        weights = jnp.where(same_request, jnp.exp(scores - highest), 0.0)
        totals = jnp.sum(weights, axis=-1, keepdims=True)
        probs = (weights / totals).astype(jnp.bfloat16)
        output = jnp.einsum("hqk,khd->qhd", probs, values_all, preferred_element_type=jnp.float32)
        return output.astype(jnp.bfloat16).reshape(block_rows, width_dev)

    attn_heads = lax.map(attend, (query_blocks, request_blocks)).reshape(1, col_tok, width_dev)
    attn_tokens = lax.all_to_all(attn_heads, "dp", split_axis=1, concat_axis=2, tiled=True)
    resid32 = (
        (hidden_in.astype(jnp.float32) + attn_tokens.astype(jnp.float32))
        .astype(jnp.bfloat16)
        .astype(jnp.float32)
    )
    mean_square = jnp.mean(resid32 * resid32, axis=-1, keepdims=True)
    normed = (resid32 * lax.rsqrt(mean_square + epsilon) * norm_gain).astype(jnp.bfloat16)
    server_gate_up, server_down = fetch_weights(trainer_gate_up, trainer_down)
    token_rows = normed.shape[1]
    width = normed.shape[2]
    expert_count = lax.axis_size("expert")
    capacity = min(token_rows, token_rows * TOPK * 5 // (4 * expert_count))
    hidden_size = server_gate_up.shape[2] // 2
    ids_flat = expert_ids[0].reshape(token_rows * TOPK)
    onehot = (ids_flat[:, None] == lax.iota(jnp.int32, expert_count)[None, :]).astype(jnp.int32)
    earlier = jnp.cumsum(onehot, axis=0) - onehot
    slot_index = jnp.sum(earlier * onehot, axis=1)
    flat_slot = ids_flat * capacity + slot_index
    placement = (
        flat_slot[:, None] == lax.iota(jnp.int32, expert_count * capacity)[None, :]
    ).astype(jnp.bfloat16)
    dispatch_matrix = jnp.sum(placement.reshape(token_rows, TOPK, expert_count * capacity), axis=1)
    outgoing = jnp.einsum(
        "ts,td->sd", dispatch_matrix, normed[0], preferred_element_type=jnp.float32
    )
    outgoing = outgoing.astype(jnp.bfloat16).reshape(expert_count, capacity, width)
    received = lax.all_to_all(outgoing, "expert", split_axis=0, concat_axis=0, tiled=True)
    sources, items, features = received.shape
    slot_rows = received.reshape(sources * items, features)
    gate_up = jnp.dot(slot_rows, server_gate_up[0], preferred_element_type=jnp.float32)
    hidden_units = (jax.nn.silu(gate_up[:, :hidden_size]) * gate_up[:, hidden_size:]).astype(
        jnp.bfloat16
    )
    outputs = jnp.dot(hidden_units, server_down[0], preferred_element_type=jnp.float32).astype(
        jnp.bfloat16
    )
    returned = lax.all_to_all(
        outputs.reshape(sources, items, features), "expert", split_axis=0, concat_axis=0, tiled=True
    )
    copies = jnp.take(returned.reshape(expert_count * capacity, width), flat_slot, axis=0)
    copies = copies.reshape(token_rows, TOPK, width).astype(jnp.float32)
    mixture = jnp.einsum("tk,tkd->td", gate_weights[0], copies)
    mixed = resid32[0] + mixture
    return mixed.astype(jnp.bfloat16)[None]

LANES = 128
VMEM_LIMIT = 32 * 2**20
VMEM_MOST = 60 * 2**20
CAST_STEPS = 4
FIRST_BLOCKS = 2
SLABS = 2
SMALL = pl.CostEstimate(flops=1, bytes_accessed=1, transcendentals=0)


def params(limit=VMEM_LIMIT):
    return pltpu.CompilerParams(vmem_limit_bytes=limit)


def vmem(count):
    return [pl.BlockSpec(memory_space=pltpu.VMEM)] * count


def attention_kernel(*refs):
    sources, outs, scratch = refs[:6], refs[6:10], refs[10:]
    own_ref, beside_ref, sent_ref, rows_ref = outs
    table, lengths, q_ref, k_ref, v_ref, weights, attn, rounded, arrived, left = scratch
    rows = weights.shape[0]
    copies = [
        pltpu.make_async_copy(source, target, arrived.at[i])
        for i, (source, target) in enumerate(
            zip(
                (*sources[:2], sources[2].at[0], *sources[3:5], sources[5].at[0, pl.ds(0, rows)]),
                (table, lengths, q_ref, k_ref, v_ref, weights),
            )
        )
    ]
    for copy in copies:
        copy.start()
    for copy in copies[:5]:
        copy.wait()
    tokens, width = q_ref.shape
    pages = k_ref.shape[0]
    row = lax.broadcasted_iota(jnp.int32, (tokens, 1), 0)
    column = lax.broadcasted_iota(jnp.int32, (1, tokens), 1)
    row_request = jnp.zeros((tokens, 1), jnp.int32)
    column_request = jnp.zeros((1, tokens), jnp.int32)
    end = jnp.int32(0)
    for r in range(lengths.shape[1]):
        end = end + lengths[0, r]
        row_request += (row >= end).astype(jnp.int32)
        column_request += (column >= end).astype(jnp.int32)
    same = row_request == column_request
    block, end, split = tokens // 4, sent_ref.shape[1], weights.shape[1]
    results = []
    for h in range(width // HDIM):
        if h == 2:
            copies[5].wait()
            rounded[...] = weights[...].astype(jnp.bfloat16)
            pairs = [(rounded, rows_ref)]
            for i in range(rows // block):
                here, there = pl.ds(i * block, block), pl.ds(i * split, split)
                pairs.append((rounded.at[here], sent_ref.at[:, there]))
            for source, target in pairs:
                results.append(pltpu.make_async_copy(source, target, left.at[len(results)]))
                results[-1].start()
        lanes = slice(h * HDIM, (h + 1) * HDIM)
        keys = jnp.concatenate([k_ref[table[0, p], :, lanes] for p in range(pages)], axis=0)
        values = jnp.concatenate([v_ref[table[0, p], :, lanes] for p in range(pages)], axis=0)
        scores = lax.dot_general(
            q_ref[:, lanes], keys, (((1,), (1,)), ((), ())), preferred_element_type=jnp.float32
        ) * (1.0 / math.sqrt(HDIM))
        scores = jnp.where(same, scores, -1e30)
        highest = jnp.max(scores, axis=-1, keepdims=True)
        weight = jnp.exp(scores - highest)
        share = 1.0 / jnp.sum(weight, axis=-1, keepdims=True)
        probs = (weight * share).astype(jnp.bfloat16)
        attn[:, lanes] = jnp.dot(probs, values, preferred_element_type=jnp.float32).astype(
            jnp.bfloat16
        )
    own = lax.axis_index("dp")
    targets = (
        own_ref,
        beside_ref,
        sent_ref.at[:, pl.ds(end - 2 * width, width)],
        sent_ref.at[:, pl.ds(end - width, width)],
    )
    for d, target in enumerate(targets):
        here = pl.ds(pl.multiple_of((own ^ d) * block, block), block)
        results.append(pltpu.make_async_copy(attn.at[here], target, left.at[len(results)]))
        results[-1].start()
    for copy in results:
        copy.wait()


def attention(queries, key_pool, value_pool, page_table, prompt_lengths, gate_up, blocks):
    tokens, width = queries.shape[1:]
    split = gate_up.shape[2]
    block = tokens // 4
    shapes = [(block, width)] * 2
    shapes += [(block, blocks * split + 2 * width), (blocks * block, split)]
    return pl.pallas_call(
        attention_kernel,
        out_shape=[jax.ShapeDtypeStruct(shape, jnp.bfloat16) for shape in shapes],
        in_specs=[pl.BlockSpec(memory_space=pltpu.HBM)] * 6,
        out_specs=[pl.BlockSpec(memory_space=pltpu.HBM)] * 4,
        scratch_shapes=[
            pltpu.SMEM(page_table.shape, jnp.int32),
            pltpu.SMEM(prompt_lengths.shape, jnp.int32),
            pltpu.VMEM((tokens, width), jnp.bfloat16),
            pltpu.VMEM(key_pool.shape, jnp.bfloat16),
            pltpu.VMEM(value_pool.shape, jnp.bfloat16),
            pltpu.VMEM((blocks * block, split), jnp.float32),
            pltpu.VMEM((tokens, width), jnp.bfloat16),
            pltpu.VMEM((blocks * block, split), jnp.bfloat16),
            pltpu.SemaphoreType.DMA((6,)),
            pltpu.SemaphoreType.DMA((blocks + 5,)),
        ],
        compiler_params=params(VMEM_MOST),
        name="attention",
    )(page_table, prompt_lengths, queries, key_pool, value_pool, gate_up)


def norm_kernel(*refs):
    sources, outs, scratch = refs[:8], refs[8:11], refs[11:]
    a0, a1, a2, a3, hidden_ref, gain_ref, ids_ref, gates_ref, arrived = scratch
    resid_ref, row_refs = outs[0], outs[1:]
    across, block = sources[2], a2.shape[1]
    across = across.at[:, pl.ds(across.shape[1] - 2 * block, block)]
    copies = [
        pltpu.make_async_copy(source, target, arrived.at[i])
        for i, (source, target) in enumerate(zip((*sources[:2], across, *sources[3:]), scratch))
    ]
    for copy in copies:
        copy.start()
    for copy in copies:
        copy.wait()
    own = lax.axis_index("dp")
    tokens, width = hidden_ref.shape
    total = jnp.zeros((tokens, 1), jnp.float32)
    for d, attn in enumerate((a0, a1, a2, a3)):
        columns = pl.ds(pl.multiple_of((own ^ d) * block, block), block)
        resid = (
            hidden_ref[:, columns].astype(jnp.float32) + attn[...].astype(jnp.float32)
        ).astype(jnp.bfloat16)
        resid_ref[:, columns] = resid
        resid32 = resid.astype(jnp.float32)
        total += jnp.sum(resid32 * resid32, axis=-1, keepdims=True)
    inverse = lax.rsqrt(total / width + epsilon)
    halves = [slice(i * tokens // 2, (i + 1) * tokens // 2) for i in range(2)]
    for d in range(4):
        columns = pl.ds(pl.multiple_of((own ^ d) * block, block), block)
        normed = resid_ref[:, columns].astype(jnp.float32) * inverse * gain_ref[:, columns]
        for here, ref in zip(halves, row_refs):
            ref[:, d * block : (d + 1) * block] = normed[here].astype(jnp.bfloat16)
    place = lax.broadcasted_iota(jnp.int32, (LANES, tokens), 0)
    gates = jnp.zeros((LANES, tokens), jnp.float32)
    for k in range(TOPK):
        gates += jnp.where(ids_ref[k : k + 1] == place % TOPK, gates_ref[k : k + 1], 0.0)
    high = gates.astype(jnp.bfloat16).astype(jnp.float32)
    middle = (gates - high).astype(jnp.bfloat16).astype(jnp.float32)
    low = gates - high - middle
    part = place // TOPK
    terms = jnp.where(part == 0, high, jnp.where(part == 1, middle, jnp.where(part == 2, low, 0.0)))
    terms = jnp.transpose(terms)
    for here, ref in zip(halves, row_refs):
        ref[:, width:] = terms[here].astype(jnp.bfloat16)


def norm(hidden_in, attn, norm_gain, expert_ids, gate_weights):
    tokens, width = hidden_in.shape
    operands = hidden_in, norm_gain[None, :], expert_ids.T, gate_weights.T
    return pl.pallas_call(
        norm_kernel,
        out_shape=[
            jax.ShapeDtypeStruct((tokens, width), jnp.bfloat16),
        ]
        + [jax.ShapeDtypeStruct((tokens // 2, width + LANES), jnp.bfloat16)] * 2,
        in_specs=[pl.BlockSpec(memory_space=pl.ANY)] * 8,
        out_specs=vmem(3),
        scratch_shapes=[pltpu.VMEM(attn[0].shape, jnp.bfloat16)] * 4
        + [pltpu.VMEM(x.shape, x.dtype) for x in operands]
        + [pltpu.SemaphoreType.DMA((8,))],
        compiler_params=params(),
        cost_estimate=SMALL,
        name="norm",
    )(*attn, *operands)


def cast_kernel(spans, *refs):
    count = len(spans)
    sources, targets, scratch = refs[:count], refs[count : 2 * count], refs[2 * count :]
    wide, narrow, arrived, left = scratch[:count], scratch[count : 2 * count], *scratch[-2:]

    def rows_of(i, step, first=0):
        rows = wide[i].shape[0] // CAST_STEPS
        return pl.ds(first + step * rows, rows)

    def copies_in(step):
        for i, (first, _, column, columns) in enumerate(spans):
            yield pltpu.make_async_copy(
                sources[i].at[0, rows_of(i, step, first), pl.ds(column, columns)],
                wide[i].at[rows_of(i, step)],
                arrived.at[step, i],
            )

    def copies_out(step):
        for i in range(count):
            here = rows_of(i, step)
            yield pltpu.make_async_copy(narrow[i].at[here], targets[i].at[here], left.at[step, i])

    for step in range(CAST_STEPS):
        for copy in copies_in(step):
            copy.start()
    for step in range(CAST_STEPS):
        for copy in copies_in(step):
            copy.wait()
        for i in range(count):
            here = rows_of(i, step)
            narrow[i][here] = wide[i][here].astype(jnp.bfloat16)
        for copy in copies_out(step):
            copy.start()
    for step in range(CAST_STEPS):
        for copy in copies_out(step):
            copy.wait()


def cast_rows(arrays, spans):
    shapes = [(rows, columns) for _, rows, _, columns in spans]
    return pl.pallas_call(
        lambda *refs: cast_kernel(spans, *refs),
        out_shape=[jax.ShapeDtypeStruct(shape, jnp.bfloat16) for shape in shapes],
        in_specs=[pl.BlockSpec(memory_space=pltpu.HBM)] * len(arrays),
        out_specs=[pl.BlockSpec(memory_space=pltpu.HBM)] * len(arrays),
        scratch_shapes=[pltpu.VMEM(shape, jnp.float32) for shape in shapes]
        + [pltpu.VMEM(shape, jnp.bfloat16) for shape in shapes]
        + [pltpu.SemaphoreType.DMA((CAST_STEPS, len(arrays)))] * 2,
        compiler_params=params(VMEM_MOST),
        name="cast_rows",
    )(*arrays)


def load_tiles(pieces, starts, weights, arrived, tiles, block):
    def copies(tile):
        first = 0
        for index, (piece, start) in enumerate(zip(pieces, starts)):
            depth = piece.shape[0]
            for part in range(2):
                column = (part * tiles + tile) * block
                yield pltpu.make_async_copy(
                    piece.at[:, pl.ds(start + column, block)],
                    weights.at[pl.ds(first, depth), pl.ds(column, block)],
                    arrived.at[tile, index, part],
                )
            first += depth

    for tile in range(tiles):
        for copy in copies(tile):
            copy.start()

    def wait(tile):
        for copy in copies(tile):
            copy.wait()

    return wait


def row_copies(pieces, weights, arrived):
    first = 0
    for i, ref in enumerate(pieces):
        depth = ref.shape[0]
        yield pltpu.make_async_copy(ref, weights.at[pl.ds(first, depth)], arrived.at[i])
        first += depth


def start_rows(pieces, weights, arrived):
    for copy in row_copies(pieces, weights, arrived):
        copy.start()


def wait_rows(pieces, weights, arrived):
    for copy in row_copies(pieces, weights, arrived):
        copy.wait()


def up_kernel(sources, starts, *refs):
    pieces = len(starts)
    row_refs = refs[:sources]
    weight_refs = refs[sources : sources + pieces]
    down_refs, refs = refs[sources + pieces : -9], refs[-9:]
    hidden_ref, own_gate_ref, total_ref, rows, weights, units, down, arrived, down_arrived = refs
    start_rows(down_refs, down, down_arrived)
    width = rows.shape[1]
    tiles, _, block = units.shape
    wait = load_tiles(weight_refs, starts, weights, arrived, tiles, block)
    expert = lax.axis_index("expert")
    first = 0
    for ref in row_refs:
        count = ref.shape[0]
        here = slice(first, first + count)
        rows[here, :] = ref[:, :width]
        terms = ref[:, width:].astype(jnp.float32)
        lane = lax.broadcasted_iota(jnp.int32, terms.shape, 1)
        own_gate_ref[here, :] = jnp.sum(
            jnp.where(lane % TOPK == expert, terms, 0.0), axis=-1, keepdims=True
        )
        first += count
    for tile in range(tiles):
        wait(tile)
        gate, up = (
            jnp.dot(
                rows[...],
                weights[:, (part * tiles + tile) * block : (part * tiles + tile + 1) * block],
                preferred_element_type=jnp.float32,
            )
            for part in range(2)
        )
        units[tile] = (gate / (1.0 + jnp.exp(-gate)) * up).astype(jnp.bfloat16)
    own = lax.axis_index("dp")
    for d in range(4):
        hidden_ref[:, d * block : (d + 1) * block] = units[own ^ d]
    wait_rows(down_refs, down, down_arrived)
    total_ref[...] = jnp.dot(
        hidden_ref[:, : down.shape[0]], down[...], preferred_element_type=jnp.float32
    )


def expert_up(rows, weights, width, down):
    weights, starts = zip(*weights)
    tokens = sum(piece.shape[0] for piece in rows)
    features = sum(piece.shape[0] for piece in weights)
    hidden_size = width // 2
    return pl.pallas_call(
        lambda *refs: up_kernel(len(rows), starts, *refs),
        out_shape=[
            jax.ShapeDtypeStruct((tokens, hidden_size), jnp.bfloat16),
            jax.ShapeDtypeStruct((tokens, 1), jnp.float32),
            jax.ShapeDtypeStruct((tokens, down[0].shape[1]), jnp.float32),
        ],
        in_specs=vmem(len(rows)) + [pl.BlockSpec(memory_space=pl.ANY)] * (len(weights) + len(down)),
        out_specs=vmem(3),
        scratch_shapes=[
            pltpu.VMEM((tokens, features), jnp.bfloat16),
            pltpu.VMEM((features, width), jnp.bfloat16),
            pltpu.VMEM((4, tokens, hidden_size // 4), jnp.bfloat16),
            pltpu.VMEM((sum(x.shape[0] for x in down), down[0].shape[1]), jnp.bfloat16),
            pltpu.SemaphoreType.DMA((4, len(weights), 2)),
            pltpu.SemaphoreType.DMA((len(down),)),
        ],
        compiler_params=params(),
        cost_estimate=SMALL,
        name="expert_up",
    )(*rows, *weights, *down)


def part_kernel(first, column, hidden_ref, before_ref, *refs):
    pieces, (total_ref, weights, arrived) = refs[:-3], refs[-3:]
    depth, width = weights.shape
    pieces = [piece.at[:, pl.ds(column, width)] for piece in pieces]
    start_rows(pieces, weights, arrived)
    wait_rows(pieces, weights, arrived)
    total_ref[...] = before_ref[:, column : column + width] + jnp.dot(
        hidden_ref[:, first : first + depth], weights[...], preferred_element_type=jnp.float32
    )


def down_part(hidden_units, before, weights, first, column, width):
    depth = sum(piece.shape[0] for piece in weights)
    return pl.pallas_call(
        lambda *refs: part_kernel(first, column, *refs),
        out_shape=jax.ShapeDtypeStruct((hidden_units.shape[0], width), jnp.float32),
        in_specs=vmem(2) + [pl.BlockSpec(memory_space=pl.ANY)] * len(weights),
        out_specs=pl.BlockSpec(memory_space=pltpu.VMEM),
        scratch_shapes=[
            pltpu.VMEM((depth, width), jnp.bfloat16),
            pltpu.SemaphoreType.DMA((len(weights),)),
        ],
        compiler_params=params(),
        cost_estimate=SMALL,
        name="down_part",
    )(hidden_units, before, *weights)


def down_kernel(first, sources, hidden_ref, total_ref, gate_ref, piece, *refs):
    outs, (weights, arrived) = refs[:-2], refs[-2:]
    start_rows([piece], weights, arrived)
    wait_rows([piece], weights, arrived)
    depth, width = weights.shape
    units = hidden_ref[:, first : first + depth]
    total = total_ref[...] + jnp.dot(
        units, weights[...], preferred_element_type=jnp.float32
    )
    weighted = (total * gate_ref[...]).astype(jnp.bfloat16)
    rows = weighted.shape[0] // sources
    for (first, count), ref in zip(down_blocks(rows, sources), outs):
        ref[...] = weighted[first : first + count]


def down_blocks(rows, sources):
    half, reach = rows // 2, sources // 2
    blocks = [(0, rows)]
    for step, middle in ((-1, reach * rows), (1, reach * rows + half)):
        blocks.append((middle, half))
        second = (reach + step) * rows
        blocks += [(second, half), (second + half, half)]
        blocks += [((reach + step * away) * rows, rows) for away in range(2, reach)]
    return blocks


def expert_down(hidden_units, total, gates, weights, sources):
    tokens, hidden_size = hidden_units.shape
    depth, width = weights.shape
    rows = tokens // sources
    return pl.pallas_call(
        lambda *refs: down_kernel(hidden_size - depth, sources, *refs),
        out_shape=[
            jax.ShapeDtypeStruct((count, width), jnp.bfloat16)
            for _, count in down_blocks(rows, sources)
        ],
        in_specs=vmem(3) + [pl.BlockSpec(memory_space=pl.ANY)],
        out_specs=vmem(sources + 3),
        scratch_shapes=[
            pltpu.VMEM((depth, width), jnp.bfloat16),
            pltpu.SemaphoreType.DMA((1,)),
        ],
        compiler_params=params(),
        cost_estimate=SMALL,
        name="expert_down",
    )(hidden_units, total, gates, weights)


def partner(x, distance):
    return lax.ppermute(x, "dp", [(i, i ^ distance) for i in range(4)])


def ring_order(count):
    return list(range(0, count, 2)) + list(range(count - 1, 0, -2))


def around(x, step):
    ring = ring_order(lax.axis_size("expert"))
    count = len(ring)
    return lax.ppermute(x, "expert", [(ring[i], ring[(i + step) % count]) for i in range(count)])


def after(x, *others):
    return lax.optimization_barrier((x, *others))[0]


def add(a, b):
    return (a.astype(jnp.float32) + b.astype(jnp.float32)).astype(jnp.bfloat16)


def gather_rows(halves):
    reach = lax.axis_size("expert") // 2
    above, below = [halves], [halves]
    for _ in range(reach - 1):
        above.append([around(half, -1) for half in above[-1]])
        below.append([around(half, 1) for half in below[-1]])
    far = [around(above[-1][0], -1), around(below[-1][1], 1)]
    rows = [half for pair in (*above, far, *below[:0:-1]) for half in pair]
    return rows, [(*a, *b) for a, b in zip(above[1:], below[1:])] + [tuple(far)]


def scatter_sum(own, *blocks):
    reach = len(blocks) // 2
    terms = [own]
    for step, (far, first, second, *near) in ((1, blocks[:reach]), (-1, blocks[reach:])):
        moving = around(far, step)
        if step > 0:
            moving = jnp.concatenate([add(first, moving), second])
        else:
            moving = jnp.concatenate([first, add(second, moving)])
        for block in near:
            moving = add(block, around(moving, step))
        terms.append(around(moving, step))
    return terms


def relayed(x, rows):
    return [partner(x[i : i + rows], 1) for i in range(0, x.shape[0], rows)]


def every_expert(
    hidden_in,
    queries,
    key_pool,
    value_pool,
    page_table,
    prompt_lengths,
    expert_ids,
    gate_weights,
    norm_gain,
    trainer_gate_up,
    trainer_down,
):
    expert_count = lax.axis_size("expert")
    width = trainer_down.shape[2]
    depth, columns = trainer_gate_up.shape[1:]
    down_depth = trainer_down.shape[1]
    slab = width // SLABS
    early = queries.shape[1] // 4 * FIRST_BLOCKS
    side = [i * columns for i in range(FIRST_BLOCKS)]
    attn_own, attn_beside, first_sent, first_own = attention(
        queries,
        key_pool,
        value_pool,
        page_table,
        prompt_lengths,
        trainer_gate_up,
        FIRST_BLOCKS,
    )
    first_across = partner(first_sent, 2)
    rest_own, down_own = cast_rows(
        [after(trainer_gate_up, attn_own), trainer_down],
        [(early, depth - early, 0, columns), (0, down_depth, 0, width)],
    )
    attn_beside = partner(attn_beside, 1)
    attn_opposite = partner(first_across[:, -attn_own.shape[1] :], 1)
    rest_across = partner(rest_own, 2)
    resid, *halves = norm(
        after(hidden_in[0], rest_own),
        (attn_own, attn_beside, first_across, attn_opposite),
        norm_gain,
        expert_ids[0],
        gate_weights[0],
    )
    gathered, arrived = gather_rows(halves)
    first_beside = partner(after(first_own, *arrived[0]), 1)
    rest_beside = partner(after(rest_own, *arrived[0]), 1)
    first_ready = after(first_across, *arrived[0])
    first_opposite = [partner(first_ready[:, start : start + columns], 1) for start in side]
    down_beside = partner(after(down_own, *arrived[1]), 1)
    down_across = partner(after(down_own, *arrived[2]), 2)
    rest_opposite = relayed(after(rest_across, *arrived[3]), (depth - early) // 2)
    hidden_units, gates, total = expert_up(
        gathered,
        [(ref, 0) for ref in (first_own, rest_own, first_beside, rest_beside)]
        + [(first_across, start) for start in side]
        + [(ref, 0) for ref in (rest_across, *first_opposite, *rest_opposite)],
        columns,
        [down_own],
    )
    down_ready = after(down_across, hidden_units)
    mixed = []
    for first in range(0, width, slab):
        opposite = partner(down_ready[:, first : first + slab], 1)
        part = down_part(
            hidden_units, total, [down_beside, down_ready], down_depth, first, slab
        )
        weighted = expert_down(hidden_units, part, gates, opposite, expert_count)
        sum_here = resid[:, first : first + slab].astype(jnp.float32)
        for term in scatter_sum(*weighted):
            sum_here = sum_here + term.astype(jnp.float32)
        mixed.append(sum_here.astype(jnp.bfloat16))
    return jnp.concatenate(mixed, axis=1)[None]


def solution(mesh):
    placed = (
        P("expert", "dp", None),
        P("expert", None, "dp"),
        P("expert", None, "dp"),
        P("expert", None, "dp"),
        P("expert", None),
        P("expert", None),
        P("expert", "dp", None),
        P("expert", "dp", None),
        P(),
        P("expert", "dp", None),
        P("expert", "dp", None),
    )
    dense = mesh.shape["expert"] == TOPK and mesh.shape["dp"] == 4
    return jax.shard_map(
        every_expert if dense else local, mesh=mesh, in_specs=placed, out_specs=P("expert", "dp", None), check_vma=False
    )
```

```python
import math

import jax
import jax.numpy as jnp
from jax import lax
from jax.experimental import pallas as pl
from jax.experimental.pallas import tpu as pltpu
from jax.sharding import PartitionSpec as P

HDIM = 128
TOPK = 8


epsilon = 1e-05


def fetch_weights(trainer_gate_up, trainer_down):
    return (
        lax.all_gather(trainer_gate_up.astype(jnp.bfloat16), "dp", axis=1, tiled=True),
        lax.all_gather(trainer_down.astype(jnp.bfloat16), "dp", axis=1, tiled=True),
    )


def local(
    hidden_in,
    queries,
    key_pool,
    value_pool,
    page_table,
    prompt_lengths,
    expert_ids,
    gate_weights,
    norm_gain,
    trainer_gate_up,
    trainer_down,
):
    col_tok = queries.shape[1]
    width_dev = queries.shape[2]
    heads_dev = width_dev // HDIM
    keys_all = jnp.take(key_pool, page_table[0], axis=0).reshape(col_tok, heads_dev, HDIM)
    values_all = jnp.take(value_pool, page_table[0], axis=0).reshape(col_tok, heads_dev, HDIM)
    request_ends = jnp.cumsum(prompt_lengths[0])
    positions = lax.iota(jnp.int32, col_tok)
    request = jnp.sum((positions[:, None] >= request_ends[None, :]).astype(jnp.int32), axis=1)
    block_rows = math.gcd(col_tok, 512)
    query_blocks = queries[0].reshape(col_tok // block_rows, block_rows, heads_dev, HDIM)
    request_blocks = request.reshape(col_tok // block_rows, block_rows)
    score_scale = 1.0 / math.sqrt(HDIM)

    def attend(pieces):
        query_block, request_block = pieces
        scores = (
            jnp.einsum("qhd,khd->hqk", query_block, keys_all, preferred_element_type=jnp.float32)
            * score_scale
        )
        same_request = (request_block[:, None] == request[None, :])[None]
        scores = jnp.where(same_request, scores, -1e30)
        highest = jnp.max(scores, axis=-1, keepdims=True)
        weights = jnp.where(same_request, jnp.exp(scores - highest), 0.0)
        totals = jnp.sum(weights, axis=-1, keepdims=True)
        probs = (weights / totals).astype(jnp.bfloat16)
        output = jnp.einsum("hqk,khd->qhd", probs, values_all, preferred_element_type=jnp.float32)
        return output.astype(jnp.bfloat16).reshape(block_rows, width_dev)

    attn_heads = lax.map(attend, (query_blocks, request_blocks)).reshape(1, col_tok, width_dev)
    attn_tokens = lax.all_to_all(attn_heads, "dp", split_axis=1, concat_axis=2, tiled=True)
    resid32 = (
        (hidden_in.astype(jnp.float32) + attn_tokens.astype(jnp.float32))
        .astype(jnp.bfloat16)
        .astype(jnp.float32)
    )
    mean_square = jnp.mean(resid32 * resid32, axis=-1, keepdims=True)
    normed = (resid32 * lax.rsqrt(mean_square + epsilon) * norm_gain).astype(jnp.bfloat16)
    server_gate_up, server_down = fetch_weights(trainer_gate_up, trainer_down)
    token_rows = normed.shape[1]
    width = normed.shape[2]
    expert_count = lax.axis_size("expert")
    capacity = min(token_rows, token_rows * TOPK * 5 // (4 * expert_count))
    hidden_size = server_gate_up.shape[2] // 2
    ids_flat = expert_ids[0].reshape(token_rows * TOPK)
    onehot = (ids_flat[:, None] == lax.iota(jnp.int32, expert_count)[None, :]).astype(jnp.int32)
    earlier = jnp.cumsum(onehot, axis=0) - onehot
    slot_index = jnp.sum(earlier * onehot, axis=1)
    flat_slot = ids_flat * capacity + slot_index
    placement = (
        flat_slot[:, None] == lax.iota(jnp.int32, expert_count * capacity)[None, :]
    ).astype(jnp.bfloat16)
    dispatch_matrix = jnp.sum(placement.reshape(token_rows, TOPK, expert_count * capacity), axis=1)
    outgoing = jnp.einsum(
        "ts,td->sd", dispatch_matrix, normed[0], preferred_element_type=jnp.float32
    )
    outgoing = outgoing.astype(jnp.bfloat16).reshape(expert_count, capacity, width)
    received = lax.all_to_all(outgoing, "expert", split_axis=0, concat_axis=0, tiled=True)
    sources, items, features = received.shape
    slot_rows = received.reshape(sources * items, features)
    gate_up = jnp.dot(slot_rows, server_gate_up[0], preferred_element_type=jnp.float32)
    hidden_units = (jax.nn.silu(gate_up[:, :hidden_size]) * gate_up[:, hidden_size:]).astype(
        jnp.bfloat16
    )
    outputs = jnp.dot(hidden_units, server_down[0], preferred_element_type=jnp.float32).astype(
        jnp.bfloat16
    )
    returned = lax.all_to_all(
        outputs.reshape(sources, items, features), "expert", split_axis=0, concat_axis=0, tiled=True
    )
    copies = jnp.take(returned.reshape(expert_count * capacity, width), flat_slot, axis=0)
    copies = copies.reshape(token_rows, TOPK, width).astype(jnp.float32)
    mixture = jnp.einsum("tk,tkd->td", gate_weights[0], copies)
    mixed = resid32[0] + mixture
    return mixed.astype(jnp.bfloat16)[None]

LANES = 128
VMEM_LIMIT = 32 * 2**20
VMEM_MOST = 60 * 2**20
CAST_STEPS = 4
FIRST_BLOCKS = 2
SLABS = 2
SMALL = pl.CostEstimate(flops=1, bytes_accessed=1, transcendentals=0)


def params(limit=VMEM_LIMIT):
    return pltpu.CompilerParams(vmem_limit_bytes=limit)


def vmem(count):
    return [pl.BlockSpec(memory_space=pltpu.VMEM)] * count


def attention_kernel(*refs):
    sources, outs, scratch = refs[:6], refs[6:9], refs[9:]
    own_ref, beside_ref, sent_ref = outs
    table, lengths, q_ref, k_ref, v_ref, weights, attn, arrived = scratch
    copies = [
        pltpu.make_async_copy(source, target, arrived.at[i])
        for i, (source, target) in enumerate(
            zip(
                (*sources[:2], sources[2].at[0], *sources[3:5]),
                (table, lengths, q_ref, k_ref, v_ref),
            )
        )
    ]
    rows = weights.shape[0]
    copies.append(
        pltpu.make_async_copy(sources[5].at[0, pl.ds(0, rows)], weights, arrived.at[5])
    )
    for copy in copies:
        copy.start()
    for copy in copies[:5]:
        copy.wait()
    tokens, width = q_ref.shape
    pages = k_ref.shape[0]
    row = lax.broadcasted_iota(jnp.int32, (tokens, 1), 0)
    column = lax.broadcasted_iota(jnp.int32, (1, tokens), 1)
    row_request = jnp.zeros((tokens, 1), jnp.int32)
    column_request = jnp.zeros((1, tokens), jnp.int32)
    end = jnp.int32(0)
    for r in range(lengths.shape[1]):
        end = end + lengths[0, r]
        row_request += (row >= end).astype(jnp.int32)
        column_request += (column >= end).astype(jnp.int32)
    same = row_request == column_request
    for h in range(width // HDIM):
        lanes = slice(h * HDIM, (h + 1) * HDIM)
        keys = jnp.concatenate([k_ref[table[0, p], :, lanes] for p in range(pages)], axis=0)
        values = jnp.concatenate([v_ref[table[0, p], :, lanes] for p in range(pages)], axis=0)
        scores = lax.dot_general(
            q_ref[:, lanes], keys, (((1,), (1,)), ((), ())), preferred_element_type=jnp.float32
        ) * (1.0 / math.sqrt(HDIM))
        scores = jnp.where(same, scores, -1e30)
        highest = jnp.max(scores, axis=-1, keepdims=True)
        weight = jnp.exp(scores - highest)
        share = 1.0 / jnp.sum(weight, axis=-1, keepdims=True)
        probs = (weight * share).astype(jnp.bfloat16)
        attn[:, lanes] = jnp.dot(probs, values, preferred_element_type=jnp.float32).astype(
            jnp.bfloat16
        )
    own = lax.axis_index("dp")
    block = tokens // 4
    split = weights.shape[1]
    end = sent_ref.shape[1]
    targets = (
        own_ref,
        beside_ref,
        sent_ref.at[:, end - 2 * width : end - width],
        sent_ref.at[:, end - width :],
    )
    for d, target in enumerate(targets):
        target[...] = attn[pl.ds(pl.multiple_of((own ^ d) * block, block), block), :]
    copies[5].wait()
    for i in range(rows // block):
        here = slice(i * block, (i + 1) * block)
        sent_ref[:, i * split : (i + 1) * split] = weights[here].astype(jnp.bfloat16)


def attention(queries, key_pool, value_pool, page_table, prompt_lengths, gate_up, blocks):
    tokens, width = queries.shape[1:]
    split = gate_up.shape[2]
    block = tokens // 4
    shapes = [(block, width)] * 2
    shapes.append((block, blocks * split + 2 * width))
    return pl.pallas_call(
        attention_kernel,
        out_shape=[jax.ShapeDtypeStruct(shape, jnp.bfloat16) for shape in shapes],
        in_specs=[pl.BlockSpec(memory_space=pltpu.HBM)] * 6,
        out_specs=vmem(3),
        scratch_shapes=[
            pltpu.SMEM(page_table.shape, jnp.int32),
            pltpu.SMEM(prompt_lengths.shape, jnp.int32),
            pltpu.VMEM((tokens, width), jnp.bfloat16),
            pltpu.VMEM(key_pool.shape, jnp.bfloat16),
            pltpu.VMEM(value_pool.shape, jnp.bfloat16),
            pltpu.VMEM((blocks * block, split), jnp.float32),
            pltpu.VMEM((tokens, width), jnp.bfloat16),
            pltpu.SemaphoreType.DMA((6,)),
        ],
        compiler_params=params(VMEM_MOST),
        name="attention",
    )(page_table, prompt_lengths, queries, key_pool, value_pool, gate_up)


def norm_kernel(*refs):
    sources, outs, scratch = refs[:8], refs[8:11], refs[11:]
    a0, a1, a2, a3, hidden_ref, gain_ref, ids_ref, gates_ref, arrived = scratch
    resid_ref, row_refs = outs[0], outs[1:]
    across, block = sources[2], a2.shape[1]
    across = across.at[:, pl.ds(across.shape[1] - 2 * block, block)]
    copies = [
        pltpu.make_async_copy(source, target, arrived.at[i])
        for i, (source, target) in enumerate(zip((*sources[:2], across, *sources[3:]), scratch))
    ]
    for copy in copies:
        copy.start()
    for copy in copies:
        copy.wait()
    own = lax.axis_index("dp")
    tokens, width = hidden_ref.shape
    total = jnp.zeros((tokens, 1), jnp.float32)
    for d, attn in enumerate((a0, a1, a2, a3)):
        columns = pl.ds(pl.multiple_of((own ^ d) * block, block), block)
        resid = (
            hidden_ref[:, columns].astype(jnp.float32) + attn[...].astype(jnp.float32)
        ).astype(jnp.bfloat16)
        resid_ref[:, columns] = resid
        resid32 = resid.astype(jnp.float32)
        total += jnp.sum(resid32 * resid32, axis=-1, keepdims=True)
    inverse = lax.rsqrt(total / width + epsilon)
    halves = [slice(i * tokens // 2, (i + 1) * tokens // 2) for i in range(2)]
    for d in range(4):
        columns = pl.ds(pl.multiple_of((own ^ d) * block, block), block)
        normed = resid_ref[:, columns].astype(jnp.float32) * inverse * gain_ref[:, columns]
        for here, ref in zip(halves, row_refs):
            ref[:, d * block : (d + 1) * block] = normed[here].astype(jnp.bfloat16)
    place = lax.broadcasted_iota(jnp.int32, (LANES, tokens), 0)
    gates = jnp.zeros((LANES, tokens), jnp.float32)
    for k in range(TOPK):
        gates += jnp.where(ids_ref[k : k + 1] == place % TOPK, gates_ref[k : k + 1], 0.0)
    high = gates.astype(jnp.bfloat16).astype(jnp.float32)
    middle = (gates - high).astype(jnp.bfloat16).astype(jnp.float32)
    low = gates - high - middle
    part = place // TOPK
    terms = jnp.where(part == 0, high, jnp.where(part == 1, middle, jnp.where(part == 2, low, 0.0)))
    terms = jnp.transpose(terms)
    for here, ref in zip(halves, row_refs):
        ref[:, width:] = terms[here].astype(jnp.bfloat16)


def norm(hidden_in, attn, norm_gain, expert_ids, gate_weights):
    tokens, width = hidden_in.shape
    operands = hidden_in, norm_gain[None, :], expert_ids.T, gate_weights.T
    return pl.pallas_call(
        norm_kernel,
        out_shape=[
            jax.ShapeDtypeStruct((tokens, width), jnp.bfloat16),
        ]
        + [jax.ShapeDtypeStruct((tokens // 2, width + LANES), jnp.bfloat16)] * 2,
        in_specs=[pl.BlockSpec(memory_space=pl.ANY)] * 8,
        out_specs=vmem(3),
        scratch_shapes=[pltpu.VMEM(attn[0].shape, jnp.bfloat16)] * 4
        + [pltpu.VMEM(x.shape, x.dtype) for x in operands]
        + [pltpu.SemaphoreType.DMA((8,))],
        compiler_params=params(),
        cost_estimate=SMALL,
        name="norm",
    )(*attn, *operands)


def cast_kernel(spans, *refs):
    count = len(spans)
    sources, targets, scratch = refs[:count], refs[count : 2 * count], refs[2 * count :]
    wide, narrow, arrived, left = scratch[:count], scratch[count : 2 * count], *scratch[-2:]

    def rows_of(i, step, first=0):
        rows = wide[i].shape[0] // CAST_STEPS
        return pl.ds(first + step * rows, rows)

    def copies_in(step):
        for i, (first, _, column, columns) in enumerate(spans):
            yield pltpu.make_async_copy(
                sources[i].at[0, rows_of(i, step, first), pl.ds(column, columns)],
                wide[i].at[rows_of(i, step)],
                arrived.at[step, i],
            )

    def copies_out(step):
        for i in range(count):
            here = rows_of(i, step)
            yield pltpu.make_async_copy(narrow[i].at[here], targets[i].at[here], left.at[step, i])

    for step in range(CAST_STEPS):
        for copy in copies_in(step):
            copy.start()
    for step in range(CAST_STEPS):
        for copy in copies_in(step):
            copy.wait()
        for i in range(count):
            here = rows_of(i, step)
            narrow[i][here] = wide[i][here].astype(jnp.bfloat16)
        for copy in copies_out(step):
            copy.start()
    for step in range(CAST_STEPS):
        for copy in copies_out(step):
            copy.wait()


def cast_rows(arrays, spans):
    shapes = [(rows, columns) for _, rows, _, columns in spans]
    return pl.pallas_call(
        lambda *refs: cast_kernel(spans, *refs),
        out_shape=[jax.ShapeDtypeStruct(shape, jnp.bfloat16) for shape in shapes],
        in_specs=[pl.BlockSpec(memory_space=pltpu.HBM)] * len(arrays),
        out_specs=[pl.BlockSpec(memory_space=pltpu.HBM)] * len(arrays),
        scratch_shapes=[pltpu.VMEM(shape, jnp.float32) for shape in shapes]
        + [pltpu.VMEM(shape, jnp.bfloat16) for shape in shapes]
        + [pltpu.SemaphoreType.DMA((CAST_STEPS, len(arrays)))] * 2,
        compiler_params=params(VMEM_MOST),
        name="cast_rows",
    )(*arrays)


def load_tiles(pieces, starts, weights, arrived, tiles, block):
    def copies(tile):
        first = 0
        for index, (piece, start) in enumerate(zip(pieces, starts)):
            depth = piece.shape[0]
            for part in range(2):
                column = (part * tiles + tile) * block
                yield pltpu.make_async_copy(
                    piece.at[:, pl.ds(start + column, block)],
                    weights.at[pl.ds(first, depth), pl.ds(column, block)],
                    arrived.at[tile, index, part],
                )
            first += depth

    for tile in range(tiles):
        for copy in copies(tile):
            copy.start()

    def wait(tile):
        for copy in copies(tile):
            copy.wait()

    return wait


def up_kernel(sources, starts, *refs):
    pieces = len(starts)
    row_refs = refs[:sources]
    weight_refs = refs[sources : sources + pieces]
    hidden_ref, own_gate_ref, rows, weights, units, arrived = refs[sources + pieces :]
    width = rows.shape[1]
    tiles, _, block = units.shape
    wait = load_tiles(weight_refs, starts, weights, arrived, tiles, block)
    expert = lax.axis_index("expert")
    first = 0
    for ref in row_refs:
        count = ref.shape[0]
        here = slice(first, first + count)
        rows[here, :] = ref[:, :width]
        terms = ref[:, width:].astype(jnp.float32)
        lane = lax.broadcasted_iota(jnp.int32, terms.shape, 1)
        own_gate_ref[here, :] = jnp.sum(
            jnp.where(lane % TOPK == expert, terms, 0.0), axis=-1, keepdims=True
        )
        first += count
    for tile in range(tiles):
        wait(tile)
        gate, up = (
            jnp.dot(
                rows[...],
                weights[:, (part * tiles + tile) * block : (part * tiles + tile + 1) * block],
                preferred_element_type=jnp.float32,
            )
            for part in range(2)
        )
        units[tile] = (gate / (1.0 + jnp.exp(-gate)) * up).astype(jnp.bfloat16)
    own = lax.axis_index("dp")
    for d in range(4):
        hidden_ref[:, d * block : (d + 1) * block] = units[own ^ d]


def expert_up(rows, weights, width):
    weights, starts = zip(*weights)
    tokens = sum(piece.shape[0] for piece in rows)
    features = sum(piece.shape[0] for piece in weights)
    hidden_size = width // 2
    return pl.pallas_call(
        lambda *refs: up_kernel(len(rows), starts, *refs),
        out_shape=[
            jax.ShapeDtypeStruct((tokens, hidden_size), jnp.bfloat16),
            jax.ShapeDtypeStruct((tokens, 1), jnp.float32),
        ],
        in_specs=vmem(len(rows)) + [pl.BlockSpec(memory_space=pl.ANY)] * len(weights),
        out_specs=vmem(2),
        scratch_shapes=[
            pltpu.VMEM((tokens, features), jnp.bfloat16),
            pltpu.VMEM((features, width), jnp.bfloat16),
            pltpu.VMEM((4, tokens, hidden_size // 4), jnp.bfloat16),
            pltpu.SemaphoreType.DMA((4, len(weights), 2)),
        ],
        compiler_params=params(),
        cost_estimate=SMALL,
        name="expert_up",
    )(*rows, *weights)


def load_rows(pieces, weights, arrived):
    copies, first = [], 0
    for i, ref in enumerate(pieces):
        depth = ref.shape[0]
        copies.append(
            pltpu.make_async_copy(ref, weights.at[pl.ds(first, depth)], arrived.at[i])
        )
        first += depth
    for copy in copies:
        copy.start()
    for copy in copies:
        copy.wait()


def part_kernel(hidden_ref, *refs):
    pieces, (total_ref, weights, arrived) = refs[:-3], refs[-3:]
    load_rows(pieces, weights, arrived)
    total_ref[...] = jnp.dot(
        hidden_ref[:, : weights.shape[0]], weights[...], preferred_element_type=jnp.float32
    )


def down_part(hidden_units, weights):
    depth = sum(piece.shape[0] for piece in weights)
    shape = hidden_units.shape[0], weights[0].shape[1]
    return pl.pallas_call(
        part_kernel,
        out_shape=jax.ShapeDtypeStruct(shape, jnp.float32),
        in_specs=vmem(1) + [pl.BlockSpec(memory_space=pl.ANY)] * len(weights),
        out_specs=pl.BlockSpec(memory_space=pltpu.VMEM),
        scratch_shapes=[
            pltpu.VMEM((depth, shape[1]), jnp.bfloat16),
            pltpu.SemaphoreType.DMA((len(weights),)),
        ],
        compiler_params=params(),
        cost_estimate=SMALL,
        name="down_part",
    )(hidden_units, *weights)


def down_kernel(first, column, sources, hidden_ref, total_ref, gate_ref, piece, *refs):
    outs, (weights, arrived) = refs[:-2], refs[-2:]
    load_rows([piece], weights, arrived)
    depth, width = weights.shape
    units = hidden_ref[:, first : first + depth]
    total = total_ref[:, column : column + width] + jnp.dot(
        units, weights[...], preferred_element_type=jnp.float32
    )
    weighted = (total * gate_ref[...]).astype(jnp.bfloat16)
    rows = weighted.shape[0] // sources
    for (first, count), ref in zip(down_blocks(rows, sources), outs):
        ref[...] = weighted[first : first + count]


def down_blocks(rows, sources):
    half, reach = rows // 2, sources // 2
    blocks = [(0, rows)]
    for step, middle in ((-1, reach * rows), (1, reach * rows + half)):
        blocks.append((middle, half))
        second = (reach + step) * rows
        blocks += [(second, half), (second + half, half)]
        blocks += [((reach + step * away) * rows, rows) for away in range(2, reach)]
    return blocks


def expert_down(hidden_units, total, gates, weights, column, sources):
    tokens, hidden_size = hidden_units.shape
    depth, width = weights.shape
    rows = tokens // sources
    return pl.pallas_call(
        lambda *refs: down_kernel(hidden_size - depth, column, sources, *refs),
        out_shape=[
            jax.ShapeDtypeStruct((count, width), jnp.bfloat16)
            for _, count in down_blocks(rows, sources)
        ],
        in_specs=vmem(3) + [pl.BlockSpec(memory_space=pl.ANY)],
        out_specs=vmem(sources + 3),
        scratch_shapes=[
            pltpu.VMEM((depth, width), jnp.bfloat16),
            pltpu.SemaphoreType.DMA((1,)),
        ],
        compiler_params=params(),
        cost_estimate=SMALL,
        name="expert_down",
    )(hidden_units, total, gates, weights)


def partner(x, distance):
    return lax.ppermute(x, "dp", [(i, i ^ distance) for i in range(4)])


def ring_order(count):
    return list(range(0, count, 2)) + list(range(count - 1, 0, -2))


def around(x, step):
    ring = ring_order(lax.axis_size("expert"))
    count = len(ring)
    return lax.ppermute(x, "expert", [(ring[i], ring[(i + step) % count]) for i in range(count)])


def after(x, *others):
    return lax.optimization_barrier((x, *others))[0]


def add(a, b):
    return (a.astype(jnp.float32) + b.astype(jnp.float32)).astype(jnp.bfloat16)


def gather_rows(halves):
    reach = lax.axis_size("expert") // 2
    above, below = [halves], [halves]
    for _ in range(reach - 1):
        above.append([around(half, -1) for half in above[-1]])
        below.append([around(half, 1) for half in below[-1]])
    far = [around(above[-1][0], -1), around(below[-1][1], 1)]
    rows = [half for pair in (*above, far, *below[:0:-1]) for half in pair]
    return rows, [(*a, *b) for a, b in zip(above[1:], below[1:])] + [tuple(far)]


def scatter_sum(own, *blocks):
    reach = len(blocks) // 2
    terms = [own]
    for step, (far, first, second, *near) in ((1, blocks[:reach]), (-1, blocks[reach:])):
        moving = around(far, step)
        if step > 0:
            moving = jnp.concatenate([add(first, moving), second])
        else:
            moving = jnp.concatenate([first, add(second, moving)])
        for block in near:
            moving = add(block, around(moving, step))
        terms.append(around(moving, step))
    return terms


def relayed(x, rows):
    return [partner(x[i : i + rows], 1) for i in range(0, x.shape[0], rows)]


def every_expert(
    hidden_in,
    queries,
    key_pool,
    value_pool,
    page_table,
    prompt_lengths,
    expert_ids,
    gate_weights,
    norm_gain,
    trainer_gate_up,
    trainer_down,
):
    expert_count = lax.axis_size("expert")
    width = trainer_down.shape[2]
    depth, columns = trainer_gate_up.shape[1:]
    down_depth = trainer_down.shape[1]
    slab = width // SLABS
    early = queries.shape[1] // 4 * FIRST_BLOCKS
    side = [i * columns for i in range(FIRST_BLOCKS)]
    attn_own, attn_beside, first_sent = attention(
        queries,
        key_pool,
        value_pool,
        page_table,
        prompt_lengths,
        trainer_gate_up,
        FIRST_BLOCKS,
    )
    first_across = partner(first_sent, 2)
    gate_up = after(trainer_gate_up, attn_own)
    rest_own, first_own, down_own = cast_rows(
        [gate_up, gate_up, trainer_down],
        [
            (early, depth - early, 0, columns),
            (0, early, 0, columns),
            (0, down_depth, 0, width),
        ],
    )
    attn_beside = partner(attn_beside, 1)
    attn_opposite = partner(first_across[:, -attn_own.shape[1] :], 1)
    rest_across = partner(rest_own, 2)
    resid, *halves = norm(
        after(hidden_in[0], rest_own),
        (attn_own, attn_beside, first_across, attn_opposite),
        norm_gain,
        expert_ids[0],
        gate_weights[0],
    )
    gathered, arrived = gather_rows(halves)
    first_beside = partner(after(first_own, *arrived[0]), 1)
    rest_beside = partner(after(rest_own, *arrived[0]), 1)
    first_ready = after(first_across, *arrived[0])
    first_opposite = [partner(first_ready[:, start : start + columns], 1) for start in side]
    down_beside = partner(after(down_own, *arrived[1]), 1)
    down_across = partner(after(down_own, *arrived[2]), 2)
    rest_opposite = relayed(after(rest_across, *arrived[3]), (depth - early) // 2)
    hidden_units, gates = expert_up(
        gathered,
        [(ref, 0) for ref in (first_own, rest_own, first_beside, rest_beside)]
        + [(first_across, start) for start in side]
        + [(ref, 0) for ref in (rest_across, *first_opposite, *rest_opposite)],
        columns,
    )
    down_ready = after(down_across, hidden_units)
    total = down_part(hidden_units, [down_own, down_beside, down_ready])
    mixed = []
    for first in range(0, width, slab):
        opposite = partner(down_ready[:, first : first + slab], 1)
        weighted = expert_down(hidden_units, total, gates, opposite, first, expert_count)
        sum_here = resid[:, first : first + slab].astype(jnp.float32)
        for term in scatter_sum(*weighted):
            sum_here = sum_here + term.astype(jnp.float32)
        mixed.append(sum_here.astype(jnp.bfloat16))
    return jnp.concatenate(mixed, axis=1)[None]


def solution(mesh):
    placed = (
        P("expert", "dp", None),
        P("expert", None, "dp"),
        P("expert", None, "dp"),
        P("expert", None, "dp"),
        P("expert", None),
        P("expert", None),
        P("expert", "dp", None),
        P("expert", "dp", None),
        P(),
        P("expert", "dp", None),
        P("expert", "dp", None),
    )
    dense = mesh.shape["expert"] == TOPK and mesh.shape["dp"] == 4
    return jax.shard_map(
        every_expert if dense else local, mesh=mesh, in_specs=placed, out_specs=P("expert", "dp", None), check_vma=False
    )
```

```python
import math

import jax
import jax.numpy as jnp
from jax import lax
from jax.experimental import pallas as pl
from jax.experimental.pallas import tpu as pltpu
from jax.sharding import PartitionSpec as P

HDIM = 128
TOPK = 8


epsilon = 1e-05


def fetch_weights(trainer_gate_up, trainer_down):
    return (
        lax.all_gather(trainer_gate_up.astype(jnp.bfloat16), "dp", axis=1, tiled=True),
        lax.all_gather(trainer_down.astype(jnp.bfloat16), "dp", axis=1, tiled=True),
    )


def local(
    hidden_in,
    queries,
    key_pool,
    value_pool,
    page_table,
    prompt_lengths,
    expert_ids,
    gate_weights,
    norm_gain,
    trainer_gate_up,
    trainer_down,
):
    col_tok = queries.shape[1]
    width_dev = queries.shape[2]
    heads_dev = width_dev // HDIM
    keys_all = jnp.take(key_pool, page_table[0], axis=0).reshape(col_tok, heads_dev, HDIM)
    values_all = jnp.take(value_pool, page_table[0], axis=0).reshape(col_tok, heads_dev, HDIM)
    request_ends = jnp.cumsum(prompt_lengths[0])
    positions = lax.iota(jnp.int32, col_tok)
    request = jnp.sum((positions[:, None] >= request_ends[None, :]).astype(jnp.int32), axis=1)
    block_rows = math.gcd(col_tok, 512)
    query_blocks = queries[0].reshape(col_tok // block_rows, block_rows, heads_dev, HDIM)
    request_blocks = request.reshape(col_tok // block_rows, block_rows)
    score_scale = 1.0 / math.sqrt(HDIM)

    def attend(pieces):
        query_block, request_block = pieces
        scores = (
            jnp.einsum("qhd,khd->hqk", query_block, keys_all, preferred_element_type=jnp.float32)
            * score_scale
        )
        same_request = (request_block[:, None] == request[None, :])[None]
        scores = jnp.where(same_request, scores, -1e30)
        highest = jnp.max(scores, axis=-1, keepdims=True)
        weights = jnp.where(same_request, jnp.exp(scores - highest), 0.0)
        totals = jnp.sum(weights, axis=-1, keepdims=True)
        probs = (weights / totals).astype(jnp.bfloat16)
        output = jnp.einsum("hqk,khd->qhd", probs, values_all, preferred_element_type=jnp.float32)
        return output.astype(jnp.bfloat16).reshape(block_rows, width_dev)

    attn_heads = lax.map(attend, (query_blocks, request_blocks)).reshape(1, col_tok, width_dev)
    attn_tokens = lax.all_to_all(attn_heads, "dp", split_axis=1, concat_axis=2, tiled=True)
    resid32 = (
        (hidden_in.astype(jnp.float32) + attn_tokens.astype(jnp.float32))
        .astype(jnp.bfloat16)
        .astype(jnp.float32)
    )
    mean_square = jnp.mean(resid32 * resid32, axis=-1, keepdims=True)
    normed = (resid32 * lax.rsqrt(mean_square + epsilon) * norm_gain).astype(jnp.bfloat16)
    server_gate_up, server_down = fetch_weights(trainer_gate_up, trainer_down)
    token_rows = normed.shape[1]
    width = normed.shape[2]
    expert_count = lax.axis_size("expert")
    capacity = min(token_rows, token_rows * TOPK * 5 // (4 * expert_count))
    hidden_size = server_gate_up.shape[2] // 2
    ids_flat = expert_ids[0].reshape(token_rows * TOPK)
    onehot = (ids_flat[:, None] == lax.iota(jnp.int32, expert_count)[None, :]).astype(jnp.int32)
    earlier = jnp.cumsum(onehot, axis=0) - onehot
    slot_index = jnp.sum(earlier * onehot, axis=1)
    flat_slot = ids_flat * capacity + slot_index
    placement = (
        flat_slot[:, None] == lax.iota(jnp.int32, expert_count * capacity)[None, :]
    ).astype(jnp.bfloat16)
    dispatch_matrix = jnp.sum(placement.reshape(token_rows, TOPK, expert_count * capacity), axis=1)
    outgoing = jnp.einsum(
        "ts,td->sd", dispatch_matrix, normed[0], preferred_element_type=jnp.float32
    )
    outgoing = outgoing.astype(jnp.bfloat16).reshape(expert_count, capacity, width)
    received = lax.all_to_all(outgoing, "expert", split_axis=0, concat_axis=0, tiled=True)
    sources, items, features = received.shape
    slot_rows = received.reshape(sources * items, features)
    gate_up = jnp.dot(slot_rows, server_gate_up[0], preferred_element_type=jnp.float32)
    hidden_units = (jax.nn.silu(gate_up[:, :hidden_size]) * gate_up[:, hidden_size:]).astype(
        jnp.bfloat16
    )
    outputs = jnp.dot(hidden_units, server_down[0], preferred_element_type=jnp.float32).astype(
        jnp.bfloat16
    )
    returned = lax.all_to_all(
        outputs.reshape(sources, items, features), "expert", split_axis=0, concat_axis=0, tiled=True
    )
    copies = jnp.take(returned.reshape(expert_count * capacity, width), flat_slot, axis=0)
    copies = copies.reshape(token_rows, TOPK, width).astype(jnp.float32)
    mixture = jnp.einsum("tk,tkd->td", gate_weights[0], copies)
    mixed = resid32[0] + mixture
    return mixed.astype(jnp.bfloat16)[None]

LANES = 128
VMEM_LIMIT = 32 * 2**20
VMEM_MOST = 60 * 2**20
CAST_STEPS = 4
FIRST_BLOCKS = 2
SLABS = 2
SMALL = pl.CostEstimate(flops=1, bytes_accessed=1, transcendentals=0)


def params(limit=VMEM_LIMIT):
    return pltpu.CompilerParams(vmem_limit_bytes=limit)


def vmem(count):
    return [pl.BlockSpec(memory_space=pltpu.VMEM)] * count


def attention_kernel(*refs):
    sources, outs, scratch = refs[:6], refs[6:9], refs[9:]
    own_ref, beside_ref, sent_ref = outs
    table, lengths, q_ref, k_ref, v_ref, weights, attn, arrived = scratch
    copies = [
        pltpu.make_async_copy(source, target, arrived.at[i])
        for i, (source, target) in enumerate(
            zip(
                (*sources[:2], sources[2].at[0], *sources[3:5]),
                (table, lengths, q_ref, k_ref, v_ref),
            )
        )
    ]
    rows = weights.shape[0]
    copies.append(
        pltpu.make_async_copy(sources[5].at[0, pl.ds(0, rows)], weights, arrived.at[5])
    )
    for copy in copies:
        copy.start()
    for copy in copies[:5]:
        copy.wait()
    tokens, width = q_ref.shape
    pages = k_ref.shape[0]
    row = lax.broadcasted_iota(jnp.int32, (tokens, 1), 0)
    column = lax.broadcasted_iota(jnp.int32, (1, tokens), 1)
    row_request = jnp.zeros((tokens, 1), jnp.int32)
    column_request = jnp.zeros((1, tokens), jnp.int32)
    end = jnp.int32(0)
    for r in range(lengths.shape[1]):
        end = end + lengths[0, r]
        row_request += (row >= end).astype(jnp.int32)
        column_request += (column >= end).astype(jnp.int32)
    same = row_request == column_request
    for h in range(width // HDIM):
        lanes = slice(h * HDIM, (h + 1) * HDIM)
        keys = jnp.concatenate([k_ref[table[0, p], :, lanes] for p in range(pages)], axis=0)
        values = jnp.concatenate([v_ref[table[0, p], :, lanes] for p in range(pages)], axis=0)
        scores = lax.dot_general(
            q_ref[:, lanes], keys, (((1,), (1,)), ((), ())), preferred_element_type=jnp.float32
        ) * (1.0 / math.sqrt(HDIM))
        scores = jnp.where(same, scores, -1e30)
        highest = jnp.max(scores, axis=-1, keepdims=True)
        weight = jnp.exp(scores - highest)
        share = 1.0 / jnp.sum(weight, axis=-1, keepdims=True)
        probs = (weight * share).astype(jnp.bfloat16)
        attn[:, lanes] = jnp.dot(probs, values, preferred_element_type=jnp.float32).astype(
            jnp.bfloat16
        )
    own = lax.axis_index("dp")
    block = tokens // 4
    split = weights.shape[1]
    end = sent_ref.shape[1]
    targets = (
        own_ref,
        beside_ref,
        sent_ref.at[:, end - 2 * width : end - width],
        sent_ref.at[:, end - width :],
    )
    for d, target in enumerate(targets):
        target[...] = attn[pl.ds(pl.multiple_of((own ^ d) * block, block), block), :]
    copies[5].wait()
    for i in range(rows // block):
        here = slice(i * block, (i + 1) * block)
        sent_ref[:, i * split : (i + 1) * split] = weights[here].astype(jnp.bfloat16)


def attention(queries, key_pool, value_pool, page_table, prompt_lengths, gate_up, blocks):
    tokens, width = queries.shape[1:]
    split = gate_up.shape[2]
    block = tokens // 4
    shapes = [(block, width)] * 2
    shapes.append((block, blocks * split + 2 * width))
    return pl.pallas_call(
        attention_kernel,
        out_shape=[jax.ShapeDtypeStruct(shape, jnp.bfloat16) for shape in shapes],
        in_specs=[pl.BlockSpec(memory_space=pltpu.HBM)] * 6,
        out_specs=vmem(3),
        scratch_shapes=[
            pltpu.SMEM(page_table.shape, jnp.int32),
            pltpu.SMEM(prompt_lengths.shape, jnp.int32),
            pltpu.VMEM((tokens, width), jnp.bfloat16),
            pltpu.VMEM(key_pool.shape, jnp.bfloat16),
            pltpu.VMEM(value_pool.shape, jnp.bfloat16),
            pltpu.VMEM((blocks * block, split), jnp.float32),
            pltpu.VMEM((tokens, width), jnp.bfloat16),
            pltpu.SemaphoreType.DMA((6,)),
        ],
        compiler_params=params(VMEM_MOST),
        name="attention",
    )(page_table, prompt_lengths, queries, key_pool, value_pool, gate_up)


def norm_kernel(*refs):
    sources, outs, scratch = refs[:8], refs[8:11], refs[11:]
    a0, a1, a2, a3, hidden_ref, gain_ref, ids_ref, gates_ref, arrived = scratch
    resid_ref, row_refs = outs[0], outs[1:]
    across, block = sources[2], a2.shape[1]
    across = across.at[:, pl.ds(across.shape[1] - 2 * block, block)]
    copies = [
        pltpu.make_async_copy(source, target, arrived.at[i])
        for i, (source, target) in enumerate(zip((*sources[:2], across, *sources[3:]), scratch))
    ]
    for copy in copies:
        copy.start()
    for copy in copies:
        copy.wait()
    own = lax.axis_index("dp")
    tokens, width = hidden_ref.shape
    total = jnp.zeros((tokens, 1), jnp.float32)
    for d, attn in enumerate((a0, a1, a2, a3)):
        columns = pl.ds(pl.multiple_of((own ^ d) * block, block), block)
        resid = (
            hidden_ref[:, columns].astype(jnp.float32) + attn[...].astype(jnp.float32)
        ).astype(jnp.bfloat16)
        resid_ref[:, columns] = resid
        resid32 = resid.astype(jnp.float32)
        total += jnp.sum(resid32 * resid32, axis=-1, keepdims=True)
    inverse = lax.rsqrt(total / width + epsilon)
    halves = [slice(i * tokens // 2, (i + 1) * tokens // 2) for i in range(2)]
    for d in range(4):
        columns = pl.ds(pl.multiple_of((own ^ d) * block, block), block)
        normed = resid_ref[:, columns].astype(jnp.float32) * inverse * gain_ref[:, columns]
        for here, ref in zip(halves, row_refs):
            ref[:, d * block : (d + 1) * block] = normed[here].astype(jnp.bfloat16)
    place = lax.broadcasted_iota(jnp.int32, (LANES, tokens), 0)
    gates = jnp.zeros((LANES, tokens), jnp.float32)
    for k in range(TOPK):
        gates += jnp.where(ids_ref[k : k + 1] == place % TOPK, gates_ref[k : k + 1], 0.0)
    high = gates.astype(jnp.bfloat16).astype(jnp.float32)
    middle = (gates - high).astype(jnp.bfloat16).astype(jnp.float32)
    low = gates - high - middle
    part = place // TOPK
    terms = jnp.where(part == 0, high, jnp.where(part == 1, middle, jnp.where(part == 2, low, 0.0)))
    terms = jnp.transpose(terms)
    for here, ref in zip(halves, row_refs):
        ref[:, width:] = terms[here].astype(jnp.bfloat16)


def norm(hidden_in, attn, norm_gain, expert_ids, gate_weights):
    tokens, width = hidden_in.shape
    operands = hidden_in, norm_gain[None, :], expert_ids.T, gate_weights.T
    return pl.pallas_call(
        norm_kernel,
        out_shape=[
            jax.ShapeDtypeStruct((tokens, width), jnp.bfloat16),
        ]
        + [jax.ShapeDtypeStruct((tokens // 2, width + LANES), jnp.bfloat16)] * 2,
        in_specs=[pl.BlockSpec(memory_space=pl.ANY)] * 8,
        out_specs=vmem(3),
        scratch_shapes=[pltpu.VMEM(attn[0].shape, jnp.bfloat16)] * 4
        + [pltpu.VMEM(x.shape, x.dtype) for x in operands]
        + [pltpu.SemaphoreType.DMA((8,))],
        compiler_params=params(),
        cost_estimate=SMALL,
        name="norm",
    )(*attn, *operands)


def cast_kernel(spans, *refs):
    count = len(spans)
    sources, targets, scratch = refs[:count], refs[count : 2 * count], refs[2 * count :]
    wide, narrow, arrived, left = scratch[:count], scratch[count : 2 * count], *scratch[-2:]

    def rows_of(i, step, first=0):
        rows = wide[i].shape[0] // CAST_STEPS
        return pl.ds(first + step * rows, rows)

    def copies_in(step):
        for i, (first, _, column, columns) in enumerate(spans):
            yield pltpu.make_async_copy(
                sources[i].at[0, rows_of(i, step, first), pl.ds(column, columns)],
                wide[i].at[rows_of(i, step)],
                arrived.at[step, i],
            )

    def copies_out(step):
        for i in range(count):
            here = rows_of(i, step)
            yield pltpu.make_async_copy(narrow[i].at[here], targets[i].at[here], left.at[step, i])

    for step in range(CAST_STEPS):
        for copy in copies_in(step):
            copy.start()
    for step in range(CAST_STEPS):
        for copy in copies_in(step):
            copy.wait()
        for i in range(count):
            here = rows_of(i, step)
            narrow[i][here] = wide[i][here].astype(jnp.bfloat16)
        for copy in copies_out(step):
            copy.start()
    for step in range(CAST_STEPS):
        for copy in copies_out(step):
            copy.wait()


def cast_rows(arrays, spans):
    shapes = [(rows, columns) for _, rows, _, columns in spans]
    return pl.pallas_call(
        lambda *refs: cast_kernel(spans, *refs),
        out_shape=[jax.ShapeDtypeStruct(shape, jnp.bfloat16) for shape in shapes],
        in_specs=[pl.BlockSpec(memory_space=pltpu.HBM)] * len(arrays),
        out_specs=[pl.BlockSpec(memory_space=pltpu.HBM)] * len(arrays),
        scratch_shapes=[pltpu.VMEM(shape, jnp.float32) for shape in shapes]
        + [pltpu.VMEM(shape, jnp.bfloat16) for shape in shapes]
        + [pltpu.SemaphoreType.DMA((CAST_STEPS, len(arrays)))] * 2,
        compiler_params=params(VMEM_MOST),
        name="cast_rows",
    )(*arrays)


def load_tiles(pieces, starts, weights, arrived, tiles, block):
    def copies(tile):
        first = 0
        for index, (piece, start) in enumerate(zip(pieces, starts)):
            depth = piece.shape[0]
            for part in range(2):
                column = (part * tiles + tile) * block
                yield pltpu.make_async_copy(
                    piece.at[:, pl.ds(start + column, block)],
                    weights.at[pl.ds(first, depth), pl.ds(column, block)],
                    arrived.at[tile, index, part],
                )
            first += depth

    for tile in range(tiles):
        for copy in copies(tile):
            copy.start()

    def wait(tile):
        for copy in copies(tile):
            copy.wait()

    return wait


def up_kernel(sources, starts, *refs):
    pieces = len(starts)
    row_refs = refs[:sources]
    weight_refs = refs[sources : sources + pieces]
    hidden_ref, own_gate_ref, rows, weights, units, arrived = refs[sources + pieces :]
    width = rows.shape[1]
    tiles, _, block = units.shape
    wait = load_tiles(weight_refs, starts, weights, arrived, tiles, block)
    expert = lax.axis_index("expert")
    first = 0
    for ref in row_refs:
        count = ref.shape[0]
        here = slice(first, first + count)
        rows[here, :] = ref[:, :width]
        terms = ref[:, width:].astype(jnp.float32)
        lane = lax.broadcasted_iota(jnp.int32, terms.shape, 1)
        own_gate_ref[here, :] = jnp.sum(
            jnp.where(lane % TOPK == expert, terms, 0.0), axis=-1, keepdims=True
        )
        first += count
    for tile in range(tiles):
        wait(tile)
        gate, up = (
            jnp.dot(
                rows[...],
                weights[:, (part * tiles + tile) * block : (part * tiles + tile + 1) * block],
                preferred_element_type=jnp.float32,
            )
            for part in range(2)
        )
        units[tile] = (gate / (1.0 + jnp.exp(-gate)) * up).astype(jnp.bfloat16)
    own = lax.axis_index("dp")
    for d in range(4):
        hidden_ref[:, d * block : (d + 1) * block] = units[own ^ d]


def expert_up(rows, weights, width):
    weights, starts = zip(*weights)
    tokens = sum(piece.shape[0] for piece in rows)
    features = sum(piece.shape[0] for piece in weights)
    hidden_size = width // 2
    return pl.pallas_call(
        lambda *refs: up_kernel(len(rows), starts, *refs),
        out_shape=[
            jax.ShapeDtypeStruct((tokens, hidden_size), jnp.bfloat16),
            jax.ShapeDtypeStruct((tokens, 1), jnp.float32),
        ],
        in_specs=vmem(len(rows)) + [pl.BlockSpec(memory_space=pl.ANY)] * len(weights),
        out_specs=vmem(2),
        scratch_shapes=[
            pltpu.VMEM((tokens, features), jnp.bfloat16),
            pltpu.VMEM((features, width), jnp.bfloat16),
            pltpu.VMEM((4, tokens, hidden_size // 4), jnp.bfloat16),
            pltpu.SemaphoreType.DMA((4, len(weights), 2)),
        ],
        compiler_params=params(),
        cost_estimate=SMALL,
        name="expert_up",
    )(*rows, *weights)


def load_rows(pieces, weights, arrived):
    copies, first = [], 0
    for i, ref in enumerate(pieces):
        depth = ref.shape[0]
        copies.append(
            pltpu.make_async_copy(ref, weights.at[pl.ds(first, depth)], arrived.at[i])
        )
        first += depth
    for copy in copies:
        copy.start()
    for copy in copies:
        copy.wait()


def part_kernel(hidden_ref, *refs):
    pieces, (total_ref, weights, arrived) = refs[:-3], refs[-3:]
    load_rows(pieces, weights, arrived)
    total_ref[...] = jnp.dot(
        hidden_ref[:, : weights.shape[0]], weights[...], preferred_element_type=jnp.float32
    )


def down_part(hidden_units, weights):
    depth = sum(piece.shape[0] for piece in weights)
    shape = hidden_units.shape[0], weights[0].shape[1]
    return pl.pallas_call(
        part_kernel,
        out_shape=jax.ShapeDtypeStruct(shape, jnp.float32),
        in_specs=vmem(1) + [pl.BlockSpec(memory_space=pl.ANY)] * len(weights),
        out_specs=pl.BlockSpec(memory_space=pltpu.VMEM),
        scratch_shapes=[
            pltpu.VMEM((depth, shape[1]), jnp.bfloat16),
            pltpu.SemaphoreType.DMA((len(weights),)),
        ],
        compiler_params=params(),
        cost_estimate=SMALL,
        name="down_part",
    )(hidden_units, *weights)


def down_kernel(first, column, sources, hidden_ref, total_ref, gate_ref, piece, *refs):
    outs, (weights, arrived) = refs[:-2], refs[-2:]
    load_rows([piece], weights, arrived)
    depth, width = weights.shape
    units = hidden_ref[:, first : first + depth]
    total = total_ref[:, column : column + width] + jnp.dot(
        units, weights[...], preferred_element_type=jnp.float32
    )
    weighted = (total * gate_ref[...]).astype(jnp.bfloat16)
    rows = weighted.shape[0] // sources
    for (first, count), ref in zip(down_blocks(rows, sources), outs):
        ref[...] = weighted[first : first + count]


def down_blocks(rows, sources):
    half, reach = rows // 2, sources // 2
    blocks = [(0, rows)]
    for step, middle in ((-1, reach * rows), (1, reach * rows + half)):
        blocks.append((middle, half))
        second = (reach + step) * rows
        blocks += [(second, half), (second + half, half)]
        blocks += [((reach + step * away) * rows, rows) for away in range(2, reach)]
    return blocks


def expert_down(hidden_units, total, gates, weights, column, sources):
    tokens, hidden_size = hidden_units.shape
    depth, width = weights.shape
    rows = tokens // sources
    return pl.pallas_call(
        lambda *refs: down_kernel(hidden_size - depth, column, sources, *refs),
        out_shape=[
            jax.ShapeDtypeStruct((count, width), jnp.bfloat16)
            for _, count in down_blocks(rows, sources)
        ],
        in_specs=vmem(3) + [pl.BlockSpec(memory_space=pl.ANY)],
        out_specs=vmem(sources + 3),
        scratch_shapes=[
            pltpu.VMEM((depth, width), jnp.bfloat16),
            pltpu.SemaphoreType.DMA((1,)),
        ],
        compiler_params=params(),
        cost_estimate=SMALL,
        name="expert_down",
    )(hidden_units, total, gates, weights)


def partner(x, distance):
    return lax.ppermute(x, "dp", [(i, i ^ distance) for i in range(4)])


def ring_order(count):
    return list(range(0, count, 2)) + list(range(count - 1, 0, -2))


def around(x, step):
    ring = ring_order(lax.axis_size("expert"))
    count = len(ring)
    return lax.ppermute(x, "expert", [(ring[i], ring[(i + step) % count]) for i in range(count)])


def after(x, *others):
    return lax.optimization_barrier((x, *others))[0]


def add(a, b):
    return (a.astype(jnp.float32) + b.astype(jnp.float32)).astype(jnp.bfloat16)


def gather_rows(halves):
    reach = lax.axis_size("expert") // 2
    above, below = [halves], [halves]
    for _ in range(reach - 1):
        above.append([around(half, -1) for half in above[-1]])
        below.append([around(half, 1) for half in below[-1]])
    far = [around(above[-1][0], -1), around(below[-1][1], 1)]
    rows = [half for pair in (*above, far, *below[:0:-1]) for half in pair]
    return rows, [(*a, *b) for a, b in zip(above[1:], below[1:])] + [tuple(far)]


def scatter_sum(own, *blocks):
    reach = len(blocks) // 2
    terms = [own]
    for step, (far, first, second, *near) in ((1, blocks[:reach]), (-1, blocks[reach:])):
        moving = around(far, step)
        if step > 0:
            moving = jnp.concatenate([add(first, moving), second])
        else:
            moving = jnp.concatenate([first, add(second, moving)])
        for block in near:
            moving = add(block, around(moving, step))
        terms.append(around(moving, step))
    return terms


def relayed(x, rows):
    return [partner(x[i : i + rows], 1) for i in range(0, x.shape[0], rows)]


def mix_kernel(resid_ref, *refs):
    terms, out_ref = refs[:-1], refs[-1]
    first = 0
    for i in range(0, len(terms), 3):
        columns = slice(first, first + terms[i].shape[1])
        total = resid_ref[:, columns].astype(jnp.float32)
        for ref in terms[i : i + 3]:
            total += ref[...].astype(jnp.float32)
        out_ref[0, :, columns] = total.astype(jnp.bfloat16)
        first = columns.stop


def mix(resid, halves):
    terms = [term for half in halves for term in half]
    return pl.pallas_call(
        mix_kernel,
        out_shape=jax.ShapeDtypeStruct((1, *resid.shape), jnp.bfloat16),
        in_specs=vmem(1 + len(terms)),
        out_specs=pl.BlockSpec(memory_space=pltpu.VMEM),
        compiler_params=params(),
        cost_estimate=SMALL,
        name="mix",
    )(resid, *terms)


def every_expert(
    hidden_in,
    queries,
    key_pool,
    value_pool,
    page_table,
    prompt_lengths,
    expert_ids,
    gate_weights,
    norm_gain,
    trainer_gate_up,
    trainer_down,
):
    expert_count = lax.axis_size("expert")
    width = trainer_down.shape[2]
    depth, columns = trainer_gate_up.shape[1:]
    down_depth = trainer_down.shape[1]
    slab = width // SLABS
    early = queries.shape[1] // 4 * FIRST_BLOCKS
    side = [i * columns for i in range(FIRST_BLOCKS)]
    attn_own, attn_beside, first_sent = attention(
        queries,
        key_pool,
        value_pool,
        page_table,
        prompt_lengths,
        trainer_gate_up,
        FIRST_BLOCKS,
    )
    first_across = partner(first_sent, 2)
    gate_up = after(trainer_gate_up, attn_own)
    rest_own, first_own, down_own = cast_rows(
        [gate_up, gate_up, trainer_down],
        [
            (early, depth - early, 0, columns),
            (0, early, 0, columns),
            (0, down_depth, 0, width),
        ],
    )
    attn_beside = partner(attn_beside, 1)
    attn_opposite = partner(first_across[:, -attn_own.shape[1] :], 1)
    rest_across = partner(rest_own, 2)
    resid, *halves = norm(
        after(hidden_in[0], rest_own),
        (attn_own, attn_beside, first_across, attn_opposite),
        norm_gain,
        expert_ids[0],
        gate_weights[0],
    )
    gathered, arrived = gather_rows(halves)
    first_beside = partner(after(first_own, *arrived[0]), 1)
    rest_beside = partner(after(rest_own, *arrived[0]), 1)
    first_ready = after(first_across, *arrived[0])
    first_opposite = [partner(first_ready[:, start : start + columns], 1) for start in side]
    down_beside = partner(after(down_own, *arrived[1]), 1)
    down_across = partner(after(down_own, *arrived[2]), 2)
    rest_opposite = relayed(after(rest_across, *arrived[3]), (depth - early) // 2)
    hidden_units, gates = expert_up(
        gathered,
        [(ref, 0) for ref in (first_own, rest_own, first_beside, rest_beside)]
        + [(first_across, start) for start in side]
        + [(ref, 0) for ref in (rest_across, *first_opposite, *rest_opposite)],
        columns,
    )
    down_ready = after(down_across, hidden_units)
    total = down_part(hidden_units, [down_own, down_beside, down_ready])
    mixed = []
    for first in range(0, width, slab):
        opposite = partner(down_ready[:, first : first + slab], 1)
        weighted = expert_down(hidden_units, total, gates, opposite, first, expert_count)
        mixed.append(scatter_sum(*weighted))
    return mix(resid, mixed)


def solution(mesh):
    placed = (
        P("expert", "dp", None),
        P("expert", None, "dp"),
        P("expert", None, "dp"),
        P("expert", None, "dp"),
        P("expert", None),
        P("expert", None),
        P("expert", "dp", None),
        P("expert", "dp", None),
        P(),
        P("expert", "dp", None),
        P("expert", "dp", None),
    )
    dense = mesh.shape["expert"] == TOPK and mesh.shape["dp"] == 4
    return jax.shard_map(
        every_expert if dense else local, mesh=mesh, in_specs=placed, out_specs=P("expert", "dp", None), check_vma=False
    )
```

```python
import math

import jax
import jax.numpy as jnp
from jax import lax
from jax.experimental import pallas as pl
from jax.experimental.pallas import tpu as pltpu
from jax.sharding import PartitionSpec as P

HDIM = 128
TOPK = 8


epsilon = 1e-05


def fetch_weights(trainer_gate_up, trainer_down):
    return (
        lax.all_gather(trainer_gate_up.astype(jnp.bfloat16), "dp", axis=1, tiled=True),
        lax.all_gather(trainer_down.astype(jnp.bfloat16), "dp", axis=1, tiled=True),
    )


def local(
    hidden_in,
    queries,
    key_pool,
    value_pool,
    page_table,
    prompt_lengths,
    expert_ids,
    gate_weights,
    norm_gain,
    trainer_gate_up,
    trainer_down,
):
    col_tok = queries.shape[1]
    width_dev = queries.shape[2]
    heads_dev = width_dev // HDIM
    keys_all = jnp.take(key_pool, page_table[0], axis=0).reshape(col_tok, heads_dev, HDIM)
    values_all = jnp.take(value_pool, page_table[0], axis=0).reshape(col_tok, heads_dev, HDIM)
    request_ends = jnp.cumsum(prompt_lengths[0])
    positions = lax.iota(jnp.int32, col_tok)
    request = jnp.sum((positions[:, None] >= request_ends[None, :]).astype(jnp.int32), axis=1)
    block_rows = math.gcd(col_tok, 512)
    query_blocks = queries[0].reshape(col_tok // block_rows, block_rows, heads_dev, HDIM)
    request_blocks = request.reshape(col_tok // block_rows, block_rows)
    score_scale = 1.0 / math.sqrt(HDIM)

    def attend(pieces):
        query_block, request_block = pieces
        scores = (
            jnp.einsum("qhd,khd->hqk", query_block, keys_all, preferred_element_type=jnp.float32)
            * score_scale
        )
        same_request = (request_block[:, None] == request[None, :])[None]
        scores = jnp.where(same_request, scores, -1e30)
        highest = jnp.max(scores, axis=-1, keepdims=True)
        weights = jnp.where(same_request, jnp.exp(scores - highest), 0.0)
        totals = jnp.sum(weights, axis=-1, keepdims=True)
        probs = (weights / totals).astype(jnp.bfloat16)
        output = jnp.einsum("hqk,khd->qhd", probs, values_all, preferred_element_type=jnp.float32)
        return output.astype(jnp.bfloat16).reshape(block_rows, width_dev)

    attn_heads = lax.map(attend, (query_blocks, request_blocks)).reshape(1, col_tok, width_dev)
    attn_tokens = lax.all_to_all(attn_heads, "dp", split_axis=1, concat_axis=2, tiled=True)
    resid32 = (
        (hidden_in.astype(jnp.float32) + attn_tokens.astype(jnp.float32))
        .astype(jnp.bfloat16)
        .astype(jnp.float32)
    )
    mean_square = jnp.mean(resid32 * resid32, axis=-1, keepdims=True)
    normed = (resid32 * lax.rsqrt(mean_square + epsilon) * norm_gain).astype(jnp.bfloat16)
    server_gate_up, server_down = fetch_weights(trainer_gate_up, trainer_down)
    token_rows = normed.shape[1]
    width = normed.shape[2]
    expert_count = lax.axis_size("expert")
    capacity = min(token_rows, token_rows * TOPK * 5 // (4 * expert_count))
    hidden_size = server_gate_up.shape[2] // 2
    ids_flat = expert_ids[0].reshape(token_rows * TOPK)
    onehot = (ids_flat[:, None] == lax.iota(jnp.int32, expert_count)[None, :]).astype(jnp.int32)
    earlier = jnp.cumsum(onehot, axis=0) - onehot
    slot_index = jnp.sum(earlier * onehot, axis=1)
    flat_slot = ids_flat * capacity + slot_index
    placement = (
        flat_slot[:, None] == lax.iota(jnp.int32, expert_count * capacity)[None, :]
    ).astype(jnp.bfloat16)
    dispatch_matrix = jnp.sum(placement.reshape(token_rows, TOPK, expert_count * capacity), axis=1)
    outgoing = jnp.einsum(
        "ts,td->sd", dispatch_matrix, normed[0], preferred_element_type=jnp.float32
    )
    outgoing = outgoing.astype(jnp.bfloat16).reshape(expert_count, capacity, width)
    received = lax.all_to_all(outgoing, "expert", split_axis=0, concat_axis=0, tiled=True)
    sources, items, features = received.shape
    slot_rows = received.reshape(sources * items, features)
    gate_up = jnp.dot(slot_rows, server_gate_up[0], preferred_element_type=jnp.float32)
    hidden_units = (jax.nn.silu(gate_up[:, :hidden_size]) * gate_up[:, hidden_size:]).astype(
        jnp.bfloat16
    )
    outputs = jnp.dot(hidden_units, server_down[0], preferred_element_type=jnp.float32).astype(
        jnp.bfloat16
    )
    returned = lax.all_to_all(
        outputs.reshape(sources, items, features), "expert", split_axis=0, concat_axis=0, tiled=True
    )
    copies = jnp.take(returned.reshape(expert_count * capacity, width), flat_slot, axis=0)
    copies = copies.reshape(token_rows, TOPK, width).astype(jnp.float32)
    mixture = jnp.einsum("tk,tkd->td", gate_weights[0], copies)
    mixed = resid32[0] + mixture
    return mixed.astype(jnp.bfloat16)[None]

LANES = 128
VMEM_LIMIT = 32 * 2**20
VMEM_MOST = 60 * 2**20
CAST_STEPS = 4
FIRST_BLOCKS = 2
SLABS = 2
SMALL = pl.CostEstimate(flops=1, bytes_accessed=1, transcendentals=0)


def params(limit=VMEM_LIMIT):
    return pltpu.CompilerParams(vmem_limit_bytes=limit)


def vmem(count):
    return [pl.BlockSpec(memory_space=pltpu.VMEM)] * count


def attention_kernel(*refs):
    sources, outs, scratch = refs[:6], refs[6:9], refs[9:]
    own_ref, beside_ref, sent_ref = outs
    table, lengths, q_ref, k_ref, v_ref, weights, attn, arrived = scratch
    copies = [
        pltpu.make_async_copy(source, target, arrived.at[i])
        for i, (source, target) in enumerate(
            zip(
                (*sources[:2], sources[2].at[0], *sources[3:5]),
                (table, lengths, q_ref, k_ref, v_ref),
            )
        )
    ]
    rows = weights.shape[0]
    copies.append(
        pltpu.make_async_copy(sources[5].at[0, pl.ds(0, rows)], weights, arrived.at[5])
    )
    for copy in copies:
        copy.start()
    for copy in copies[:5]:
        copy.wait()
    tokens, width = q_ref.shape
    pages = k_ref.shape[0]
    row = lax.broadcasted_iota(jnp.int32, (tokens, 1), 0)
    column = lax.broadcasted_iota(jnp.int32, (1, tokens), 1)
    row_request = jnp.zeros((tokens, 1), jnp.int32)
    column_request = jnp.zeros((1, tokens), jnp.int32)
    end = jnp.int32(0)
    for r in range(lengths.shape[1]):
        end = end + lengths[0, r]
        row_request += (row >= end).astype(jnp.int32)
        column_request += (column >= end).astype(jnp.int32)
    same = row_request == column_request
    for h in range(width // HDIM):
        lanes = slice(h * HDIM, (h + 1) * HDIM)
        keys = jnp.concatenate([k_ref[table[0, p], :, lanes] for p in range(pages)], axis=0)
        values = jnp.concatenate([v_ref[table[0, p], :, lanes] for p in range(pages)], axis=0)
        scores = lax.dot_general(
            q_ref[:, lanes], keys, (((1,), (1,)), ((), ())), preferred_element_type=jnp.float32
        ) * (1.0 / math.sqrt(HDIM))
        scores = jnp.where(same, scores, -1e30)
        highest = jnp.max(scores, axis=-1, keepdims=True)
        weight = jnp.exp(scores - highest)
        share = 1.0 / jnp.sum(weight, axis=-1, keepdims=True)
        probs = (weight * share).astype(jnp.bfloat16)
        attn[:, lanes] = jnp.dot(probs, values, preferred_element_type=jnp.float32).astype(
            jnp.bfloat16
        )
    own = lax.axis_index("dp")
    block = tokens // 4
    split = weights.shape[1]
    end = sent_ref.shape[1]
    targets = (
        own_ref,
        beside_ref,
        sent_ref.at[:, end - 2 * width : end - width],
        sent_ref.at[:, end - width :],
    )
    for d, target in enumerate(targets):
        target[...] = attn[pl.ds(pl.multiple_of((own ^ d) * block, block), block), :]
    copies[5].wait()
    for i in range(rows // block):
        here = slice(i * block, (i + 1) * block)
        sent_ref[:, i * split : (i + 1) * split] = weights[here].astype(jnp.bfloat16)


def attention(queries, key_pool, value_pool, page_table, prompt_lengths, gate_up, blocks):
    tokens, width = queries.shape[1:]
    split = gate_up.shape[2]
    block = tokens // 4
    shapes = [(block, width)] * 2
    shapes.append((block, blocks * split + 2 * width))
    return pl.pallas_call(
        attention_kernel,
        out_shape=[jax.ShapeDtypeStruct(shape, jnp.bfloat16) for shape in shapes],
        in_specs=[pl.BlockSpec(memory_space=pltpu.HBM)] * 6,
        out_specs=vmem(3),
        scratch_shapes=[
            pltpu.SMEM(page_table.shape, jnp.int32),
            pltpu.SMEM(prompt_lengths.shape, jnp.int32),
            pltpu.VMEM((tokens, width), jnp.bfloat16),
            pltpu.VMEM(key_pool.shape, jnp.bfloat16),
            pltpu.VMEM(value_pool.shape, jnp.bfloat16),
            pltpu.VMEM((blocks * block, split), jnp.float32),
            pltpu.VMEM((tokens, width), jnp.bfloat16),
            pltpu.SemaphoreType.DMA((6,)),
        ],
        compiler_params=params(VMEM_MOST),
        name="attention",
    )(page_table, prompt_lengths, queries, key_pool, value_pool, gate_up)


def norm_kernel(*refs):
    sources, outs, scratch = refs[:8], refs[8:11], refs[11:]
    a0, a1, a2, a3, hidden_ref, gain_ref, ids_ref, gates_ref, arrived = scratch
    resid_ref, row_refs = outs[0], outs[1:]
    across, block = sources[2], a2.shape[1]
    across = across.at[:, pl.ds(across.shape[1] - 2 * block, block)]
    copies = [
        pltpu.make_async_copy(source, target, arrived.at[i])
        for i, (source, target) in enumerate(zip((*sources[:2], across, *sources[3:]), scratch))
    ]
    for copy in copies:
        copy.start()
    for copy in copies:
        copy.wait()
    own = lax.axis_index("dp")
    tokens, width = hidden_ref.shape
    total = jnp.zeros((tokens, 1), jnp.float32)
    for d, attn in enumerate((a0, a1, a2, a3)):
        columns = pl.ds(pl.multiple_of((own ^ d) * block, block), block)
        resid = (
            hidden_ref[:, columns].astype(jnp.float32) + attn[...].astype(jnp.float32)
        ).astype(jnp.bfloat16)
        resid_ref[:, columns] = resid
        resid32 = resid.astype(jnp.float32)
        total += jnp.sum(resid32 * resid32, axis=-1, keepdims=True)
    inverse = lax.rsqrt(total / width + epsilon)
    halves = [slice(i * tokens // 2, (i + 1) * tokens // 2) for i in range(2)]
    for d in range(4):
        columns = pl.ds(pl.multiple_of((own ^ d) * block, block), block)
        normed = resid_ref[:, columns].astype(jnp.float32) * inverse * gain_ref[:, columns]
        for here, ref in zip(halves, row_refs):
            ref[:, d * block : (d + 1) * block] = normed[here].astype(jnp.bfloat16)
    place = lax.broadcasted_iota(jnp.int32, (LANES, tokens), 0)
    gates = jnp.zeros((LANES, tokens), jnp.float32)
    for k in range(TOPK):
        gates += jnp.where(ids_ref[k : k + 1] == place % TOPK, gates_ref[k : k + 1], 0.0)
    high = gates.astype(jnp.bfloat16).astype(jnp.float32)
    middle = (gates - high).astype(jnp.bfloat16).astype(jnp.float32)
    low = gates - high - middle
    part = place // TOPK
    terms = jnp.where(part == 0, high, jnp.where(part == 1, middle, jnp.where(part == 2, low, 0.0)))
    terms = jnp.transpose(terms)
    for here, ref in zip(halves, row_refs):
        ref[:, width:] = terms[here].astype(jnp.bfloat16)


def norm(hidden_in, attn, norm_gain, expert_ids, gate_weights):
    tokens, width = hidden_in.shape
    operands = hidden_in, norm_gain[None, :], expert_ids.T, gate_weights.T
    return pl.pallas_call(
        norm_kernel,
        out_shape=[
            jax.ShapeDtypeStruct((tokens, width), jnp.bfloat16),
        ]
        + [jax.ShapeDtypeStruct((tokens // 2, width + LANES), jnp.bfloat16)] * 2,
        in_specs=[pl.BlockSpec(memory_space=pl.ANY)] * 8,
        out_specs=vmem(3),
        scratch_shapes=[pltpu.VMEM(attn[0].shape, jnp.bfloat16)] * 4
        + [pltpu.VMEM(x.shape, x.dtype) for x in operands]
        + [pltpu.SemaphoreType.DMA((8,))],
        compiler_params=params(),
        cost_estimate=SMALL,
        name="norm",
    )(*attn, *operands)


def cast_kernel(spans, *refs):
    count = len(spans)
    sources, targets, scratch = refs[:count], refs[count : 2 * count], refs[2 * count :]
    wide, narrow, arrived, left = scratch[:count], scratch[count : 2 * count], *scratch[-2:]

    def rows_of(i, step, first=0):
        rows = wide[i].shape[0] // CAST_STEPS
        return pl.ds(first + step * rows, rows)

    def copies_in(step):
        for i, (first, _, column, columns) in enumerate(spans):
            yield pltpu.make_async_copy(
                sources[i].at[0, rows_of(i, step, first), pl.ds(column, columns)],
                wide[i].at[rows_of(i, step)],
                arrived.at[step, i],
            )

    def copies_out(step):
        for i in range(count):
            here = rows_of(i, step)
            yield pltpu.make_async_copy(narrow[i].at[here], targets[i].at[here], left.at[step, i])

    for step in range(CAST_STEPS):
        for copy in copies_in(step):
            copy.start()
    for step in range(CAST_STEPS):
        for copy in copies_in(step):
            copy.wait()
        for i in range(count):
            here = rows_of(i, step)
            narrow[i][here] = wide[i][here].astype(jnp.bfloat16)
        for copy in copies_out(step):
            copy.start()
    for step in range(CAST_STEPS):
        for copy in copies_out(step):
            copy.wait()


def cast_rows(arrays, spans):
    shapes = [(rows, columns) for _, rows, _, columns in spans]
    return pl.pallas_call(
        lambda *refs: cast_kernel(spans, *refs),
        out_shape=[jax.ShapeDtypeStruct(shape, jnp.bfloat16) for shape in shapes],
        in_specs=[pl.BlockSpec(memory_space=pltpu.HBM)] * len(arrays),
        out_specs=[pl.BlockSpec(memory_space=pltpu.HBM)] * len(arrays),
        scratch_shapes=[pltpu.VMEM(shape, jnp.float32) for shape in shapes]
        + [pltpu.VMEM(shape, jnp.bfloat16) for shape in shapes]
        + [pltpu.SemaphoreType.DMA((CAST_STEPS, len(arrays)))] * 2,
        compiler_params=params(VMEM_MOST),
        name="cast_rows",
    )(*arrays)


def load_tiles(pieces, starts, weights, arrived, tiles, block):
    def copies(tile):
        first = 0
        for index, (piece, start) in enumerate(zip(pieces, starts)):
            depth = piece.shape[0]
            for part in range(2):
                column = (part * tiles + tile) * block
                yield pltpu.make_async_copy(
                    piece.at[:, pl.ds(start + column, block)],
                    weights.at[pl.ds(first, depth), pl.ds(column, block)],
                    arrived.at[tile, index, part],
                )
            first += depth

    for tile in range(tiles):
        for copy in copies(tile):
            copy.start()

    def wait(tile):
        for copy in copies(tile):
            copy.wait()

    return wait


def row_copies(pieces, weights, arrived):
    first = 0
    for i, ref in enumerate(pieces):
        depth = ref.shape[0]
        yield pltpu.make_async_copy(ref, weights.at[pl.ds(first, depth)], arrived.at[i])
        first += depth


def start_rows(pieces, weights, arrived):
    for copy in row_copies(pieces, weights, arrived):
        copy.start()


def wait_rows(pieces, weights, arrived):
    for copy in row_copies(pieces, weights, arrived):
        copy.wait()


def up_kernel(sources, starts, *refs):
    pieces = len(starts)
    row_refs = refs[:sources]
    weight_refs = refs[sources : sources + pieces]
    down_refs, refs = refs[sources + pieces : -9], refs[-9:]
    hidden_ref, own_gate_ref, total_ref, rows, weights, units, down, arrived, down_arrived = refs
    start_rows(down_refs, down, down_arrived)
    width = rows.shape[1]
    tiles, _, block = units.shape
    wait = load_tiles(weight_refs, starts, weights, arrived, tiles, block)
    expert = lax.axis_index("expert")
    first = 0
    for ref in row_refs:
        count = ref.shape[0]
        here = slice(first, first + count)
        rows[here, :] = ref[:, :width]
        terms = ref[:, width:].astype(jnp.float32)
        lane = lax.broadcasted_iota(jnp.int32, terms.shape, 1)
        own_gate_ref[here, :] = jnp.sum(
            jnp.where(lane % TOPK == expert, terms, 0.0), axis=-1, keepdims=True
        )
        first += count
    for tile in range(tiles):
        wait(tile)
        gate, up = (
            jnp.dot(
                rows[...],
                weights[:, (part * tiles + tile) * block : (part * tiles + tile + 1) * block],
                preferred_element_type=jnp.float32,
            )
            for part in range(2)
        )
        units[tile] = (gate / (1.0 + jnp.exp(-gate)) * up).astype(jnp.bfloat16)
    own = lax.axis_index("dp")
    for d in range(4):
        hidden_ref[:, d * block : (d + 1) * block] = units[own ^ d]
    wait_rows(down_refs, down, down_arrived)
    total_ref[...] = jnp.dot(
        hidden_ref[:, : down.shape[0]], down[...], preferred_element_type=jnp.float32
    )


def expert_up(rows, weights, width, down):
    weights, starts = zip(*weights)
    tokens = sum(piece.shape[0] for piece in rows)
    features = sum(piece.shape[0] for piece in weights)
    hidden_size = width // 2
    return pl.pallas_call(
        lambda *refs: up_kernel(len(rows), starts, *refs),
        out_shape=[
            jax.ShapeDtypeStruct((tokens, hidden_size), jnp.bfloat16),
            jax.ShapeDtypeStruct((tokens, 1), jnp.float32),
            jax.ShapeDtypeStruct((tokens, down[0].shape[1]), jnp.float32),
        ],
        in_specs=vmem(len(rows)) + [pl.BlockSpec(memory_space=pl.ANY)] * (len(weights) + len(down)),
        out_specs=vmem(3),
        scratch_shapes=[
            pltpu.VMEM((tokens, features), jnp.bfloat16),
            pltpu.VMEM((features, width), jnp.bfloat16),
            pltpu.VMEM((4, tokens, hidden_size // 4), jnp.bfloat16),
            pltpu.VMEM((sum(x.shape[0] for x in down), down[0].shape[1]), jnp.bfloat16),
            pltpu.SemaphoreType.DMA((4, len(weights), 2)),
            pltpu.SemaphoreType.DMA((len(down),)),
        ],
        compiler_params=params(),
        cost_estimate=SMALL,
        name="expert_up",
    )(*rows, *weights, *down)


def part_kernel(first, hidden_ref, before_ref, *refs):
    pieces, (total_ref, weights, arrived) = refs[:-3], refs[-3:]
    start_rows(pieces, weights, arrived)
    wait_rows(pieces, weights, arrived)
    units = hidden_ref[:, first : first + weights.shape[0]]
    total_ref[...] = before_ref[...] + jnp.dot(
        units, weights[...], preferred_element_type=jnp.float32
    )


def down_part(hidden_units, before, weights, first):
    depth = sum(piece.shape[0] for piece in weights)
    return pl.pallas_call(
        lambda *refs: part_kernel(first, *refs),
        out_shape=jax.ShapeDtypeStruct(before.shape, jnp.float32),
        in_specs=vmem(2) + [pl.BlockSpec(memory_space=pl.ANY)] * len(weights),
        out_specs=pl.BlockSpec(memory_space=pltpu.VMEM),
        scratch_shapes=[
            pltpu.VMEM((depth, before.shape[1]), jnp.bfloat16),
            pltpu.SemaphoreType.DMA((len(weights),)),
        ],
        compiler_params=params(),
        cost_estimate=SMALL,
        name="down_part",
    )(hidden_units, before, *weights)


def down_kernel(first, column, sources, hidden_ref, total_ref, gate_ref, piece, *refs):
    outs, (weights, arrived) = refs[:-2], refs[-2:]
    start_rows([piece], weights, arrived)
    wait_rows([piece], weights, arrived)
    depth, width = weights.shape
    units = hidden_ref[:, first : first + depth]
    total = total_ref[:, column : column + width] + jnp.dot(
        units, weights[...], preferred_element_type=jnp.float32
    )
    weighted = (total * gate_ref[...]).astype(jnp.bfloat16)
    rows = weighted.shape[0] // sources
    for (first, count), ref in zip(down_blocks(rows, sources), outs):
        ref[...] = weighted[first : first + count]


def down_blocks(rows, sources):
    half, reach = rows // 2, sources // 2
    blocks = [(0, rows)]
    for step, middle in ((-1, reach * rows), (1, reach * rows + half)):
        blocks.append((middle, half))
        second = (reach + step) * rows
        blocks += [(second, half), (second + half, half)]
        blocks += [((reach + step * away) * rows, rows) for away in range(2, reach)]
    return blocks


def expert_down(hidden_units, total, gates, weights, column, sources):
    tokens, hidden_size = hidden_units.shape
    depth, width = weights.shape
    rows = tokens // sources
    return pl.pallas_call(
        lambda *refs: down_kernel(hidden_size - depth, column, sources, *refs),
        out_shape=[
            jax.ShapeDtypeStruct((count, width), jnp.bfloat16)
            for _, count in down_blocks(rows, sources)
        ],
        in_specs=vmem(3) + [pl.BlockSpec(memory_space=pl.ANY)],
        out_specs=vmem(sources + 3),
        scratch_shapes=[
            pltpu.VMEM((depth, width), jnp.bfloat16),
            pltpu.SemaphoreType.DMA((1,)),
        ],
        compiler_params=params(),
        cost_estimate=SMALL,
        name="expert_down",
    )(hidden_units, total, gates, weights)


def partner(x, distance):
    return lax.ppermute(x, "dp", [(i, i ^ distance) for i in range(4)])


def ring_order(count):
    return list(range(0, count, 2)) + list(range(count - 1, 0, -2))


def around(x, step):
    ring = ring_order(lax.axis_size("expert"))
    count = len(ring)
    return lax.ppermute(x, "expert", [(ring[i], ring[(i + step) % count]) for i in range(count)])


def after(x, *others):
    return lax.optimization_barrier((x, *others))[0]


def add(a, b):
    return (a.astype(jnp.float32) + b.astype(jnp.float32)).astype(jnp.bfloat16)


def gather_rows(halves):
    reach = lax.axis_size("expert") // 2
    above, below = [halves], [halves]
    for _ in range(reach - 1):
        above.append([around(half, -1) for half in above[-1]])
        below.append([around(half, 1) for half in below[-1]])
    far = [around(above[-1][0], -1), around(below[-1][1], 1)]
    rows = [half for pair in (*above, far, *below[:0:-1]) for half in pair]
    return rows, [(*a, *b) for a, b in zip(above[1:], below[1:])] + [tuple(far)]


def scatter_sum(own, *blocks):
    reach = len(blocks) // 2
    terms = [own]
    for step, (far, first, second, *near) in ((1, blocks[:reach]), (-1, blocks[reach:])):
        moving = around(far, step)
        if step > 0:
            moving = jnp.concatenate([add(first, moving), second])
        else:
            moving = jnp.concatenate([first, add(second, moving)])
        for block in near:
            moving = add(block, around(moving, step))
        terms.append(around(moving, step))
    return terms


def relayed(x, rows):
    return [partner(x[i : i + rows], 1) for i in range(0, x.shape[0], rows)]


def mix_kernel(resid_ref, *refs):
    terms, out_ref = refs[:-1], refs[-1]
    first = 0
    for i in range(0, len(terms), 3):
        columns = slice(first, first + terms[i].shape[1])
        total = resid_ref[:, columns].astype(jnp.float32)
        for ref in terms[i : i + 3]:
            total += ref[...].astype(jnp.float32)
        out_ref[0, :, columns] = total.astype(jnp.bfloat16)
        first = columns.stop


def mix(resid, halves):
    terms = [term for half in halves for term in half]
    return pl.pallas_call(
        mix_kernel,
        out_shape=jax.ShapeDtypeStruct((1, *resid.shape), jnp.bfloat16),
        in_specs=vmem(1 + len(terms)),
        out_specs=pl.BlockSpec(memory_space=pltpu.VMEM),
        compiler_params=params(),
        cost_estimate=SMALL,
        name="mix",
    )(resid, *terms)


def every_expert(
    hidden_in,
    queries,
    key_pool,
    value_pool,
    page_table,
    prompt_lengths,
    expert_ids,
    gate_weights,
    norm_gain,
    trainer_gate_up,
    trainer_down,
):
    expert_count = lax.axis_size("expert")
    width = trainer_down.shape[2]
    depth, columns = trainer_gate_up.shape[1:]
    down_depth = trainer_down.shape[1]
    slab = width // SLABS
    early = queries.shape[1] // 4 * FIRST_BLOCKS
    side = [i * columns for i in range(FIRST_BLOCKS)]
    attn_own, attn_beside, first_sent = attention(
        queries,
        key_pool,
        value_pool,
        page_table,
        prompt_lengths,
        trainer_gate_up,
        FIRST_BLOCKS,
    )
    first_across = partner(first_sent, 2)
    gate_up = after(trainer_gate_up, attn_own)
    rest_own, first_own, down_own = cast_rows(
        [gate_up, gate_up, trainer_down],
        [
            (early, depth - early, 0, columns),
            (0, early, 0, columns),
            (0, down_depth, 0, width),
        ],
    )
    attn_beside = partner(attn_beside, 1)
    attn_opposite = partner(first_across[:, -attn_own.shape[1] :], 1)
    rest_across = partner(rest_own, 2)
    resid, *halves = norm(
        after(hidden_in[0], rest_own),
        (attn_own, attn_beside, first_across, attn_opposite),
        norm_gain,
        expert_ids[0],
        gate_weights[0],
    )
    gathered, arrived = gather_rows(halves)
    first_beside = partner(after(first_own, *arrived[0]), 1)
    rest_beside = partner(after(rest_own, *arrived[0]), 1)
    first_ready = after(first_across, *arrived[0])
    first_opposite = [partner(first_ready[:, start : start + columns], 1) for start in side]
    down_beside = partner(after(down_own, *arrived[1]), 1)
    down_across = partner(after(down_own, *arrived[2]), 2)
    rest_opposite = relayed(after(rest_across, *arrived[3]), (depth - early) // 2)
    hidden_units, gates, total = expert_up(
        gathered,
        [(ref, 0) for ref in (first_own, rest_own, first_beside, rest_beside)]
        + [(first_across, start) for start in side]
        + [(ref, 0) for ref in (rest_across, *first_opposite, *rest_opposite)],
        columns,
        [down_own],
    )
    down_ready = after(down_across, hidden_units)
    total = down_part(hidden_units, total, [down_beside, down_ready], down_depth)
    mixed = []
    for first in range(0, width, slab):
        opposite = partner(down_ready[:, first : first + slab], 1)
        weighted = expert_down(hidden_units, total, gates, opposite, first, expert_count)
        mixed.append(scatter_sum(*weighted))
    return mix(resid, mixed)


def solution(mesh):
    placed = (
        P("expert", "dp", None),
        P("expert", None, "dp"),
        P("expert", None, "dp"),
        P("expert", None, "dp"),
        P("expert", None),
        P("expert", None),
        P("expert", "dp", None),
        P("expert", "dp", None),
        P(),
        P("expert", "dp", None),
        P("expert", "dp", None),
    )
    dense = mesh.shape["expert"] == TOPK and mesh.shape["dp"] == 4
    return jax.shard_map(
        every_expert if dense else local, mesh=mesh, in_specs=placed, out_specs=P("expert", "dp", None), check_vma=False
    )
```

```python
import math

import jax
import jax.numpy as jnp
from jax import lax
from jax.experimental import pallas as pl
from jax.experimental.pallas import tpu as pltpu
from jax.sharding import PartitionSpec as P

HDIM = 128
TOPK = 8


epsilon = 1e-05


def fetch_weights(trainer_gate_up, trainer_down):
    return (
        lax.all_gather(trainer_gate_up.astype(jnp.bfloat16), "dp", axis=1, tiled=True),
        lax.all_gather(trainer_down.astype(jnp.bfloat16), "dp", axis=1, tiled=True),
    )


def local(
    hidden_in,
    queries,
    key_pool,
    value_pool,
    page_table,
    prompt_lengths,
    expert_ids,
    gate_weights,
    norm_gain,
    trainer_gate_up,
    trainer_down,
):
    col_tok = queries.shape[1]
    width_dev = queries.shape[2]
    heads_dev = width_dev // HDIM
    keys_all = jnp.take(key_pool, page_table[0], axis=0).reshape(col_tok, heads_dev, HDIM)
    values_all = jnp.take(value_pool, page_table[0], axis=0).reshape(col_tok, heads_dev, HDIM)
    request_ends = jnp.cumsum(prompt_lengths[0])
    positions = lax.iota(jnp.int32, col_tok)
    request = jnp.sum((positions[:, None] >= request_ends[None, :]).astype(jnp.int32), axis=1)
    block_rows = math.gcd(col_tok, 512)
    query_blocks = queries[0].reshape(col_tok // block_rows, block_rows, heads_dev, HDIM)
    request_blocks = request.reshape(col_tok // block_rows, block_rows)
    score_scale = 1.0 / math.sqrt(HDIM)

    def attend(pieces):
        query_block, request_block = pieces
        scores = (
            jnp.einsum("qhd,khd->hqk", query_block, keys_all, preferred_element_type=jnp.float32)
            * score_scale
        )
        same_request = (request_block[:, None] == request[None, :])[None]
        scores = jnp.where(same_request, scores, -1e30)
        highest = jnp.max(scores, axis=-1, keepdims=True)
        weights = jnp.where(same_request, jnp.exp(scores - highest), 0.0)
        totals = jnp.sum(weights, axis=-1, keepdims=True)
        probs = (weights / totals).astype(jnp.bfloat16)
        output = jnp.einsum("hqk,khd->qhd", probs, values_all, preferred_element_type=jnp.float32)
        return output.astype(jnp.bfloat16).reshape(block_rows, width_dev)

    attn_heads = lax.map(attend, (query_blocks, request_blocks)).reshape(1, col_tok, width_dev)
    attn_tokens = lax.all_to_all(attn_heads, "dp", split_axis=1, concat_axis=2, tiled=True)
    resid32 = (
        (hidden_in.astype(jnp.float32) + attn_tokens.astype(jnp.float32))
        .astype(jnp.bfloat16)
        .astype(jnp.float32)
    )
    mean_square = jnp.mean(resid32 * resid32, axis=-1, keepdims=True)
    normed = (resid32 * lax.rsqrt(mean_square + epsilon) * norm_gain).astype(jnp.bfloat16)
    server_gate_up, server_down = fetch_weights(trainer_gate_up, trainer_down)
    token_rows = normed.shape[1]
    width = normed.shape[2]
    expert_count = lax.axis_size("expert")
    capacity = min(token_rows, token_rows * TOPK * 5 // (4 * expert_count))
    hidden_size = server_gate_up.shape[2] // 2
    ids_flat = expert_ids[0].reshape(token_rows * TOPK)
    onehot = (ids_flat[:, None] == lax.iota(jnp.int32, expert_count)[None, :]).astype(jnp.int32)
    earlier = jnp.cumsum(onehot, axis=0) - onehot
    slot_index = jnp.sum(earlier * onehot, axis=1)
    flat_slot = ids_flat * capacity + slot_index
    placement = (
        flat_slot[:, None] == lax.iota(jnp.int32, expert_count * capacity)[None, :]
    ).astype(jnp.bfloat16)
    dispatch_matrix = jnp.sum(placement.reshape(token_rows, TOPK, expert_count * capacity), axis=1)
    outgoing = jnp.einsum(
        "ts,td->sd", dispatch_matrix, normed[0], preferred_element_type=jnp.float32
    )
    outgoing = outgoing.astype(jnp.bfloat16).reshape(expert_count, capacity, width)
    received = lax.all_to_all(outgoing, "expert", split_axis=0, concat_axis=0, tiled=True)
    sources, items, features = received.shape
    slot_rows = received.reshape(sources * items, features)
    gate_up = jnp.dot(slot_rows, server_gate_up[0], preferred_element_type=jnp.float32)
    hidden_units = (jax.nn.silu(gate_up[:, :hidden_size]) * gate_up[:, hidden_size:]).astype(
        jnp.bfloat16
    )
    outputs = jnp.dot(hidden_units, server_down[0], preferred_element_type=jnp.float32).astype(
        jnp.bfloat16
    )
    returned = lax.all_to_all(
        outputs.reshape(sources, items, features), "expert", split_axis=0, concat_axis=0, tiled=True
    )
    copies = jnp.take(returned.reshape(expert_count * capacity, width), flat_slot, axis=0)
    copies = copies.reshape(token_rows, TOPK, width).astype(jnp.float32)
    mixture = jnp.einsum("tk,tkd->td", gate_weights[0], copies)
    mixed = resid32[0] + mixture
    return mixed.astype(jnp.bfloat16)[None]

LANES = 128
VMEM_LIMIT = 32 * 2**20
VMEM_MOST = 60 * 2**20
CAST_STEPS = 4
FIRST_BLOCKS = 2
SLABS = 2
SMALL = pl.CostEstimate(flops=1, bytes_accessed=1, transcendentals=0)


def params(limit=VMEM_LIMIT):
    return pltpu.CompilerParams(vmem_limit_bytes=limit)


def vmem(count):
    return [pl.BlockSpec(memory_space=pltpu.VMEM)] * count


def attention_kernel(*refs):
    sources, outs, scratch = refs[:6], refs[6:9], refs[9:]
    own_ref, beside_ref, sent_ref = outs
    table, lengths, q_ref, k_ref, v_ref, weights, attn, arrived = scratch
    copies = [
        pltpu.make_async_copy(source, target, arrived.at[i])
        for i, (source, target) in enumerate(
            zip(
                (*sources[:2], sources[2].at[0], *sources[3:5]),
                (table, lengths, q_ref, k_ref, v_ref),
            )
        )
    ]
    rows = weights.shape[0]
    copies.append(
        pltpu.make_async_copy(sources[5].at[0, pl.ds(0, rows)], weights, arrived.at[5])
    )
    for copy in copies:
        copy.start()
    for copy in copies[:5]:
        copy.wait()
    tokens, width = q_ref.shape
    pages = k_ref.shape[0]
    row = lax.broadcasted_iota(jnp.int32, (tokens, 1), 0)
    column = lax.broadcasted_iota(jnp.int32, (1, tokens), 1)
    row_request = jnp.zeros((tokens, 1), jnp.int32)
    column_request = jnp.zeros((1, tokens), jnp.int32)
    end = jnp.int32(0)
    for r in range(lengths.shape[1]):
        end = end + lengths[0, r]
        row_request += (row >= end).astype(jnp.int32)
        column_request += (column >= end).astype(jnp.int32)
    same = row_request == column_request
    for h in range(width // HDIM):
        lanes = slice(h * HDIM, (h + 1) * HDIM)
        keys = jnp.concatenate([k_ref[table[0, p], :, lanes] for p in range(pages)], axis=0)
        values = jnp.concatenate([v_ref[table[0, p], :, lanes] for p in range(pages)], axis=0)
        scores = lax.dot_general(
            q_ref[:, lanes], keys, (((1,), (1,)), ((), ())), preferred_element_type=jnp.float32
        ) * (1.0 / math.sqrt(HDIM))
        scores = jnp.where(same, scores, -1e30)
        highest = jnp.max(scores, axis=-1, keepdims=True)
        weight = jnp.exp(scores - highest)
        share = 1.0 / jnp.sum(weight, axis=-1, keepdims=True)
        probs = (weight * share).astype(jnp.bfloat16)
        attn[:, lanes] = jnp.dot(probs, values, preferred_element_type=jnp.float32).astype(
            jnp.bfloat16
        )
    own = lax.axis_index("dp")
    block = tokens // 4
    split = weights.shape[1]
    end = sent_ref.shape[1]
    targets = (
        own_ref,
        beside_ref,
        sent_ref.at[:, end - 2 * width : end - width],
        sent_ref.at[:, end - width :],
    )
    for d, target in enumerate(targets):
        target[...] = attn[pl.ds(pl.multiple_of((own ^ d) * block, block), block), :]
    copies[5].wait()
    for i in range(rows // block):
        here = slice(i * block, (i + 1) * block)
        sent_ref[:, i * split : (i + 1) * split] = weights[here].astype(jnp.bfloat16)


def attention(queries, key_pool, value_pool, page_table, prompt_lengths, gate_up, blocks):
    tokens, width = queries.shape[1:]
    split = gate_up.shape[2]
    block = tokens // 4
    shapes = [(block, width)] * 2
    shapes.append((block, blocks * split + 2 * width))
    return pl.pallas_call(
        attention_kernel,
        out_shape=[jax.ShapeDtypeStruct(shape, jnp.bfloat16) for shape in shapes],
        in_specs=[pl.BlockSpec(memory_space=pltpu.HBM)] * 6,
        out_specs=vmem(3),
        scratch_shapes=[
            pltpu.SMEM(page_table.shape, jnp.int32),
            pltpu.SMEM(prompt_lengths.shape, jnp.int32),
            pltpu.VMEM((tokens, width), jnp.bfloat16),
            pltpu.VMEM(key_pool.shape, jnp.bfloat16),
            pltpu.VMEM(value_pool.shape, jnp.bfloat16),
            pltpu.VMEM((blocks * block, split), jnp.float32),
            pltpu.VMEM((tokens, width), jnp.bfloat16),
            pltpu.SemaphoreType.DMA((6,)),
        ],
        compiler_params=params(VMEM_MOST),
        name="attention",
    )(page_table, prompt_lengths, queries, key_pool, value_pool, gate_up)


def norm_kernel(*refs):
    sources, outs, scratch = refs[:8], refs[8:11], refs[11:]
    a0, a1, a2, a3, hidden_ref, gain_ref, ids_ref, gates_ref, arrived = scratch
    resid_ref, row_refs = outs[0], outs[1:]
    across, block = sources[2], a2.shape[1]
    across = across.at[:, pl.ds(across.shape[1] - 2 * block, block)]
    copies = [
        pltpu.make_async_copy(source, target, arrived.at[i])
        for i, (source, target) in enumerate(zip((*sources[:2], across, *sources[3:]), scratch))
    ]
    for copy in copies:
        copy.start()
    for copy in copies:
        copy.wait()
    own = lax.axis_index("dp")
    tokens, width = hidden_ref.shape
    total = jnp.zeros((tokens, 1), jnp.float32)
    for d, attn in enumerate((a0, a1, a2, a3)):
        columns = pl.ds(pl.multiple_of((own ^ d) * block, block), block)
        resid = (
            hidden_ref[:, columns].astype(jnp.float32) + attn[...].astype(jnp.float32)
        ).astype(jnp.bfloat16)
        resid_ref[:, columns] = resid
        resid32 = resid.astype(jnp.float32)
        total += jnp.sum(resid32 * resid32, axis=-1, keepdims=True)
    inverse = lax.rsqrt(total / width + epsilon)
    halves = [slice(i * tokens // 2, (i + 1) * tokens // 2) for i in range(2)]
    for d in range(4):
        columns = pl.ds(pl.multiple_of((own ^ d) * block, block), block)
        normed = resid_ref[:, columns].astype(jnp.float32) * inverse * gain_ref[:, columns]
        for here, ref in zip(halves, row_refs):
            ref[:, d * block : (d + 1) * block] = normed[here].astype(jnp.bfloat16)
    place = lax.broadcasted_iota(jnp.int32, (LANES, tokens), 0)
    gates = jnp.zeros((LANES, tokens), jnp.float32)
    for k in range(TOPK):
        gates += jnp.where(ids_ref[k : k + 1] == place % TOPK, gates_ref[k : k + 1], 0.0)
    high = gates.astype(jnp.bfloat16).astype(jnp.float32)
    middle = (gates - high).astype(jnp.bfloat16).astype(jnp.float32)
    low = gates - high - middle
    part = place // TOPK
    terms = jnp.where(part == 0, high, jnp.where(part == 1, middle, jnp.where(part == 2, low, 0.0)))
    terms = jnp.transpose(terms)
    for here, ref in zip(halves, row_refs):
        ref[:, width:] = terms[here].astype(jnp.bfloat16)


def norm(hidden_in, attn, norm_gain, expert_ids, gate_weights):
    tokens, width = hidden_in.shape
    operands = hidden_in, norm_gain[None, :], expert_ids.T, gate_weights.T
    return pl.pallas_call(
        norm_kernel,
        out_shape=[
            jax.ShapeDtypeStruct((tokens, width), jnp.bfloat16),
        ]
        + [jax.ShapeDtypeStruct((tokens // 2, width + LANES), jnp.bfloat16)] * 2,
        in_specs=[pl.BlockSpec(memory_space=pl.ANY)] * 8,
        out_specs=vmem(3),
        scratch_shapes=[pltpu.VMEM(attn[0].shape, jnp.bfloat16)] * 4
        + [pltpu.VMEM(x.shape, x.dtype) for x in operands]
        + [pltpu.SemaphoreType.DMA((8,))],
        compiler_params=params(),
        cost_estimate=SMALL,
        name="norm",
    )(*attn, *operands)


def cast_kernel(spans, *refs):
    count = len(spans)
    sources, targets, scratch = refs[:count], refs[count : 2 * count], refs[2 * count :]
    wide, narrow, arrived, left = scratch[:count], scratch[count : 2 * count], *scratch[-2:]

    def rows_of(i, step, first=0):
        rows = wide[i].shape[0] // CAST_STEPS
        return pl.ds(first + step * rows, rows)

    def copies_in(step):
        for i, (first, _, column, columns) in enumerate(spans):
            yield pltpu.make_async_copy(
                sources[i].at[0, rows_of(i, step, first), pl.ds(column, columns)],
                wide[i].at[rows_of(i, step)],
                arrived.at[step, i],
            )

    def copies_out(step):
        for i in range(count):
            here = rows_of(i, step)
            yield pltpu.make_async_copy(narrow[i].at[here], targets[i].at[here], left.at[step, i])

    for step in range(CAST_STEPS):
        for copy in copies_in(step):
            copy.start()
    for step in range(CAST_STEPS):
        for copy in copies_in(step):
            copy.wait()
        for i in range(count):
            here = rows_of(i, step)
            narrow[i][here] = wide[i][here].astype(jnp.bfloat16)
        for copy in copies_out(step):
            copy.start()
    for step in range(CAST_STEPS):
        for copy in copies_out(step):
            copy.wait()


def cast_rows(arrays, spans):
    shapes = [(rows, columns) for _, rows, _, columns in spans]
    return pl.pallas_call(
        lambda *refs: cast_kernel(spans, *refs),
        out_shape=[jax.ShapeDtypeStruct(shape, jnp.bfloat16) for shape in shapes],
        in_specs=[pl.BlockSpec(memory_space=pltpu.HBM)] * len(arrays),
        out_specs=[pl.BlockSpec(memory_space=pltpu.HBM)] * len(arrays),
        scratch_shapes=[pltpu.VMEM(shape, jnp.float32) for shape in shapes]
        + [pltpu.VMEM(shape, jnp.bfloat16) for shape in shapes]
        + [pltpu.SemaphoreType.DMA((CAST_STEPS, len(arrays)))] * 2,
        compiler_params=params(VMEM_MOST),
        name="cast_rows",
    )(*arrays)


def load_tiles(pieces, starts, weights, arrived, tiles, block):
    def copies(tile):
        first = 0
        for index, (piece, start) in enumerate(zip(pieces, starts)):
            depth = piece.shape[0]
            for part in range(2):
                column = (part * tiles + tile) * block
                yield pltpu.make_async_copy(
                    piece.at[:, pl.ds(start + column, block)],
                    weights.at[pl.ds(first, depth), pl.ds(column, block)],
                    arrived.at[tile, index, part],
                )
            first += depth

    for tile in range(tiles):
        for copy in copies(tile):
            copy.start()

    def wait(tile):
        for copy in copies(tile):
            copy.wait()

    return wait


def row_copies(pieces, weights, arrived):
    first = 0
    for i, ref in enumerate(pieces):
        depth = ref.shape[0]
        yield pltpu.make_async_copy(ref, weights.at[pl.ds(first, depth)], arrived.at[i])
        first += depth


def start_rows(pieces, weights, arrived):
    for copy in row_copies(pieces, weights, arrived):
        copy.start()


def wait_rows(pieces, weights, arrived):
    for copy in row_copies(pieces, weights, arrived):
        copy.wait()


def up_kernel(sources, starts, *refs):
    pieces = len(starts)
    row_refs = refs[:sources]
    weight_refs = refs[sources : sources + pieces]
    down_refs, refs = refs[sources + pieces : -9], refs[-9:]
    hidden_ref, own_gate_ref, total_ref, rows, weights, units, down, arrived, down_arrived = refs
    start_rows(down_refs, down, down_arrived)
    width = rows.shape[1]
    tiles, _, block = units.shape
    wait = load_tiles(weight_refs, starts, weights, arrived, tiles, block)
    expert = lax.axis_index("expert")
    first = 0
    for ref in row_refs:
        count = ref.shape[0]
        here = slice(first, first + count)
        rows[here, :] = ref[:, :width]
        terms = ref[:, width:].astype(jnp.float32)
        lane = lax.broadcasted_iota(jnp.int32, terms.shape, 1)
        own_gate_ref[here, :] = jnp.sum(
            jnp.where(lane % TOPK == expert, terms, 0.0), axis=-1, keepdims=True
        )
        first += count
    for tile in range(tiles):
        wait(tile)
        gate, up = (
            jnp.dot(
                rows[...],
                weights[:, (part * tiles + tile) * block : (part * tiles + tile + 1) * block],
                preferred_element_type=jnp.float32,
            )
            for part in range(2)
        )
        units[tile] = (gate / (1.0 + jnp.exp(-gate)) * up).astype(jnp.bfloat16)
    own = lax.axis_index("dp")
    for d in range(4):
        hidden_ref[:, d * block : (d + 1) * block] = units[own ^ d]
    wait_rows(down_refs, down, down_arrived)
    total_ref[...] = jnp.dot(
        hidden_ref[:, : down.shape[0]], down[...], preferred_element_type=jnp.float32
    )


def expert_up(rows, weights, width, down):
    weights, starts = zip(*weights)
    tokens = sum(piece.shape[0] for piece in rows)
    features = sum(piece.shape[0] for piece in weights)
    hidden_size = width // 2
    return pl.pallas_call(
        lambda *refs: up_kernel(len(rows), starts, *refs),
        out_shape=[
            jax.ShapeDtypeStruct((tokens, hidden_size), jnp.bfloat16),
            jax.ShapeDtypeStruct((tokens, 1), jnp.float32),
            jax.ShapeDtypeStruct((tokens, down[0].shape[1]), jnp.float32),
        ],
        in_specs=vmem(len(rows)) + [pl.BlockSpec(memory_space=pl.ANY)] * (len(weights) + len(down)),
        out_specs=vmem(3),
        scratch_shapes=[
            pltpu.VMEM((tokens, features), jnp.bfloat16),
            pltpu.VMEM((features, width), jnp.bfloat16),
            pltpu.VMEM((4, tokens, hidden_size // 4), jnp.bfloat16),
            pltpu.VMEM((sum(x.shape[0] for x in down), down[0].shape[1]), jnp.bfloat16),
            pltpu.SemaphoreType.DMA((4, len(weights), 2)),
            pltpu.SemaphoreType.DMA((len(down),)),
        ],
        compiler_params=params(),
        cost_estimate=SMALL,
        name="expert_up",
    )(*rows, *weights, *down)


def part_kernel(first, hidden_ref, before_ref, *refs):
    pieces, (total_ref, weights, arrived) = refs[:-3], refs[-3:]
    start_rows(pieces, weights, arrived)
    wait_rows(pieces, weights, arrived)
    units = hidden_ref[:, first : first + weights.shape[0]]
    total_ref[...] = before_ref[...] + jnp.dot(
        units, weights[...], preferred_element_type=jnp.float32
    )


def down_part(hidden_units, before, weights, first):
    depth = sum(piece.shape[0] for piece in weights)
    return pl.pallas_call(
        lambda *refs: part_kernel(first, *refs),
        out_shape=jax.ShapeDtypeStruct(before.shape, jnp.float32),
        in_specs=vmem(2) + [pl.BlockSpec(memory_space=pl.ANY)] * len(weights),
        out_specs=pl.BlockSpec(memory_space=pltpu.VMEM),
        scratch_shapes=[
            pltpu.VMEM((depth, before.shape[1]), jnp.bfloat16),
            pltpu.SemaphoreType.DMA((len(weights),)),
        ],
        compiler_params=params(),
        cost_estimate=SMALL,
        name="down_part",
    )(hidden_units, before, *weights)


def down_kernel(first, column, sources, hidden_ref, total_ref, gate_ref, piece, *refs):
    depth, width = piece.shape
    units = hidden_ref[:, first : first + depth]
    total = total_ref[:, column : column + width] + jnp.dot(
        units, piece[...], preferred_element_type=jnp.float32
    )
    weighted = (total * gate_ref[...]).astype(jnp.bfloat16)
    rows = weighted.shape[0] // sources
    for (first, count), ref in zip(down_blocks(rows, sources), refs):
        ref[...] = weighted[first : first + count]


def down_blocks(rows, sources):
    half, reach = rows // 2, sources // 2
    blocks = [(0, rows)]
    for step, middle in ((-1, reach * rows), (1, reach * rows + half)):
        blocks.append((middle, half))
        second = (reach + step) * rows
        blocks += [(second, half), (second + half, half)]
        blocks += [((reach + step * away) * rows, rows) for away in range(2, reach)]
    return blocks


def expert_down(hidden_units, total, gates, weights, column, sources):
    tokens, hidden_size = hidden_units.shape
    depth, width = weights.shape
    rows = tokens // sources
    return pl.pallas_call(
        lambda *refs: down_kernel(hidden_size - depth, column, sources, *refs),
        out_shape=[
            jax.ShapeDtypeStruct((count, width), jnp.bfloat16)
            for _, count in down_blocks(rows, sources)
        ],
        in_specs=vmem(4),
        out_specs=vmem(sources + 3),
        compiler_params=params(),
        cost_estimate=SMALL,
        name="expert_down",
    )(hidden_units, total, gates, weights)


def partner(x, distance):
    return lax.ppermute(x, "dp", [(i, i ^ distance) for i in range(4)])


def ring_order(count):
    return list(range(0, count, 2)) + list(range(count - 1, 0, -2))


def around(x, step):
    ring = ring_order(lax.axis_size("expert"))
    count = len(ring)
    return lax.ppermute(x, "expert", [(ring[i], ring[(i + step) % count]) for i in range(count)])


def after(x, *others):
    return lax.optimization_barrier((x, *others))[0]


def add(a, b):
    return (a.astype(jnp.float32) + b.astype(jnp.float32)).astype(jnp.bfloat16)


def gather_rows(halves):
    reach = lax.axis_size("expert") // 2
    above, below = [halves], [halves]
    for _ in range(reach - 1):
        above.append([around(half, -1) for half in above[-1]])
        below.append([around(half, 1) for half in below[-1]])
    far = [around(above[-1][0], -1), around(below[-1][1], 1)]
    rows = [half for pair in (*above, far, *below[:0:-1]) for half in pair]
    return rows, [(*a, *b) for a, b in zip(above[1:], below[1:])] + [tuple(far)]


def scatter_sum(own, *blocks):
    reach = len(blocks) // 2
    terms = [own]
    for step, (far, first, second, *near) in ((1, blocks[:reach]), (-1, blocks[reach:])):
        moving = around(far, step)
        if step > 0:
            moving = jnp.concatenate([add(first, moving), second])
        else:
            moving = jnp.concatenate([first, add(second, moving)])
        for block in near:
            moving = add(block, around(moving, step))
        terms.append(around(moving, step))
    return terms


def relayed(x, rows):
    return [partner(x[i : i + rows], 1) for i in range(0, x.shape[0], rows)]


def mix_kernel(resid_ref, *refs):
    terms, out_ref = refs[:-1], refs[-1]
    first = 0
    for i in range(0, len(terms), 3):
        columns = slice(first, first + terms[i].shape[1])
        total = resid_ref[:, columns].astype(jnp.float32)
        for ref in terms[i : i + 3]:
            total += ref[...].astype(jnp.float32)
        out_ref[0, :, columns] = total.astype(jnp.bfloat16)
        first = columns.stop


def mix(resid, halves):
    terms = [term for half in halves for term in half]
    return pl.pallas_call(
        mix_kernel,
        out_shape=jax.ShapeDtypeStruct((1, *resid.shape), jnp.bfloat16),
        in_specs=vmem(1 + len(terms)),
        out_specs=pl.BlockSpec(memory_space=pltpu.VMEM),
        compiler_params=params(),
        cost_estimate=SMALL,
        name="mix",
    )(resid, *terms)


def every_expert(
    hidden_in,
    queries,
    key_pool,
    value_pool,
    page_table,
    prompt_lengths,
    expert_ids,
    gate_weights,
    norm_gain,
    trainer_gate_up,
    trainer_down,
):
    expert_count = lax.axis_size("expert")
    width = trainer_down.shape[2]
    depth, columns = trainer_gate_up.shape[1:]
    down_depth = trainer_down.shape[1]
    slab = width // SLABS
    early = queries.shape[1] // 4 * FIRST_BLOCKS
    side = [i * columns for i in range(FIRST_BLOCKS)]
    attn_own, attn_beside, first_sent = attention(
        queries,
        key_pool,
        value_pool,
        page_table,
        prompt_lengths,
        trainer_gate_up,
        FIRST_BLOCKS,
    )
    first_across = partner(first_sent, 2)
    gate_up = after(trainer_gate_up, attn_own)
    rest_own, first_own, down_own = cast_rows(
        [gate_up, gate_up, trainer_down],
        [
            (early, depth - early, 0, columns),
            (0, early, 0, columns),
            (0, down_depth, 0, width),
        ],
    )
    attn_beside = partner(attn_beside, 1)
    attn_opposite = partner(first_across[:, -attn_own.shape[1] :], 1)
    rest_across = partner(rest_own, 2)
    resid, *halves = norm(
        after(hidden_in[0], rest_own),
        (attn_own, attn_beside, first_across, attn_opposite),
        norm_gain,
        expert_ids[0],
        gate_weights[0],
    )
    gathered, arrived = gather_rows(halves)
    first_beside = partner(after(first_own, *arrived[0]), 1)
    rest_beside = partner(after(rest_own, *arrived[0]), 1)
    first_ready = after(first_across, *arrived[0])
    first_opposite = [partner(first_ready[:, start : start + columns], 1) for start in side]
    down_beside = partner(after(down_own, *arrived[1]), 1)
    down_across = partner(after(down_own, *arrived[2]), 2)
    rest_opposite = relayed(after(rest_across, *arrived[3]), (depth - early) // 2)
    hidden_units, gates, total = expert_up(
        gathered,
        [(ref, 0) for ref in (first_own, rest_own, first_beside, rest_beside)]
        + [(first_across, start) for start in side]
        + [(ref, 0) for ref in (rest_across, *first_opposite, *rest_opposite)],
        columns,
        [down_own],
    )
    down_ready = after(down_across, hidden_units)
    total = down_part(hidden_units, total, [down_beside, down_ready], down_depth)
    mixed = []
    for first in range(0, width, slab):
        opposite = partner(down_ready[:, first : first + slab], 1)
        weighted = expert_down(hidden_units, total, gates, opposite, first, expert_count)
        mixed.append(scatter_sum(*weighted))
    return mix(resid, mixed)


def solution(mesh):
    placed = (
        P("expert", "dp", None),
        P("expert", None, "dp"),
        P("expert", None, "dp"),
        P("expert", None, "dp"),
        P("expert", None),
        P("expert", None),
        P("expert", "dp", None),
        P("expert", "dp", None),
        P(),
        P("expert", "dp", None),
        P("expert", "dp", None),
    )
    dense = mesh.shape["expert"] == TOPK and mesh.shape["dp"] == 4
    return jax.shard_map(
        every_expert if dense else local, mesh=mesh, in_specs=placed, out_specs=P("expert", "dp", None), check_vma=False
    )
```
